32 devices in a mesh: groups: 2 (over y), seq: 4 (over z), segment: 2 (over x), cfg: 2 (over core).
Axes of the slice: x: 2, y: 2, z: 4, core: 2. Of those that a mesh axis runs over, the one named last changes fastest.
Arguments:
- latent: float32 [2, 64, 64], P(None, ('groups', 'seq')), parts along dimension 1, may hold values from -0.1 to 0.1
- w_embed: bfloat16 [64, 3072], replicated, may hold values from -0.75 to 0.75
- w_qkv: bfloat16 [2, 9216, 3072], P('segment', 'seq'), may hold values from -0.109375 to 0.109375
- w_out: bfloat16 [2, 3072, 3072], P('segment', 'seq'), may hold values from -0.109375 to 0.109375
- mod_table: bfloat16 [50, 3, 3072], replicated, may hold values from -3 to 3
- cond_mod: float32 [2, 4, 3, 3072], P('cfg', ('groups', 'segment')), parts along dimension 1, may hold values from -3 to 3
- stale_kv: bfloat16 [2, 2, 4, 2, 64, 1536], P('segment', 'cfg', 'seq', None, 'groups'), parts along dimension 4, may hold values from -6 to 6
- w_final: bfloat16 [3072, 64], replicated, may hold values from -0.109375 to 0.109375
- w_conv: bfloat16 [27, 16, 512], P(None, None, ('segment', 'cfg')), may hold values from -0.3125 to 0.3125
- patch_order: int32 [4], P('groups'), parts along dimension 0, may hold values from 0 to 1, each once
- timestep: int32 [2], P('groups'), parts along dimension 0, may hold values from 0 to 49
- slab_rows: int32 [8], P('groups'), parts along dimension 0, may hold values from 1 to 4, 8 in all
Outputs:
- velocity: float32 [2, 64, 64], P(None, ('groups', 'seq')), parts along dimension 1
- decoded: bfloat16 [8, 4, 4, 8, 512], P(('groups', 'seq'), None, None, None, ('segment', 'cfg')), parts along dimension 0
The draws below stay inside these ranges and needn't reach their ends.
There are 2 independent parts, one for each index of `groups`. The reference program is written for one: setup_inputs(seed, part) draws one part's arguments, and reference() takes and returns one part's arrays. A program takes and returns all parts, laid end to end along the dimension named above; an argument that names none is the same for every part. Nothing has to cross between parts.
Inputs may be any that keep to these rules, and one draw needn't show every extreme that they name: `patch_order`: each patch once. `slab_rows`: the rows sum to 8; some slab has exactly 4 rows.
All inputs are finite; a program needn't handle non-finite values.
Results may differ from the reference program's by a relative error of at most 0.03.
Values may be sent and summed in bfloat16 or wider, within the bound.
No kernel may reach another device: no remote copies, remote signals or barrier semaphores. Data moves between devices by JAX's collectives and lax.ppermute only.
A program may use at most 128 MiB of HBM per device.

```python
import math
import jax
import jax.numpy as jnp
import numpy as np
from jax import lax

HEADS = 24
HEAD_DIM = 128
D = 3072
LAT_CH = 16
DEC_CH = 512
SCHED_STEPS = 50
MICRO = 2
TOK_DEV = 8
FRAMES = 4
LAT_W = 8
LAYERS = 2
HGROUPS = 4
CYCLE = 1
GHEADS = 6
TOK_PATCH = 32
TOK_LANES = 64
LAT_H = 8
SLAB_MAX = 4
N_SEQ = 4


def steps_of(rng, extent, split, smallest, largest):
    def one(dim, blocks):
        steps = jax.random.uniform(jax.random.fold_in(jax.random.fold_in(rng, 6), dim), (blocks,), jnp.float32, smallest / len(split), largest / len(split))
        return jnp.repeat(jnp.exp(steps), extent[dim] // blocks).reshape((-1,) + (1,) * (len(extent) - dim - 1))

    loudness = one(*split[0])
    for cut in split[1:]:
        loudness = loudness * one(*cut)
    return loudness


def length_profile(number_of, total, limit, skew):
    portions = [(1 << 20) // math.isqrt(standing ** skew) + 1 for standing in range(2, number_of + 1)]
    rest, given = total - limit - (number_of - 1), [1] * (number_of - 1)
    while rest > 0:
        movable = [i for i in range(number_of - 1) if given[i] < limit]
        mass, remaining = sum([portions[i] for i in movable]), rest
        for i in movable:
            extra = min(limit - given[i], max(1, remaining * portions[i] // mass), rest)
            given[i] = given[i] + extra
            rest = rest - extra
    return np.array([limit] + given)


def ragged(own_key, number_of, total, reach, lean):
    if number_of == 2:
        one = jax.random.randint(own_key, (), max(1, total - reach), min(reach, total - 1) + 1)
        return jnp.stack([one, total - one])
    tallies = jnp.asarray(length_profile(number_of, total, reach, lean), jnp.int32)
    twos = (number_of - 1) // 2
    donor, taker = tallies[1:1 + 2 * twos:2], tallies[2:2 + 2 * twos:2]
    margin = jnp.minimum(donor - 1, reach - taker)
    passed = jax.random.randint(jax.random.fold_in(own_key, 1), (twos,), 0, 1 << 20) % (margin + 1)
    tallies = tallies.at[1:1 + 2 * twos:2].set(donor - passed).at[2:2 + 2 * twos:2].set(taker + passed)
    return tallies[jax.random.permutation(jax.random.fold_in(own_key, 2), number_of)]


def normal_values(rng, shape, scale, reach, cuts=(), kind=jnp.bfloat16):
    values = scale * jax.random.normal(rng, shape, jnp.float32)
    if cuts:
        values = values * steps_of(rng, shape, cuts, -0.22, 0.18)
    return jnp.clip(values, -reach, reach).astype(kind)


def setup_inputs(seed: int = 0, part: int = 0) -> dict:
    arg_keys = jax.random.split(jax.random.key(seed), 13)
    part_splits = jax.random.split(jax.random.fold_in(arg_keys[12], part), 13)
    latent = jnp.clip(jax.random.uniform(part_splits[0], (MICRO, TOK_PATCH, TOK_LANES), jnp.float32, -0.1, 0.1) * steps_of(part_splits[0], (MICRO, TOK_PATCH, TOK_LANES), ((1, 4),), -0.4, 0.0), -0.1, 0.1)
    w_embed = normal_values(arg_keys[1], (TOK_LANES, D), TOK_LANES ** -0.5, 0.75)
    w_qkv = normal_values(arg_keys[2], (LAYERS, 3 * D, D), D ** -0.5, 0.109375, ((0, 2), (1, 4)))
    w_out = normal_values(arg_keys[3], (LAYERS, D, D), D ** -0.5, 0.109375, ((0, 2), (1, 4)))
    mod_table = normal_values(arg_keys[4], (SCHED_STEPS, 3, D), 0.5, 3.0)
    cond_mod = normal_values(part_splits[5], (2, LAYERS, 3, D), 0.5, 3.0, ((0, 2), (1, 2)), jnp.float32)
    stale_kv = normal_values(part_splits[6], (LAYERS, 2, N_SEQ, MICRO, HGROUPS * TOK_DEV, 2 * GHEADS * HEAD_DIM), 1.0, 6.0, ((0, 2), (1, 2), (2, 4)))
    w_final = normal_values(arg_keys[7], (D, TOK_LANES), D ** -0.5, 0.109375)
    w_conv = normal_values(arg_keys[8], (27, LAT_CH, DEC_CH), (27 * LAT_CH) ** -0.5, 0.3125, ((2, 4),))
    patch_order = jax.random.permutation(part_splits[9], MICRO).astype(jnp.int32)
    timestep = jax.random.randint(part_splits[10], (1,), 0, SCHED_STEPS).astype(jnp.int32)
    slab_rows = ragged(part_splits[11], N_SEQ, LAT_H, SLAB_MAX, 2).astype(jnp.int32)
    return {"latent": latent, "w_embed": w_embed, "w_qkv": w_qkv, "w_out": w_out, "mod_table": mod_table, "cond_mod": cond_mod, "stale_kv": stale_kv, "w_final": w_final, "w_conv": w_conv, "patch_order": patch_order, "timestep": timestep, "slab_rows": slab_rows}


guide_scale = 5.0
norm_eps = 1e-06

def rms_scaled(values):
    wide = values.astype(jnp.float32)
    return wide * lax.rsqrt(lax.optimization_barrier(jnp.mean(wide * wide, axis=-1, keepdims=True)) + norm_eps)

def causal_conv(image, kernel):
    frames, rows, width = (image.shape[0], image.shape[1], image.shape[2])
    padded = jnp.concatenate([image[:1], image[:1], image], 0)
    padded = jnp.pad(padded, ((0, 0), (1, 1), (1, 1), (0, 0)))
    pieces = []
    for frame_shift in range(3):
        for row_shift in range(3):
            for col_shift in range(3):
                pieces.append(padded[frame_shift:frame_shift + frames, row_shift:row_shift + rows, col_shift:col_shift + width])
    columns = jnp.concatenate(pieces, -1)
    flat = columns.reshape(frames * rows * width, columns.shape[-1])
    result = jnp.dot(flat, kernel.reshape(-1, kernel.shape[-1]), preferred_element_type=jnp.float32)
    return result.reshape(frames, rows, width, kernel.shape[-1]).astype(jnp.bfloat16)

def reference(latent, w_embed, w_qkv, w_out, mod_table, cond_mod, stale_kv, w_final, w_conv, patch_order, timestep, slab_rows):
    stale = stale_kv.reshape(LAYERS, 2, HGROUPS, CYCLE, MICRO, N_SEQ, TOK_DEV // CYCLE, 2, GHEADS, HEAD_DIM)
    stale = jnp.transpose(stale, (0, 1, 4, 5, 3, 6, 7, 2, 8, 9)).reshape(LAYERS, 2, MICRO, TOK_PATCH, 2, HEADS, HEAD_DIM)
    table_row = lax.dynamic_index_in_dim(mod_table, timestep[0], 0, keepdims=False).astype(jnp.float32)
    flat_latent = latent.astype(jnp.bfloat16).reshape(MICRO * TOK_PATCH, TOK_LANES)
    embedded = jnp.dot(flat_latent, w_embed, preferred_element_type=jnp.float32).astype(jnp.bfloat16)
    embedded = embedded.reshape(MICRO, TOK_PATCH, D)
    predictions = []
    for branch in range(2):
        hidden = embedded
        for layer in range(LAYERS):
            modulation = table_row + cond_mod[branch, layer]
            cache = stale[layer, branch]
            for micro_index in range(MICRO):
                patch_id = patch_order[micro_index]
                current = lax.dynamic_index_in_dim(hidden, patch_id, 0, keepdims=False)
                normed = (rms_scaled(current) * (1.0 + modulation[1]) + modulation[0]).astype(jnp.bfloat16)
                projected = jnp.dot(normed, w_qkv[layer].T, preferred_element_type=jnp.float32).astype(jnp.bfloat16)
                projected = projected.reshape(TOK_PATCH, HEADS, 3, HEAD_DIM)
                fresh = jnp.transpose(projected[:, :, 1:], (0, 2, 1, 3))
                cache = lax.dynamic_update_index_in_dim(cache, fresh, patch_id, 0)
                keys = cache[:, :, 0].reshape(MICRO * TOK_PATCH, HEADS, HEAD_DIM)
                values = cache[:, :, 1].reshape(MICRO * TOK_PATCH, HEADS, HEAD_DIM)
                queries = projected[:, :, 0]
                scores = jnp.einsum('thd,khd->htk', queries.astype(jnp.float32), keys.astype(jnp.float32)) * HEAD_DIM ** (-0.5)
                probs = jax.nn.softmax(scores, axis=-1).astype(jnp.bfloat16)
                attended = jnp.einsum('htk,khd->thd', probs.astype(jnp.float32), values.astype(jnp.float32)).astype(jnp.bfloat16)
                mixed = jnp.dot(attended.reshape(TOK_PATCH, D), w_out[layer], preferred_element_type=jnp.float32)
                updated = (current.astype(jnp.float32) + modulation[2] * mixed).astype(jnp.bfloat16)
                hidden = lax.dynamic_update_index_in_dim(hidden, updated, patch_id, 0)
        final_normed = rms_scaled(hidden).astype(jnp.bfloat16).reshape(MICRO * TOK_PATCH, D)
        predicted = jnp.dot(final_normed, w_final, preferred_element_type=jnp.float32)
        predictions.append(predicted.reshape(MICRO, TOK_PATCH, TOK_LANES))
    velocity = (1.0 - guide_scale) * predictions[0] + guide_scale * predictions[1]
    stepped = latent - velocity / SCHED_STEPS
    image = stepped.reshape(FRAMES, LAT_H // 2, LAT_W // 2, 2, 2, LAT_CH)
    image = jnp.transpose(image, (0, 1, 3, 2, 4, 5)).reshape(FRAMES, LAT_H, LAT_W, LAT_CH).astype(jnp.bfloat16)
    features = causal_conv(image, w_conv)
    starts = jnp.cumsum(slab_rows) - slab_rows
    offsets = jnp.arange(SLAB_MAX).astype(jnp.int32)
    row_index = jnp.clip(starts[:, None] + offsets[None, :], 0, LAT_H - 1).astype(jnp.int32)
    valid = offsets[None, :] < slab_rows[:, None]
    picked = jnp.take(features, row_index.reshape(-1), axis=1).reshape(FRAMES, N_SEQ, SLAB_MAX, LAT_W, DEC_CH)
    picked = jnp.transpose(picked, (1, 0, 2, 3, 4))
    decoded = jnp.where(valid[:, None, :, None, None], picked, jnp.zeros_like(picked))
    return (velocity, decoded)
```

```python
import jax
import jax.numpy as jnp
from jax import lax
from jax.experimental import pallas as pl
from jax.experimental.pallas import tpu as pltpu
from jax.sharding import PartitionSpec as P

HEADS = 24
HEAD_DIM = 128
D = 3072
LAT_CH = 16
SCHED_STEPS = 50
MICRO = 2
TOK_DEV = 8
FRAMES = 4
LAT_W = 8


guide_scale = 5.0
norm_eps = 1e-06


def swapped(value, axis, bit):
    return lax.ppermute(value, axis, [(i, i ^ 1 << bit) for i in range(lax.axis_size(axis))])


def passed_along(value, axis, by):
    size = lax.axis_size(axis)
    pairs = [(i, i + by) for i in range(size) if 0 <= i + by < size]
    return lax.ppermute(value, axis, pairs)


def rms_scaled(values):
    wide = values.astype(jnp.float32)
    return wide * lax.rsqrt(jnp.mean(wide * wide, axis=-1, keepdims=True) + norm_eps)


def cycle_join(piece, seq_index, cycle_bits):
    joined = piece
    for bit_number in range(cycle_bits):
        partner = swapped(joined, "seq", bit_number)
        upper_half = (seq_index // 2**bit_number % 2).astype(jnp.int32)
        part_rows = joined.shape[0]
        combined = jnp.zeros((2 * part_rows,) + joined.shape[1:], joined.dtype)
        combined = lax.dynamic_update_slice_in_dim(combined, joined, upper_half * part_rows, 0)
        joined = lax.dynamic_update_slice_in_dim(combined, partner, (1 - upper_half) * part_rows, 0)
    return joined


def cycled_shards(
    latent,
    w_embed,
    w_qkv,
    w_out,
    mod_table,
    cond_mod,
    stale_kv,
    w_final,
    w_conv,
    patch_order,
    timestep,
    slab_rows,
):
    seq_count = lax.axis_size("seq")
    segment_count = lax.axis_size("segment")
    seq_index = lax.axis_index("seq")
    segment_index = lax.axis_index("segment")
    branch_index = lax.axis_index("cfg")
    group_count = min(seq_count, 8)
    cycle_size = seq_count // group_count
    cycle_bits = cycle_size.bit_length() - 1
    group_heads = HEADS // group_count
    sub_rows = TOK_DEV // cycle_size
    share_rows = seq_count * sub_rows
    kv_lanes = 2 * group_heads * HEAD_DIM
    table_row = lax.dynamic_index_in_dim(mod_table, timestep[0], 0, keepdims=False).astype(
        jnp.float32
    )
    modulation = table_row + cond_mod[0, 0]
    shift_row = modulation[0]
    scale_row = modulation[1]
    gate_row = modulation[2]
    joined_weights = (
        cycle_join(w_qkv[0], seq_index, cycle_bits),
        cycle_join(w_out[0], seq_index, cycle_bits),
    )
    stale_joined = cycle_join(stale_kv[0, 0], seq_index, cycle_bits)
    cache = jnp.transpose(stale_joined, (1, 0, 2, 3)).reshape(
        MICRO, cycle_size * share_rows, kv_lanes
    )
    received = jnp.zeros((TOK_DEV, D), jnp.bfloat16)
    finished = jnp.zeros((MICRO, TOK_DEV, D), jnp.bfloat16)
    slot_ids = jnp.arange(MICRO)
    tick_count = MICRO + segment_count - 1
    for tick_index in range(tick_count):
        qkv_rows, out_rows = joined_weights
        micro_index = tick_index - segment_index
        active = (micro_index >= 0) & (micro_index < MICRO)
        clipped = jnp.clip(micro_index, 0, MICRO - 1)
        patch_id = jnp.sum(jnp.where(slot_ids == clipped, patch_order, 0))
        own_latent = lax.dynamic_index_in_dim(latent, patch_id, 0, keepdims=False).astype(
            jnp.bfloat16
        )
        embedded = jnp.dot(own_latent, w_embed, preferred_element_type=jnp.float32).astype(
            jnp.bfloat16
        )
        layer_input = jnp.where(segment_index == 0, embedded, received)
        normed = (rms_scaled(layer_input) * (1.0 + scale_row) + shift_row).astype(jnp.bfloat16)
        outgoing = jnp.broadcast_to(
            normed.reshape(1, cycle_size, sub_rows, D), (group_count, cycle_size, sub_rows, D)
        )
        shared = lax.all_to_all(
            outgoing.reshape(share_rows, D), "seq", split_axis=0, concat_axis=0, tiled=True
        )
        projected = lax.dot_general(
            shared, qkv_rows, (((1,), (1,)), ((), ())), preferred_element_type=jnp.float32
        )
        projected = projected.astype(jnp.bfloat16).reshape(share_rows, group_heads, 3, HEAD_DIM)
        queries = projected[:, :, 0]
        fresh_local = jnp.transpose(projected[:, :, 1:], (0, 2, 1, 3)).reshape(
            1, share_rows, kv_lanes
        )
        fresh = cycle_join(fresh_local, seq_index, cycle_bits).reshape(
            cycle_size * share_rows, kv_lanes
        )
        previous = lax.dynamic_index_in_dim(cache, patch_id, 0, keepdims=False)
        cache = lax.dynamic_update_index_in_dim(
            cache, jnp.where(active, fresh, previous), patch_id, 0
        )
        keyvals = cache.reshape(MICRO * cycle_size * share_rows, 2, group_heads, HEAD_DIM)
        scores = jnp.einsum(
            "shd,khd->hsk", queries, keyvals[:, 0], preferred_element_type=jnp.float32
        ) * HEAD_DIM ** (-0.5)
        probs = jax.nn.softmax(scores, axis=-1).astype(jnp.bfloat16)
        attended = jnp.einsum(
            "hsk,khd->shd", probs, keyvals[:, 1], preferred_element_type=jnp.float32
        ).astype(jnp.bfloat16)
        partial_out = jnp.dot(
            attended.reshape(share_rows, group_heads * HEAD_DIM),
            out_rows,
            preferred_element_type=jnp.float32,
        )
        returned = lax.all_to_all(
            partial_out.astype(jnp.bfloat16), "seq", split_axis=0, concat_axis=0, tiled=True
        ).astype(partial_out.dtype)
        mixed = jnp.sum(returned.reshape(group_count, cycle_size, sub_rows, D), axis=0).reshape(
            TOK_DEV, D
        )
        layer_output = (layer_input.astype(jnp.float32) + gate_row * mixed).astype(jnp.bfloat16)
        keep_final = active & (segment_index == segment_count - 1)
        earlier = lax.dynamic_index_in_dim(finished, patch_id, 0, keepdims=False)
        finished = lax.dynamic_update_index_in_dim(
            finished, jnp.where(keep_final, layer_output, earlier), patch_id, 0
        )
        if tick_index + 1 < tick_count:
            received = passed_along(layer_output, "segment", 1)
    final_normed = rms_scaled(finished).astype(jnp.bfloat16)
    predicted = jnp.einsum("mtd,dc->mtc", final_normed, w_final, preferred_element_type=jnp.float32)
    is_last = segment_index == segment_count - 1
    branch_weight = jnp.where(branch_index == 0, 1.0 - guide_scale, guide_scale)
    velocity_term = jnp.where(is_last, branch_weight * predicted, 0.0)
    latent_term = jnp.where(is_last & (branch_index == 0), latent, 0.0)
    velocity_own, latent_own = lax.psum((velocity_term, latent_term), ("segment", "cfg"))
    velocity_full, latent_full = (
        lax.all_gather(velocity_own, "seq", axis=1, tiled=True),
        lax.all_gather(latent_own, "seq", axis=1, tiled=True),
    )
    stepped = (latent_full - velocity_full / SCHED_STEPS).astype(jnp.bfloat16)
    decoded = decoder_input(stepped, w_conv, slab_rows, seq_index, seq_count)
    return (velocity_own, decoded)


def nt_kernel(lhs_ref, weight_ref, out_ref):
    out_ref[...] = lax.dot_general(
        lhs_ref[...],
        weight_ref[...],
        (((1,), (1,)), ((), ())),
        preferred_element_type=jnp.float32,
    )


def nt_dot(lhs, weight, tile):
    rows, depth = lhs.shape
    columns = weight.shape[0]
    return pl.pallas_call(
        nt_kernel,
        grid=(columns // tile,),
        in_specs=[
            pl.BlockSpec((rows, depth), lambda i: (0, 0)),
            pl.BlockSpec((tile, depth), lambda i: (i, 0)),
        ],
        out_specs=pl.BlockSpec((rows, tile), lambda i: (0, i)),
        out_shape=jax.ShapeDtypeStruct((rows, columns), jnp.float32),
        cost_estimate=pl.CostEstimate(
            flops=2 * rows * depth * columns,
            bytes_accessed=2 * depth * columns,
            transcendentals=0,
        ),
        compiler_params=pltpu.CompilerParams(vmem_limit_bytes=32 * 2**20),
    )(lhs, weight)


def exchanged(value_for, axis, pairs_for, count):
    return [lax.ppermute(value_for(k), axis, pairs_for(k)) for k in range(count)]


def shards(
    latent,
    w_embed,
    w_qkv,
    w_out,
    mod_table,
    cond_mod,
    stale_kv,
    w_final,
    w_conv,
    patch_order,
    timestep,
    slab_rows,
):
    seq_count = lax.axis_size("seq")
    segment_count = lax.axis_size("segment")
    seq_index = lax.axis_index("seq")
    segment_index = lax.axis_index("segment")
    branch_index = lax.axis_index("cfg")
    group_heads = HEADS // seq_count
    lanes = group_heads * HEAD_DIM
    rows_dev = MICRO * TOK_DEV
    rows = seq_count * rows_dev
    patch_rows = seq_count * TOK_DEV
    table_row = lax.dynamic_index_in_dim(mod_table, timestep[0], 0, keepdims=False).astype(
        jnp.float32
    )
    modulation = table_row + cond_mod[0, 0]
    shift_row = modulation[0]
    scale_row = 1.0 + modulation[1]
    gate_row = modulation[2]
    flipped = patch_order[0] == 1

    def micro_ordered(value):
        return jnp.where(flipped, value[::-1], value)

    def within(k):
        return [(i, i ^ k) for i in range(seq_count)]

    def seq_ordered(pieces):
        stacked = jnp.stack(pieces)
        return jnp.take(stacked, jnp.arange(seq_count) ^ seq_index, axis=0)

    own_latent = micro_ordered(latent).astype(jnp.bfloat16).reshape(rows_dev, -1)
    latents = seq_ordered(
        [own_latent]
        + [lax.ppermute(own_latent, "seq", within(k)) for k in range(1, seq_count)]
    ).reshape(rows, -1)

    spare = 16 - 1
    embed_rows = w_embed.shape[0]
    scaled_embed = (w_embed.astype(jnp.float32) * scale_row).astype(jnp.bfloat16)
    lhs = jnp.concatenate(
        [scaled_embed, shift_row[None].astype(jnp.bfloat16), jnp.zeros((spare, D), jnp.bfloat16)]
    )
    head_embed = nt_dot(lhs, w_qkv[0], 256)
    shift_term = head_embed[embed_rows : embed_rows + 1]

    embedded = jnp.dot(latents, w_embed, preferred_element_type=jnp.float32).astype(jnp.bfloat16)
    wide = embedded.astype(jnp.float32)
    norm = lax.rsqrt(jnp.mean(wide * wide, axis=-1, keepdims=True) + norm_eps)
    projected = (
        norm
        * jnp.dot(
            latents,
            head_embed[:embed_rows].astype(jnp.bfloat16),
            preferred_element_type=jnp.float32,
        )
        + shift_term
    ).astype(jnp.bfloat16)

    stale = jnp.where(flipped, stale_kv[0, 0, 0, 0], stale_kv[0, 0, 0, 1])
    stale = stale.reshape(patch_rows, 2, group_heads, HEAD_DIM)
    row_micro = jnp.arange(rows) // TOK_DEV % MICRO
    fresh_seen = row_micro[:, None] >= row_micro[None, :]
    stale_seen = jnp.broadcast_to(row_micro[:, None] == 0, (rows, patch_rows))
    seen = jnp.concatenate([fresh_seen, stale_seen], axis=1)

    def attention(projected):
        heads = projected.reshape(rows, group_heads, 3, HEAD_DIM)
        keys = jnp.concatenate([heads[:, :, 1], stale[:, 0]], axis=0)
        values = jnp.concatenate([heads[:, :, 2], stale[:, 1]], axis=0)
        scores = jnp.einsum(
            "shd,khd->hsk", heads[:, :, 0], keys, preferred_element_type=jnp.float32
        ) * HEAD_DIM ** (-0.5)
        scores = jnp.where(seen[None], scores, -jnp.inf)
        probs = jax.nn.softmax(scores, axis=-1).astype(jnp.bfloat16)
        attended = jnp.einsum(
            "hsk,khd->shd", probs, values, preferred_element_type=jnp.float32
        ).astype(jnp.bfloat16)
        return attended.reshape(rows, lanes)

    columns = D // seq_count
    hidden = embedded
    for step in range(segment_count):
        partial_out = jnp.dot(
            attention(projected), w_out[0], preferred_element_type=jnp.float32
        ).astype(jnp.bfloat16)
        if step + 1 == segment_count:
            break

        def column_block(value, place):
            return lax.dynamic_slice_in_dim(value, place * columns, columns, value.ndim - 1)

        mixed = column_block(partial_out, seq_index).astype(jnp.float32)
        for k in range(1, seq_count):
            mixed = mixed + lax.ppermute(
                column_block(partial_out, seq_index ^ k), "seq", within(k)
            ).astype(jnp.float32)
        block = (
            column_block(hidden, seq_index).astype(jnp.float32)
            + column_block(gate_row, seq_index) * mixed
        ).astype(jnp.bfloat16)
        pieces = []
        for k in range(seq_count):
            pairs = [
                (i * segment_count + step, (i ^ k) * segment_count + step + 1)
                for i in range(seq_count)
            ]
            pieces.append(lax.ppermute(block, ("seq", "segment"), pairs))
        hidden = jnp.transpose(seq_ordered(pieces), (1, 0, 2)).reshape(rows, D)
        wide = hidden.astype(jnp.float32)
        norm = lax.rsqrt(jnp.mean(wide * wide, axis=-1, keepdims=True) + norm_eps)
        scaled = (wide * scale_row).astype(jnp.bfloat16)
        projected = (norm * nt_dot(scaled, w_qkv[0], 256) + shift_term).astype(jnp.bfloat16)

    def row_block(value, place):
        return lax.dynamic_slice_in_dim(value, place * rows_dev, rows_dev, 0)

    mixed = row_block(partial_out, seq_index).astype(jnp.float32)
    for k in range(1, seq_count):
        mixed = mixed + lax.ppermute(
            row_block(partial_out, seq_index ^ k), "seq", within(k)
        ).astype(jnp.float32)
    final = (row_block(hidden, seq_index).astype(jnp.float32) + gate_row * mixed).astype(
        jnp.bfloat16
    )
    predicted = jnp.dot(
        rms_scaled(final).astype(jnp.bfloat16), w_final, preferred_element_type=jnp.float32
    )
    term = jnp.where(branch_index == 0, 1.0 - guide_scale, guide_scale) * predicted
    velocity_own = term + swapped(term, "cfg", 0)
    hop = [(segment_count - 1, i) for i in range(segment_count - 1)]
    for pair in hop:
        moved = lax.ppermute(velocity_own, "segment", [pair])
        velocity_own = jnp.where(segment_index == pair[1], moved, velocity_own)
    velocity_own = micro_ordered(velocity_own.reshape(MICRO, TOK_DEV, -1))
    stepped_own = (latent - velocity_own / SCHED_STEPS).astype(jnp.bfloat16)
    stepped = seq_ordered(
        [stepped_own]
        + [lax.ppermute(stepped_own, "seq", within(k)) for k in range(1, seq_count)]
    )
    stepped = jnp.transpose(stepped, (1, 0, 2, 3))
    decoded = decoder_input(stepped, w_conv, slab_rows, seq_index, seq_count)
    return (velocity_own, decoded)


def decoder_input(stepped, w_conv, slab_rows, seq_index, seq_count):
    token_rows = MICRO * seq_count * TOK_DEV // (FRAMES * (LAT_W // 2))
    image_rows = 2 * token_rows
    slab_most = 2 * image_rows // seq_count
    image = stepped.reshape(FRAMES, token_rows, LAT_W // 2, 2, 2, LAT_CH)
    image = (
        jnp.transpose(image, (0, 1, 3, 2, 4, 5))
        .reshape(FRAMES, image_rows, LAT_W, LAT_CH)
    )
    padded = jnp.concatenate([image[:1], image[:1], image], 0)
    padded = jnp.pad(padded, ((0, 0), (1, 1 + slab_most), (1, 1), (0, 0)))
    positions = jnp.arange(seq_count)
    slab_count = jnp.sum(jnp.where(positions == seq_index, slab_rows, 0))
    slab_start = jnp.sum(jnp.where(positions < seq_index, slab_rows, 0))
    window = lax.dynamic_slice_in_dim(padded, slab_start, slab_most + 2, 1)
    pieces = []
    for frame_shift in range(3):
        for row_shift in range(3):
            for col_shift in range(3):
                pieces.append(
                    window[
                        frame_shift : frame_shift + FRAMES,
                        row_shift : row_shift + slab_most,
                        col_shift : col_shift + LAT_W,
                    ]
                )
    columns = jnp.concatenate(pieces, -1).reshape(FRAMES * slab_most * LAT_W, 27 * LAT_CH)
    kernel = w_conv.reshape(27 * LAT_CH, w_conv.shape[2])
    features = jnp.dot(columns, kernel, preferred_element_type=jnp.float32).astype(jnp.bfloat16)
    features = features.reshape(FRAMES, slab_most, LAT_W, w_conv.shape[2])
    row_valid = jnp.arange(slab_most)[None, :, None, None] < slab_count
    decoded = jnp.where(row_valid, features, jnp.zeros_like(features))
    return decoded[None]


def solution(mesh):
    in_specs = (
        P(None, ("groups", "seq"), None),
        P(),
        P("segment", "seq", None),
        P("segment", "seq", None),
        P(),
        P("cfg", ("groups", "segment"), None, None),
        P("segment", "cfg", "seq", None, "groups", None),
        P(),
        P(None, None, ("segment", "cfg")),
        P("groups"),
        P("groups"),
        P("groups"),
    )
    out_specs = (
        P(None, ("groups", "seq"), None),
        P(("groups", "seq"), None, None, None, ("segment", "cfg")),
    )
    whole_groups = HEADS % mesh.shape["seq"] == 0 and mesh.shape["seq"] <= 8
    program = shards if whole_groups else cycled_shards
    return jax.shard_map(program, mesh=mesh, in_specs=in_specs, out_specs=out_specs, check_vma=False)
```

```python
import functools

import jax
import jax.numpy as jnp
from jax import lax
from jax.experimental import pallas as pl
from jax.experimental.pallas import tpu as pltpu
from jax.sharding import PartitionSpec as P

HEADS = 24
HEAD_DIM = 128
D = 3072
LAT_CH = 16
SCHED_STEPS = 50
MICRO = 2
TOK_DEV = 8
FRAMES = 4
LAT_W = 8


guide_scale = 5.0
norm_eps = 1e-06


def swapped(value, axis, bit):
    return lax.ppermute(value, axis, [(i, i ^ 1 << bit) for i in range(lax.axis_size(axis))])


def passed_along(value, axis, by):
    size = lax.axis_size(axis)
    pairs = [(i, i + by) for i in range(size) if 0 <= i + by < size]
    return lax.ppermute(value, axis, pairs)


def rms_scaled(values):
    wide = values.astype(jnp.float32)
    return wide * lax.rsqrt(jnp.mean(wide * wide, axis=-1, keepdims=True) + norm_eps)


def cycle_join(piece, seq_index, cycle_bits):
    joined = piece
    for bit_number in range(cycle_bits):
        partner = swapped(joined, "seq", bit_number)
        upper_half = (seq_index // 2**bit_number % 2).astype(jnp.int32)
        part_rows = joined.shape[0]
        combined = jnp.zeros((2 * part_rows,) + joined.shape[1:], joined.dtype)
        combined = lax.dynamic_update_slice_in_dim(combined, joined, upper_half * part_rows, 0)
        joined = lax.dynamic_update_slice_in_dim(combined, partner, (1 - upper_half) * part_rows, 0)
    return joined


def cycled_shards(
    latent,
    w_embed,
    w_qkv,
    w_out,
    mod_table,
    cond_mod,
    stale_kv,
    w_final,
    w_conv,
    patch_order,
    timestep,
    slab_rows,
):
    seq_count = lax.axis_size("seq")
    segment_count = lax.axis_size("segment")
    seq_index = lax.axis_index("seq")
    segment_index = lax.axis_index("segment")
    branch_index = lax.axis_index("cfg")
    group_count = min(seq_count, 8)
    cycle_size = seq_count // group_count
    cycle_bits = cycle_size.bit_length() - 1
    group_heads = HEADS // group_count
    sub_rows = TOK_DEV // cycle_size
    share_rows = seq_count * sub_rows
    kv_lanes = 2 * group_heads * HEAD_DIM
    table_row = lax.dynamic_index_in_dim(mod_table, timestep[0], 0, keepdims=False).astype(
        jnp.float32
    )
    modulation = table_row + cond_mod[0, 0]
    shift_row = modulation[0]
    scale_row = modulation[1]
    gate_row = modulation[2]
    joined_weights = (
        cycle_join(w_qkv[0], seq_index, cycle_bits),
        cycle_join(w_out[0], seq_index, cycle_bits),
    )
    stale_joined = cycle_join(stale_kv[0, 0], seq_index, cycle_bits)
    cache = jnp.transpose(stale_joined, (1, 0, 2, 3)).reshape(
        MICRO, cycle_size * share_rows, kv_lanes
    )
    received = jnp.zeros((TOK_DEV, D), jnp.bfloat16)
    finished = jnp.zeros((MICRO, TOK_DEV, D), jnp.bfloat16)
    slot_ids = jnp.arange(MICRO)
    tick_count = MICRO + segment_count - 1
    for tick_index in range(tick_count):
        qkv_rows, out_rows = joined_weights
        micro_index = tick_index - segment_index
        active = (micro_index >= 0) & (micro_index < MICRO)
        clipped = jnp.clip(micro_index, 0, MICRO - 1)
        patch_id = jnp.sum(jnp.where(slot_ids == clipped, patch_order, 0))
        own_latent = lax.dynamic_index_in_dim(latent, patch_id, 0, keepdims=False).astype(
            jnp.bfloat16
        )
        embedded = jnp.dot(own_latent, w_embed, preferred_element_type=jnp.float32).astype(
            jnp.bfloat16
        )
        layer_input = jnp.where(segment_index == 0, embedded, received)
        normed = (rms_scaled(layer_input) * (1.0 + scale_row) + shift_row).astype(jnp.bfloat16)
        outgoing = jnp.broadcast_to(
            normed.reshape(1, cycle_size, sub_rows, D), (group_count, cycle_size, sub_rows, D)
        )
        shared = lax.all_to_all(
            outgoing.reshape(share_rows, D), "seq", split_axis=0, concat_axis=0, tiled=True
        )
        projected = lax.dot_general(
            shared, qkv_rows, (((1,), (1,)), ((), ())), preferred_element_type=jnp.float32
        )
        projected = projected.astype(jnp.bfloat16).reshape(share_rows, group_heads, 3, HEAD_DIM)
        queries = projected[:, :, 0]
        fresh_local = jnp.transpose(projected[:, :, 1:], (0, 2, 1, 3)).reshape(
            1, share_rows, kv_lanes
        )
        fresh = cycle_join(fresh_local, seq_index, cycle_bits).reshape(
            cycle_size * share_rows, kv_lanes
        )
        previous = lax.dynamic_index_in_dim(cache, patch_id, 0, keepdims=False)
        cache = lax.dynamic_update_index_in_dim(
            cache, jnp.where(active, fresh, previous), patch_id, 0
        )
        keyvals = cache.reshape(MICRO * cycle_size * share_rows, 2, group_heads, HEAD_DIM)
        scores = jnp.einsum(
            "shd,khd->hsk", queries, keyvals[:, 0], preferred_element_type=jnp.float32
        ) * HEAD_DIM ** (-0.5)
        probs = jax.nn.softmax(scores, axis=-1).astype(jnp.bfloat16)
        attended = jnp.einsum(
            "hsk,khd->shd", probs, keyvals[:, 1], preferred_element_type=jnp.float32
        ).astype(jnp.bfloat16)
        partial_out = jnp.dot(
            attended.reshape(share_rows, group_heads * HEAD_DIM),
            out_rows,
            preferred_element_type=jnp.float32,
        )
        returned = lax.all_to_all(
            partial_out.astype(jnp.bfloat16), "seq", split_axis=0, concat_axis=0, tiled=True
        ).astype(partial_out.dtype)
        mixed = jnp.sum(returned.reshape(group_count, cycle_size, sub_rows, D), axis=0).reshape(
            TOK_DEV, D
        )
        layer_output = (layer_input.astype(jnp.float32) + gate_row * mixed).astype(jnp.bfloat16)
        keep_final = active & (segment_index == segment_count - 1)
        earlier = lax.dynamic_index_in_dim(finished, patch_id, 0, keepdims=False)
        finished = lax.dynamic_update_index_in_dim(
            finished, jnp.where(keep_final, layer_output, earlier), patch_id, 0
        )
        if tick_index + 1 < tick_count:
            received = passed_along(layer_output, "segment", 1)
    final_normed = rms_scaled(finished).astype(jnp.bfloat16)
    predicted = jnp.einsum("mtd,dc->mtc", final_normed, w_final, preferred_element_type=jnp.float32)
    is_last = segment_index == segment_count - 1
    branch_weight = jnp.where(branch_index == 0, 1.0 - guide_scale, guide_scale)
    velocity_term = jnp.where(is_last, branch_weight * predicted, 0.0)
    latent_term = jnp.where(is_last & (branch_index == 0), latent, 0.0)
    velocity_own, latent_own = lax.psum((velocity_term, latent_term), ("segment", "cfg"))
    velocity_full, latent_full = (
        lax.all_gather(velocity_own, "seq", axis=1, tiled=True),
        lax.all_gather(latent_own, "seq", axis=1, tiled=True),
    )
    stepped = (latent_full - velocity_full / SCHED_STEPS).astype(jnp.bfloat16)
    decoded = decoder_input(stepped, w_conv, slab_rows, seq_index, seq_count)
    return (velocity_own, decoded)


VMEM_LIMIT = 24 * 2**20
NT = (((1,), (1,)), ((), ()))


def kernel_params():
    return pltpu.CompilerParams(vmem_limit_bytes=VMEM_LIMIT)


def whole(space=pltpu.VMEM):
    return pl.BlockSpec(memory_space=space)


def prepare_kernel(
    embed_ref, shift_ref, scale_ref, qkv_hbm, out_hbm, heads_ref, term_ref, qkv_ref, out_ref, lhs, sems
):
    tiles = sems.shape[0] - 1
    tile = qkv_ref.shape[0] // tiles

    def qkv_copy(i):
        part = pl.ds(i * tile, tile)
        return pltpu.make_async_copy(qkv_hbm.at[part], qkv_ref.at[part], sems.at[i])

    out_copy = pltpu.make_async_copy(out_hbm, out_ref, sems.at[tiles])
    for i in range(tiles):
        qkv_copy(i).start()
    out_copy.start()
    count = embed_ref.shape[0]
    lhs[:count] = (embed_ref[...].astype(jnp.float32) * scale_ref[...]).astype(jnp.bfloat16)
    lhs[count:] = jnp.broadcast_to(shift_ref[...], (16, lhs.shape[1])).astype(jnp.bfloat16)
    for i in range(tiles):
        qkv_copy(i).wait()
        part = pl.ds(i * tile, tile)
        product = lax.dot_general(
            lhs[...], qkv_ref[part, :], NT, preferred_element_type=jnp.float32
        )
        heads_ref[:, part] = product[:count].astype(jnp.bfloat16)
        term_ref[:, part] = product[count:]
    out_copy.wait()


def prepared(w_embed, shift_row, scale_row, qkv, out):
    count, depth = w_embed.shape
    lanes = qkv.shape[0]
    tiles = lanes // 256
    return pl.pallas_call(
        prepare_kernel,
        in_specs=[whole(), whole(), whole(), whole(pltpu.HBM), whole(pltpu.HBM)],
        out_specs=[whole()] * 4,
        out_shape=[
            jax.ShapeDtypeStruct((count, lanes), jnp.bfloat16),
            jax.ShapeDtypeStruct((16, lanes), jnp.float32),
            pltpu.VMEM(qkv.shape, qkv.dtype),
            pltpu.VMEM(out.shape, out.dtype),
        ],
        scratch_shapes=[
            pltpu.VMEM((count + 16, depth), jnp.bfloat16),
            pltpu.SemaphoreType.DMA((tiles + 1,)),
        ],
        cost_estimate=pl.CostEstimate(
            flops=2 * count * depth * lanes,
            bytes_accessed=2 * (qkv.size + out.size),
            transcendentals=0,
        ),
        compiler_params=kernel_params(),
    )(w_embed, shift_row, scale_row, qkv, out)


def attend(projected, stale_ref, attended):
    rows = projected.shape[0]
    patch_rows = stale_ref.shape[0]
    lanes = attended.shape[1]

    def micro_of(shape, dim):
        return lax.broadcasted_iota(jnp.int32, shape, dim) // TOK_DEV % MICRO

    unseen = micro_of((rows, rows), 0) < micro_of((rows, rows), 1)
    late = micro_of((rows, patch_rows), 0) > 0
    for head in range(lanes // HEAD_DIM):
        first = 3 * HEAD_DIM * head
        queries = projected[:, first : first + HEAD_DIM]
        keys = projected[:, first + HEAD_DIM : first + 2 * HEAD_DIM]
        values = projected[:, first + 2 * HEAD_DIM : first + 3 * HEAD_DIM]
        part = slice(head * HEAD_DIM, (head + 1) * HEAD_DIM)
        value_part = slice(lanes + head * HEAD_DIM, lanes + (head + 1) * HEAD_DIM)
        fresh = lax.dot_general(queries, keys, NT, preferred_element_type=jnp.float32)
        stale = lax.dot_general(
            queries, stale_ref[:, part], NT, preferred_element_type=jnp.float32
        )
        fresh = jnp.where(unseen, -jnp.inf, fresh * HEAD_DIM ** (-0.5))
        stale = jnp.where(late, -jnp.inf, stale * HEAD_DIM ** (-0.5))
        top = jnp.maximum(
            jnp.max(fresh, axis=-1, keepdims=True), jnp.max(stale, axis=-1, keepdims=True)
        )
        fresh = jnp.exp(fresh - top)
        stale = jnp.exp(stale - top)
        total = jnp.sum(fresh, axis=-1, keepdims=True) + jnp.sum(stale, axis=-1, keepdims=True)
        fresh = (fresh / total).astype(jnp.bfloat16)
        stale = (stale / total).astype(jnp.bfloat16)
        attended[:, part] = (
            jnp.dot(fresh, values, preferred_element_type=jnp.float32)
            + jnp.dot(stale, stale_ref[:, value_part], preferred_element_type=jnp.float32)
        ).astype(jnp.bfloat16)


def column_blocks(place, attended, out_ref, block_refs):
    count = len(block_refs)
    columns = out_ref.shape[1] // count
    for k in range(count):
        first = pl.multiple_of((place ^ k) * columns, columns)
        block_refs[k][...] = jnp.dot(
            attended[...], out_ref[:, pl.ds(first, columns)], preferred_element_type=jnp.float32
        ).astype(jnp.bfloat16)


def first_layer_kernel(count, place_ref, embed_ref, heads_ref, term_ref, stale_ref, out_ref, *refs):
    latent_refs, refs = refs[:count], refs[count:]
    block_refs, own_ref, latents, attended = refs[:count], *refs[count:]
    place = place_ref[0]
    rows_dev = latent_refs[0].shape[0]
    for k in range(count):
        first = pl.multiple_of((place ^ k) * rows_dev, rows_dev)
        latents[pl.ds(first, rows_dev), :] = latent_refs[k][...]
    embedded = jnp.dot(latents[...], embed_ref[...], preferred_element_type=jnp.float32)
    embedded = embedded.astype(jnp.bfloat16).astype(jnp.float32)
    norm = lax.rsqrt(jnp.mean(embedded * embedded, axis=-1, keepdims=True) + norm_eps)
    projected = jnp.dot(latents[...], heads_ref[...], preferred_element_type=jnp.float32)
    projected = (norm * projected + term_ref[:1]).astype(jnp.bfloat16)
    attend(projected, stale_ref, attended)
    column_blocks(place, attended, out_ref, block_refs)
    columns = own_ref.shape[1]
    first = pl.multiple_of(place * columns, columns)
    own_ref[...] = jnp.dot(
        latents[...], embed_ref[:, pl.ds(first, columns)], preferred_element_type=jnp.float32
    ).astype(jnp.bfloat16)


def first_layer(place, latent_pieces, w_embed, heads, term, stale, out):
    count = len(latent_pieces)
    rows = count * latent_pieces[0].shape[0]
    lanes, depth = out.shape
    block = jax.ShapeDtypeStruct((rows, depth // count), jnp.bfloat16)
    return pl.pallas_call(
        functools.partial(first_layer_kernel, count),
        in_specs=[whole(pltpu.SMEM)] + [whole()] * (5 + count),
        out_specs=[whole()] * (count + 1),
        out_shape=[block] * (count + 1),
        scratch_shapes=[
            pltpu.VMEM((rows, w_embed.shape[0]), jnp.bfloat16),
            pltpu.VMEM((rows, lanes), jnp.bfloat16),
        ],
        compiler_params=kernel_params(),
    )(place, w_embed, heads, term, stale, out, *latent_pieces)


def add_products(place, numbers, piece_refs, scale_ref, qkv_ref, sums_ref, squares):
    columns = piece_refs[0].shape[1]
    scaled = []
    for k, piece_ref in zip(numbers, piece_refs):
        first = pl.multiple_of((place ^ k) * columns, columns)
        wide = piece_ref[...].astype(jnp.float32)
        squares = squares + jnp.sum(wide * wide, axis=-1, keepdims=True)
        scaled.append(
            (first, (wide * scale_ref[:, pl.ds(first, columns)]).astype(jnp.bfloat16))
        )
    for i in range(qkv_ref.shape[0] // 256):
        part = slice(i * 256, (i + 1) * 256)
        total = sums_ref[:, part]
        for first, piece in scaled:
            total = total + lax.dot_general(
                piece, qkv_ref[part, pl.ds(first, columns)], NT, preferred_element_type=jnp.float32
            )
        sums_ref[:, part] = total
    return squares


def sums_kernel(numbers, place_ref, scale_ref, qkv_ref, sums_in, squares_in, *refs):
    piece_refs, sums_ref, squares_ref = refs[: len(numbers)], *refs[len(numbers) :]
    sums_ref[...] = sums_in[...]
    squares_ref[...] = add_products(
        place_ref[0], numbers, piece_refs, scale_ref, qkv_ref, sums_ref, squares_in[...]
    )


def product_sums(place, numbers, pieces, scale_row, qkv, sums, squares):
    return pl.pallas_call(
        functools.partial(sums_kernel, numbers),
        in_specs=[whole(pltpu.SMEM)] + [whole()] * (4 + len(numbers)),
        out_specs=[whole()] * 2,
        out_shape=[
            jax.ShapeDtypeStruct(sums.shape, sums.dtype),
            jax.ShapeDtypeStruct(squares.shape, squares.dtype),
        ],
        compiler_params=kernel_params(),
    )(place, scale_row, qkv, sums, squares, *pieces)


def later_layer_kernel(
    count, numbers, last, place_ref, scale_ref, qkv_ref, term_ref, stale_ref, out_ref, sums_in, squares_in, *refs
):
    piece_refs, refs = refs[:count], refs[count:]
    block_refs, own_ref, sums, attended, partial_out = refs[:count], *refs[count:]
    place = place_ref[0]
    sums[...] = sums_in[...]
    squares = add_products(
        place,
        numbers,
        [piece_refs[k] for k in numbers],
        scale_ref,
        qkv_ref,
        sums,
        squares_in[...],
    )
    norm = lax.rsqrt(squares / scale_ref.shape[1] + norm_eps)
    projected = (norm * sums[...] + term_ref[:1]).astype(jnp.bfloat16)
    attend(projected, stale_ref, attended)
    if not last:
        column_blocks(place, attended, out_ref, block_refs)
        own_ref[...] = piece_refs[0][...]
        return
    partial_out[...] = jnp.dot(
        attended[...], out_ref[...], preferred_element_type=jnp.float32
    ).astype(jnp.bfloat16)
    rows_dev = own_ref.shape[0]
    columns = piece_refs[0].shape[1]
    own_rows = pl.ds(pl.multiple_of(place * rows_dev, rows_dev), rows_dev)
    for k in range(count):
        first = pl.multiple_of((place ^ k) * rows_dev, rows_dev)
        block_refs[k][...] = partial_out[pl.ds(first, rows_dev), :]
        first = pl.multiple_of((place ^ k) * columns, columns)
        own_ref[:, pl.ds(first, columns)] = piece_refs[k][own_rows, :]


def later_layer(place, numbers, last, pieces, scale_row, qkv, term, stale, out, sums, squares):
    count = len(pieces)
    rows, columns = pieces[0].shape
    lanes, depth = out.shape
    shape = (rows // count, depth) if last else (rows, columns)
    block = jax.ShapeDtypeStruct(shape, jnp.bfloat16)
    return pl.pallas_call(
        functools.partial(later_layer_kernel, count, numbers, last),
        in_specs=[whole(pltpu.SMEM)] + [whole()] * (7 + count),
        out_specs=[whole()] * (count + 1),
        out_shape=[block] * (count + 1),
        scratch_shapes=[
            pltpu.VMEM(sums.shape, jnp.float32),
            pltpu.VMEM((rows, lanes), jnp.bfloat16),
            pltpu.VMEM((rows, depth), jnp.bfloat16),
        ],
        compiler_params=kernel_params(),
    )(place, scale_row, qkv, term, stale, out, sums, squares, *pieces)


def shards(
    latent,
    w_embed,
    w_qkv,
    w_out,
    mod_table,
    cond_mod,
    stale_kv,
    w_final,
    w_conv,
    patch_order,
    timestep,
    slab_rows,
):
    seq_count = lax.axis_size("seq")
    segment_count = lax.axis_size("segment")
    seq_index = lax.axis_index("seq")
    segment_index = lax.axis_index("segment")
    branch_index = lax.axis_index("cfg")
    group_heads = HEADS // seq_count
    lanes = group_heads * HEAD_DIM
    rows_dev = MICRO * TOK_DEV
    rows = seq_count * rows_dev
    patch_rows = seq_count * TOK_DEV
    table_row = lax.dynamic_index_in_dim(mod_table, timestep[0], 0, keepdims=False).astype(
        jnp.float32
    )
    modulation = table_row + cond_mod[0, 0]
    shift_row = modulation[0]
    scale_row = 1.0 + modulation[1]
    gate_row = modulation[2]
    flipped = patch_order[0] == 1

    def micro_ordered(value):
        return jnp.where(flipped, value[::-1], value)

    def within(k):
        return [(i, i ^ k) for i in range(seq_count)]

    def seq_ordered(pieces):
        stacked = jnp.stack(pieces)
        return jnp.take(stacked, jnp.arange(seq_count) ^ seq_index, axis=0)

    place = seq_index.astype(jnp.int32)[None]
    own_latent = micro_ordered(latent).astype(jnp.bfloat16).reshape(rows_dev, -1)
    latent_pieces = [own_latent] + [
        lax.ppermute(own_latent, "seq", within(k)) for k in range(1, seq_count)
    ]
    head_embed, shift_term, qkv, out = prepared(
        w_embed, shift_row[None], scale_row[None], w_qkv[0], w_out[0]
    )
    stale = jnp.where(flipped, stale_kv[0, 0, 0, 0], stale_kv[0, 0, 0, 1])
    *blocks, own = first_layer(
        place, latent_pieces, w_embed, head_embed, shift_term, stale, out
    )
    columns = D // seq_count
    own_gate = lax.dynamic_slice_in_dim(gate_row, seq_index * columns, columns, 0)
    for step in range(1, segment_count):
        mixed = blocks[0].astype(jnp.float32)
        for k in range(1, seq_count):
            mixed = mixed + lax.ppermute(blocks[k], "seq", within(k)).astype(jnp.float32)
        block = (own.astype(jnp.float32) + own_gate * mixed).astype(jnp.bfloat16)
        pieces = []
        for k in range(seq_count):
            pairs = [
                (i * segment_count + step - 1, (i ^ k) * segment_count + step)
                for i in range(seq_count)
            ]
            pieces.append(lax.ppermute(block, ("seq", "segment"), pairs))
        sums = jnp.zeros((rows, qkv.shape[0]), jnp.float32)
        squares = jnp.zeros((rows, 1), jnp.float32)
        numbers = tuple(range(seq_count))
        half = seq_count // 2
        for some in (numbers[:half], numbers[half:-1]):
            if some:
                sums, squares = product_sums(
                    place, some, [pieces[k] for k in some], scale_row[None], qkv, sums, squares
                )
        *blocks, own = later_layer(
            place,
            numbers[-1:],
            step + 1 == segment_count,
            pieces,
            scale_row[None],
            qkv,
            shift_term,
            stale,
            out,
            sums,
            squares,
        )

    mixed = blocks[0].astype(jnp.float32)
    for k in range(1, seq_count):
        mixed = mixed + lax.ppermute(blocks[k], "seq", within(k)).astype(jnp.float32)
    final = (own.astype(jnp.float32) + gate_row * mixed).astype(jnp.bfloat16)
    predicted = jnp.dot(
        rms_scaled(final).astype(jnp.bfloat16), w_final, preferred_element_type=jnp.float32
    )
    term = jnp.where(branch_index == 0, 1.0 - guide_scale, guide_scale) * predicted
    velocity_own = term + swapped(term, "cfg", 0)
    hop = [(segment_count - 1, i) for i in range(segment_count - 1)]
    for pair in hop:
        moved = lax.ppermute(velocity_own, "segment", [pair])
        velocity_own = jnp.where(segment_index == pair[1], moved, velocity_own)
    velocity_own = micro_ordered(velocity_own.reshape(MICRO, TOK_DEV, -1))
    stepped_own = (latent - velocity_own / SCHED_STEPS).astype(jnp.bfloat16)
    stepped = seq_ordered(
        [stepped_own]
        + [lax.ppermute(stepped_own, "seq", within(k)) for k in range(1, seq_count)]
    )
    stepped = jnp.transpose(stepped, (1, 0, 2, 3))
    decoded = decoder_input(stepped, w_conv, slab_rows, seq_index, seq_count)
    return (velocity_own, decoded)


def decoder_input(stepped, w_conv, slab_rows, seq_index, seq_count):
    token_rows = MICRO * seq_count * TOK_DEV // (FRAMES * (LAT_W // 2))
    image_rows = 2 * token_rows
    slab_most = 2 * image_rows // seq_count
    image = stepped.reshape(FRAMES, token_rows, LAT_W // 2, 2, 2, LAT_CH)
    image = (
        jnp.transpose(image, (0, 1, 3, 2, 4, 5))
        .reshape(FRAMES, image_rows, LAT_W, LAT_CH)
    )
    padded = jnp.concatenate([image[:1], image[:1], image], 0)
    padded = jnp.pad(padded, ((0, 0), (1, 1 + slab_most), (1, 1), (0, 0)))
    positions = jnp.arange(seq_count)
    slab_count = jnp.sum(jnp.where(positions == seq_index, slab_rows, 0))
    slab_start = jnp.sum(jnp.where(positions < seq_index, slab_rows, 0))
    window = lax.dynamic_slice_in_dim(padded, slab_start, slab_most + 2, 1)
    pieces = []
    for frame_shift in range(3):
        for row_shift in range(3):
            for col_shift in range(3):
                pieces.append(
                    window[
                        frame_shift : frame_shift + FRAMES,
                        row_shift : row_shift + slab_most,
                        col_shift : col_shift + LAT_W,
                    ]
                )
    columns = jnp.concatenate(pieces, -1).reshape(FRAMES * slab_most * LAT_W, 27 * LAT_CH)
    kernel = w_conv.reshape(27 * LAT_CH, w_conv.shape[2])
    features = jnp.dot(columns, kernel, preferred_element_type=jnp.float32).astype(jnp.bfloat16)
    features = features.reshape(FRAMES, slab_most, LAT_W, w_conv.shape[2])
    row_valid = jnp.arange(slab_most)[None, :, None, None] < slab_count
    decoded = jnp.where(row_valid, features, jnp.zeros_like(features))
    return decoded[None]


def solution(mesh):
    in_specs = (
        P(None, ("groups", "seq"), None),
        P(),
        P("segment", "seq", None),
        P("segment", "seq", None),
        P(),
        P("cfg", ("groups", "segment"), None, None),
        P("segment", "cfg", "seq", None, "groups", None),
        P(),
        P(None, None, ("segment", "cfg")),
        P("groups"),
        P("groups"),
        P("groups"),
    )
    out_specs = (
        P(None, ("groups", "seq"), None),
        P(("groups", "seq"), None, None, None, ("segment", "cfg")),
    )
    whole_groups = HEADS % mesh.shape["seq"] == 0 and mesh.shape["seq"] <= 8
    program = shards if whole_groups else cycled_shards
    return jax.shard_map(program, mesh=mesh, in_specs=in_specs, out_specs=out_specs, check_vma=False)
```

```python
import functools

import jax
import jax.numpy as jnp
from jax import lax
from jax.experimental import pallas as pl
from jax.experimental.pallas import tpu as pltpu
from jax.sharding import PartitionSpec as P

HEADS = 24
HEAD_DIM = 128
D = 3072
LAT_CH = 16
SCHED_STEPS = 50
MICRO = 2
TOK_DEV = 8
FRAMES = 4
LAT_W = 8


guide_scale = 5.0
norm_eps = 1e-06


def swapped(value, axis, bit):
    return lax.ppermute(value, axis, [(i, i ^ 1 << bit) for i in range(lax.axis_size(axis))])


def passed_along(value, axis, by):
    size = lax.axis_size(axis)
    pairs = [(i, i + by) for i in range(size) if 0 <= i + by < size]
    return lax.ppermute(value, axis, pairs)


def rms_scaled(values):
    wide = values.astype(jnp.float32)
    return wide * lax.rsqrt(jnp.mean(wide * wide, axis=-1, keepdims=True) + norm_eps)


def cycle_join(piece, seq_index, cycle_bits):
    joined = piece
    for bit_number in range(cycle_bits):
        partner = swapped(joined, "seq", bit_number)
        upper_half = (seq_index // 2**bit_number % 2).astype(jnp.int32)
        part_rows = joined.shape[0]
        combined = jnp.zeros((2 * part_rows,) + joined.shape[1:], joined.dtype)
        combined = lax.dynamic_update_slice_in_dim(combined, joined, upper_half * part_rows, 0)
        joined = lax.dynamic_update_slice_in_dim(combined, partner, (1 - upper_half) * part_rows, 0)
    return joined


def cycled_shards(
    latent,
    w_embed,
    w_qkv,
    w_out,
    mod_table,
    cond_mod,
    stale_kv,
    w_final,
    w_conv,
    patch_order,
    timestep,
    slab_rows,
):
    seq_count = lax.axis_size("seq")
    segment_count = lax.axis_size("segment")
    seq_index = lax.axis_index("seq")
    segment_index = lax.axis_index("segment")
    branch_index = lax.axis_index("cfg")
    group_count = min(seq_count, 8)
    cycle_size = seq_count // group_count
    cycle_bits = cycle_size.bit_length() - 1
    group_heads = HEADS // group_count
    sub_rows = TOK_DEV // cycle_size
    share_rows = seq_count * sub_rows
    kv_lanes = 2 * group_heads * HEAD_DIM
    table_row = lax.dynamic_index_in_dim(mod_table, timestep[0], 0, keepdims=False).astype(
        jnp.float32
    )
    modulation = table_row + cond_mod[0, 0]
    shift_row = modulation[0]
    scale_row = modulation[1]
    gate_row = modulation[2]
    joined_weights = (
        cycle_join(w_qkv[0], seq_index, cycle_bits),
        cycle_join(w_out[0], seq_index, cycle_bits),
    )
    stale_joined = cycle_join(stale_kv[0, 0], seq_index, cycle_bits)
    cache = jnp.transpose(stale_joined, (1, 0, 2, 3)).reshape(
        MICRO, cycle_size * share_rows, kv_lanes
    )
    received = jnp.zeros((TOK_DEV, D), jnp.bfloat16)
    finished = jnp.zeros((MICRO, TOK_DEV, D), jnp.bfloat16)
    slot_ids = jnp.arange(MICRO)
    tick_count = MICRO + segment_count - 1
    for tick_index in range(tick_count):
        qkv_rows, out_rows = joined_weights
        micro_index = tick_index - segment_index
        active = (micro_index >= 0) & (micro_index < MICRO)
        clipped = jnp.clip(micro_index, 0, MICRO - 1)
        patch_id = jnp.sum(jnp.where(slot_ids == clipped, patch_order, 0))
        own_latent = lax.dynamic_index_in_dim(latent, patch_id, 0, keepdims=False).astype(
            jnp.bfloat16
        )
        embedded = jnp.dot(own_latent, w_embed, preferred_element_type=jnp.float32).astype(
            jnp.bfloat16
        )
        layer_input = jnp.where(segment_index == 0, embedded, received)
        normed = (rms_scaled(layer_input) * (1.0 + scale_row) + shift_row).astype(jnp.bfloat16)
        outgoing = jnp.broadcast_to(
            normed.reshape(1, cycle_size, sub_rows, D), (group_count, cycle_size, sub_rows, D)
        )
        shared = lax.all_to_all(
            outgoing.reshape(share_rows, D), "seq", split_axis=0, concat_axis=0, tiled=True
        )
        projected = lax.dot_general(
            shared, qkv_rows, (((1,), (1,)), ((), ())), preferred_element_type=jnp.float32
        )
        projected = projected.astype(jnp.bfloat16).reshape(share_rows, group_heads, 3, HEAD_DIM)
        queries = projected[:, :, 0]
        fresh_local = jnp.transpose(projected[:, :, 1:], (0, 2, 1, 3)).reshape(
            1, share_rows, kv_lanes
        )
        fresh = cycle_join(fresh_local, seq_index, cycle_bits).reshape(
            cycle_size * share_rows, kv_lanes
        )
        previous = lax.dynamic_index_in_dim(cache, patch_id, 0, keepdims=False)
        cache = lax.dynamic_update_index_in_dim(
            cache, jnp.where(active, fresh, previous), patch_id, 0
        )
        keyvals = cache.reshape(MICRO * cycle_size * share_rows, 2, group_heads, HEAD_DIM)
        scores = jnp.einsum(
            "shd,khd->hsk", queries, keyvals[:, 0], preferred_element_type=jnp.float32
        ) * HEAD_DIM ** (-0.5)
        probs = jax.nn.softmax(scores, axis=-1).astype(jnp.bfloat16)
        attended = jnp.einsum(
            "hsk,khd->shd", probs, keyvals[:, 1], preferred_element_type=jnp.float32
        ).astype(jnp.bfloat16)
        partial_out = jnp.dot(
            attended.reshape(share_rows, group_heads * HEAD_DIM),
            out_rows,
            preferred_element_type=jnp.float32,
        )
        returned = lax.all_to_all(
            partial_out.astype(jnp.bfloat16), "seq", split_axis=0, concat_axis=0, tiled=True
        ).astype(partial_out.dtype)
        mixed = jnp.sum(returned.reshape(group_count, cycle_size, sub_rows, D), axis=0).reshape(
            TOK_DEV, D
        )
        layer_output = (layer_input.astype(jnp.float32) + gate_row * mixed).astype(jnp.bfloat16)
        keep_final = active & (segment_index == segment_count - 1)
        earlier = lax.dynamic_index_in_dim(finished, patch_id, 0, keepdims=False)
        finished = lax.dynamic_update_index_in_dim(
            finished, jnp.where(keep_final, layer_output, earlier), patch_id, 0
        )
        if tick_index + 1 < tick_count:
            received = passed_along(layer_output, "segment", 1)
    final_normed = rms_scaled(finished).astype(jnp.bfloat16)
    predicted = jnp.einsum("mtd,dc->mtc", final_normed, w_final, preferred_element_type=jnp.float32)
    is_last = segment_index == segment_count - 1
    branch_weight = jnp.where(branch_index == 0, 1.0 - guide_scale, guide_scale)
    velocity_term = jnp.where(is_last, branch_weight * predicted, 0.0)
    latent_term = jnp.where(is_last & (branch_index == 0), latent, 0.0)
    velocity_own, latent_own = lax.psum((velocity_term, latent_term), ("segment", "cfg"))
    velocity_full, latent_full = (
        lax.all_gather(velocity_own, "seq", axis=1, tiled=True),
        lax.all_gather(latent_own, "seq", axis=1, tiled=True),
    )
    stepped = (latent_full - velocity_full / SCHED_STEPS).astype(jnp.bfloat16)
    decoded = decoder_input(stepped, w_conv, slab_rows, seq_index, seq_count)
    return (velocity_own, decoded)


NT = (((1,), (1,)), ((), ()))


def kernel_params(mebibytes=8):
    return pltpu.CompilerParams(vmem_limit_bytes=mebibytes * 2**20)


def whole(space=pltpu.VMEM):
    return pl.BlockSpec(memory_space=space)


def in_order(copies, ahead):
    for copy in copies[:ahead]:
        copy.start()

    def landed():
        for i, copy in enumerate(copies):
            copy.wait()
            if i + ahead < len(copies):
                copies[i + ahead].start()
            yield i

    return landed()


def prepare_kernel(
    timestep_ref, table_hbm, cond_hbm, embed_hbm, qkv_hbm, rows_ref, heads_ref, term_ref, table, cond, embed, qkv, lhs, sems
):
    tiles, tile = qkv.shape[:2]
    small = [
        pltpu.make_async_copy(source, target, sems.at[tiles + i])
        for i, (source, target) in enumerate(
            ((table_hbm, table), (cond_hbm, cond), (embed_hbm, embed))
        )
    ]
    for copy in small:
        copy.start()
    landed = in_order(
        [
            pltpu.make_async_copy(qkv_hbm.at[pl.ds(i * tile, tile)], qkv.at[i], sems.at[i])
            for i in range(tiles)
        ],
        4,
    )
    for copy in small:
        copy.wait()
    steps = table.shape[1]
    chosen = lax.broadcasted_iota(jnp.int32, (16, steps), 1) == timestep_ref[0]
    chosen = jnp.where(chosen, 1.0, 0.0).astype(jnp.bfloat16)
    for j in range(3):
        row = jnp.dot(chosen, table[j], preferred_element_type=jnp.float32)[:1]
        rows_ref[j : j + 1, :] = row + cond[j] + (1.0 if j == 1 else 0.0)
    count = embed.shape[0]
    lhs[:count] = (embed[...].astype(jnp.float32) * rows_ref[1:2]).astype(jnp.bfloat16)
    lhs[count:] = jnp.broadcast_to(rows_ref[0:1], (16, lhs.shape[1])).astype(jnp.bfloat16)
    for i in landed:
        part = pl.ds(i * tile, tile)
        product = lax.dot_general(lhs[...], qkv[i], NT, preferred_element_type=jnp.float32)
        heads_ref[:, part] = product[:count].astype(jnp.bfloat16)
        term_ref[:, part] = product[count:]


def in_hbm(*values):
    return [pltpu.with_memory_space_constraint(value, pltpu.HBM) for value in values]


def prepared(timestep, table, cond, w_embed, qkv):
    count, depth = w_embed.shape
    lanes = qkv.shape[0]
    tiles = lanes // 256
    return pl.pallas_call(
        prepare_kernel,
        in_specs=[whole(pltpu.SMEM)] + [whole(pltpu.HBM)] * 4,
        out_specs=[whole()] * 3,
        out_shape=[
            jax.ShapeDtypeStruct((3, depth), jnp.float32),
            jax.ShapeDtypeStruct((count, lanes), jnp.bfloat16),
            jax.ShapeDtypeStruct((16, lanes), jnp.float32),
        ],
        scratch_shapes=[
            pltpu.VMEM(table.shape, table.dtype),
            pltpu.VMEM(cond.shape, cond.dtype),
            pltpu.VMEM(w_embed.shape, w_embed.dtype),
            pltpu.VMEM((tiles, 256, depth), qkv.dtype),
            pltpu.VMEM((count + 16, depth), jnp.bfloat16),
            pltpu.SemaphoreType.DMA((tiles + 3,)),
        ],
        cost_estimate=pl.CostEstimate(
            flops=2 * count * depth * lanes, bytes_accessed=2 * qkv.size, transcendentals=0
        ),
        compiler_params=kernel_params(24),
    )(timestep, *in_hbm(table, cond, w_embed, qkv))


def attend(projected, order_ref, stale_ref, attended):
    rows = projected.shape[0]
    patch_rows = stale_ref.shape[1]
    lanes = attended.shape[1]
    kept = order_ref[1]

    def micro_of(shape, dim):
        patch = lax.broadcasted_iota(jnp.int32, shape, dim) // TOK_DEV % MICRO
        return jnp.where(patch == kept, 1, 0)

    unseen = micro_of((rows, rows), 0) < micro_of((rows, rows), 1)
    late = micro_of((rows, patch_rows), 0) > 0
    for head in range(lanes // HEAD_DIM):
        first = 3 * HEAD_DIM * head
        queries = projected[:, first : first + HEAD_DIM]
        keys = projected[:, first + HEAD_DIM : first + 2 * HEAD_DIM]
        values = projected[:, first + 2 * HEAD_DIM : first + 3 * HEAD_DIM]
        part = slice(head * HEAD_DIM, (head + 1) * HEAD_DIM)
        value_part = slice(lanes + head * HEAD_DIM, lanes + (head + 1) * HEAD_DIM)
        fresh = lax.dot_general(queries, keys, NT, preferred_element_type=jnp.float32)
        stale = lax.dot_general(
            queries, stale_ref[kept, :, part], NT, preferred_element_type=jnp.float32
        )
        fresh = jnp.where(unseen, -jnp.inf, fresh * HEAD_DIM ** (-0.5))
        stale = jnp.where(late, -jnp.inf, stale * HEAD_DIM ** (-0.5))
        top = jnp.maximum(
            jnp.max(fresh, axis=-1, keepdims=True), jnp.max(stale, axis=-1, keepdims=True)
        )
        fresh = jnp.exp(fresh - top)
        stale = jnp.exp(stale - top)
        total = jnp.sum(fresh, axis=-1, keepdims=True) + jnp.sum(stale, axis=-1, keepdims=True)
        fresh = (fresh / total).astype(jnp.bfloat16)
        stale = (stale / total).astype(jnp.bfloat16)
        attended[:, part] = (
            jnp.dot(fresh, values, preferred_element_type=jnp.float32)
            + jnp.dot(stale, stale_ref[kept, :, value_part], preferred_element_type=jnp.float32)
        ).astype(jnp.bfloat16)


def column_blocks(place, attended, out_ref, block_refs):
    count = len(block_refs)
    columns = out_ref.shape[1] // count
    for k in range(count):
        first = pl.multiple_of((place ^ k) * columns, columns)
        block_refs[k][...] = jnp.dot(
            attended[...], out_ref[:, pl.ds(first, columns)], preferred_element_type=jnp.float32
        ).astype(jnp.bfloat16)


def first_layer_kernel(
    count, order_ref, embed_ref, heads_ref, term_ref, stale_ref, out_hbm, *refs
):
    latent_refs, refs = refs[:count], refs[count:]
    block_refs, own_ref, latents, attended, out_ref, sem = refs[:count], *refs[count:]
    out_copy = pltpu.make_async_copy(out_hbm, out_ref, sem)
    out_copy.start()
    place = lax.axis_index("seq")
    rows_dev = MICRO * TOK_DEV
    for k in range(count):
        first = pl.multiple_of((place ^ k) * rows_dev, rows_dev)
        latents[pl.ds(first, rows_dev), :] = (
            latent_refs[k][...].reshape(rows_dev, latents.shape[1]).astype(jnp.bfloat16)
        )
    embedded = jnp.dot(latents[...], embed_ref[...], preferred_element_type=jnp.float32)
    embedded = embedded.astype(jnp.bfloat16).astype(jnp.float32)
    norm = lax.rsqrt(jnp.mean(embedded * embedded, axis=-1, keepdims=True) + norm_eps)
    projected = jnp.dot(latents[...], heads_ref[...], preferred_element_type=jnp.float32)
    projected = (norm * projected + term_ref[:1]).astype(jnp.bfloat16)
    attend(projected, order_ref, stale_ref, attended)
    columns = own_ref.shape[1]
    first = pl.multiple_of(place * columns, columns)
    own_ref[...] = jnp.dot(
        latents[...], embed_ref[:, pl.ds(first, columns)], preferred_element_type=jnp.float32
    ).astype(jnp.bfloat16)
    out_copy.wait()
    column_blocks(place, attended, out_ref, block_refs)


def first_layer(patch_order, latent_pieces, w_embed, heads, term, stale, out):
    count = len(latent_pieces)
    rows = count * MICRO * TOK_DEV
    lanes, depth = out.shape
    block = jax.ShapeDtypeStruct((rows, depth // count), jnp.bfloat16)
    return pl.pallas_call(
        functools.partial(first_layer_kernel, count),
        in_specs=[whole(pltpu.SMEM)] + [whole()] * 4 + [whole(pltpu.HBM)] + [whole()] * count,
        out_specs=[whole()] * (count + 1),
        out_shape=[block] * (count + 1),
        scratch_shapes=[
            pltpu.VMEM((rows, w_embed.shape[0]), jnp.bfloat16),
            pltpu.VMEM((rows, lanes), jnp.bfloat16),
            pltpu.VMEM(out.shape, out.dtype),
            pltpu.SemaphoreType.DMA,
        ],
        compiler_params=kernel_params(12),
    )(
        patch_order,
        w_embed,
        heads,
        term,
        stale,
        *in_hbm(out),
        *latent_pieces,
    )


def fetch_kernel(qkv_hbm, out_hbm, after_ref, *refs):
    block_refs, out_ref, done_ref, sems = refs[:-3], *refs[-3:]
    count = len(block_refs)
    place = lax.axis_index("seq")
    copies = []
    for k, block_ref in enumerate(block_refs):
        columns = block_ref.shape[1]
        first = pl.multiple_of((place ^ k) * columns, columns)
        copies.append(
            pltpu.make_async_copy(qkv_hbm.at[:, pl.ds(first, columns)], block_ref, sems.at[k])
        )
    copies.append(pltpu.make_async_copy(out_hbm, out_ref, sems.at[count]))
    for _ in in_order(copies, len(copies)):
        pass
    done_ref[...] = jnp.zeros_like(done_ref)


def fetched(count, qkv, out, after):
    lanes, depth = qkv.shape
    return pl.pallas_call(
        fetch_kernel,
        in_specs=[whole(pltpu.HBM)] * 2 + [whole(pl.ANY)],
        out_specs=[whole()] * (count + 2),
        out_shape=[pltpu.VMEM((lanes, depth // count), qkv.dtype)] * count
        + [pltpu.VMEM(out.shape, out.dtype), jax.ShapeDtypeStruct((8, 128), jnp.float32)],
        scratch_shapes=[pltpu.SemaphoreType.DMA((count + 1,))],
        cost_estimate=pl.CostEstimate(
            flops=0, bytes_accessed=2 * (qkv.size + out.size), transcendentals=0
        ),
        compiler_params=kernel_params(),
    )(*in_hbm(qkv, out), after)


def block_sum_kernel(rows_ref, own_ref, done_ref, *refs):
    part_refs, block_ref = refs[:-1], refs[-1]
    columns = own_ref.shape[1]
    first = pl.multiple_of(lax.axis_index("seq") * columns, columns)
    mixed = part_refs[0][...].astype(jnp.float32)
    for part_ref in part_refs[1:]:
        mixed = mixed + part_ref[...].astype(jnp.float32)
    gate = rows_ref[2:3, pl.ds(first, columns)]
    block_ref[...] = (own_ref[...].astype(jnp.float32) + gate * mixed).astype(jnp.bfloat16)


def block_sum(mod_rows, own, done, parts):
    return pl.pallas_call(
        block_sum_kernel,
        in_specs=[whole()] * (3 + len(parts)),
        out_specs=whole(),
        out_shape=jax.ShapeDtypeStruct(own.shape, own.dtype),
        compiler_params=kernel_params(),
    )(mod_rows, own, done, *parts)


def scaled_piece(place, k, piece_ref, rows_ref):
    columns = piece_ref.shape[1]
    first = pl.multiple_of((place ^ k) * columns, columns)
    wide = piece_ref[...].astype(jnp.float32)
    scaled = (wide * rows_ref[1:2, pl.ds(first, columns)]).astype(jnp.bfloat16)
    return scaled, jnp.sum(wide * wide, axis=-1, keepdims=True)


TILE = 256


def sums_kernel(numbers, rows_ref, *refs):
    count = len(numbers)
    piece_refs, weight_refs = refs[:count], refs[count : 2 * count]
    earlier, (sums_ref, squares_ref) = refs[2 * count : -2], refs[-2:]
    place = lax.axis_index("seq")
    squares = earlier[1][...] if earlier else 0.0
    scaled = []
    for k, piece_ref in zip(numbers, piece_refs):
        piece, square = scaled_piece(place, k, piece_ref, rows_ref)
        scaled.append(piece)
        squares = squares + square
    squares_ref[...] = squares
    for i in range(0, sums_ref.shape[1], TILE):
        lane = slice(i, i + TILE)
        total = earlier[0][:, lane] if earlier else 0.0
        for piece, weight_ref in zip(scaled, weight_refs):
            total = total + lax.dot_general(
                piece, weight_ref[lane, :], NT, preferred_element_type=jnp.float32
            )
        sums_ref[:, lane] = total


def in_vmem(*values):
    return [pltpu.with_memory_space_constraint(value, pltpu.VMEM) for value in values]


def product_sums(numbers, pieces, mod_rows, weights, earlier):
    rows, columns = pieces[0].shape
    lanes = weights[0].shape[0]
    return pl.pallas_call(
        functools.partial(sums_kernel, numbers),
        in_specs=[whole()] * (1 + 2 * len(numbers) + len(earlier)),
        out_specs=[whole()] * 2,
        out_shape=[
            jax.ShapeDtypeStruct((rows, lanes), jnp.float32),
            jax.ShapeDtypeStruct((rows, 1), jnp.float32),
        ],
        compiler_params=kernel_params(),
    )(mod_rows, *pieces, *in_vmem(*weights), *earlier)


def later_layer_kernel(
    count, last, order_ref, rows_ref, qkv_ref, out_ref, term_ref, stale_ref, sums_ref, squares_ref, *refs
):
    piece_refs, refs = refs[:count], refs[count:]
    block_refs, own_ref, sums, attended, partial_out = refs[:count], *refs[count:]
    place = lax.axis_index("seq")
    scaled, squares = scaled_piece(place, count - 1, piece_refs[-1], rows_ref)
    norm = lax.rsqrt((squares_ref[...] + squares) / rows_ref.shape[1] + norm_eps)
    for i in range(0, sums.shape[1], TILE):
        lane = slice(i, i + TILE)
        product = lax.dot_general(
            scaled, qkv_ref[lane, :], NT, preferred_element_type=jnp.float32
        )
        sums[:, lane] = (norm * (product + sums_ref[:, lane]) + term_ref[:1, lane]).astype(
            jnp.bfloat16
        )
    attend(sums, order_ref, stale_ref, attended)
    if not last:
        column_blocks(place, attended, out_ref, block_refs)
        own_ref[...] = piece_refs[0][...]
        return
    partial_out[...] = jnp.dot(
        attended[...], out_ref[...], preferred_element_type=jnp.float32
    ).astype(jnp.bfloat16)
    rows_dev = own_ref.shape[0]
    columns = piece_refs[0].shape[1]
    own_rows = pl.ds(pl.multiple_of(place * rows_dev, rows_dev), rows_dev)
    for k in range(count):
        first = pl.multiple_of((place ^ k) * rows_dev, rows_dev)
        block_refs[k][...] = partial_out[pl.ds(first, rows_dev), :]
        first = pl.multiple_of((place ^ k) * columns, columns)
        own_ref[:, pl.ds(first, columns)] = piece_refs[k][own_rows, :]


def later_layer(last, patch_order, pieces, mod_rows, qkv_block, out, term, stale, sums, squares):
    count = len(pieces)
    rows, columns = pieces[0].shape
    lanes, depth = out.shape
    shape = (rows // count, depth) if last else (rows, columns)
    block = jax.ShapeDtypeStruct(shape, jnp.bfloat16)
    return pl.pallas_call(
        functools.partial(later_layer_kernel, count, last),
        in_specs=[whole(pltpu.SMEM)] + [whole()] * (7 + count),
        out_specs=[whole()] * (count + 1),
        out_shape=[block] * (count + 1),
        scratch_shapes=[
            pltpu.VMEM(sums.shape, jnp.bfloat16),
            pltpu.VMEM((rows, lanes), jnp.bfloat16),
            pltpu.VMEM((rows, depth), jnp.bfloat16),
        ],
        compiler_params=kernel_params(),
    )(patch_order, mod_rows, *in_vmem(qkv_block, out), term, stale, sums, squares, *pieces)


def shards(
    latent,
    w_embed,
    w_qkv,
    w_out,
    mod_table,
    cond_mod,
    stale_kv,
    w_final,
    w_conv,
    patch_order,
    timestep,
    slab_rows,
):
    seq_count = lax.axis_size("seq")
    segment_count = lax.axis_size("segment")
    seq_index = lax.axis_index("seq")
    segment_index = lax.axis_index("segment")
    branch_index = lax.axis_index("cfg")
    rows_dev = MICRO * TOK_DEV

    def within(k):
        return [(i, i ^ k) for i in range(seq_count)]

    def spread(value):
        return [value] + [lax.ppermute(value, "seq", within(k)) for k in range(1, seq_count)]

    def returned(values):
        return values[:1] + [
            lax.ppermute(values[k], "seq", within(k)) for k in range(1, seq_count)
        ]

    latent_pieces = spread(latent)
    mod_rows, head_embed, shift_term = prepared(
        timestep, jnp.transpose(mod_table, (1, 0, 2)), jnp.transpose(cond_mod[0], (1, 0, 2)), w_embed, w_qkv[0]
    )
    stale = stale_kv[0, 0, 0]
    *blocks, own = first_layer(
        patch_order, latent_pieces, w_embed, head_embed, shift_term, stale, w_out[0]
    )
    numbers = tuple(range(seq_count))
    *qkv_blocks, out, done = fetched(seq_count, w_qkv[0], w_out[0], own)
    for step in range(1, segment_count):
        block = block_sum(mod_rows, own, done, returned(blocks))
        pieces = []
        for k in numbers:
            pairs = [
                (i * segment_count + step - 1, (i ^ k) * segment_count + step)
                for i in range(seq_count)
            ]
            pieces.append(lax.ppermute(block, ("seq", "segment"), pairs))
        half = (seq_count + 1) // 2
        sums = ()
        for some in (numbers[:half], numbers[half:-1]):
            if some:
                sums = product_sums(
                    some,
                    [pieces[k] for k in some],
                    mod_rows,
                    [qkv_blocks[k] for k in some],
                    sums,
                )
        *blocks, own = later_layer(
            step + 1 == segment_count,
            patch_order,
            pieces,
            mod_rows,
            qkv_blocks[-1],
            out,
            shift_term,
            stale,
            *sums,
        )

    blocks, latent_pieces, slab_rows, w_conv, w_final = lax.optimization_barrier(
        (blocks, latent_pieces, slab_rows, w_conv, w_final)
    )
    mixed = sum(part.astype(jnp.float32) for part in returned(blocks))
    final = (own.astype(jnp.float32) + mod_rows[2] * mixed).astype(jnp.bfloat16)
    predicted = jnp.dot(
        rms_scaled(final).astype(jnp.bfloat16), w_final, preferred_element_type=jnp.float32
    )
    term = jnp.where(branch_index == 0, 1.0 - guide_scale, guide_scale) * predicted
    peers = ("seq", "segment", "cfg")
    sizes = tuple(lax.axis_size(axis) for axis in peers)
    terms = lax.all_to_all(
        jnp.broadcast_to(term, sizes + term.shape).reshape(-1, term.shape[1]),
        peers,
        split_axis=0,
        concat_axis=0,
        tiled=True,
    ).reshape(sizes + (MICRO, TOK_DEV, -1))
    velocity = terms[:, -1, 0] + terms[:, -1, 1]
    velocity_own = lax.dynamic_index_in_dim(velocity, seq_index, 0, keepdims=False)
    latents = jnp.take(jnp.stack(latent_pieces), jnp.arange(seq_count) ^ seq_index, axis=0)
    stepped = (latents - velocity / SCHED_STEPS).astype(jnp.bfloat16)
    stepped = jnp.transpose(stepped, (1, 0, 2, 3))
    decoded = decoder_input(stepped, w_conv, slab_rows, seq_index, seq_count)
    return (velocity_own, decoded)


def decoder_input(stepped, w_conv, slab_rows, seq_index, seq_count):
    token_rows = MICRO * seq_count * TOK_DEV // (FRAMES * (LAT_W // 2))
    image_rows = 2 * token_rows
    slab_most = 2 * image_rows // seq_count
    image = stepped.reshape(FRAMES, token_rows, LAT_W // 2, 2, 2, LAT_CH)
    image = (
        jnp.transpose(image, (0, 1, 3, 2, 4, 5))
        .reshape(FRAMES, image_rows, LAT_W, LAT_CH)
    )
    padded = jnp.concatenate([image[:1], image[:1], image], 0)
    padded = jnp.pad(padded, ((0, 0), (1, 1 + slab_most), (1, 1), (0, 0)))
    positions = jnp.arange(seq_count)
    slab_count = jnp.sum(jnp.where(positions == seq_index, slab_rows, 0))
    slab_start = jnp.sum(jnp.where(positions < seq_index, slab_rows, 0))
    window = lax.dynamic_slice_in_dim(padded, slab_start, slab_most + 2, 1)
    pieces = []
    for frame_shift in range(3):
        for row_shift in range(3):
            for col_shift in range(3):
                pieces.append(
                    window[
                        frame_shift : frame_shift + FRAMES,
                        row_shift : row_shift + slab_most,
                        col_shift : col_shift + LAT_W,
                    ]
                )
    columns = jnp.concatenate(pieces, -1).reshape(FRAMES * slab_most * LAT_W, 27 * LAT_CH)
    kernel = w_conv.reshape(27 * LAT_CH, w_conv.shape[2])
    features = jnp.dot(columns, kernel, preferred_element_type=jnp.float32).astype(jnp.bfloat16)
    features = features.reshape(FRAMES, slab_most, LAT_W, w_conv.shape[2])
    row_valid = jnp.arange(slab_most)[None, :, None, None] < slab_count
    decoded = jnp.where(row_valid, features, jnp.zeros_like(features))
    return decoded[None]


def solution(mesh):
    in_specs = (
        P(None, ("groups", "seq"), None),
        P(),
        P("segment", "seq", None),
        P("segment", "seq", None),
        P(),
        P("cfg", ("groups", "segment"), None, None),
        P("segment", "cfg", "seq", None, "groups", None),
        P(),
        P(None, None, ("segment", "cfg")),
        P("groups"),
        P("groups"),
        P("groups"),
    )
    out_specs = (
        P(None, ("groups", "seq"), None),
        P(("groups", "seq"), None, None, None, ("segment", "cfg")),
    )
    whole_groups = 2 <= mesh.shape["seq"] <= 8
    program = shards if whole_groups else cycled_shards
    return jax.shard_map(program, mesh=mesh, in_specs=in_specs, out_specs=out_specs, check_vma=False)
```

```python
import functools

import jax
import jax.numpy as jnp
from jax import lax
from jax.experimental import pallas as pl
from jax.experimental.pallas import tpu as pltpu
from jax.sharding import PartitionSpec as P

HEADS = 24
HEAD_DIM = 128
D = 3072
LAT_CH = 16
SCHED_STEPS = 50
MICRO = 2
TOK_DEV = 8
FRAMES = 4
LAT_W = 8


guide_scale = 5.0
norm_eps = 1e-06


def swapped(value, axis, bit):
    return lax.ppermute(value, axis, [(i, i ^ 1 << bit) for i in range(lax.axis_size(axis))])


def passed_along(value, axis, by):
    size = lax.axis_size(axis)
    pairs = [(i, i + by) for i in range(size) if 0 <= i + by < size]
    return lax.ppermute(value, axis, pairs)


def rms_scaled(values):
    wide = values.astype(jnp.float32)
    return wide * lax.rsqrt(jnp.mean(wide * wide, axis=-1, keepdims=True) + norm_eps)


def cycle_join(piece, seq_index, cycle_bits):
    joined = piece
    for bit_number in range(cycle_bits):
        partner = swapped(joined, "seq", bit_number)
        upper_half = (seq_index // 2**bit_number % 2).astype(jnp.int32)
        part_rows = joined.shape[0]
        combined = jnp.zeros((2 * part_rows,) + joined.shape[1:], joined.dtype)
        combined = lax.dynamic_update_slice_in_dim(combined, joined, upper_half * part_rows, 0)
        joined = lax.dynamic_update_slice_in_dim(combined, partner, (1 - upper_half) * part_rows, 0)
    return joined


def cycled_shards(
    latent,
    w_embed,
    w_qkv,
    w_out,
    mod_table,
    cond_mod,
    stale_kv,
    w_final,
    w_conv,
    patch_order,
    timestep,
    slab_rows,
):
    seq_count = lax.axis_size("seq")
    segment_count = lax.axis_size("segment")
    seq_index = lax.axis_index("seq")
    segment_index = lax.axis_index("segment")
    branch_index = lax.axis_index("cfg")
    group_count = min(seq_count, 8)
    cycle_size = seq_count // group_count
    cycle_bits = cycle_size.bit_length() - 1
    group_heads = HEADS // group_count
    sub_rows = TOK_DEV // cycle_size
    share_rows = seq_count * sub_rows
    kv_lanes = 2 * group_heads * HEAD_DIM
    table_row = lax.dynamic_index_in_dim(mod_table, timestep[0], 0, keepdims=False).astype(
        jnp.float32
    )
    modulation = table_row + cond_mod[0, 0]
    shift_row = modulation[0]
    scale_row = modulation[1]
    gate_row = modulation[2]
    joined_weights = (
        cycle_join(w_qkv[0], seq_index, cycle_bits),
        cycle_join(w_out[0], seq_index, cycle_bits),
    )
    stale_joined = cycle_join(stale_kv[0, 0], seq_index, cycle_bits)
    cache = jnp.transpose(stale_joined, (1, 0, 2, 3)).reshape(
        MICRO, cycle_size * share_rows, kv_lanes
    )
    received = jnp.zeros((TOK_DEV, D), jnp.bfloat16)
    finished = jnp.zeros((MICRO, TOK_DEV, D), jnp.bfloat16)
    slot_ids = jnp.arange(MICRO)
    tick_count = MICRO + segment_count - 1
    for tick_index in range(tick_count):
        qkv_rows, out_rows = joined_weights
        micro_index = tick_index - segment_index
        active = (micro_index >= 0) & (micro_index < MICRO)
        clipped = jnp.clip(micro_index, 0, MICRO - 1)
        patch_id = jnp.sum(jnp.where(slot_ids == clipped, patch_order, 0))
        own_latent = lax.dynamic_index_in_dim(latent, patch_id, 0, keepdims=False).astype(
            jnp.bfloat16
        )
        embedded = jnp.dot(own_latent, w_embed, preferred_element_type=jnp.float32).astype(
            jnp.bfloat16
        )
        layer_input = jnp.where(segment_index == 0, embedded, received)
        normed = (rms_scaled(layer_input) * (1.0 + scale_row) + shift_row).astype(jnp.bfloat16)
        outgoing = jnp.broadcast_to(
            normed.reshape(1, cycle_size, sub_rows, D), (group_count, cycle_size, sub_rows, D)
        )
        shared = lax.all_to_all(
            outgoing.reshape(share_rows, D), "seq", split_axis=0, concat_axis=0, tiled=True
        )
        projected = lax.dot_general(
            shared, qkv_rows, (((1,), (1,)), ((), ())), preferred_element_type=jnp.float32
        )
        projected = projected.astype(jnp.bfloat16).reshape(share_rows, group_heads, 3, HEAD_DIM)
        queries = projected[:, :, 0]
        fresh_local = jnp.transpose(projected[:, :, 1:], (0, 2, 1, 3)).reshape(
            1, share_rows, kv_lanes
        )
        fresh = cycle_join(fresh_local, seq_index, cycle_bits).reshape(
            cycle_size * share_rows, kv_lanes
        )
        previous = lax.dynamic_index_in_dim(cache, patch_id, 0, keepdims=False)
        cache = lax.dynamic_update_index_in_dim(
            cache, jnp.where(active, fresh, previous), patch_id, 0
        )
        keyvals = cache.reshape(MICRO * cycle_size * share_rows, 2, group_heads, HEAD_DIM)
        scores = jnp.einsum(
            "shd,khd->hsk", queries, keyvals[:, 0], preferred_element_type=jnp.float32
        ) * HEAD_DIM ** (-0.5)
        probs = jax.nn.softmax(scores, axis=-1).astype(jnp.bfloat16)
        attended = jnp.einsum(
            "hsk,khd->shd", probs, keyvals[:, 1], preferred_element_type=jnp.float32
        ).astype(jnp.bfloat16)
        partial_out = jnp.dot(
            attended.reshape(share_rows, group_heads * HEAD_DIM),
            out_rows,
            preferred_element_type=jnp.float32,
        )
        returned = lax.all_to_all(
            partial_out.astype(jnp.bfloat16), "seq", split_axis=0, concat_axis=0, tiled=True
        ).astype(partial_out.dtype)
        mixed = jnp.sum(returned.reshape(group_count, cycle_size, sub_rows, D), axis=0).reshape(
            TOK_DEV, D
        )
        layer_output = (layer_input.astype(jnp.float32) + gate_row * mixed).astype(jnp.bfloat16)
        keep_final = active & (segment_index == segment_count - 1)
        earlier = lax.dynamic_index_in_dim(finished, patch_id, 0, keepdims=False)
        finished = lax.dynamic_update_index_in_dim(
            finished, jnp.where(keep_final, layer_output, earlier), patch_id, 0
        )
        if tick_index + 1 < tick_count:
            received = passed_along(layer_output, "segment", 1)
    final_normed = rms_scaled(finished).astype(jnp.bfloat16)
    predicted = jnp.einsum("mtd,dc->mtc", final_normed, w_final, preferred_element_type=jnp.float32)
    is_last = segment_index == segment_count - 1
    branch_weight = jnp.where(branch_index == 0, 1.0 - guide_scale, guide_scale)
    velocity_term = jnp.where(is_last, branch_weight * predicted, 0.0)
    latent_term = jnp.where(is_last & (branch_index == 0), latent, 0.0)
    velocity_own, latent_own = lax.psum((velocity_term, latent_term), ("segment", "cfg"))
    velocity_full, latent_full = (
        lax.all_gather(velocity_own, "seq", axis=1, tiled=True),
        lax.all_gather(latent_own, "seq", axis=1, tiled=True),
    )
    stepped = (latent_full - velocity_full / SCHED_STEPS).astype(jnp.bfloat16)
    decoded = decoder_input(stepped, w_conv, slab_rows, seq_index, seq_count)
    return (velocity_own, decoded)


NT = (((1,), (1,)), ((), ()))


def kernel_params(mebibytes=8):
    return pltpu.CompilerParams(vmem_limit_bytes=mebibytes * 2**20)


def whole(space=pltpu.VMEM):
    return pl.BlockSpec(memory_space=space)


def in_order(copies, ahead):
    for copy in copies[:ahead]:
        copy.start()

    def landed():
        for i, copy in enumerate(copies):
            copy.wait()
            if i + ahead < len(copies):
                copies[i + ahead].start()
            yield i

    return landed()


def prepare_kernel(
    timestep_ref, table_hbm, cond_hbm, embed_hbm, qkv_hbm, rows_ref, heads_ref, term_ref, table, cond, embed, qkv, sums, sems
):
    blocks, lanes, width = qkv.shape
    small = [
        pltpu.make_async_copy(source, target, sems.at[blocks + i])
        for i, (source, target) in enumerate(
            ((table_hbm, table), (cond_hbm, cond), (embed_hbm, embed))
        )
    ]
    for copy in small:
        copy.start()
    landed = in_order(
        [
            pltpu.make_async_copy(
                qkv_hbm.at[:, pl.ds(i * width, width)], qkv.at[i], sems.at[i]
            )
            for i in range(blocks)
        ],
        4,
    )
    for copy in small:
        copy.wait()
    steps = table.shape[1]
    chosen = lax.broadcasted_iota(jnp.int32, (16, steps), 1) == timestep_ref[0]
    chosen = jnp.where(chosen, 1.0, 0.0).astype(jnp.bfloat16)
    for j in range(3):
        row = jnp.dot(chosen, table[j], preferred_element_type=jnp.float32)[:1]
        rows_ref[j : j + 1, :] = row + cond[j] + (1.0 if j == 1 else 0.0)
    count = embed.shape[0]
    for i in landed:
        part = slice(i * width, (i + 1) * width)
        scaled = (embed[:, part].astype(jnp.float32) * rows_ref[1:2, part]).astype(jnp.bfloat16)
        shift = jnp.broadcast_to(rows_ref[0:1, part], (16, width)).astype(jnp.bfloat16)
        lhs = jnp.concatenate([scaled, shift], axis=0)
        for j in range(0, lanes, TILE):
            lane = slice(j, j + TILE)
            product = lax.dot_general(
                lhs, qkv[i, lane, :], NT, preferred_element_type=jnp.float32
            )
            if i:
                product = product + sums[:, lane]
            if i + 1 < blocks:
                sums[:, lane] = product
            else:
                heads_ref[:, lane] = product[:count].astype(jnp.bfloat16)
                term_ref[:, lane] = product[count:]


def in_hbm(*values):
    return [pltpu.with_memory_space_constraint(value, pltpu.HBM) for value in values]


def prepared(timestep, table, cond, w_embed, qkv):
    count, depth = w_embed.shape
    lanes = qkv.shape[0]
    blocks = 6
    return pl.pallas_call(
        prepare_kernel,
        in_specs=[whole(pltpu.SMEM)] + [whole(pltpu.HBM)] * 4,
        out_specs=[whole()] * 3,
        out_shape=[
            jax.ShapeDtypeStruct((3, depth), jnp.float32),
            jax.ShapeDtypeStruct((count, lanes), jnp.bfloat16),
            jax.ShapeDtypeStruct((16, lanes), jnp.float32),
        ],
        scratch_shapes=[
            pltpu.VMEM(table.shape, table.dtype),
            pltpu.VMEM(cond.shape, cond.dtype),
            pltpu.VMEM(w_embed.shape, w_embed.dtype),
            pltpu.VMEM((blocks, lanes, depth // blocks), qkv.dtype),
            pltpu.VMEM((count + 16, lanes), jnp.float32),
            pltpu.SemaphoreType.DMA((blocks + 3,)),
        ],
        cost_estimate=pl.CostEstimate(
            flops=2 * count * depth * lanes, bytes_accessed=2 * qkv.size, transcendentals=0
        ),
        compiler_params=kernel_params(24),
    )(timestep, *in_hbm(table, cond, w_embed, qkv))


def attend(projected, order_ref, stale_ref, attended):
    rows = projected.shape[0]
    patch_rows = stale_ref.shape[1]
    lanes = attended.shape[1]
    kept = order_ref[1]

    def micro_of(shape, dim):
        patch = lax.broadcasted_iota(jnp.int32, shape, dim) // TOK_DEV % MICRO
        return jnp.where(patch == kept, 1, 0)

    unseen = micro_of((rows, rows), 0) < micro_of((rows, rows), 1)
    late = micro_of((rows, patch_rows), 0) > 0
    for head in range(lanes // HEAD_DIM):
        first = 3 * HEAD_DIM * head
        queries = projected[:, first : first + HEAD_DIM]
        keys = projected[:, first + HEAD_DIM : first + 2 * HEAD_DIM]
        values = projected[:, first + 2 * HEAD_DIM : first + 3 * HEAD_DIM]
        part = slice(head * HEAD_DIM, (head + 1) * HEAD_DIM)
        value_part = slice(lanes + head * HEAD_DIM, lanes + (head + 1) * HEAD_DIM)
        fresh = lax.dot_general(queries, keys, NT, preferred_element_type=jnp.float32)
        stale = lax.dot_general(
            queries, stale_ref[kept, :, part], NT, preferred_element_type=jnp.float32
        )
        fresh = jnp.where(unseen, -jnp.inf, fresh * HEAD_DIM ** (-0.5))
        stale = jnp.where(late, -jnp.inf, stale * HEAD_DIM ** (-0.5))
        top = jnp.maximum(
            jnp.max(fresh, axis=-1, keepdims=True), jnp.max(stale, axis=-1, keepdims=True)
        )
        fresh = jnp.exp(fresh - top)
        stale = jnp.exp(stale - top)
        total = jnp.sum(fresh, axis=-1, keepdims=True) + jnp.sum(stale, axis=-1, keepdims=True)
        fresh = (fresh / total).astype(jnp.bfloat16)
        stale = (stale / total).astype(jnp.bfloat16)
        attended[:, part] = (
            jnp.dot(fresh, values, preferred_element_type=jnp.float32)
            + jnp.dot(stale, stale_ref[kept, :, value_part], preferred_element_type=jnp.float32)
        ).astype(jnp.bfloat16)


def column_blocks(place, attended, out_ref, block_refs):
    count = len(block_refs)
    columns = out_ref.shape[1] // count
    for k in range(count):
        first = pl.multiple_of((place ^ k) * columns, columns)
        block_refs[k][...] = jnp.dot(
            attended[...], out_ref[:, pl.ds(first, columns)], preferred_element_type=jnp.float32
        ).astype(jnp.bfloat16)


def first_layer_kernel(
    count, order_ref, embed_ref, heads_ref, term_ref, stale_ref, out_hbm, *refs
):
    latent_refs, refs = refs[:count], refs[count:]
    block_refs, own_ref, latents, attended, out_ref, sem = refs[:count], *refs[count:]
    out_copy = pltpu.make_async_copy(out_hbm, out_ref, sem)
    out_copy.start()
    place = lax.axis_index("seq")
    rows_dev = MICRO * TOK_DEV
    for k in range(count):
        first = pl.multiple_of((place ^ k) * rows_dev, rows_dev)
        latents[pl.ds(first, rows_dev), :] = (
            latent_refs[k][...].reshape(rows_dev, latents.shape[1]).astype(jnp.bfloat16)
        )
    embedded = jnp.dot(latents[...], embed_ref[...], preferred_element_type=jnp.float32)
    embedded = embedded.astype(jnp.bfloat16).astype(jnp.float32)
    norm = lax.rsqrt(jnp.mean(embedded * embedded, axis=-1, keepdims=True) + norm_eps)
    projected = jnp.dot(latents[...], heads_ref[...], preferred_element_type=jnp.float32)
    projected = (norm * projected + term_ref[:1]).astype(jnp.bfloat16)
    attend(projected, order_ref, stale_ref, attended)
    columns = own_ref.shape[1]
    first = pl.multiple_of(place * columns, columns)
    own_ref[...] = jnp.dot(
        latents[...], embed_ref[:, pl.ds(first, columns)], preferred_element_type=jnp.float32
    ).astype(jnp.bfloat16)
    out_copy.wait()
    column_blocks(place, attended, out_ref, block_refs)


def first_layer(patch_order, latent_pieces, w_embed, heads, term, stale, out):
    count = len(latent_pieces)
    rows = count * MICRO * TOK_DEV
    lanes, depth = out.shape
    block = jax.ShapeDtypeStruct((rows, depth // count), jnp.bfloat16)
    return pl.pallas_call(
        functools.partial(first_layer_kernel, count),
        in_specs=[whole(pltpu.SMEM)] + [whole()] * 4 + [whole(pltpu.HBM)] + [whole()] * count,
        out_specs=[whole()] * (count + 1),
        out_shape=[block] * (count + 1),
        scratch_shapes=[
            pltpu.VMEM((rows, w_embed.shape[0]), jnp.bfloat16),
            pltpu.VMEM((rows, lanes), jnp.bfloat16),
            pltpu.VMEM(out.shape, out.dtype),
            pltpu.SemaphoreType.DMA,
        ],
        compiler_params=kernel_params(12),
    )(
        patch_order,
        w_embed,
        heads,
        term,
        stale,
        *in_hbm(out),
        *latent_pieces,
    )


def fetch_kernel(qkv_hbm, out_hbm, after_ref, *refs):
    block_refs, out_ref, done_ref, sems = refs[:-3], *refs[-3:]
    count = len(block_refs)
    place = lax.axis_index("seq")
    copies = []
    for k, block_ref in enumerate(block_refs):
        columns = block_ref.shape[1]
        first = pl.multiple_of((place ^ k) * columns, columns)
        copies.append(
            pltpu.make_async_copy(qkv_hbm.at[:, pl.ds(first, columns)], block_ref, sems.at[k])
        )
    copies.append(pltpu.make_async_copy(out_hbm, out_ref, sems.at[count]))
    for _ in in_order(copies, len(copies)):
        pass
    done_ref[...] = jnp.zeros_like(done_ref)


def fetched(count, qkv, out, after):
    lanes, depth = qkv.shape
    return pl.pallas_call(
        fetch_kernel,
        in_specs=[whole(pltpu.HBM)] * 2 + [whole(pl.ANY)],
        out_specs=[whole()] * (count + 2),
        out_shape=[pltpu.VMEM((lanes, depth // count), qkv.dtype)] * count
        + [pltpu.VMEM(out.shape, out.dtype), jax.ShapeDtypeStruct((8, 128), jnp.float32)],
        scratch_shapes=[pltpu.SemaphoreType.DMA((count + 1,))],
        cost_estimate=pl.CostEstimate(
            flops=0, bytes_accessed=2 * (qkv.size + out.size), transcendentals=0
        ),
        compiler_params=kernel_params(),
    )(*in_hbm(qkv, out), after)


def block_sum_kernel(rows_ref, own_ref, done_ref, *refs):
    part_refs, block_ref = refs[:-1], refs[-1]
    columns = own_ref.shape[1]
    first = pl.multiple_of(lax.axis_index("seq") * columns, columns)
    mixed = part_refs[0][...].astype(jnp.float32)
    for part_ref in part_refs[1:]:
        mixed = mixed + part_ref[...].astype(jnp.float32)
    gate = rows_ref[2:3, pl.ds(first, columns)]
    block_ref[...] = (own_ref[...].astype(jnp.float32) + gate * mixed).astype(jnp.bfloat16)


def block_sum(mod_rows, own, done, parts):
    return pl.pallas_call(
        block_sum_kernel,
        in_specs=[whole()] * (3 + len(parts)),
        out_specs=whole(),
        out_shape=jax.ShapeDtypeStruct(own.shape, own.dtype),
        compiler_params=kernel_params(),
    )(mod_rows, own, done, *parts)


def scaled_piece(place, k, piece_ref, rows_ref):
    columns = piece_ref.shape[1]
    first = pl.multiple_of((place ^ k) * columns, columns)
    wide = piece_ref[...].astype(jnp.float32)
    scaled = (wide * rows_ref[1:2, pl.ds(first, columns)]).astype(jnp.bfloat16)
    return scaled, jnp.sum(wide * wide, axis=-1, keepdims=True)


TILE = 256


def sums_kernel(numbers, rows_ref, *refs):
    count = len(numbers)
    piece_refs, weight_refs = refs[:count], refs[count : 2 * count]
    earlier, (sums_ref, squares_ref) = refs[2 * count : -2], refs[-2:]
    place = lax.axis_index("seq")
    squares = earlier[1][...] if earlier else 0.0
    scaled = []
    for k, piece_ref in zip(numbers, piece_refs):
        piece, square = scaled_piece(place, k, piece_ref, rows_ref)
        scaled.append(piece)
        squares = squares + square
    squares_ref[...] = squares
    for i in range(0, sums_ref.shape[1], TILE):
        lane = slice(i, i + TILE)
        total = earlier[0][:, lane] if earlier else 0.0
        for piece, weight_ref in zip(scaled, weight_refs):
            total = total + lax.dot_general(
                piece, weight_ref[lane, :], NT, preferred_element_type=jnp.float32
            )
        sums_ref[:, lane] = total


def in_vmem(*values):
    return [pltpu.with_memory_space_constraint(value, pltpu.VMEM) for value in values]


def product_sums(numbers, pieces, mod_rows, weights, earlier):
    rows, columns = pieces[0].shape
    lanes = weights[0].shape[0]
    return pl.pallas_call(
        functools.partial(sums_kernel, numbers),
        in_specs=[whole()] * (1 + 2 * len(numbers) + len(earlier)),
        out_specs=[whole()] * 2,
        out_shape=[
            jax.ShapeDtypeStruct((rows, lanes), jnp.float32),
            jax.ShapeDtypeStruct((rows, 1), jnp.float32),
        ],
        compiler_params=kernel_params(),
    )(mod_rows, *pieces, *in_vmem(*weights), *earlier)


def later_layer_kernel(
    count, last, order_ref, rows_ref, qkv_ref, out_ref, term_ref, stale_ref, sums_ref, squares_ref, *refs
):
    piece_refs, refs = refs[:count], refs[count:]
    block_refs, own_ref, sums, attended, partial_out = refs[:count], *refs[count:]
    place = lax.axis_index("seq")
    scaled, squares = scaled_piece(place, count - 1, piece_refs[-1], rows_ref)
    norm = lax.rsqrt((squares_ref[...] + squares) / rows_ref.shape[1] + norm_eps)
    for i in range(0, sums.shape[1], TILE):
        lane = slice(i, i + TILE)
        product = lax.dot_general(
            scaled, qkv_ref[lane, :], NT, preferred_element_type=jnp.float32
        )
        sums[:, lane] = (norm * (product + sums_ref[:, lane]) + term_ref[:1, lane]).astype(
            jnp.bfloat16
        )
    attend(sums, order_ref, stale_ref, attended)
    if not last:
        column_blocks(place, attended, out_ref, block_refs)
        own_ref[...] = piece_refs[0][...]
        return
    partial_out[...] = jnp.dot(
        attended[...], out_ref[...], preferred_element_type=jnp.float32
    ).astype(jnp.bfloat16)
    rows_dev = own_ref.shape[0]
    columns = piece_refs[0].shape[1]
    own_rows = pl.ds(pl.multiple_of(place * rows_dev, rows_dev), rows_dev)
    for k in range(count):
        first = pl.multiple_of((place ^ k) * rows_dev, rows_dev)
        block_refs[k][...] = partial_out[pl.ds(first, rows_dev), :]
        first = pl.multiple_of((place ^ k) * columns, columns)
        own_ref[:, pl.ds(first, columns)] = piece_refs[k][own_rows, :]


def later_layer(last, patch_order, pieces, mod_rows, qkv_block, out, term, stale, sums, squares):
    count = len(pieces)
    rows, columns = pieces[0].shape
    lanes, depth = out.shape
    shape = (rows // count, depth) if last else (rows, columns)
    block = jax.ShapeDtypeStruct(shape, jnp.bfloat16)
    return pl.pallas_call(
        functools.partial(later_layer_kernel, count, last),
        in_specs=[whole(pltpu.SMEM)] + [whole()] * (7 + count),
        out_specs=[whole()] * (count + 1),
        out_shape=[block] * (count + 1),
        scratch_shapes=[
            pltpu.VMEM(sums.shape, jnp.bfloat16),
            pltpu.VMEM((rows, lanes), jnp.bfloat16),
            pltpu.VMEM((rows, depth), jnp.bfloat16),
        ],
        compiler_params=kernel_params(),
    )(patch_order, mod_rows, *in_vmem(qkv_block, out), term, stale, sums, squares, *pieces)


def shards(
    latent,
    w_embed,
    w_qkv,
    w_out,
    mod_table,
    cond_mod,
    stale_kv,
    w_final,
    w_conv,
    patch_order,
    timestep,
    slab_rows,
):
    seq_count = lax.axis_size("seq")
    segment_count = lax.axis_size("segment")
    seq_index = lax.axis_index("seq")
    segment_index = lax.axis_index("segment")
    branch_index = lax.axis_index("cfg")
    rows_dev = MICRO * TOK_DEV

    def within(k):
        return [(i, i ^ k) for i in range(seq_count)]

    def spread(value):
        return [value] + [lax.ppermute(value, "seq", within(k)) for k in range(1, seq_count)]

    def returned(values):
        return values[:1] + [
            lax.ppermute(values[k], "seq", within(k)) for k in range(1, seq_count)
        ]

    latent_pieces = spread(latent)
    mod_rows, head_embed, shift_term = prepared(
        timestep, jnp.transpose(mod_table, (1, 0, 2)), jnp.transpose(cond_mod[0], (1, 0, 2)), w_embed, w_qkv[0]
    )
    stale = stale_kv[0, 0, 0]
    *blocks, own = first_layer(
        patch_order, latent_pieces, w_embed, head_embed, shift_term, stale, w_out[0]
    )
    numbers = tuple(range(seq_count))
    *qkv_blocks, out, done = fetched(seq_count, w_qkv[0], w_out[0], own)
    for step in range(1, segment_count):
        block = block_sum(mod_rows, own, done, returned(blocks))
        pieces = []
        for k in numbers:
            pairs = [
                (i * segment_count + j, (i ^ k) * segment_count + (j + 1) % segment_count)
                for i in range(seq_count)
                for j in range(segment_count)
            ]
            pieces.append(lax.ppermute(block, ("seq", "segment"), pairs))
        half = (seq_count + 1) // 2
        sums = ()
        for some in (numbers[:half], numbers[half:-1]):
            if some:
                sums = product_sums(
                    some,
                    [pieces[k] for k in some],
                    mod_rows,
                    [qkv_blocks[k] for k in some],
                    sums,
                )
        *blocks, own = later_layer(
            step + 1 == segment_count,
            patch_order,
            pieces,
            mod_rows,
            qkv_blocks[-1],
            out,
            shift_term,
            stale,
            *sums,
        )

    blocks, latent_pieces, slab_rows, w_conv, w_final = lax.optimization_barrier(
        (blocks, latent_pieces, slab_rows, w_conv, w_final)
    )
    mixed = sum(part.astype(jnp.float32) for part in returned(blocks))
    final = (own.astype(jnp.float32) + mod_rows[2] * mixed).astype(jnp.bfloat16)
    predicted = jnp.dot(
        rms_scaled(final).astype(jnp.bfloat16), w_final, preferred_element_type=jnp.float32
    )
    term = jnp.where(branch_index == 0, 1.0 - guide_scale, guide_scale) * predicted
    peers = ("seq", "segment", "cfg")
    sizes = tuple(lax.axis_size(axis) for axis in peers)
    terms = lax.all_to_all(
        jnp.broadcast_to(term, sizes + term.shape).reshape(-1, term.shape[1]),
        peers,
        split_axis=0,
        concat_axis=0,
        tiled=True,
    ).reshape(sizes + (MICRO, TOK_DEV, -1))
    velocity = terms[:, -1, 0] + terms[:, -1, 1]
    velocity_own = lax.dynamic_index_in_dim(velocity, seq_index, 0, keepdims=False)
    latents = jnp.take(jnp.stack(latent_pieces), jnp.arange(seq_count) ^ seq_index, axis=0)
    stepped = (latents - velocity / SCHED_STEPS).astype(jnp.bfloat16)
    stepped = jnp.transpose(stepped, (1, 0, 2, 3))
    decoded = decoder_input(stepped, w_conv, slab_rows, seq_index, seq_count)
    return (velocity_own, decoded)


def decoder_input(stepped, w_conv, slab_rows, seq_index, seq_count):
    token_rows = MICRO * seq_count * TOK_DEV // (FRAMES * (LAT_W // 2))
    image_rows = 2 * token_rows
    slab_most = 2 * image_rows // seq_count
    image = stepped.reshape(FRAMES, token_rows, LAT_W // 2, 2, 2, LAT_CH)
    image = (
        jnp.transpose(image, (0, 1, 3, 2, 4, 5))
        .reshape(FRAMES, image_rows, LAT_W, LAT_CH)
    )
    padded = jnp.concatenate([image[:1], image[:1], image], 0)
    padded = jnp.pad(padded, ((0, 0), (1, 1 + slab_most), (1, 1), (0, 0)))
    positions = jnp.arange(seq_count)
    slab_count = jnp.sum(jnp.where(positions == seq_index, slab_rows, 0))
    slab_start = jnp.sum(jnp.where(positions < seq_index, slab_rows, 0))
    window = lax.dynamic_slice_in_dim(padded, slab_start, slab_most + 2, 1)
    pieces = []
    for frame_shift in range(3):
        for row_shift in range(3):
            for col_shift in range(3):
                pieces.append(
                    window[
                        frame_shift : frame_shift + FRAMES,
                        row_shift : row_shift + slab_most,
                        col_shift : col_shift + LAT_W,
                    ]
                )
    columns = jnp.concatenate(pieces, -1).reshape(FRAMES * slab_most * LAT_W, 27 * LAT_CH)
    kernel = w_conv.reshape(27 * LAT_CH, w_conv.shape[2])
    features = jnp.dot(columns, kernel, preferred_element_type=jnp.float32).astype(jnp.bfloat16)
    features = features.reshape(FRAMES, slab_most, LAT_W, w_conv.shape[2])
    row_valid = jnp.arange(slab_most)[None, :, None, None] < slab_count
    decoded = jnp.where(row_valid, features, jnp.zeros_like(features))
    return decoded[None]


def solution(mesh):
    in_specs = (
        P(None, ("groups", "seq"), None),
        P(),
        P("segment", "seq", None),
        P("segment", "seq", None),
        P(),
        P("cfg", ("groups", "segment"), None, None),
        P("segment", "cfg", "seq", None, "groups", None),
        P(),
        P(None, None, ("segment", "cfg")),
        P("groups"),
        P("groups"),
        P("groups"),
    )
    out_specs = (
        P(None, ("groups", "seq"), None),
        P(("groups", "seq"), None, None, None, ("segment", "cfg")),
    )
    whole_groups = 2 <= mesh.shape["seq"] <= 8
    program = shards if whole_groups else cycled_shards
    return jax.shard_map(program, mesh=mesh, in_specs=in_specs, out_specs=out_specs, check_vma=False)
```

```python
import functools

import jax
import jax.numpy as jnp
from jax import lax
from jax.experimental import pallas as pl
from jax.experimental.pallas import tpu as pltpu
from jax.sharding import PartitionSpec as P

HEADS = 24
HEAD_DIM = 128
D = 3072
LAT_CH = 16
SCHED_STEPS = 50
MICRO = 2
TOK_DEV = 8
FRAMES = 4
LAT_W = 8


guide_scale = 5.0
norm_eps = 1e-06


def swapped(value, axis, bit):
    return lax.ppermute(value, axis, [(i, i ^ 1 << bit) for i in range(lax.axis_size(axis))])


def passed_along(value, axis, by):
    size = lax.axis_size(axis)
    pairs = [(i, i + by) for i in range(size) if 0 <= i + by < size]
    return lax.ppermute(value, axis, pairs)


def rms_scaled(values):
    wide = values.astype(jnp.float32)
    return wide * lax.rsqrt(jnp.mean(wide * wide, axis=-1, keepdims=True) + norm_eps)


def cycle_join(piece, seq_index, cycle_bits):
    joined = piece
    for bit_number in range(cycle_bits):
        partner = swapped(joined, "seq", bit_number)
        upper_half = (seq_index // 2**bit_number % 2).astype(jnp.int32)
        part_rows = joined.shape[0]
        combined = jnp.zeros((2 * part_rows,) + joined.shape[1:], joined.dtype)
        combined = lax.dynamic_update_slice_in_dim(combined, joined, upper_half * part_rows, 0)
        joined = lax.dynamic_update_slice_in_dim(combined, partner, (1 - upper_half) * part_rows, 0)
    return joined


def cycled_shards(
    latent,
    w_embed,
    w_qkv,
    w_out,
    mod_table,
    cond_mod,
    stale_kv,
    w_final,
    w_conv,
    patch_order,
    timestep,
    slab_rows,
):
    seq_count = lax.axis_size("seq")
    segment_count = lax.axis_size("segment")
    seq_index = lax.axis_index("seq")
    segment_index = lax.axis_index("segment")
    branch_index = lax.axis_index("cfg")
    group_count = min(seq_count, 8)
    cycle_size = seq_count // group_count
    cycle_bits = cycle_size.bit_length() - 1
    group_heads = HEADS // group_count
    sub_rows = TOK_DEV // cycle_size
    share_rows = seq_count * sub_rows
    kv_lanes = 2 * group_heads * HEAD_DIM
    table_row = lax.dynamic_index_in_dim(mod_table, timestep[0], 0, keepdims=False).astype(
        jnp.float32
    )
    modulation = table_row + cond_mod[0, 0]
    shift_row = modulation[0]
    scale_row = modulation[1]
    gate_row = modulation[2]
    joined_weights = (
        cycle_join(w_qkv[0], seq_index, cycle_bits),
        cycle_join(w_out[0], seq_index, cycle_bits),
    )
    stale_joined = cycle_join(stale_kv[0, 0], seq_index, cycle_bits)
    cache = jnp.transpose(stale_joined, (1, 0, 2, 3)).reshape(
        MICRO, cycle_size * share_rows, kv_lanes
    )
    received = jnp.zeros((TOK_DEV, D), jnp.bfloat16)
    finished = jnp.zeros((MICRO, TOK_DEV, D), jnp.bfloat16)
    slot_ids = jnp.arange(MICRO)
    tick_count = MICRO + segment_count - 1
    for tick_index in range(tick_count):
        qkv_rows, out_rows = joined_weights
        micro_index = tick_index - segment_index
        active = (micro_index >= 0) & (micro_index < MICRO)
        clipped = jnp.clip(micro_index, 0, MICRO - 1)
        patch_id = jnp.sum(jnp.where(slot_ids == clipped, patch_order, 0))
        own_latent = lax.dynamic_index_in_dim(latent, patch_id, 0, keepdims=False).astype(
            jnp.bfloat16
        )
        embedded = jnp.dot(own_latent, w_embed, preferred_element_type=jnp.float32).astype(
            jnp.bfloat16
        )
        layer_input = jnp.where(segment_index == 0, embedded, received)
        normed = (rms_scaled(layer_input) * (1.0 + scale_row) + shift_row).astype(jnp.bfloat16)
        outgoing = jnp.broadcast_to(
            normed.reshape(1, cycle_size, sub_rows, D), (group_count, cycle_size, sub_rows, D)
        )
        shared = lax.all_to_all(
            outgoing.reshape(share_rows, D), "seq", split_axis=0, concat_axis=0, tiled=True
        )
        projected = lax.dot_general(
            shared, qkv_rows, (((1,), (1,)), ((), ())), preferred_element_type=jnp.float32
        )
        projected = projected.astype(jnp.bfloat16).reshape(share_rows, group_heads, 3, HEAD_DIM)
        queries = projected[:, :, 0]
        fresh_local = jnp.transpose(projected[:, :, 1:], (0, 2, 1, 3)).reshape(
            1, share_rows, kv_lanes
        )
        fresh = cycle_join(fresh_local, seq_index, cycle_bits).reshape(
            cycle_size * share_rows, kv_lanes
        )
        previous = lax.dynamic_index_in_dim(cache, patch_id, 0, keepdims=False)
        cache = lax.dynamic_update_index_in_dim(
            cache, jnp.where(active, fresh, previous), patch_id, 0
        )
        keyvals = cache.reshape(MICRO * cycle_size * share_rows, 2, group_heads, HEAD_DIM)
        scores = jnp.einsum(
            "shd,khd->hsk", queries, keyvals[:, 0], preferred_element_type=jnp.float32
        ) * HEAD_DIM ** (-0.5)
        probs = jax.nn.softmax(scores, axis=-1).astype(jnp.bfloat16)
        attended = jnp.einsum(
            "hsk,khd->shd", probs, keyvals[:, 1], preferred_element_type=jnp.float32
        ).astype(jnp.bfloat16)
        partial_out = jnp.dot(
            attended.reshape(share_rows, group_heads * HEAD_DIM),
            out_rows,
            preferred_element_type=jnp.float32,
        )
        returned = lax.all_to_all(
            partial_out.astype(jnp.bfloat16), "seq", split_axis=0, concat_axis=0, tiled=True
        ).astype(partial_out.dtype)
        mixed = jnp.sum(returned.reshape(group_count, cycle_size, sub_rows, D), axis=0).reshape(
            TOK_DEV, D
        )
        layer_output = (layer_input.astype(jnp.float32) + gate_row * mixed).astype(jnp.bfloat16)
        keep_final = active & (segment_index == segment_count - 1)
        earlier = lax.dynamic_index_in_dim(finished, patch_id, 0, keepdims=False)
        finished = lax.dynamic_update_index_in_dim(
            finished, jnp.where(keep_final, layer_output, earlier), patch_id, 0
        )
        if tick_index + 1 < tick_count:
            received = passed_along(layer_output, "segment", 1)
    final_normed = rms_scaled(finished).astype(jnp.bfloat16)
    predicted = jnp.einsum("mtd,dc->mtc", final_normed, w_final, preferred_element_type=jnp.float32)
    is_last = segment_index == segment_count - 1
    branch_weight = jnp.where(branch_index == 0, 1.0 - guide_scale, guide_scale)
    velocity_term = jnp.where(is_last, branch_weight * predicted, 0.0)
    latent_term = jnp.where(is_last & (branch_index == 0), latent, 0.0)
    velocity_own, latent_own = lax.psum((velocity_term, latent_term), ("segment", "cfg"))
    velocity_full, latent_full = (
        lax.all_gather(velocity_own, "seq", axis=1, tiled=True),
        lax.all_gather(latent_own, "seq", axis=1, tiled=True),
    )
    stepped = (latent_full - velocity_full / SCHED_STEPS).astype(jnp.bfloat16)
    decoded = decoder_input(stepped, w_conv, slab_rows, seq_index, seq_count)
    return (velocity_own, decoded)


NT = (((1,), (1,)), ((), ()))


def kernel_params(mebibytes=8):
    return pltpu.CompilerParams(vmem_limit_bytes=mebibytes * 2**20)


def whole(space=pltpu.VMEM):
    return pl.BlockSpec(memory_space=space)


def in_order(copies, ahead):
    for copy in copies[:ahead]:
        copy.start()

    def landed():
        for i, copy in enumerate(copies):
            copy.wait()
            if i + ahead < len(copies):
                copies[i + ahead].start()
            yield i

    return landed()


def prepare_kernel(
    timestep_ref, table_hbm, cond_hbm, embed_hbm, qkv_hbm, rows_ref, heads_ref, term_ref, table, cond, embed, qkv, sums, sems
):
    blocks, lanes, width = qkv.shape
    small = [
        pltpu.make_async_copy(source, target, sems.at[blocks + i])
        for i, (source, target) in enumerate(
            ((table_hbm, table), (cond_hbm, cond), (embed_hbm, embed))
        )
    ]
    for copy in small:
        copy.start()
    landed = in_order(
        [
            pltpu.make_async_copy(
                qkv_hbm.at[:, pl.ds(i * width, width)], qkv.at[i], sems.at[i]
            )
            for i in range(blocks)
        ],
        4,
    )
    for copy in small:
        copy.wait()
    steps = table.shape[1]
    chosen = lax.broadcasted_iota(jnp.int32, (16, steps), 1) == timestep_ref[0]
    chosen = jnp.where(chosen, 1.0, 0.0).astype(jnp.bfloat16)
    for j in range(3):
        row = jnp.dot(chosen, table[j], preferred_element_type=jnp.float32)[:1]
        rows_ref[j : j + 1, :] = row + cond[j] + (1.0 if j == 1 else 0.0)
    count = embed.shape[0]
    for i in landed:
        part = slice(i * width, (i + 1) * width)
        scaled = (embed[:, part].astype(jnp.float32) * rows_ref[1:2, part]).astype(jnp.bfloat16)
        shift = jnp.broadcast_to(rows_ref[0:1, part], (16, width)).astype(jnp.bfloat16)
        lhs = jnp.concatenate([scaled, shift], axis=0)
        for j in range(0, lanes, TILE):
            lane = slice(j, j + TILE)
            product = lax.dot_general(
                lhs, qkv[i, lane, :], NT, preferred_element_type=jnp.float32
            )
            if i:
                product = product + sums[:, lane]
            if i + 1 < blocks:
                sums[:, lane] = product
            else:
                heads_ref[:, lane] = product[:count].astype(jnp.bfloat16)
                term_ref[:, lane] = product[count:]


def in_hbm(*values):
    return [pltpu.with_memory_space_constraint(value, pltpu.HBM) for value in values]


def prepared(timestep, table, cond, w_embed, qkv):
    count, depth = w_embed.shape
    lanes = qkv.shape[0]
    blocks = 6
    return pl.pallas_call(
        prepare_kernel,
        in_specs=[whole(pltpu.SMEM)] + [whole(pltpu.HBM)] * 4,
        out_specs=[whole()] * 3,
        out_shape=[
            jax.ShapeDtypeStruct((3, depth), jnp.float32),
            jax.ShapeDtypeStruct((count, lanes), jnp.bfloat16),
            jax.ShapeDtypeStruct((16, lanes), jnp.float32),
        ],
        scratch_shapes=[
            pltpu.VMEM(table.shape, table.dtype),
            pltpu.VMEM(cond.shape, cond.dtype),
            pltpu.VMEM(w_embed.shape, w_embed.dtype),
            pltpu.VMEM((blocks, lanes, depth // blocks), qkv.dtype),
            pltpu.VMEM((count + 16, lanes), jnp.float32),
            pltpu.SemaphoreType.DMA((blocks + 3,)),
        ],
        cost_estimate=pl.CostEstimate(
            flops=2 * count * depth * lanes, bytes_accessed=2 * qkv.size, transcendentals=0
        ),
        compiler_params=kernel_params(24),
    )(timestep, *in_hbm(table, cond, w_embed, qkv))


def span_of(rows, patch_rows):
    return -(-(rows + patch_rows) // 128) * 128


def attention_scratch(rows, patch_rows, lanes):
    shape = (lanes // HEAD_DIM, span_of(rows, patch_rows), HEAD_DIM)
    return [pltpu.VMEM((rows, lanes), jnp.bfloat16)] + [pltpu.VMEM(shape, jnp.bfloat16)] * 2


def attend(projected, order_ref, stale_ref, attended, keys, values):
    rows = projected.shape[0]
    patch_rows = stale_ref.shape[1]
    heads, span, _ = keys.shape
    kept = order_ref[1]
    filled = rows + patch_rows

    def micro_of(index):
        return jnp.where(index // TOK_DEV % MICRO == kept, 1, 0)

    query = micro_of(lax.broadcasted_iota(jnp.int32, (rows, span), 0))
    column = lax.broadcasted_iota(jnp.int32, (rows, span), 1)
    fresh_seen = (column < rows) & (query >= micro_of(column))
    stale_seen = (column >= rows) & (column < filled) & (query == 0)
    seen = fresh_seen | stale_seen
    scores = []
    for head in range(heads):
        first = 3 * HEAD_DIM * head
        for j, buffer in enumerate((keys, values)):
            lane = first + (j + 1) * HEAD_DIM
            stale_lane = (j * heads + head) * HEAD_DIM
            buffer[head, :rows] = projected[:, lane : lane + HEAD_DIM]
            buffer[head, rows:filled] = stale_ref[kept, :, stale_lane : stale_lane + HEAD_DIM]
            if filled < span:
                buffer[head, filled:] = jnp.zeros((span - filled, HEAD_DIM), jnp.bfloat16)
        queries = projected[:, first : first + HEAD_DIM]
        scores.append(
            lax.dot_general(queries, keys[head], NT, preferred_element_type=jnp.float32)
        )
    scores = [jnp.where(seen, score * HEAD_DIM ** (-0.5), -jnp.inf) for score in scores]
    tops = [jnp.max(score, axis=-1, keepdims=True) for score in scores]
    weights = [jnp.exp(score - top) for score, top in zip(scores, tops)]
    totals = [jnp.sum(weight, axis=-1, keepdims=True) for weight in weights]
    for head in range(heads):
        probs = (weights[head] / totals[head]).astype(jnp.bfloat16)
        attended[:, head * HEAD_DIM : (head + 1) * HEAD_DIM] = jnp.dot(
            probs, values[head], preferred_element_type=jnp.float32
        ).astype(jnp.bfloat16)


def column_blocks(place, attended, out_ref, block_refs):
    count = len(block_refs)
    columns = out_ref.shape[1] // count
    for k in range(count):
        first = pl.multiple_of((place ^ k) * columns, columns)
        block_refs[k][...] = jnp.dot(
            attended[...], out_ref[:, pl.ds(first, columns)], preferred_element_type=jnp.float32
        ).astype(jnp.bfloat16)


def first_layer_kernel(
    count, order_ref, embed_ref, heads_ref, term_ref, stale_ref, out_hbm, *refs
):
    latent_refs, refs = refs[:count], refs[count:]
    block_refs, own_ref, latents, attended, keys, values, out_ref, sem = refs[:count], *refs[count:]
    out_copy = pltpu.make_async_copy(out_hbm, out_ref, sem)
    out_copy.start()
    place = lax.axis_index("seq")
    rows_dev = MICRO * TOK_DEV
    for k in range(count):
        first = pl.multiple_of((place ^ k) * rows_dev, rows_dev)
        latents[pl.ds(first, rows_dev), :] = (
            latent_refs[k][...].reshape(rows_dev, latents.shape[1]).astype(jnp.bfloat16)
        )
    embedded = jnp.dot(latents[...], embed_ref[...], preferred_element_type=jnp.float32)
    embedded = embedded.astype(jnp.bfloat16).astype(jnp.float32)
    norm = lax.rsqrt(jnp.mean(embedded * embedded, axis=-1, keepdims=True) + norm_eps)
    projected = jnp.dot(latents[...], heads_ref[...], preferred_element_type=jnp.float32)
    projected = (norm * projected + term_ref[:1]).astype(jnp.bfloat16)
    attend(projected, order_ref, stale_ref, attended, keys, values)
    columns = own_ref.shape[1]
    first = pl.multiple_of(place * columns, columns)
    own_ref[...] = jnp.dot(
        latents[...], embed_ref[:, pl.ds(first, columns)], preferred_element_type=jnp.float32
    ).astype(jnp.bfloat16)
    out_copy.wait()
    column_blocks(place, attended, out_ref, block_refs)


def first_layer(patch_order, latent_pieces, w_embed, heads, term, stale, out):
    count = len(latent_pieces)
    rows = count * MICRO * TOK_DEV
    lanes, depth = out.shape
    block = jax.ShapeDtypeStruct((rows, depth // count), jnp.bfloat16)
    return pl.pallas_call(
        functools.partial(first_layer_kernel, count),
        in_specs=[whole(pltpu.SMEM)] + [whole()] * 4 + [whole(pltpu.HBM)] + [whole()] * count,
        out_specs=[whole()] * (count + 1),
        out_shape=[block] * (count + 1),
        scratch_shapes=[
            pltpu.VMEM((rows, w_embed.shape[0]), jnp.bfloat16),
            *attention_scratch(rows, stale.shape[1], lanes),
            pltpu.VMEM(out.shape, out.dtype),
            pltpu.SemaphoreType.DMA,
        ],
        compiler_params=kernel_params(12),
    )(
        patch_order,
        w_embed,
        heads,
        term,
        stale,
        *in_hbm(out),
        *latent_pieces,
    )


def fetch_kernel(qkv_hbm, out_hbm, after_ref, *refs):
    block_refs, out_ref, done_ref, sems = refs[:-3], *refs[-3:]
    count = len(block_refs)
    place = lax.axis_index("seq")
    copies = []
    for k, block_ref in enumerate(block_refs):
        columns = block_ref.shape[1]
        first = pl.multiple_of((place ^ k) * columns, columns)
        copies.append(
            pltpu.make_async_copy(qkv_hbm.at[:, pl.ds(first, columns)], block_ref, sems.at[k])
        )
    copies.append(pltpu.make_async_copy(out_hbm, out_ref, sems.at[count]))
    for _ in in_order(copies, len(copies)):
        pass
    done_ref[...] = jnp.zeros_like(done_ref)


def fetched(count, qkv, out, after):
    lanes, depth = qkv.shape
    return pl.pallas_call(
        fetch_kernel,
        in_specs=[whole(pltpu.HBM)] * 2 + [whole(pl.ANY)],
        out_specs=[whole()] * (count + 2),
        out_shape=[pltpu.VMEM((lanes, depth // count), qkv.dtype)] * count
        + [pltpu.VMEM(out.shape, out.dtype), jax.ShapeDtypeStruct((8, 128), jnp.float32)],
        scratch_shapes=[pltpu.SemaphoreType.DMA((count + 1,))],
        cost_estimate=pl.CostEstimate(
            flops=0, bytes_accessed=2 * (qkv.size + out.size), transcendentals=0
        ),
        compiler_params=kernel_params(),
    )(*in_hbm(qkv, out), after)


def block_sum_kernel(rows_ref, own_ref, done_ref, *refs):
    part_refs, block_ref = refs[:-1], refs[-1]
    columns = own_ref.shape[1]
    first = pl.multiple_of(lax.axis_index("seq") * columns, columns)
    mixed = part_refs[0][...].astype(jnp.float32)
    for part_ref in part_refs[1:]:
        mixed = mixed + part_ref[...].astype(jnp.float32)
    gate = rows_ref[2:3, pl.ds(first, columns)]
    block_ref[...] = (own_ref[...].astype(jnp.float32) + gate * mixed).astype(jnp.bfloat16)


def block_sum(mod_rows, own, done, parts):
    return pl.pallas_call(
        block_sum_kernel,
        in_specs=[whole()] * (3 + len(parts)),
        out_specs=whole(),
        out_shape=jax.ShapeDtypeStruct(own.shape, own.dtype),
        compiler_params=kernel_params(),
    )(mod_rows, own, done, *parts)


def scaled_piece(place, k, piece_ref, rows_ref):
    columns = piece_ref.shape[1]
    first = pl.multiple_of((place ^ k) * columns, columns)
    wide = piece_ref[...].astype(jnp.float32)
    scaled = (wide * rows_ref[1:2, pl.ds(first, columns)]).astype(jnp.bfloat16)
    return scaled, jnp.sum(wide * wide, axis=-1, keepdims=True)


TILE = 256


def sums_kernel(numbers, rows_ref, *refs):
    count = len(numbers)
    piece_refs, weight_refs = refs[:count], refs[count : 2 * count]
    earlier, (sums_ref, squares_ref) = refs[2 * count : -2], refs[-2:]
    place = lax.axis_index("seq")
    squares = earlier[1][...] if earlier else 0.0
    scaled = []
    for k, piece_ref in zip(numbers, piece_refs):
        piece, square = scaled_piece(place, k, piece_ref, rows_ref)
        scaled.append(piece)
        squares = squares + square
    squares_ref[...] = squares
    for i in range(0, sums_ref.shape[1], TILE):
        lane = slice(i, i + TILE)
        total = earlier[0][:, lane] if earlier else 0.0
        for piece, weight_ref in zip(scaled, weight_refs):
            total = total + lax.dot_general(
                piece, weight_ref[lane, :], NT, preferred_element_type=jnp.float32
            )
        sums_ref[:, lane] = total


def in_vmem(*values):
    return [pltpu.with_memory_space_constraint(value, pltpu.VMEM) for value in values]


def product_sums(numbers, pieces, mod_rows, weights, earlier):
    rows, columns = pieces[0].shape
    lanes = weights[0].shape[0]
    return pl.pallas_call(
        functools.partial(sums_kernel, numbers),
        in_specs=[whole()] * (1 + 2 * len(numbers) + len(earlier)),
        out_specs=[whole()] * 2,
        out_shape=[
            jax.ShapeDtypeStruct((rows, lanes), jnp.float32),
            jax.ShapeDtypeStruct((rows, 1), jnp.float32),
        ],
        compiler_params=kernel_params(),
    )(mod_rows, *pieces, *in_vmem(*weights), *earlier)


def later_layer_kernel(
    count, last, order_ref, rows_ref, qkv_ref, out_ref, term_ref, stale_ref, sums_ref, squares_ref, *refs
):
    piece_refs, refs = refs[:count], refs[count:]
    block_refs, own_ref, sums, attended, keys, values, partial_out = refs[:count], *refs[count:]
    place = lax.axis_index("seq")
    scaled, squares = scaled_piece(place, count - 1, piece_refs[-1], rows_ref)
    norm = lax.rsqrt((squares_ref[...] + squares) / rows_ref.shape[1] + norm_eps)
    for i in range(0, sums.shape[1], TILE):
        lane = slice(i, i + TILE)
        product = lax.dot_general(
            scaled, qkv_ref[lane, :], NT, preferred_element_type=jnp.float32
        )
        sums[:, lane] = (norm * (product + sums_ref[:, lane]) + term_ref[:1, lane]).astype(
            jnp.bfloat16
        )
    attend(sums, order_ref, stale_ref, attended, keys, values)
    if not last:
        column_blocks(place, attended, out_ref, block_refs)
        own_ref[...] = piece_refs[0][...]
        return
    partial_out[...] = jnp.dot(
        attended[...], out_ref[...], preferred_element_type=jnp.float32
    ).astype(jnp.bfloat16)
    rows_dev = own_ref.shape[0]
    columns = piece_refs[0].shape[1]
    own_rows = pl.ds(pl.multiple_of(place * rows_dev, rows_dev), rows_dev)
    for k in range(count):
        first = pl.multiple_of((place ^ k) * rows_dev, rows_dev)
        block_refs[k][...] = partial_out[pl.ds(first, rows_dev), :]
        first = pl.multiple_of((place ^ k) * columns, columns)
        own_ref[:, pl.ds(first, columns)] = piece_refs[k][own_rows, :]


def later_layer(last, patch_order, pieces, mod_rows, qkv_block, out, term, stale, sums, squares):
    count = len(pieces)
    rows, columns = pieces[0].shape
    lanes, depth = out.shape
    shape = (rows // count, depth) if last else (rows, columns)
    block = jax.ShapeDtypeStruct(shape, jnp.bfloat16)
    return pl.pallas_call(
        functools.partial(later_layer_kernel, count, last),
        in_specs=[whole(pltpu.SMEM)] + [whole()] * (7 + count),
        out_specs=[whole()] * (count + 1),
        out_shape=[block] * (count + 1),
        scratch_shapes=[
            pltpu.VMEM(sums.shape, jnp.bfloat16),
            *attention_scratch(rows, stale.shape[1], lanes),
            pltpu.VMEM((rows, depth), jnp.bfloat16),
        ],
        compiler_params=kernel_params(),
    )(patch_order, mod_rows, *in_vmem(qkv_block, out), term, stale, sums, squares, *pieces)


def term_kernel(rows_ref, own_ref, final_ref, *refs):
    part_refs, term_ref = refs[:-1], refs[-1]
    mixed = part_refs[0][...].astype(jnp.float32)
    for part_ref in part_refs[1:]:
        mixed = mixed + part_ref[...].astype(jnp.float32)
    hidden = (own_ref[...].astype(jnp.float32) + rows_ref[2:3] * mixed).astype(jnp.bfloat16)
    predicted = lax.dot_general(
        rms_scaled(hidden).astype(jnp.bfloat16),
        final_ref[...],
        NT,
        preferred_element_type=jnp.float32,
    )
    weight = jnp.where(lax.axis_index("cfg") == 0, 1.0 - guide_scale, guide_scale)
    patches = [predicted[i * TOK_DEV : (i + 1) * TOK_DEV] for i in range(MICRO)]
    term = weight * jnp.concatenate(patches, axis=1)
    term_ref[...] = jnp.broadcast_to(term, term_ref.shape)


def velocity_terms(peers, mod_rows, own, final, parts):
    shape = (peers, TOK_DEV, MICRO * final.shape[0])
    return pl.pallas_call(
        term_kernel,
        in_specs=[whole()] * (3 + len(parts)),
        out_specs=whole(),
        out_shape=jax.ShapeDtypeStruct(shape, jnp.float32),
        compiler_params=kernel_params(),
    )(mod_rows, own, final, *parts)


TAPS = 27
TAP_GROUP = 4
HALF = LAT_W // 2


def window_kernel(sizes, slab_ref, conv_ref, chosen_ref, weights_ref):
    seq_count, slab_most, token_rows = sizes
    place = lax.axis_index("seq")
    rows = seq_count * MICRO * TOK_DEV
    start = 0
    for j in range(seq_count - 1):
        start = start + jnp.where(j < place, slab_ref[j], 0)
    shape = (chosen_ref.shape[0], 2 * rows)
    target = lax.broadcasted_iota(jnp.int32, shape, 0)
    column = lax.broadcasted_iota(jnp.int32, shape, 1)
    across = target % HALF
    down = target // HALF % slab_most
    frame = target // (HALF * slab_most)
    kept = down < slab_ref[place]
    patch_rows = seq_count * TOK_DEV
    for tap in range(TAPS):
        time, row_shift, token_shift = tap // 9, tap // 3 % 3, tap % 3
        source_frame = jnp.maximum(frame + (time - 2), 0)
        row = start + down + (row_shift - 1)
        token = across + (token_shift - 1)
        inside = kept & (row >= 0) & (row < 2 * token_rows) & (token >= 0) & (token < HALF)
        row = jnp.maximum(row, 0)
        index = (source_frame * token_rows + row // 2) * HALF + jnp.maximum(token, 0)
        patch = index // patch_rows
        slot = index % patch_rows
        source = (slot // TOK_DEV * MICRO + patch) * TOK_DEV + slot % TOK_DEV + row % 2 * rows
        chosen_ref[:, tap * 2 * rows : (tap + 1) * 2 * rows] = jnp.where(
            inside & (column == source), 1.0, 0.0
        ).astype(jnp.bfloat16)
    chosen_ref[:, TAPS * 2 * rows :] = jnp.zeros(
        (shape[0], chosen_ref.shape[1] - TAPS * 2 * rows), jnp.bfloat16
    )
    weights_ref[...] = jnp.zeros_like(weights_ref)
    channels = conv_ref.shape[2]
    for tap in range(TAPS):
        for source in range(2):
            for side in range(2):
                shift = 2 * (tap % 3 - 1) + source - side + 1
                if 0 <= shift < 3:
                    first = (tap * 2 + source) * LAT_CH
                    weights_ref[first : first + LAT_CH, side * channels : (side + 1) * channels] = (
                        conv_ref[tap // 3 * 3 + shift]
                    )


def window_parts(seq_count, slab_most, token_rows, slab_rows, w_conv):
    rows = seq_count * MICRO * TOK_DEV
    groups = -(-TAPS // TAP_GROUP)
    return pl.pallas_call(
        functools.partial(window_kernel, (seq_count, slab_most, token_rows)),
        in_specs=[whole(pltpu.SMEM), whole()],
        out_specs=[whole()] * 2,
        out_shape=[
            jax.ShapeDtypeStruct(
                (FRAMES * slab_most * HALF, groups * TAP_GROUP * 2 * rows), jnp.bfloat16
            ),
            jax.ShapeDtypeStruct(
                (groups * TAP_GROUP * 2 * LAT_CH, 2 * w_conv.shape[2]), jnp.bfloat16
            ),
        ],
        compiler_params=kernel_params(),
    )(slab_rows, w_conv)


def decode_kernel(segment_count, terms_ref, chosen_ref, weights_ref, *refs):
    latent_refs, refs = refs[:-7], refs[-7:]
    velocity_ref, decoded_ref, latents, tokens, halves, columns, features = refs
    place = lax.axis_index("seq")
    count = len(latent_refs)
    for k in range(count):
        latents[place ^ k] = latent_refs[k][...]

    def velocity_of(z):
        first = (z * segment_count + segment_count - 1) * 2
        both = terms_ref[first] + terms_ref[first + 1]
        width = both.shape[1] // MICRO
        return [both[:, i * width : (i + 1) * width] for i in range(MICRO)]

    for i, value in enumerate(velocity_of(place)):
        velocity_ref[i] = value
    for z in range(count):
        stepped = [
            latents[z, i] - value / SCHED_STEPS for i, value in enumerate(velocity_of(z))
        ]
        tokens[z * MICRO * TOK_DEV : (z + 1) * MICRO * TOK_DEV] = jnp.concatenate(
            stepped, axis=0
        ).astype(jnp.bfloat16)
    rows, width = tokens.shape
    half = width // 2
    halves[...] = jnp.zeros_like(halves)
    for j in range(TAP_GROUP):
        for side in range(2):
            first = (j * 2 + side) * rows
            halves[first : first + rows, j * half : (j + 1) * half] = tokens[
                :, side * half : (side + 1) * half
            ]
    depth, group_width = halves.shape
    for group in range(chosen_ref.shape[1] // depth):
        columns[:, group * group_width : (group + 1) * group_width] = jnp.dot(
            chosen_ref[:, group * depth : (group + 1) * depth],
            halves[...],
            preferred_element_type=jnp.float32,
        ).astype(jnp.bfloat16)
    result = jnp.dot(columns[...], weights_ref[...], preferred_element_type=jnp.float32)
    channels = features.shape[1]
    for side in range(2):
        features[pl.ds(side, result.shape[0], stride=2), :] = result[
            :, side * channels : (side + 1) * channels
        ]
    decoded_ref[...] = features[...].astype(jnp.bfloat16)


def decoded_slab(segment_count, terms, chosen, weights, latent_pieces):
    count = len(latent_pieces)
    rows = count * MICRO * TOK_DEV
    width = latent_pieces[0].shape[-1]
    targets = chosen.shape[0]
    channels = weights.shape[1] // 2
    return pl.pallas_call(
        functools.partial(decode_kernel, segment_count),
        in_specs=[whole()] * (3 + count),
        out_specs=[whole()] * 2,
        out_shape=[
            jax.ShapeDtypeStruct(latent_pieces[0].shape, jnp.float32),
            jax.ShapeDtypeStruct((2 * targets, channels), jnp.bfloat16),
        ],
        scratch_shapes=[
            pltpu.VMEM((count,) + latent_pieces[0].shape, jnp.float32),
            pltpu.VMEM((rows, width), jnp.bfloat16),
            pltpu.VMEM((TAP_GROUP * 2 * rows, TAP_GROUP * width // 2), jnp.bfloat16),
            pltpu.VMEM((targets, weights.shape[0]), jnp.bfloat16),
            pltpu.VMEM((2 * targets, channels), jnp.float32),
        ],
        compiler_params=kernel_params(),
    )(terms, chosen, weights, *latent_pieces)


def shards(
    latent,
    w_embed,
    w_qkv,
    w_out,
    mod_table,
    cond_mod,
    stale_kv,
    w_final,
    w_conv,
    patch_order,
    timestep,
    slab_rows,
):
    seq_count = lax.axis_size("seq")
    segment_count = lax.axis_size("segment")

    def within(k):
        return [(i, i ^ k) for i in range(seq_count)]

    def spread(value):
        return [value] + [lax.ppermute(value, "seq", within(k)) for k in range(1, seq_count)]

    def returned(values):
        return values[:1] + [
            lax.ppermute(values[k], "seq", within(k)) for k in range(1, seq_count)
        ]

    latent_pieces = spread(latent)
    mod_rows, head_embed, shift_term = prepared(
        timestep, jnp.transpose(mod_table, (1, 0, 2)), jnp.transpose(cond_mod[0], (1, 0, 2)), w_embed, w_qkv[0]
    )
    stale = stale_kv[0, 0, 0]
    *blocks, own = first_layer(
        patch_order, latent_pieces, w_embed, head_embed, shift_term, stale, w_out[0]
    )
    numbers = tuple(range(seq_count))
    *qkv_blocks, out, done = fetched(seq_count, w_qkv[0], w_out[0], own)
    for step in range(1, segment_count):
        block = block_sum(mod_rows, own, done, returned(blocks))
        pieces = []
        for k in numbers:
            pairs = [
                (i * segment_count + j, (i ^ k) * segment_count + (j + 1) % segment_count)
                for i in range(seq_count)
                for j in range(segment_count)
            ]
            pieces.append(lax.ppermute(block, ("seq", "segment"), pairs))
        half = (seq_count + 1) // 2
        sums = ()
        for some in (numbers[:half], numbers[half:-1]):
            if some:
                sums = product_sums(
                    some,
                    [pieces[k] for k in some],
                    mod_rows,
                    [qkv_blocks[k] for k in some],
                    sums,
                )
        *blocks, own = later_layer(
            step + 1 == segment_count,
            patch_order,
            pieces,
            mod_rows,
            qkv_blocks[-1],
            out,
            shift_term,
            stale,
            *sums,
        )

    blocks, slab_rows, w_conv = lax.optimization_barrier((blocks, slab_rows, w_conv))
    token_rows = MICRO * seq_count * TOK_DEV // (FRAMES * HALF)
    slab_most = 4 * token_rows // seq_count
    chosen, weights = window_parts(seq_count, slab_most, token_rows, slab_rows, w_conv)
    peers = ("seq", "segment", "cfg")
    peer_count = seq_count * segment_count * lax.axis_size("cfg")
    terms = velocity_terms(peer_count, mod_rows, own, w_final.T, returned(blocks))
    terms = lax.all_to_all(terms, peers, split_axis=0, concat_axis=0, tiled=True)
    velocity, decoded = decoded_slab(segment_count, terms, chosen, weights, latent_pieces)
    return (velocity, decoded.reshape(1, FRAMES, slab_most, LAT_W, w_conv.shape[2]))


def decoder_input(stepped, w_conv, slab_rows, seq_index, seq_count):
    token_rows = MICRO * seq_count * TOK_DEV // (FRAMES * (LAT_W // 2))
    image_rows = 2 * token_rows
    slab_most = 2 * image_rows // seq_count
    image = stepped.reshape(FRAMES, token_rows, LAT_W // 2, 2, 2, LAT_CH)
    image = (
        jnp.transpose(image, (0, 1, 3, 2, 4, 5))
        .reshape(FRAMES, image_rows, LAT_W, LAT_CH)
    )
    padded = jnp.concatenate([image[:1], image[:1], image], 0)
    padded = jnp.pad(padded, ((0, 0), (1, 1 + slab_most), (1, 1), (0, 0)))
    positions = jnp.arange(seq_count)
    slab_count = jnp.sum(jnp.where(positions == seq_index, slab_rows, 0))
    slab_start = jnp.sum(jnp.where(positions < seq_index, slab_rows, 0))
    window = lax.dynamic_slice_in_dim(padded, slab_start, slab_most + 2, 1)
    pieces = []
    for frame_shift in range(3):
        for row_shift in range(3):
            for col_shift in range(3):
                pieces.append(
                    window[
                        frame_shift : frame_shift + FRAMES,
                        row_shift : row_shift + slab_most,
                        col_shift : col_shift + LAT_W,
                    ]
                )
    columns = jnp.concatenate(pieces, -1).reshape(FRAMES * slab_most * LAT_W, 27 * LAT_CH)
    kernel = w_conv.reshape(27 * LAT_CH, w_conv.shape[2])
    features = jnp.dot(columns, kernel, preferred_element_type=jnp.float32).astype(jnp.bfloat16)
    features = features.reshape(FRAMES, slab_most, LAT_W, w_conv.shape[2])
    row_valid = jnp.arange(slab_most)[None, :, None, None] < slab_count
    decoded = jnp.where(row_valid, features, jnp.zeros_like(features))
    return decoded[None]


def solution(mesh):
    in_specs = (
        P(None, ("groups", "seq"), None),
        P(),
        P("segment", "seq", None),
        P("segment", "seq", None),
        P(),
        P("cfg", ("groups", "segment"), None, None),
        P("segment", "cfg", "seq", None, "groups", None),
        P(),
        P(None, None, ("segment", "cfg")),
        P("groups"),
        P("groups"),
        P("groups"),
    )
    out_specs = (
        P(None, ("groups", "seq"), None),
        P(("groups", "seq"), None, None, None, ("segment", "cfg")),
    )
    whole_groups = 2 <= mesh.shape["seq"] <= 8
    program = shards if whole_groups else cycled_shards
    return jax.shard_map(program, mesh=mesh, in_specs=in_specs, out_specs=out_specs, check_vma=False)
```

```python
import functools

import jax
import jax.numpy as jnp
from jax import lax
from jax.experimental import pallas as pl
from jax.experimental.pallas import tpu as pltpu
from jax.sharding import PartitionSpec as P

HEADS = 24
HEAD_DIM = 128
D = 3072
LAT_CH = 16
SCHED_STEPS = 50
MICRO = 2
TOK_DEV = 8
FRAMES = 4
LAT_W = 8


guide_scale = 5.0
norm_eps = 1e-06


def swapped(value, axis, bit):
    return lax.ppermute(value, axis, [(i, i ^ 1 << bit) for i in range(lax.axis_size(axis))])


def passed_along(value, axis, by):
    size = lax.axis_size(axis)
    pairs = [(i, i + by) for i in range(size) if 0 <= i + by < size]
    return lax.ppermute(value, axis, pairs)


def rms_scaled(values):
    wide = values.astype(jnp.float32)
    return wide * lax.rsqrt(jnp.mean(wide * wide, axis=-1, keepdims=True) + norm_eps)


def cycle_join(piece, seq_index, cycle_bits):
    joined = piece
    for bit_number in range(cycle_bits):
        partner = swapped(joined, "seq", bit_number)
        upper_half = (seq_index // 2**bit_number % 2).astype(jnp.int32)
        part_rows = joined.shape[0]
        combined = jnp.zeros((2 * part_rows,) + joined.shape[1:], joined.dtype)
        combined = lax.dynamic_update_slice_in_dim(combined, joined, upper_half * part_rows, 0)
        joined = lax.dynamic_update_slice_in_dim(combined, partner, (1 - upper_half) * part_rows, 0)
    return joined


def cycled_shards(
    latent,
    w_embed,
    w_qkv,
    w_out,
    mod_table,
    cond_mod,
    stale_kv,
    w_final,
    w_conv,
    patch_order,
    timestep,
    slab_rows,
):
    seq_count = lax.axis_size("seq")
    segment_count = lax.axis_size("segment")
    seq_index = lax.axis_index("seq")
    segment_index = lax.axis_index("segment")
    branch_index = lax.axis_index("cfg")
    group_count = min(seq_count, 8)
    cycle_size = seq_count // group_count
    cycle_bits = cycle_size.bit_length() - 1
    group_heads = HEADS // group_count
    sub_rows = TOK_DEV // cycle_size
    share_rows = seq_count * sub_rows
    kv_lanes = 2 * group_heads * HEAD_DIM
    table_row = lax.dynamic_index_in_dim(mod_table, timestep[0], 0, keepdims=False).astype(
        jnp.float32
    )
    modulation = table_row + cond_mod[0, 0]
    shift_row = modulation[0]
    scale_row = modulation[1]
    gate_row = modulation[2]
    joined_weights = (
        cycle_join(w_qkv[0], seq_index, cycle_bits),
        cycle_join(w_out[0], seq_index, cycle_bits),
    )
    stale_joined = cycle_join(stale_kv[0, 0], seq_index, cycle_bits)
    cache = jnp.transpose(stale_joined, (1, 0, 2, 3)).reshape(
        MICRO, cycle_size * share_rows, kv_lanes
    )
    received = jnp.zeros((TOK_DEV, D), jnp.bfloat16)
    finished = jnp.zeros((MICRO, TOK_DEV, D), jnp.bfloat16)
    slot_ids = jnp.arange(MICRO)
    tick_count = MICRO + segment_count - 1
    for tick_index in range(tick_count):
        qkv_rows, out_rows = joined_weights
        micro_index = tick_index - segment_index
        active = (micro_index >= 0) & (micro_index < MICRO)
        clipped = jnp.clip(micro_index, 0, MICRO - 1)
        patch_id = jnp.sum(jnp.where(slot_ids == clipped, patch_order, 0))
        own_latent = lax.dynamic_index_in_dim(latent, patch_id, 0, keepdims=False).astype(
            jnp.bfloat16
        )
        embedded = jnp.dot(own_latent, w_embed, preferred_element_type=jnp.float32).astype(
            jnp.bfloat16
        )
        layer_input = jnp.where(segment_index == 0, embedded, received)
        normed = (rms_scaled(layer_input) * (1.0 + scale_row) + shift_row).astype(jnp.bfloat16)
        outgoing = jnp.broadcast_to(
            normed.reshape(1, cycle_size, sub_rows, D), (group_count, cycle_size, sub_rows, D)
        )
        shared = lax.all_to_all(
            outgoing.reshape(share_rows, D), "seq", split_axis=0, concat_axis=0, tiled=True
        )
        projected = lax.dot_general(
            shared, qkv_rows, (((1,), (1,)), ((), ())), preferred_element_type=jnp.float32
        )
        projected = projected.astype(jnp.bfloat16).reshape(share_rows, group_heads, 3, HEAD_DIM)
        queries = projected[:, :, 0]
        fresh_local = jnp.transpose(projected[:, :, 1:], (0, 2, 1, 3)).reshape(
            1, share_rows, kv_lanes
        )
        fresh = cycle_join(fresh_local, seq_index, cycle_bits).reshape(
            cycle_size * share_rows, kv_lanes
        )
        previous = lax.dynamic_index_in_dim(cache, patch_id, 0, keepdims=False)
        cache = lax.dynamic_update_index_in_dim(
            cache, jnp.where(active, fresh, previous), patch_id, 0
        )
        keyvals = cache.reshape(MICRO * cycle_size * share_rows, 2, group_heads, HEAD_DIM)
        scores = jnp.einsum(
            "shd,khd->hsk", queries, keyvals[:, 0], preferred_element_type=jnp.float32
        ) * HEAD_DIM ** (-0.5)
        probs = jax.nn.softmax(scores, axis=-1).astype(jnp.bfloat16)
        attended = jnp.einsum(
            "hsk,khd->shd", probs, keyvals[:, 1], preferred_element_type=jnp.float32
        ).astype(jnp.bfloat16)
        partial_out = jnp.dot(
            attended.reshape(share_rows, group_heads * HEAD_DIM),
            out_rows,
            preferred_element_type=jnp.float32,
        )
        returned = lax.all_to_all(
            partial_out.astype(jnp.bfloat16), "seq", split_axis=0, concat_axis=0, tiled=True
        ).astype(partial_out.dtype)
        mixed = jnp.sum(returned.reshape(group_count, cycle_size, sub_rows, D), axis=0).reshape(
            TOK_DEV, D
        )
        layer_output = (layer_input.astype(jnp.float32) + gate_row * mixed).astype(jnp.bfloat16)
        keep_final = active & (segment_index == segment_count - 1)
        earlier = lax.dynamic_index_in_dim(finished, patch_id, 0, keepdims=False)
        finished = lax.dynamic_update_index_in_dim(
            finished, jnp.where(keep_final, layer_output, earlier), patch_id, 0
        )
        if tick_index + 1 < tick_count:
            received = passed_along(layer_output, "segment", 1)
    final_normed = rms_scaled(finished).astype(jnp.bfloat16)
    predicted = jnp.einsum("mtd,dc->mtc", final_normed, w_final, preferred_element_type=jnp.float32)
    is_last = segment_index == segment_count - 1
    branch_weight = jnp.where(branch_index == 0, 1.0 - guide_scale, guide_scale)
    velocity_term = jnp.where(is_last, branch_weight * predicted, 0.0)
    latent_term = jnp.where(is_last & (branch_index == 0), latent, 0.0)
    velocity_own, latent_own = lax.psum((velocity_term, latent_term), ("segment", "cfg"))
    velocity_full, latent_full = (
        lax.all_gather(velocity_own, "seq", axis=1, tiled=True),
        lax.all_gather(latent_own, "seq", axis=1, tiled=True),
    )
    stepped = (latent_full - velocity_full / SCHED_STEPS).astype(jnp.bfloat16)
    decoded = decoder_input(stepped, w_conv, slab_rows, seq_index, seq_count)
    return (velocity_own, decoded)


NT = (((1,), (1,)), ((), ()))
TILE = 256
PART = 768
AHEAD = 4


def kernel_params(mebibytes=8):
    return pltpu.CompilerParams(vmem_limit_bytes=mebibytes * 2**20)


def whole(space=pltpu.VMEM):
    return pl.BlockSpec(memory_space=space)


def in_order(copies, ahead):
    for copy in copies[:ahead]:
        copy.start()

    def landed():
        for i, copy in enumerate(copies):
            copy.wait()
            if i + ahead < len(copies):
                copies[i + ahead].start()
            yield i

    return landed()


def in_hbm(*values):
    return [pltpu.with_memory_space_constraint(value, pltpu.HBM) for value in values]


def modulation_kernel(
    timestep_ref, table_hbm, cond_hbm, embed_hbm, rows_ref, lhs_ref, table, cond, embed, sems
):
    copies = [
        pltpu.make_async_copy(source, target, sems.at[i])
        for i, (source, target) in enumerate(
            ((table_hbm, table), (cond_hbm, cond), (embed_hbm, embed))
        )
    ]
    for _ in in_order(copies, 3):
        pass
    steps = table.shape[1]
    chosen = lax.broadcasted_iota(jnp.int32, (16, steps), 1) == timestep_ref[0]
    chosen = jnp.where(chosen, 1.0, 0.0).astype(jnp.bfloat16)
    for j in range(3):
        row = jnp.dot(chosen, table[j], preferred_element_type=jnp.float32)[:1]
        rows_ref[j : j + 1, :] = row + cond[j] + (1.0 if j == 1 else 0.0)
    count = embed.shape[0]
    lhs_ref[:count] = (embed[...].astype(jnp.float32) * rows_ref[1:2]).astype(jnp.bfloat16)
    lhs_ref[count:] = jnp.broadcast_to(rows_ref[0:1], (16, lhs_ref.shape[1])).astype(jnp.bfloat16)


def modulated(timestep, table, cond, w_embed):
    count, depth = w_embed.shape
    return pl.pallas_call(
        modulation_kernel,
        in_specs=[whole(pltpu.SMEM)] + [whole(pltpu.HBM)] * 3,
        out_specs=[whole()] * 2,
        out_shape=[
            jax.ShapeDtypeStruct((3, depth), jnp.float32),
            jax.ShapeDtypeStruct((count + 16, depth), jnp.bfloat16),
        ],
        scratch_shapes=[
            pltpu.VMEM(table.shape, table.dtype),
            pltpu.VMEM(cond.shape, cond.dtype),
            pltpu.VMEM(w_embed.shape, w_embed.dtype),
            pltpu.SemaphoreType.DMA((3,)),
        ],
        cost_estimate=pl.CostEstimate(
            flops=10**10, bytes_accessed=2 * (table.size + w_embed.size), transcendentals=0
        ),
        compiler_params=kernel_params(),
    )(timestep, *in_hbm(table, cond, w_embed))


def prepare_kernel(lhs_ref, qkv_ref, out_hbm, heads_ref, term_ref, out_ref, sem):
    out_copy = pltpu.make_async_copy(out_hbm, out_ref, sem)
    out_copy.start()
    count = heads_ref.shape[0]
    for j in range(0, qkv_ref.shape[0], PART):
        lane = slice(j, j + PART)
        product = lax.dot_general(
            lhs_ref[...], qkv_ref[lane, :], NT, preferred_element_type=jnp.float32
        )
        heads_ref[:, lane] = product[:count].astype(jnp.bfloat16)
        term_ref[:, lane] = product[count:]
    out_copy.wait()


def prepared(lhs, qkv, out):
    rows, depth = lhs.shape
    lanes = qkv.shape[0]
    return pl.pallas_call(
        prepare_kernel,
        in_specs=[whole()] * 2 + [whole(pltpu.HBM)],
        out_specs=[whole()] * 3,
        out_shape=[
            jax.ShapeDtypeStruct((rows - 16, lanes), jnp.bfloat16),
            jax.ShapeDtypeStruct((16, lanes), jnp.float32),
            pltpu.VMEM(out.shape, out.dtype),
        ],
        scratch_shapes=[pltpu.SemaphoreType.DMA],
        compiler_params=kernel_params(),
    )(lhs, qkv, *in_hbm(out))


def span_of(rows, patch_rows):
    return -(-(rows + patch_rows) // 128) * 128


def attention_scratch(rows, patch_rows, lanes):
    shape = (lanes // HEAD_DIM, span_of(rows, patch_rows), HEAD_DIM)
    return [pltpu.VMEM((rows, lanes), jnp.bfloat16)] + [pltpu.VMEM(shape, jnp.bfloat16)] * 2


def attend(projected, order_ref, stale_ref, attended, keys, values):
    rows = projected.shape[0]
    patch_rows = stale_ref.shape[1]
    heads, span, _ = keys.shape
    kept = order_ref[1]
    filled = rows + patch_rows

    def micro_of(index):
        return jnp.where(index // TOK_DEV % MICRO == kept, 1, 0)

    query = micro_of(lax.broadcasted_iota(jnp.int32, (rows, span), 0))
    column = lax.broadcasted_iota(jnp.int32, (rows, span), 1)
    fresh_seen = (column < rows) & (query >= micro_of(column))
    stale_seen = (column >= rows) & (column < filled) & (query == 0)
    seen = fresh_seen | stale_seen
    scores = []
    for head in range(heads):
        first = 3 * HEAD_DIM * head
        for j, buffer in enumerate((keys, values)):
            lane = first + (j + 1) * HEAD_DIM
            stale_lane = (j * heads + head) * HEAD_DIM
            buffer[head, :rows] = projected[:, lane : lane + HEAD_DIM]
            buffer[head, rows:filled] = stale_ref[kept, :, stale_lane : stale_lane + HEAD_DIM]
            if filled < span:
                buffer[head, filled:] = jnp.zeros((span - filled, HEAD_DIM), jnp.bfloat16)
        queries = projected[:, first : first + HEAD_DIM]
        scores.append(
            lax.dot_general(queries, keys[head], NT, preferred_element_type=jnp.float32)
        )
    scores = [jnp.where(seen, score * HEAD_DIM ** (-0.5), -jnp.inf) for score in scores]
    tops = [jnp.max(score, axis=-1, keepdims=True) for score in scores]
    weights = [jnp.exp(score - top) for score, top in zip(scores, tops)]
    totals = [jnp.sum(weight, axis=-1, keepdims=True) for weight in weights]
    for head in range(heads):
        probs = (weights[head] / totals[head]).astype(jnp.bfloat16)
        attended[:, head * HEAD_DIM : (head + 1) * HEAD_DIM] = jnp.dot(
            probs, values[head], preferred_element_type=jnp.float32
        ).astype(jnp.bfloat16)


def column_blocks(place, attended, out_ref, block_refs):
    count = len(block_refs)
    columns = out_ref.shape[1] // count
    for k in range(count):
        first = pl.multiple_of((place ^ k) * columns, columns)
        block_refs[k][...] = jnp.dot(
            attended[...], out_ref[:, pl.ds(first, columns)], preferred_element_type=jnp.float32
        ).astype(jnp.bfloat16)


def first_layer_kernel(
    count, order_ref, embed_ref, heads_ref, term_ref, stale_ref, out_ref, *refs
):
    latent_refs, refs = refs[:count], refs[count:]
    block_refs, (own_ref, latents, attended, keys, values) = refs[:count], refs[count:]
    place = lax.axis_index("seq")
    rows_dev = MICRO * TOK_DEV
    for k in range(count):
        first = pl.multiple_of((place ^ k) * rows_dev, rows_dev)
        latents[pl.ds(first, rows_dev), :] = (
            latent_refs[k][...].reshape(rows_dev, latents.shape[1]).astype(jnp.bfloat16)
        )
    embedded = jnp.dot(latents[...], embed_ref[...], preferred_element_type=jnp.float32)
    embedded = embedded.astype(jnp.bfloat16).astype(jnp.float32)
    norm = lax.rsqrt(jnp.mean(embedded * embedded, axis=-1, keepdims=True) + norm_eps)
    projected = jnp.dot(latents[...], heads_ref[...], preferred_element_type=jnp.float32)
    projected = (norm * projected + term_ref[:1]).astype(jnp.bfloat16)
    attend(projected, order_ref, stale_ref, attended, keys, values)
    columns = own_ref.shape[1]
    first = pl.multiple_of(place * columns, columns)
    own_ref[...] = jnp.dot(
        latents[...], embed_ref[:, pl.ds(first, columns)], preferred_element_type=jnp.float32
    ).astype(jnp.bfloat16)
    column_blocks(place, attended, out_ref, block_refs)


def first_layer(patch_order, latents, w_embed, heads, term, stale, out):
    count = len(latents)
    rows = count * MICRO * TOK_DEV
    lanes, depth = out.shape
    block = jax.ShapeDtypeStruct((rows, depth // count), jnp.bfloat16)
    return pl.pallas_call(
        functools.partial(first_layer_kernel, count),
        in_specs=[whole(pltpu.SMEM)] + [whole()] * (5 + count),
        out_specs=[whole()] * (count + 1),
        out_shape=[block] * (count + 1),
        scratch_shapes=[
            pltpu.VMEM((rows, w_embed.shape[0]), jnp.bfloat16),
            *attention_scratch(rows, stale.shape[1], lanes),
        ],
        compiler_params=kernel_params(),
    )(patch_order, w_embed, heads, term, stale, out, *latents)


def block_sum_kernel(rows_ref, own_ref, *refs):
    part_refs, block_ref = refs[:-1], refs[-1]
    columns = own_ref.shape[1]
    first = pl.multiple_of(lax.axis_index("seq") * columns, columns)
    mixed = part_refs[0][...].astype(jnp.float32)
    for part_ref in part_refs[1:]:
        mixed = mixed + part_ref[...].astype(jnp.float32)
    gate = rows_ref[2:3, pl.ds(first, columns)]
    block_ref[...] = (own_ref[...].astype(jnp.float32) + gate * mixed).astype(jnp.bfloat16)


def block_sum(mod_rows, own, parts):
    return pl.pallas_call(
        block_sum_kernel,
        in_specs=[whole()] * (2 + len(parts)),
        out_specs=whole(),
        out_shape=jax.ShapeDtypeStruct(own.shape, own.dtype),
        compiler_params=kernel_params(),
    )(mod_rows, own, *parts)


def scaled_piece(place, k, piece_ref, rows_ref):
    columns = piece_ref.shape[1]
    first = pl.multiple_of((place ^ k) * columns, columns)
    wide = piece_ref[...].astype(jnp.float32)
    scaled = (wide * rows_ref[1:2, pl.ds(first, columns)]).astype(jnp.bfloat16)
    return scaled, jnp.sum(wide * wide, axis=-1, keepdims=True)


def sums_kernel(numbers, rows_ref, qkv_ref, *refs):
    count = len(numbers)
    piece_refs, earlier, (sums_ref, squares_ref) = refs[:count], refs[count:-2], refs[-2:]
    place = lax.axis_index("seq")
    columns = piece_refs[0].shape[1]
    squares = earlier[1][...] if earlier else 0.0
    scaled = []
    for k, piece_ref in zip(numbers, piece_refs):
        piece, square = scaled_piece(place, k, piece_ref, rows_ref)
        scaled.append((piece, pl.ds(pl.multiple_of((place ^ k) * columns, columns), columns)))
        squares = squares + square
    squares_ref[...] = squares
    for i in range(0, sums_ref.shape[1], TILE):
        lane = slice(i, i + TILE)
        total = earlier[0][:, lane] if earlier else 0.0
        for piece, part in scaled:
            total = total + lax.dot_general(
                piece, qkv_ref[lane, part], NT, preferred_element_type=jnp.float32
            )
        sums_ref[:, lane] = total


def product_sums(numbers, pieces, mod_rows, qkv, earlier):
    rows = pieces[0].shape[0]
    lanes = qkv.shape[0]
    return pl.pallas_call(
        functools.partial(sums_kernel, numbers),
        in_specs=[whole()] * (2 + len(numbers) + len(earlier)),
        out_specs=[whole()] * 2,
        out_shape=[
            jax.ShapeDtypeStruct((rows, lanes), jnp.float32),
            jax.ShapeDtypeStruct((rows, 1), jnp.float32),
        ],
        compiler_params=kernel_params(),
    )(mod_rows, qkv, *pieces, *earlier)


def later_layer_kernel(
    count, last, order_ref, rows_ref, qkv_ref, out_ref, term_ref, stale_ref, sums_ref, squares_ref, *refs
):
    piece_refs, refs = refs[:count], refs[count:]
    block_refs, own_ref, sums, attended, keys, values, partial_out = refs[:count], *refs[count:]
    place = lax.axis_index("seq")
    scaled, squares = scaled_piece(place, count - 1, piece_refs[-1], rows_ref)
    norm = lax.rsqrt((squares_ref[...] + squares) / rows_ref.shape[1] + norm_eps)
    columns = piece_refs[-1].shape[1]
    part = pl.ds(pl.multiple_of((place ^ (count - 1)) * columns, columns), columns)
    for i in range(0, sums.shape[1], TILE):
        lane = slice(i, i + TILE)
        product = lax.dot_general(
            scaled, qkv_ref[lane, part], NT, preferred_element_type=jnp.float32
        )
        sums[:, lane] = (norm * (product + sums_ref[:, lane]) + term_ref[:1, lane]).astype(
            jnp.bfloat16
        )
    attend(sums, order_ref, stale_ref, attended, keys, values)
    if not last:
        column_blocks(place, attended, out_ref, block_refs)
        own_ref[...] = piece_refs[0][...]
        return
    partial_out[...] = jnp.dot(
        attended[...], out_ref[...], preferred_element_type=jnp.float32
    ).astype(jnp.bfloat16)
    rows_dev = own_ref.shape[0]
    columns = piece_refs[0].shape[1]
    own_rows = pl.ds(pl.multiple_of(place * rows_dev, rows_dev), rows_dev)
    for k in range(count):
        first = pl.multiple_of((place ^ k) * rows_dev, rows_dev)
        block_refs[k][...] = partial_out[pl.ds(first, rows_dev), :]
        first = pl.multiple_of((place ^ k) * columns, columns)
        own_ref[:, pl.ds(first, columns)] = piece_refs[k][own_rows, :]


def later_layer(last, patch_order, pieces, mod_rows, qkv, out, term, stale, sums, squares):
    count = len(pieces)
    rows, columns = pieces[0].shape
    lanes, depth = out.shape
    shape = (rows // count, depth) if last else (rows, columns)
    block = jax.ShapeDtypeStruct(shape, jnp.bfloat16)
    return pl.pallas_call(
        functools.partial(later_layer_kernel, count, last),
        in_specs=[whole(pltpu.SMEM)] + [whole()] * (7 + count),
        out_specs=[whole()] * (count + 1),
        out_shape=[block] * (count + 1),
        scratch_shapes=[
            pltpu.VMEM(sums.shape, jnp.bfloat16),
            *attention_scratch(rows, stale.shape[1], lanes),
            pltpu.VMEM((rows, depth), jnp.bfloat16),
        ],
        compiler_params=kernel_params(),
    )(patch_order, mod_rows, qkv, out, term, stale, sums, squares, *pieces)


def term_kernel(rows_ref, own_ref, final_ref, *refs):
    part_refs, term_ref = refs[:-1], refs[-1]
    mixed = part_refs[0][...].astype(jnp.float32)
    for part_ref in part_refs[1:]:
        mixed = mixed + part_ref[...].astype(jnp.float32)
    hidden = (own_ref[...].astype(jnp.float32) + rows_ref[2:3] * mixed).astype(jnp.bfloat16)
    predicted = lax.dot_general(
        rms_scaled(hidden).astype(jnp.bfloat16),
        final_ref[...],
        NT,
        preferred_element_type=jnp.float32,
    )
    weight = jnp.where(lax.axis_index("cfg") == 0, 1.0 - guide_scale, guide_scale)
    patches = [predicted[i * TOK_DEV : (i + 1) * TOK_DEV] for i in range(MICRO)]
    term = weight * jnp.concatenate(patches, axis=1)
    term_ref[...] = jnp.broadcast_to(term, term_ref.shape)


def velocity_terms(peers, mod_rows, own, final, parts):
    shape = (peers, TOK_DEV, MICRO * final.shape[0])
    return pl.pallas_call(
        term_kernel,
        in_specs=[whole()] * (3 + len(parts)),
        out_specs=whole(),
        out_shape=jax.ShapeDtypeStruct(shape, jnp.float32),
        compiler_params=kernel_params(),
    )(mod_rows, own, final, *parts)


TAPS = 27
TAP_GROUP = 4
HALF = LAT_W // 2


def window_kernel(sizes, slab_ref, conv_ref, chosen_ref, weights_ref):
    seq_count, slab_most, token_rows = sizes
    place = lax.axis_index("seq")
    rows = seq_count * MICRO * TOK_DEV
    start = 0
    for j in range(seq_count - 1):
        start = start + jnp.where(j < place, slab_ref[j], 0)
    shape = (chosen_ref.shape[0], 2 * rows)
    target = lax.broadcasted_iota(jnp.int32, shape, 0)
    column = lax.broadcasted_iota(jnp.int32, shape, 1)
    across = target % HALF
    down = target // HALF % slab_most
    frame = target // (HALF * slab_most)
    kept = down < slab_ref[place]
    patch_rows = seq_count * TOK_DEV
    for tap in range(TAPS):
        time, row_shift, token_shift = tap // 9, tap // 3 % 3, tap % 3
        source_frame = jnp.maximum(frame + (time - 2), 0)
        row = start + down + (row_shift - 1)
        token = across + (token_shift - 1)
        inside = kept & (row >= 0) & (row < 2 * token_rows) & (token >= 0) & (token < HALF)
        row = jnp.maximum(row, 0)
        index = (source_frame * token_rows + row // 2) * HALF + jnp.maximum(token, 0)
        patch = index // patch_rows
        slot = index % patch_rows
        source = (slot // TOK_DEV * MICRO + patch) * TOK_DEV + slot % TOK_DEV + row % 2 * rows
        chosen_ref[:, tap * 2 * rows : (tap + 1) * 2 * rows] = jnp.where(
            inside & (column == source), 1.0, 0.0
        ).astype(jnp.bfloat16)
    chosen_ref[:, TAPS * 2 * rows :] = jnp.zeros(
        (shape[0], chosen_ref.shape[1] - TAPS * 2 * rows), jnp.bfloat16
    )
    weights_ref[...] = jnp.zeros_like(weights_ref)
    channels = conv_ref.shape[2]
    for tap in range(TAPS):
        for source in range(2):
            for side in range(2):
                shift = 2 * (tap % 3 - 1) + source - side + 1
                if 0 <= shift < 3:
                    first = (tap * 2 + source) * LAT_CH
                    weights_ref[first : first + LAT_CH, side * channels : (side + 1) * channels] = (
                        conv_ref[tap // 3 * 3 + shift]
                    )


def window_parts(seq_count, slab_most, token_rows, slab_rows, w_conv):
    rows = seq_count * MICRO * TOK_DEV
    groups = -(-TAPS // TAP_GROUP)
    return pl.pallas_call(
        functools.partial(window_kernel, (seq_count, slab_most, token_rows)),
        in_specs=[whole(pltpu.SMEM), whole()],
        out_specs=[whole()] * 2,
        out_shape=[
            jax.ShapeDtypeStruct(
                (FRAMES * slab_most * HALF, groups * TAP_GROUP * 2 * rows), jnp.bfloat16
            ),
            jax.ShapeDtypeStruct(
                (groups * TAP_GROUP * 2 * LAT_CH, 2 * w_conv.shape[2]), jnp.bfloat16
            ),
        ],
        compiler_params=kernel_params(),
    )(slab_rows, w_conv)


def decode_kernel(
    segment_count, count, terms_ref, chosen_ref, weights_ref, *refs
):
    latent_refs, refs = refs[:count], refs[count:]
    velocity_ref, decoded_ref, latents, tokens, halves, columns, features = refs
    place = lax.axis_index("seq")
    for k in range(count):
        latents[place ^ k] = latent_refs[k][...]

    def velocity_of(z):
        first = (z * segment_count + segment_count - 1) * 2
        both = terms_ref[first] + terms_ref[first + 1]
        width = both.shape[1] // MICRO
        return [both[:, i * width : (i + 1) * width] for i in range(MICRO)]

    for i, value in enumerate(velocity_of(place)):
        velocity_ref[i] = value
    for z in range(count):
        stepped = [
            latents[z, i] - value / SCHED_STEPS for i, value in enumerate(velocity_of(z))
        ]
        tokens[z * MICRO * TOK_DEV : (z + 1) * MICRO * TOK_DEV] = jnp.concatenate(
            stepped, axis=0
        ).astype(jnp.bfloat16)
    rows, width = tokens.shape
    half = width // 2
    halves[...] = jnp.zeros_like(halves)
    for j in range(TAP_GROUP):
        for side in range(2):
            first = (j * 2 + side) * rows
            halves[first : first + rows, j * half : (j + 1) * half] = tokens[
                :, side * half : (side + 1) * half
            ]
    depth, group_width = halves.shape
    for group in range(chosen_ref.shape[1] // depth):
        columns[:, group * group_width : (group + 1) * group_width] = jnp.dot(
            chosen_ref[:, group * depth : (group + 1) * depth],
            halves[...],
            preferred_element_type=jnp.float32,
        ).astype(jnp.bfloat16)
    result = jnp.dot(columns[...], weights_ref[...], preferred_element_type=jnp.float32)
    channels = features.shape[1]
    for side in range(2):
        features[pl.ds(side, result.shape[0], stride=2), :] = result[
            :, side * channels : (side + 1) * channels
        ]
    decoded_ref[...] = features[...].astype(jnp.bfloat16)


def decoded_slab(segment_count, terms, chosen, weights, latents):
    count = len(latents)
    rows = count * MICRO * TOK_DEV
    width = latents[0].shape[-1]
    targets = chosen.shape[0]
    channels = weights.shape[1] // 2
    return pl.pallas_call(
        functools.partial(decode_kernel, segment_count, count),
        in_specs=[whole()] * (3 + count),
        out_specs=[whole()] * 2,
        out_shape=[
            jax.ShapeDtypeStruct(latents[0].shape, jnp.float32),
            jax.ShapeDtypeStruct((2 * targets, channels), jnp.bfloat16),
        ],
        scratch_shapes=[
            pltpu.VMEM((count,) + latents[0].shape, jnp.float32),
            pltpu.VMEM((rows, width), jnp.bfloat16),
            pltpu.VMEM((TAP_GROUP * 2 * rows, TAP_GROUP * width // 2), jnp.bfloat16),
            pltpu.VMEM((targets, weights.shape[0]), jnp.bfloat16),
            pltpu.VMEM((2 * targets, channels), jnp.float32),
        ],
        compiler_params=kernel_params(),
    )(terms, chosen, weights, *latents)


def shards(
    latent,
    w_embed,
    w_qkv,
    w_out,
    mod_table,
    cond_mod,
    stale_kv,
    w_final,
    w_conv,
    patch_order,
    timestep,
    slab_rows,
):
    seq_count = lax.axis_size("seq")
    segment_count = lax.axis_size("segment")

    def within(k):
        return [(i, i ^ k) for i in range(seq_count)]

    def returned(values):
        far_first = [lax.ppermute(values[k], "seq", within(k)) for k in range(seq_count - 1, 0, -1)]
        return values[:1] + far_first[::-1]

    numbers = tuple(range(seq_count))
    half = (seq_count + 1) // 2
    mod_rows, lhs = modulated(
        timestep,
        jnp.transpose(mod_table, (1, 0, 2)),
        jnp.transpose(cond_mod[0], (1, 0, 2)),
        w_embed,
    )
    latent, mod_rows = lax.optimization_barrier((latent, mod_rows))
    latents = returned([latent] * seq_count)
    head_embed, shift_term, out = prepared(lhs, w_qkv[0], w_out[0])
    stale = stale_kv[0, 0, 0]
    *blocks, own = first_layer(
        patch_order, latents, w_embed, head_embed, shift_term, stale, out
    )
    for step in range(1, segment_count):
        block = block_sum(mod_rows, own, returned(blocks))
        pieces = []
        for k in numbers[::-1]:
            pairs = [
                (i * segment_count + j, (i ^ k) * segment_count + (j + 1) % segment_count)
                for i in range(seq_count)
                for j in range(segment_count)
            ]
            pieces.insert(0, lax.ppermute(block, ("seq", "segment"), pairs))
        sums = ()
        for some in (numbers[:half], numbers[half:-1]):
            if some:
                sums = product_sums(
                    some,
                    [pieces[k] for k in some],
                    mod_rows,
                    w_qkv[0],
                    sums,
                )
        *blocks, own = later_layer(
            step + 1 == segment_count,
            patch_order,
            pieces,
            mod_rows,
            w_qkv[0],
            out,
            shift_term,
            stale,
            *sums,
        )

    blocks, slab_rows, w_conv = lax.optimization_barrier((blocks, slab_rows, w_conv))
    token_rows = MICRO * seq_count * TOK_DEV // (FRAMES * HALF)
    slab_most = 4 * token_rows // seq_count
    chosen, weights = window_parts(seq_count, slab_most, token_rows, slab_rows, w_conv)
    peers = ("seq", "segment", "cfg")
    peer_count = seq_count * segment_count * lax.axis_size("cfg")
    terms = velocity_terms(peer_count, mod_rows, own, w_final.T, returned(blocks))
    terms = lax.all_to_all(terms, peers, split_axis=0, concat_axis=0, tiled=True)
    velocity, decoded = decoded_slab(segment_count, terms, chosen, weights, latents)
    return (velocity, decoded.reshape(1, FRAMES, slab_most, LAT_W, w_conv.shape[2]))


def decoder_input(stepped, w_conv, slab_rows, seq_index, seq_count):
    token_rows = MICRO * seq_count * TOK_DEV // (FRAMES * (LAT_W // 2))
    image_rows = 2 * token_rows
    slab_most = 2 * image_rows // seq_count
    image = stepped.reshape(FRAMES, token_rows, LAT_W // 2, 2, 2, LAT_CH)
    image = (
        jnp.transpose(image, (0, 1, 3, 2, 4, 5))
        .reshape(FRAMES, image_rows, LAT_W, LAT_CH)
    )
    padded = jnp.concatenate([image[:1], image[:1], image], 0)
    padded = jnp.pad(padded, ((0, 0), (1, 1 + slab_most), (1, 1), (0, 0)))
    positions = jnp.arange(seq_count)
    slab_count = jnp.sum(jnp.where(positions == seq_index, slab_rows, 0))
    slab_start = jnp.sum(jnp.where(positions < seq_index, slab_rows, 0))
    window = lax.dynamic_slice_in_dim(padded, slab_start, slab_most + 2, 1)
    pieces = []
    for frame_shift in range(3):
        for row_shift in range(3):
            for col_shift in range(3):
                pieces.append(
                    window[
                        frame_shift : frame_shift + FRAMES,
                        row_shift : row_shift + slab_most,
                        col_shift : col_shift + LAT_W,
                    ]
                )
    columns = jnp.concatenate(pieces, -1).reshape(FRAMES * slab_most * LAT_W, 27 * LAT_CH)
    kernel = w_conv.reshape(27 * LAT_CH, w_conv.shape[2])
    features = jnp.dot(columns, kernel, preferred_element_type=jnp.float32).astype(jnp.bfloat16)
    features = features.reshape(FRAMES, slab_most, LAT_W, w_conv.shape[2])
    row_valid = jnp.arange(slab_most)[None, :, None, None] < slab_count
    decoded = jnp.where(row_valid, features, jnp.zeros_like(features))
    return decoded[None]


def solution(mesh):
    in_specs = (
        P(None, ("groups", "seq"), None),
        P(),
        P("segment", "seq", None),
        P("segment", "seq", None),
        P(),
        P("cfg", ("groups", "segment"), None, None),
        P("segment", "cfg", "seq", None, "groups", None),
        P(),
        P(None, None, ("segment", "cfg")),
        P("groups"),
        P("groups"),
        P("groups"),
    )
    out_specs = (
        P(None, ("groups", "seq"), None),
        P(("groups", "seq"), None, None, None, ("segment", "cfg")),
    )
    whole_groups = 2 <= mesh.shape["seq"] <= 8
    program = shards if whole_groups else cycled_shards
    return jax.shard_map(program, mesh=mesh, in_specs=in_specs, out_specs=out_specs, check_vma=False)
```

```python
import functools

import jax
import jax.numpy as jnp
from jax import lax
from jax.experimental import pallas as pl
from jax.experimental.pallas import tpu as pltpu
from jax.sharding import PartitionSpec as P

HEADS = 24
HEAD_DIM = 128
D = 3072
LAT_CH = 16
SCHED_STEPS = 50
MICRO = 2
TOK_DEV = 8
FRAMES = 4
LAT_W = 8


guide_scale = 5.0
norm_eps = 1e-06


def swapped(value, axis, bit):
    return lax.ppermute(value, axis, [(i, i ^ 1 << bit) for i in range(lax.axis_size(axis))])


def passed_along(value, axis, by):
    size = lax.axis_size(axis)
    pairs = [(i, i + by) for i in range(size) if 0 <= i + by < size]
    return lax.ppermute(value, axis, pairs)


def rms_scaled(values):
    wide = values.astype(jnp.float32)
    return wide * lax.rsqrt(jnp.mean(wide * wide, axis=-1, keepdims=True) + norm_eps)


def cycle_join(piece, seq_index, cycle_bits):
    joined = piece
    for bit_number in range(cycle_bits):
        partner = swapped(joined, "seq", bit_number)
        upper_half = (seq_index // 2**bit_number % 2).astype(jnp.int32)
        part_rows = joined.shape[0]
        combined = jnp.zeros((2 * part_rows,) + joined.shape[1:], joined.dtype)
        combined = lax.dynamic_update_slice_in_dim(combined, joined, upper_half * part_rows, 0)
        joined = lax.dynamic_update_slice_in_dim(combined, partner, (1 - upper_half) * part_rows, 0)
    return joined


def cycled_shards(
    latent,
    w_embed,
    w_qkv,
    w_out,
    mod_table,
    cond_mod,
    stale_kv,
    w_final,
    w_conv,
    patch_order,
    timestep,
    slab_rows,
):
    seq_count = lax.axis_size("seq")
    segment_count = lax.axis_size("segment")
    seq_index = lax.axis_index("seq")
    segment_index = lax.axis_index("segment")
    branch_index = lax.axis_index("cfg")
    group_count = min(seq_count, 8)
    cycle_size = seq_count // group_count
    cycle_bits = cycle_size.bit_length() - 1
    group_heads = HEADS // group_count
    sub_rows = TOK_DEV // cycle_size
    share_rows = seq_count * sub_rows
    kv_lanes = 2 * group_heads * HEAD_DIM
    table_row = lax.dynamic_index_in_dim(mod_table, timestep[0], 0, keepdims=False).astype(
        jnp.float32
    )
    modulation = table_row + cond_mod[0, 0]
    shift_row = modulation[0]
    scale_row = modulation[1]
    gate_row = modulation[2]
    joined_weights = (
        cycle_join(w_qkv[0], seq_index, cycle_bits),
        cycle_join(w_out[0], seq_index, cycle_bits),
    )
    stale_joined = cycle_join(stale_kv[0, 0], seq_index, cycle_bits)
    cache = jnp.transpose(stale_joined, (1, 0, 2, 3)).reshape(
        MICRO, cycle_size * share_rows, kv_lanes
    )
    received = jnp.zeros((TOK_DEV, D), jnp.bfloat16)
    finished = jnp.zeros((MICRO, TOK_DEV, D), jnp.bfloat16)
    slot_ids = jnp.arange(MICRO)
    tick_count = MICRO + segment_count - 1
    for tick_index in range(tick_count):
        qkv_rows, out_rows = joined_weights
        micro_index = tick_index - segment_index
        active = (micro_index >= 0) & (micro_index < MICRO)
        clipped = jnp.clip(micro_index, 0, MICRO - 1)
        patch_id = jnp.sum(jnp.where(slot_ids == clipped, patch_order, 0))
        own_latent = lax.dynamic_index_in_dim(latent, patch_id, 0, keepdims=False).astype(
            jnp.bfloat16
        )
        embedded = jnp.dot(own_latent, w_embed, preferred_element_type=jnp.float32).astype(
            jnp.bfloat16
        )
        layer_input = jnp.where(segment_index == 0, embedded, received)
        normed = (rms_scaled(layer_input) * (1.0 + scale_row) + shift_row).astype(jnp.bfloat16)
        outgoing = jnp.broadcast_to(
            normed.reshape(1, cycle_size, sub_rows, D), (group_count, cycle_size, sub_rows, D)
        )
        shared = lax.all_to_all(
            outgoing.reshape(share_rows, D), "seq", split_axis=0, concat_axis=0, tiled=True
        )
        projected = lax.dot_general(
            shared, qkv_rows, (((1,), (1,)), ((), ())), preferred_element_type=jnp.float32
        )
        projected = projected.astype(jnp.bfloat16).reshape(share_rows, group_heads, 3, HEAD_DIM)
        queries = projected[:, :, 0]
        fresh_local = jnp.transpose(projected[:, :, 1:], (0, 2, 1, 3)).reshape(
            1, share_rows, kv_lanes
        )
        fresh = cycle_join(fresh_local, seq_index, cycle_bits).reshape(
            cycle_size * share_rows, kv_lanes
        )
        previous = lax.dynamic_index_in_dim(cache, patch_id, 0, keepdims=False)
        cache = lax.dynamic_update_index_in_dim(
            cache, jnp.where(active, fresh, previous), patch_id, 0
        )
        keyvals = cache.reshape(MICRO * cycle_size * share_rows, 2, group_heads, HEAD_DIM)
        scores = jnp.einsum(
            "shd,khd->hsk", queries, keyvals[:, 0], preferred_element_type=jnp.float32
        ) * HEAD_DIM ** (-0.5)
        probs = jax.nn.softmax(scores, axis=-1).astype(jnp.bfloat16)
        attended = jnp.einsum(
            "hsk,khd->shd", probs, keyvals[:, 1], preferred_element_type=jnp.float32
        ).astype(jnp.bfloat16)
        partial_out = jnp.dot(
            attended.reshape(share_rows, group_heads * HEAD_DIM),
            out_rows,
            preferred_element_type=jnp.float32,
        )
        returned = lax.all_to_all(
            partial_out.astype(jnp.bfloat16), "seq", split_axis=0, concat_axis=0, tiled=True
        ).astype(partial_out.dtype)
        mixed = jnp.sum(returned.reshape(group_count, cycle_size, sub_rows, D), axis=0).reshape(
            TOK_DEV, D
        )
        layer_output = (layer_input.astype(jnp.float32) + gate_row * mixed).astype(jnp.bfloat16)
        keep_final = active & (segment_index == segment_count - 1)
        earlier = lax.dynamic_index_in_dim(finished, patch_id, 0, keepdims=False)
        finished = lax.dynamic_update_index_in_dim(
            finished, jnp.where(keep_final, layer_output, earlier), patch_id, 0
        )
        if tick_index + 1 < tick_count:
            received = passed_along(layer_output, "segment", 1)
    final_normed = rms_scaled(finished).astype(jnp.bfloat16)
    predicted = jnp.einsum("mtd,dc->mtc", final_normed, w_final, preferred_element_type=jnp.float32)
    is_last = segment_index == segment_count - 1
    branch_weight = jnp.where(branch_index == 0, 1.0 - guide_scale, guide_scale)
    velocity_term = jnp.where(is_last, branch_weight * predicted, 0.0)
    latent_term = jnp.where(is_last & (branch_index == 0), latent, 0.0)
    velocity_own, latent_own = lax.psum((velocity_term, latent_term), ("segment", "cfg"))
    velocity_full, latent_full = (
        lax.all_gather(velocity_own, "seq", axis=1, tiled=True),
        lax.all_gather(latent_own, "seq", axis=1, tiled=True),
    )
    stepped = (latent_full - velocity_full / SCHED_STEPS).astype(jnp.bfloat16)
    decoded = decoder_input(stepped, w_conv, slab_rows, seq_index, seq_count)
    return (velocity_own, decoded)


NT = (((1,), (1,)), ((), ()))
TILE = 256
PART = 768
AHEAD = 4


def kernel_params(mebibytes=8):
    return pltpu.CompilerParams(vmem_limit_bytes=mebibytes * 2**20)


def whole(space=pltpu.VMEM):
    return pl.BlockSpec(memory_space=space)


def in_order(copies, ahead):
    for copy in copies[:ahead]:
        copy.start()

    def landed():
        for i, copy in enumerate(copies):
            copy.wait()
            if i + ahead < len(copies):
                copies[i + ahead].start()
            yield i

    return landed()


def in_hbm(*values):
    return [pltpu.with_memory_space_constraint(value, pltpu.HBM) for value in values]


def stage_kernel(latent_ref, staged_ref):
    staged_ref[...] = latent_ref[...]


def staged(latent):
    return pl.pallas_call(
        stage_kernel,
        in_specs=[whole()],
        out_specs=whole(),
        out_shape=jax.ShapeDtypeStruct(latent.shape, latent.dtype),
        cost_estimate=pl.CostEstimate(flops=10**10, bytes_accessed=0, transcendentals=0),
        compiler_params=kernel_params(),
    )(latent)


def prepare_kernel(
    timestep_ref, table_ref, cond_ref, embed_ref, qkv_ref, out_hbm, rows_ref, heads_ref, term_ref, out_ref, lhs, sem
):
    out_copy = pltpu.make_async_copy(out_hbm, out_ref, sem)
    out_copy.start()
    steps = table_ref.shape[1]
    chosen = lax.broadcasted_iota(jnp.int32, (16, steps), 1) == timestep_ref[0]
    chosen = jnp.where(chosen, 1.0, 0.0).astype(jnp.bfloat16)
    for j in range(3):
        row = jnp.dot(chosen, table_ref[j], preferred_element_type=jnp.float32)[:1]
        rows_ref[j : j + 1, :] = row + cond_ref[j] + (1.0 if j == 1 else 0.0)
    count = embed_ref.shape[0]
    lhs[:count] = (embed_ref[...].astype(jnp.float32) * rows_ref[1:2]).astype(jnp.bfloat16)
    lhs[count:] = jnp.broadcast_to(rows_ref[0:1], (16, lhs.shape[1])).astype(jnp.bfloat16)
    for j in range(0, qkv_ref.shape[0], PART):
        lane = slice(j, j + PART)
        product = lax.dot_general(
            lhs[...], qkv_ref[lane, :], NT, preferred_element_type=jnp.float32
        )
        heads_ref[:, lane] = product[:count].astype(jnp.bfloat16)
        term_ref[:, lane] = product[count:]
    out_copy.wait()


def prepared(timestep, table, cond, w_embed, qkv, out):
    count, depth = w_embed.shape
    lanes = qkv.shape[0]
    return pl.pallas_call(
        prepare_kernel,
        in_specs=[whole(pltpu.SMEM)] + [whole()] * 4 + [whole(pltpu.HBM)],
        out_specs=[whole()] * 4,
        out_shape=[
            jax.ShapeDtypeStruct((3, depth), jnp.float32),
            jax.ShapeDtypeStruct((count, lanes), jnp.bfloat16),
            jax.ShapeDtypeStruct((16, lanes), jnp.float32),
            pltpu.VMEM(out.shape, out.dtype),
        ],
        scratch_shapes=[
            pltpu.VMEM((count + 16, depth), jnp.bfloat16),
            pltpu.SemaphoreType.DMA,
        ],
        compiler_params=kernel_params(),
    )(timestep, table, cond, w_embed, qkv, *in_hbm(out))


def span_of(rows, patch_rows):
    return -(-(rows + patch_rows) // 128) * 128


def attention_scratch(rows, patch_rows, lanes):
    shape = (lanes // HEAD_DIM, span_of(rows, patch_rows), HEAD_DIM)
    return [pltpu.VMEM((rows, lanes), jnp.bfloat16)] + [pltpu.VMEM(shape, jnp.bfloat16)] * 2


def attend(projected, order_ref, stale_ref, attended, keys, values):
    rows = projected.shape[0]
    patch_rows = stale_ref.shape[1]
    heads, span, _ = keys.shape
    kept = order_ref[1]
    filled = rows + patch_rows

    def micro_of(index):
        return jnp.where(index // TOK_DEV % MICRO == kept, 1, 0)

    query = micro_of(lax.broadcasted_iota(jnp.int32, (rows, span), 0))
    column = lax.broadcasted_iota(jnp.int32, (rows, span), 1)
    fresh_seen = (column < rows) & (query >= micro_of(column))
    stale_seen = (column >= rows) & (column < filled) & (query == 0)
    seen = fresh_seen | stale_seen
    scores = []
    for head in range(heads):
        first = 3 * HEAD_DIM * head
        for j, buffer in enumerate((keys, values)):
            lane = first + (j + 1) * HEAD_DIM
            stale_lane = (j * heads + head) * HEAD_DIM
            buffer[head, :rows] = projected[:, lane : lane + HEAD_DIM]
            buffer[head, rows:filled] = stale_ref[kept, :, stale_lane : stale_lane + HEAD_DIM]
            if filled < span:
                buffer[head, filled:] = jnp.zeros((span - filled, HEAD_DIM), jnp.bfloat16)
        queries = projected[:, first : first + HEAD_DIM]
        scores.append(
            lax.dot_general(queries, keys[head], NT, preferred_element_type=jnp.float32)
        )
    scores = [jnp.where(seen, score * HEAD_DIM ** (-0.5), -jnp.inf) for score in scores]
    tops = [jnp.max(score, axis=-1, keepdims=True) for score in scores]
    weights = [jnp.exp(score - top) for score, top in zip(scores, tops)]
    totals = [jnp.sum(weight, axis=-1, keepdims=True) for weight in weights]
    for head in range(heads):
        probs = (weights[head] / totals[head]).astype(jnp.bfloat16)
        attended[:, head * HEAD_DIM : (head + 1) * HEAD_DIM] = jnp.dot(
            probs, values[head], preferred_element_type=jnp.float32
        ).astype(jnp.bfloat16)


def column_blocks(place, attended, out_ref, block_refs):
    count = len(block_refs)
    columns = out_ref.shape[1] // count
    for k in range(count):
        first = pl.multiple_of((place ^ k) * columns, columns)
        block_refs[k][...] = jnp.dot(
            attended[...], out_ref[:, pl.ds(first, columns)], preferred_element_type=jnp.float32
        ).astype(jnp.bfloat16)


def first_layer_kernel(
    count, order_ref, embed_ref, heads_ref, term_ref, stale_ref, out_ref, *refs
):
    latent_refs, refs = refs[:count], refs[count:]
    block_refs, (own_ref, latents, attended, keys, values) = refs[:count], refs[count:]
    place = lax.axis_index("seq")
    rows_dev = MICRO * TOK_DEV
    for k in range(count):
        first = pl.multiple_of((place ^ k) * rows_dev, rows_dev)
        latents[pl.ds(first, rows_dev), :] = (
            latent_refs[k][...].reshape(rows_dev, latents.shape[1]).astype(jnp.bfloat16)
        )
    embedded = jnp.dot(latents[...], embed_ref[...], preferred_element_type=jnp.float32)
    embedded = embedded.astype(jnp.bfloat16).astype(jnp.float32)
    norm = lax.rsqrt(jnp.mean(embedded * embedded, axis=-1, keepdims=True) + norm_eps)
    projected = jnp.dot(latents[...], heads_ref[...], preferred_element_type=jnp.float32)
    projected = (norm * projected + term_ref[:1]).astype(jnp.bfloat16)
    attend(projected, order_ref, stale_ref, attended, keys, values)
    columns = own_ref.shape[1]
    first = pl.multiple_of(place * columns, columns)
    own_ref[...] = jnp.dot(
        latents[...], embed_ref[:, pl.ds(first, columns)], preferred_element_type=jnp.float32
    ).astype(jnp.bfloat16)
    column_blocks(place, attended, out_ref, block_refs)


def first_layer(patch_order, latents, w_embed, heads, term, stale, out):
    count = len(latents)
    rows = count * MICRO * TOK_DEV
    lanes, depth = out.shape
    block = jax.ShapeDtypeStruct((rows, depth // count), jnp.bfloat16)
    return pl.pallas_call(
        functools.partial(first_layer_kernel, count),
        in_specs=[whole(pltpu.SMEM)] + [whole()] * (5 + count),
        out_specs=[whole()] * (count + 1),
        out_shape=[block] * (count + 1),
        scratch_shapes=[
            pltpu.VMEM((rows, w_embed.shape[0]), jnp.bfloat16),
            *attention_scratch(rows, stale.shape[1], lanes),
        ],
        compiler_params=kernel_params(),
    )(patch_order, w_embed, heads, term, stale, out, *latents)


def turn_kernel(after_ref, qkv_ref, turned_ref, done_ref):
    lanes, depth = qkv_ref.shape
    for i in range(0, lanes, TILE):
        for j in range(0, depth, TILE):
            turned_ref[j : j + TILE, i : i + TILE] = qkv_ref[i : i + TILE, j : j + TILE].T
    done_ref[...] = jnp.zeros_like(done_ref)


def turned(qkv, after):
    return pl.pallas_call(
        turn_kernel,
        in_specs=[whole(pl.ANY), whole()],
        out_specs=[whole()] * 2,
        out_shape=[
            pltpu.VMEM(qkv.shape[::-1], qkv.dtype),
            jax.ShapeDtypeStruct((8, 128), jnp.float32),
        ],
        cost_estimate=pl.CostEstimate(flops=5 * 10**9, bytes_accessed=0, transcendentals=0),
        compiler_params=kernel_params(),
    )(after, qkv)


def block_sum_kernel(rows_ref, own_ref, done_ref, *refs):
    part_refs, block_ref = refs[:-1], refs[-1]
    columns = own_ref.shape[1]
    first = pl.multiple_of(lax.axis_index("seq") * columns, columns)
    mixed = part_refs[0][...].astype(jnp.float32)
    for part_ref in part_refs[1:]:
        mixed = mixed + part_ref[...].astype(jnp.float32)
    gate = rows_ref[2:3, pl.ds(first, columns)]
    block_ref[...] = (own_ref[...].astype(jnp.float32) + gate * mixed).astype(jnp.bfloat16)


def block_sum(mod_rows, own, done, parts):
    return pl.pallas_call(
        block_sum_kernel,
        in_specs=[whole()] * (3 + len(parts)),
        out_specs=whole(),
        out_shape=jax.ShapeDtypeStruct(own.shape, own.dtype),
        compiler_params=kernel_params(),
    )(mod_rows, own, done, *parts)


def scaled_piece(place, k, piece_ref, rows_ref):
    columns = piece_ref.shape[1]
    first = pl.multiple_of((place ^ k) * columns, columns)
    wide = piece_ref[...].astype(jnp.float32)
    scaled = (wide * rows_ref[1:2, pl.ds(first, columns)]).astype(jnp.bfloat16)
    return scaled, jnp.sum(wide * wide, axis=-1, keepdims=True)


def sums_kernel(numbers, rows_ref, turned_ref, *refs):
    count = len(numbers)
    piece_refs, earlier, (sums_ref, squares_ref) = refs[:count], refs[count:-2], refs[-2:]
    place = lax.axis_index("seq")
    columns = piece_refs[0].shape[1]
    squares = earlier[1][...] if earlier else 0.0
    scaled = []
    for k, piece_ref in zip(numbers, piece_refs):
        piece, square = scaled_piece(place, k, piece_ref, rows_ref)
        scaled.append((piece, pl.ds(pl.multiple_of((place ^ k) * columns, columns), columns)))
        squares = squares + square
    squares_ref[...] = squares
    for i in range(0, sums_ref.shape[1], PART):
        lane = slice(i, i + PART)
        total = earlier[0][:, lane] if earlier else 0.0
        for piece, part in scaled:
            total = total + jnp.dot(
                piece, turned_ref[part, lane], preferred_element_type=jnp.float32
            )
        sums_ref[:, lane] = total


def product_sums(numbers, pieces, mod_rows, qkv, earlier):
    rows = pieces[0].shape[0]
    lanes = qkv.shape[1]
    return pl.pallas_call(
        functools.partial(sums_kernel, numbers),
        in_specs=[whole()] * (2 + len(numbers) + len(earlier)),
        out_specs=[whole()] * 2,
        out_shape=[
            jax.ShapeDtypeStruct((rows, lanes), jnp.float32),
            jax.ShapeDtypeStruct((rows, 1), jnp.float32),
        ],
        compiler_params=kernel_params(),
    )(mod_rows, qkv, *pieces, *earlier)


def later_layer_kernel(
    count, last, order_ref, rows_ref, qkv_ref, out_ref, term_ref, stale_ref, sums_ref, squares_ref, *refs
):
    piece_refs, refs = refs[:count], refs[count:]
    block_refs, own_ref, sums, attended, keys, values, partial_out = refs[:count], *refs[count:]
    place = lax.axis_index("seq")
    scaled, squares = scaled_piece(place, count - 1, piece_refs[-1], rows_ref)
    norm = lax.rsqrt((squares_ref[...] + squares) / rows_ref.shape[1] + norm_eps)
    columns = piece_refs[-1].shape[1]
    part = pl.ds(pl.multiple_of((place ^ (count - 1)) * columns, columns), columns)
    for i in range(0, sums.shape[1], PART):
        lane = slice(i, i + PART)
        product = jnp.dot(scaled, qkv_ref[part, lane], preferred_element_type=jnp.float32)
        sums[:, lane] = (norm * (product + sums_ref[:, lane]) + term_ref[:1, lane]).astype(
            jnp.bfloat16
        )
    attend(sums, order_ref, stale_ref, attended, keys, values)
    if not last:
        column_blocks(place, attended, out_ref, block_refs)
        own_ref[...] = piece_refs[0][...]
        return
    partial_out[...] = jnp.dot(
        attended[...], out_ref[...], preferred_element_type=jnp.float32
    ).astype(jnp.bfloat16)
    rows_dev = own_ref.shape[0]
    columns = piece_refs[0].shape[1]
    own_rows = pl.ds(pl.multiple_of(place * rows_dev, rows_dev), rows_dev)
    for k in range(count):
        first = pl.multiple_of((place ^ k) * rows_dev, rows_dev)
        block_refs[k][...] = partial_out[pl.ds(first, rows_dev), :]
        first = pl.multiple_of((place ^ k) * columns, columns)
        own_ref[:, pl.ds(first, columns)] = piece_refs[k][own_rows, :]


def later_layer(last, patch_order, pieces, mod_rows, qkv, out, term, stale, sums, squares):
    count = len(pieces)
    rows, columns = pieces[0].shape
    lanes, depth = out.shape
    shape = (rows // count, depth) if last else (rows, columns)
    block = jax.ShapeDtypeStruct(shape, jnp.bfloat16)
    return pl.pallas_call(
        functools.partial(later_layer_kernel, count, last),
        in_specs=[whole(pltpu.SMEM)] + [whole()] * (7 + count),
        out_specs=[whole()] * (count + 1),
        out_shape=[block] * (count + 1),
        scratch_shapes=[
            pltpu.VMEM(sums.shape, jnp.bfloat16),
            *attention_scratch(rows, stale.shape[1], lanes),
            pltpu.VMEM((rows, depth), jnp.bfloat16),
        ],
        compiler_params=kernel_params(),
    )(patch_order, mod_rows, qkv, out, term, stale, sums, squares, *pieces)


def term_kernel(rows_ref, own_ref, final_ref, *refs):
    part_refs, term_ref = refs[:-1], refs[-1]
    mixed = part_refs[0][...].astype(jnp.float32)
    for part_ref in part_refs[1:]:
        mixed = mixed + part_ref[...].astype(jnp.float32)
    hidden = (own_ref[...].astype(jnp.float32) + rows_ref[2:3] * mixed).astype(jnp.bfloat16)
    predicted = lax.dot_general(
        hidden, final_ref[...], NT, preferred_element_type=jnp.float32
    )
    wide = hidden.astype(jnp.float32)
    norm = lax.rsqrt(jnp.mean(wide * wide, axis=-1, keepdims=True) + norm_eps)
    predicted = norm * predicted
    weight = jnp.where(lax.axis_index("cfg") == 0, 1.0 - guide_scale, guide_scale)
    patches = [predicted[i * TOK_DEV : (i + 1) * TOK_DEV] for i in range(MICRO)]
    term = weight * jnp.concatenate(patches, axis=1)
    term_ref[...] = jnp.broadcast_to(term, term_ref.shape)


def velocity_terms(peers, mod_rows, own, final, parts):
    shape = (peers, TOK_DEV, MICRO * final.shape[0])
    return pl.pallas_call(
        term_kernel,
        in_specs=[whole()] * (3 + len(parts)),
        out_specs=whole(),
        out_shape=jax.ShapeDtypeStruct(shape, jnp.float32),
        compiler_params=kernel_params(),
    )(mod_rows, own, final, *parts)


TAPS = 27
TAP_GROUP = 4
HALF = LAT_W // 2


def window_kernel(sizes, slab_ref, conv_ref, chosen_ref, weights_ref):
    seq_count, slab_most, token_rows = sizes
    place = lax.axis_index("seq")
    rows = seq_count * MICRO * TOK_DEV
    start = 0
    for j in range(seq_count - 1):
        start = start + jnp.where(j < place, slab_ref[j], 0)
    shape = (chosen_ref.shape[0], 2 * rows)
    target = lax.broadcasted_iota(jnp.int32, shape, 0)
    column = lax.broadcasted_iota(jnp.int32, shape, 1)
    across = target % HALF
    down = target // HALF % slab_most
    frame = target // (HALF * slab_most)
    kept = down < slab_ref[place]
    patch_rows = seq_count * TOK_DEV
    for tap in range(TAPS):
        time, row_shift, token_shift = tap // 9, tap // 3 % 3, tap % 3
        source_frame = jnp.maximum(frame + (time - 2), 0)
        row = start + down + (row_shift - 1)
        token = across + (token_shift - 1)
        inside = kept & (row >= 0) & (row < 2 * token_rows) & (token >= 0) & (token < HALF)
        row = jnp.maximum(row, 0)
        index = (source_frame * token_rows + row // 2) * HALF + jnp.maximum(token, 0)
        patch = index // patch_rows
        slot = index % patch_rows
        source = (slot // TOK_DEV * MICRO + patch) * TOK_DEV + slot % TOK_DEV + row % 2 * rows
        chosen_ref[:, tap * 2 * rows : (tap + 1) * 2 * rows] = jnp.where(
            inside & (column == source), 1.0, 0.0
        ).astype(jnp.bfloat16)
    chosen_ref[:, TAPS * 2 * rows :] = jnp.zeros(
        (shape[0], chosen_ref.shape[1] - TAPS * 2 * rows), jnp.bfloat16
    )
    weights_ref[...] = jnp.zeros_like(weights_ref)
    channels = conv_ref.shape[2]
    for tap in range(TAPS):
        for source in range(2):
            for side in range(2):
                shift = 2 * (tap % 3 - 1) + source - side + 1
                if 0 <= shift < 3:
                    first = (tap * 2 + source) * LAT_CH
                    weights_ref[first : first + LAT_CH, side * channels : (side + 1) * channels] = (
                        conv_ref[tap // 3 * 3 + shift]
                    )


def window_parts(seq_count, slab_most, token_rows, slab_rows, w_conv):
    rows = seq_count * MICRO * TOK_DEV
    groups = -(-TAPS // TAP_GROUP)
    return pl.pallas_call(
        functools.partial(window_kernel, (seq_count, slab_most, token_rows)),
        in_specs=[whole(pltpu.SMEM), whole()],
        out_specs=[whole()] * 2,
        out_shape=[
            jax.ShapeDtypeStruct(
                (FRAMES * slab_most * HALF, groups * TAP_GROUP * 2 * rows), jnp.bfloat16
            ),
            jax.ShapeDtypeStruct(
                (groups * TAP_GROUP * 2 * LAT_CH, 2 * w_conv.shape[2]), jnp.bfloat16
            ),
        ],
        compiler_params=kernel_params(),
    )(slab_rows, w_conv)


def decode_kernel(
    segment_count, count, terms_ref, chosen_ref, weights_ref, *refs
):
    latent_refs, refs = refs[:count], refs[count:]
    velocity_ref, decoded_ref, latents, tokens, halves, columns, features = refs
    place = lax.axis_index("seq")
    for k in range(count):
        latents[place ^ k] = latent_refs[k][...]

    def velocity_of(z):
        first = (z * segment_count + segment_count - 1) * 2
        both = terms_ref[first] + terms_ref[first + 1]
        width = both.shape[1] // MICRO
        return [both[:, i * width : (i + 1) * width] for i in range(MICRO)]

    for i, value in enumerate(velocity_of(place)):
        velocity_ref[i] = value
    for z in range(count):
        stepped = [
            latents[z, i] - value / SCHED_STEPS for i, value in enumerate(velocity_of(z))
        ]
        tokens[z * MICRO * TOK_DEV : (z + 1) * MICRO * TOK_DEV] = jnp.concatenate(
            stepped, axis=0
        ).astype(jnp.bfloat16)
    rows, width = tokens.shape
    half = width // 2
    halves[...] = jnp.zeros_like(halves)
    for j in range(TAP_GROUP):
        for side in range(2):
            first = (j * 2 + side) * rows
            halves[first : first + rows, j * half : (j + 1) * half] = tokens[
                :, side * half : (side + 1) * half
            ]
    depth, group_width = halves.shape
    for group in range(chosen_ref.shape[1] // depth):
        columns[:, group * group_width : (group + 1) * group_width] = jnp.dot(
            chosen_ref[:, group * depth : (group + 1) * depth],
            halves[...],
            preferred_element_type=jnp.float32,
        ).astype(jnp.bfloat16)
    result = jnp.dot(columns[...], weights_ref[...], preferred_element_type=jnp.float32)
    channels = features.shape[1]
    for side in range(2):
        features[pl.ds(side, result.shape[0], stride=2), :] = result[
            :, side * channels : (side + 1) * channels
        ]
    decoded_ref[...] = features[...].astype(jnp.bfloat16)


def decoded_slab(segment_count, terms, chosen, weights, latents):
    count = len(latents)
    rows = count * MICRO * TOK_DEV
    width = latents[0].shape[-1]
    targets = chosen.shape[0]
    channels = weights.shape[1] // 2
    return pl.pallas_call(
        functools.partial(decode_kernel, segment_count, count),
        in_specs=[whole()] * (3 + count),
        out_specs=[whole()] * 2,
        out_shape=[
            jax.ShapeDtypeStruct(latents[0].shape, jnp.float32),
            jax.ShapeDtypeStruct((2 * targets, channels), jnp.bfloat16),
        ],
        scratch_shapes=[
            pltpu.VMEM((count,) + latents[0].shape, jnp.float32),
            pltpu.VMEM((rows, width), jnp.bfloat16),
            pltpu.VMEM((TAP_GROUP * 2 * rows, TAP_GROUP * width // 2), jnp.bfloat16),
            pltpu.VMEM((targets, weights.shape[0]), jnp.bfloat16),
            pltpu.VMEM((2 * targets, channels), jnp.float32),
        ],
        compiler_params=kernel_params(),
    )(terms, chosen, weights, *latents)


def shards(
    latent,
    w_embed,
    w_qkv,
    w_out,
    mod_table,
    cond_mod,
    stale_kv,
    w_final,
    w_conv,
    patch_order,
    timestep,
    slab_rows,
):
    seq_count = lax.axis_size("seq")
    segment_count = lax.axis_size("segment")

    def within(k):
        return [(i, i ^ k) for i in range(seq_count)]

    def returned(values):
        far_first = [lax.ppermute(values[k], "seq", within(k)) for k in range(seq_count - 1, 0, -1)]
        return values[:1] + far_first[::-1]

    numbers = tuple(range(seq_count))
    half = (seq_count + 1) // 2
    latents = returned([staged(latent)] * seq_count)
    mod_rows, head_embed, shift_term, out = prepared(
        timestep,
        jnp.transpose(mod_table, (1, 0, 2)),
        jnp.transpose(cond_mod[0], (1, 0, 2)),
        w_embed,
        w_qkv[0],
        w_out[0],
    )
    stale = stale_kv[0, 0, 0]
    *blocks, own = first_layer(
        patch_order, latents, w_embed, head_embed, shift_term, stale, out
    )
    qkv, done = turned(w_qkv[0], own)
    for step in range(1, segment_count):
        block = block_sum(mod_rows, own, done, returned(blocks))
        pieces = []
        for k in numbers[::-1]:
            pairs = [
                (i * segment_count + j, (i ^ k) * segment_count + (j + 1) % segment_count)
                for i in range(seq_count)
                for j in range(segment_count)
            ]
            pieces.insert(0, lax.ppermute(block, ("seq", "segment"), pairs))
        sums = ()
        for some in (numbers[:half], numbers[half:-1]):
            if some:
                sums = product_sums(
                    some,
                    [pieces[k] for k in some],
                    mod_rows,
                    qkv,
                    sums,
                )
        *blocks, own = later_layer(
            step + 1 == segment_count,
            patch_order,
            pieces,
            mod_rows,
            qkv,
            out,
            shift_term,
            stale,
            *sums,
        )

    blocks, slab_rows, w_conv = lax.optimization_barrier((blocks, slab_rows, w_conv))
    token_rows = MICRO * seq_count * TOK_DEV // (FRAMES * HALF)
    slab_most = 4 * token_rows // seq_count
    chosen, weights = window_parts(seq_count, slab_most, token_rows, slab_rows, w_conv)
    peers = ("seq", "segment", "cfg")
    peer_count = seq_count * segment_count * lax.axis_size("cfg")
    terms = velocity_terms(peer_count, mod_rows, own, w_final.T, returned(blocks))
    terms = lax.all_to_all(terms, peers, split_axis=0, concat_axis=0, tiled=True)
    velocity, decoded = decoded_slab(segment_count, terms, chosen, weights, latents)
    return (velocity, decoded.reshape(1, FRAMES, slab_most, LAT_W, w_conv.shape[2]))


def decoder_input(stepped, w_conv, slab_rows, seq_index, seq_count):
    token_rows = MICRO * seq_count * TOK_DEV // (FRAMES * (LAT_W // 2))
    image_rows = 2 * token_rows
    slab_most = 2 * image_rows // seq_count
    image = stepped.reshape(FRAMES, token_rows, LAT_W // 2, 2, 2, LAT_CH)
    image = (
        jnp.transpose(image, (0, 1, 3, 2, 4, 5))
        .reshape(FRAMES, image_rows, LAT_W, LAT_CH)
    )
    padded = jnp.concatenate([image[:1], image[:1], image], 0)
    padded = jnp.pad(padded, ((0, 0), (1, 1 + slab_most), (1, 1), (0, 0)))
    positions = jnp.arange(seq_count)
    slab_count = jnp.sum(jnp.where(positions == seq_index, slab_rows, 0))
    slab_start = jnp.sum(jnp.where(positions < seq_index, slab_rows, 0))
    window = lax.dynamic_slice_in_dim(padded, slab_start, slab_most + 2, 1)
    pieces = []
    for frame_shift in range(3):
        for row_shift in range(3):
            for col_shift in range(3):
                pieces.append(
                    window[
                        frame_shift : frame_shift + FRAMES,
                        row_shift : row_shift + slab_most,
                        col_shift : col_shift + LAT_W,
                    ]
                )
    columns = jnp.concatenate(pieces, -1).reshape(FRAMES * slab_most * LAT_W, 27 * LAT_CH)
    kernel = w_conv.reshape(27 * LAT_CH, w_conv.shape[2])
    features = jnp.dot(columns, kernel, preferred_element_type=jnp.float32).astype(jnp.bfloat16)
    features = features.reshape(FRAMES, slab_most, LAT_W, w_conv.shape[2])
    row_valid = jnp.arange(slab_most)[None, :, None, None] < slab_count
    decoded = jnp.where(row_valid, features, jnp.zeros_like(features))
    return decoded[None]


def solution(mesh):
    in_specs = (
        P(None, ("groups", "seq"), None),
        P(),
        P("segment", "seq", None),
        P("segment", "seq", None),
        P(),
        P("cfg", ("groups", "segment"), None, None),
        P("segment", "cfg", "seq", None, "groups", None),
        P(),
        P(None, None, ("segment", "cfg")),
        P("groups"),
        P("groups"),
        P("groups"),
    )
    out_specs = (
        P(None, ("groups", "seq"), None),
        P(("groups", "seq"), None, None, None, ("segment", "cfg")),
    )
    whole_groups = 2 <= mesh.shape["seq"] <= 8
    program = shards if whole_groups else cycled_shards
    return jax.shard_map(program, mesh=mesh, in_specs=in_specs, out_specs=out_specs, check_vma=False)
```

```python
import functools

import jax
import jax.numpy as jnp
from jax import lax
from jax.experimental import pallas as pl
from jax.experimental.pallas import tpu as pltpu
from jax.sharding import PartitionSpec as P

HEADS = 24
HEAD_DIM = 128
D = 3072
LAT_CH = 16
SCHED_STEPS = 50
MICRO = 2
TOK_DEV = 8
FRAMES = 4
LAT_W = 8


guide_scale = 5.0
norm_eps = 1e-06


def swapped(value, axis, bit):
    return lax.ppermute(value, axis, [(i, i ^ 1 << bit) for i in range(lax.axis_size(axis))])


def passed_along(value, axis, by):
    size = lax.axis_size(axis)
    pairs = [(i, i + by) for i in range(size) if 0 <= i + by < size]
    return lax.ppermute(value, axis, pairs)


def rms_scaled(values):
    wide = values.astype(jnp.float32)
    return wide * lax.rsqrt(jnp.mean(wide * wide, axis=-1, keepdims=True) + norm_eps)


def cycle_join(piece, seq_index, cycle_bits):
    joined = piece
    for bit_number in range(cycle_bits):
        partner = swapped(joined, "seq", bit_number)
        upper_half = (seq_index // 2**bit_number % 2).astype(jnp.int32)
        part_rows = joined.shape[0]
        combined = jnp.zeros((2 * part_rows,) + joined.shape[1:], joined.dtype)
        combined = lax.dynamic_update_slice_in_dim(combined, joined, upper_half * part_rows, 0)
        joined = lax.dynamic_update_slice_in_dim(combined, partner, (1 - upper_half) * part_rows, 0)
    return joined


def cycled_shards(
    latent,
    w_embed,
    w_qkv,
    w_out,
    mod_table,
    cond_mod,
    stale_kv,
    w_final,
    w_conv,
    patch_order,
    timestep,
    slab_rows,
):
    seq_count = lax.axis_size("seq")
    segment_count = lax.axis_size("segment")
    seq_index = lax.axis_index("seq")
    segment_index = lax.axis_index("segment")
    branch_index = lax.axis_index("cfg")
    group_count = min(seq_count, 8)
    cycle_size = seq_count // group_count
    cycle_bits = cycle_size.bit_length() - 1
    group_heads = HEADS // group_count
    sub_rows = TOK_DEV // cycle_size
    share_rows = seq_count * sub_rows
    kv_lanes = 2 * group_heads * HEAD_DIM
    table_row = lax.dynamic_index_in_dim(mod_table, timestep[0], 0, keepdims=False).astype(
        jnp.float32
    )
    modulation = table_row + cond_mod[0, 0]
    shift_row = modulation[0]
    scale_row = modulation[1]
    gate_row = modulation[2]
    joined_weights = (
        cycle_join(w_qkv[0], seq_index, cycle_bits),
        cycle_join(w_out[0], seq_index, cycle_bits),
    )
    stale_joined = cycle_join(stale_kv[0, 0], seq_index, cycle_bits)
    cache = jnp.transpose(stale_joined, (1, 0, 2, 3)).reshape(
        MICRO, cycle_size * share_rows, kv_lanes
    )
    received = jnp.zeros((TOK_DEV, D), jnp.bfloat16)
    finished = jnp.zeros((MICRO, TOK_DEV, D), jnp.bfloat16)
    slot_ids = jnp.arange(MICRO)
    tick_count = MICRO + segment_count - 1
    for tick_index in range(tick_count):
        qkv_rows, out_rows = joined_weights
        micro_index = tick_index - segment_index
        active = (micro_index >= 0) & (micro_index < MICRO)
        clipped = jnp.clip(micro_index, 0, MICRO - 1)
        patch_id = jnp.sum(jnp.where(slot_ids == clipped, patch_order, 0))
        own_latent = lax.dynamic_index_in_dim(latent, patch_id, 0, keepdims=False).astype(
            jnp.bfloat16
        )
        embedded = jnp.dot(own_latent, w_embed, preferred_element_type=jnp.float32).astype(
            jnp.bfloat16
        )
        layer_input = jnp.where(segment_index == 0, embedded, received)
        normed = (rms_scaled(layer_input) * (1.0 + scale_row) + shift_row).astype(jnp.bfloat16)
        outgoing = jnp.broadcast_to(
            normed.reshape(1, cycle_size, sub_rows, D), (group_count, cycle_size, sub_rows, D)
        )
        shared = lax.all_to_all(
            outgoing.reshape(share_rows, D), "seq", split_axis=0, concat_axis=0, tiled=True
        )
        projected = lax.dot_general(
            shared, qkv_rows, (((1,), (1,)), ((), ())), preferred_element_type=jnp.float32
        )
        projected = projected.astype(jnp.bfloat16).reshape(share_rows, group_heads, 3, HEAD_DIM)
        queries = projected[:, :, 0]
        fresh_local = jnp.transpose(projected[:, :, 1:], (0, 2, 1, 3)).reshape(
            1, share_rows, kv_lanes
        )
        fresh = cycle_join(fresh_local, seq_index, cycle_bits).reshape(
            cycle_size * share_rows, kv_lanes
        )
        previous = lax.dynamic_index_in_dim(cache, patch_id, 0, keepdims=False)
        cache = lax.dynamic_update_index_in_dim(
            cache, jnp.where(active, fresh, previous), patch_id, 0
        )
        keyvals = cache.reshape(MICRO * cycle_size * share_rows, 2, group_heads, HEAD_DIM)
        scores = jnp.einsum(
            "shd,khd->hsk", queries, keyvals[:, 0], preferred_element_type=jnp.float32
        ) * HEAD_DIM ** (-0.5)
        probs = jax.nn.softmax(scores, axis=-1).astype(jnp.bfloat16)
        attended = jnp.einsum(
            "hsk,khd->shd", probs, keyvals[:, 1], preferred_element_type=jnp.float32
        ).astype(jnp.bfloat16)
        partial_out = jnp.dot(
            attended.reshape(share_rows, group_heads * HEAD_DIM),
            out_rows,
            preferred_element_type=jnp.float32,
        )
        returned = lax.all_to_all(
            partial_out.astype(jnp.bfloat16), "seq", split_axis=0, concat_axis=0, tiled=True
        ).astype(partial_out.dtype)
        mixed = jnp.sum(returned.reshape(group_count, cycle_size, sub_rows, D), axis=0).reshape(
            TOK_DEV, D
        )
        layer_output = (layer_input.astype(jnp.float32) + gate_row * mixed).astype(jnp.bfloat16)
        keep_final = active & (segment_index == segment_count - 1)
        earlier = lax.dynamic_index_in_dim(finished, patch_id, 0, keepdims=False)
        finished = lax.dynamic_update_index_in_dim(
            finished, jnp.where(keep_final, layer_output, earlier), patch_id, 0
        )
        if tick_index + 1 < tick_count:
            received = passed_along(layer_output, "segment", 1)
    final_normed = rms_scaled(finished).astype(jnp.bfloat16)
    predicted = jnp.einsum("mtd,dc->mtc", final_normed, w_final, preferred_element_type=jnp.float32)
    is_last = segment_index == segment_count - 1
    branch_weight = jnp.where(branch_index == 0, 1.0 - guide_scale, guide_scale)
    velocity_term = jnp.where(is_last, branch_weight * predicted, 0.0)
    latent_term = jnp.where(is_last & (branch_index == 0), latent, 0.0)
    velocity_own, latent_own = lax.psum((velocity_term, latent_term), ("segment", "cfg"))
    velocity_full, latent_full = (
        lax.all_gather(velocity_own, "seq", axis=1, tiled=True),
        lax.all_gather(latent_own, "seq", axis=1, tiled=True),
    )
    stepped = (latent_full - velocity_full / SCHED_STEPS).astype(jnp.bfloat16)
    decoded = decoder_input(stepped, w_conv, slab_rows, seq_index, seq_count)
    return (velocity_own, decoded)


NT = (((1,), (1,)), ((), ()))
TILE = 256
PART = 768
AHEAD = 4


def kernel_params(mebibytes=8):
    return pltpu.CompilerParams(vmem_limit_bytes=mebibytes * 2**20)


def whole(space=pltpu.VMEM):
    return pl.BlockSpec(memory_space=space)


def in_order(copies, ahead):
    for copy in copies[:ahead]:
        copy.start()

    def landed():
        for i, copy in enumerate(copies):
            copy.wait()
            if i + ahead < len(copies):
                copies[i + ahead].start()
            yield i

    return landed()


def in_hbm(*values):
    return [pltpu.with_memory_space_constraint(value, pltpu.HBM) for value in values]


def stage_kernel(latent_hbm, staged_ref, sem):
    copy = pltpu.make_async_copy(latent_hbm, staged_ref, sem)
    copy.start()
    copy.wait()


def staged(latent):
    return pl.pallas_call(
        stage_kernel,
        in_specs=[whole(pltpu.HBM)],
        out_specs=whole(),
        out_shape=pltpu.VMEM(latent.shape, latent.dtype),
        scratch_shapes=[pltpu.SemaphoreType.DMA],
        cost_estimate=pl.CostEstimate(flops=10**10, bytes_accessed=0, transcendentals=0),
        compiler_params=kernel_params(),
    )(*in_hbm(latent))


def prepare_kernel(
    timestep_ref, table_ref, cond_ref, embed_ref, qkv_ref, out_hbm, rows_ref, heads_ref, out_ref, lhs, sem
):
    out_copy = pltpu.make_async_copy(out_hbm, out_ref, sem)
    out_copy.start()
    steps = table_ref.shape[1]
    chosen = lax.broadcasted_iota(jnp.int32, (16, steps), 1) == timestep_ref[0]
    chosen = jnp.where(chosen, 1.0, 0.0).astype(jnp.bfloat16)
    for j in range(3):
        row = jnp.dot(chosen, table_ref[j], preferred_element_type=jnp.float32)[:1]
        rows_ref[j : j + 1, :] = row + cond_ref[j] + (1.0 if j == 1 else 0.0)
    count = embed_ref.shape[0]
    spare, depth = lhs.shape[0] - count, lhs.shape[1]
    lhs[:count] = (embed_ref[...].astype(jnp.float32) * rows_ref[1:2]).astype(jnp.bfloat16)
    lhs[count:] = jnp.broadcast_to(rows_ref[0:1], (spare, depth)).astype(jnp.bfloat16)
    lane = lax.broadcasted_iota(jnp.int32, (PART, lhs.shape[0]), 1)
    for j in range(0, qkv_ref.shape[0], PART):
        product = lax.dot_general(
            qkv_ref[j : j + PART, :], lhs[...], NT, preferred_element_type=jnp.float32
        )
        upper = product.astype(jnp.bfloat16).astype(jnp.float32)
        value = jnp.where(lane == count + 1, product - upper, upper)
        heads_ref[j : j + PART, :] = jnp.where(lane <= count + 2, value, 0.0).astype(jnp.bfloat16)
    out_copy.wait()


def prepared(timestep, table, cond, w_embed, qkv, out):
    count, depth = w_embed.shape
    lanes = qkv.shape[0]
    return pl.pallas_call(
        prepare_kernel,
        in_specs=[whole(pltpu.SMEM)] + [whole()] * 4 + [whole(pltpu.HBM)],
        out_specs=[whole()] * 3,
        out_shape=[
            jax.ShapeDtypeStruct((3, depth), jnp.float32),
            jax.ShapeDtypeStruct((lanes, 2 * count), jnp.bfloat16),
            pltpu.VMEM(out.shape, out.dtype),
        ],
        scratch_shapes=[
            pltpu.VMEM((2 * count, depth), jnp.bfloat16),
            pltpu.SemaphoreType.DMA,
        ],
        compiler_params=kernel_params(),
    )(timestep, table, cond, w_embed, qkv, *in_hbm(out))


def span_of(rows, patch_rows):
    return -(-(rows + patch_rows) // 128) * 128


def attention_scratch(rows, patch_rows, lanes):
    shape = (lanes // HEAD_DIM, span_of(rows, patch_rows), HEAD_DIM)
    return [pltpu.VMEM((rows, lanes), jnp.bfloat16)] + [pltpu.VMEM(shape, jnp.bfloat16)] * 2


def attend(projected, order_ref, stale_ref, attended, keys, values):
    rows = projected.shape[0]
    patch_rows = stale_ref.shape[1]
    heads, span, _ = keys.shape
    kept = order_ref[1]
    filled = rows + patch_rows

    def micro_of(index):
        return jnp.where(index // TOK_DEV % MICRO == kept, 1, 0)

    query = micro_of(lax.broadcasted_iota(jnp.int32, (rows, span), 0))
    column = lax.broadcasted_iota(jnp.int32, (rows, span), 1)
    fresh_seen = (column < rows) & (query >= micro_of(column))
    stale_seen = (column >= rows) & (column < filled) & (query == 0)
    seen = fresh_seen | stale_seen
    scores = []
    for head in range(heads):
        first = 3 * HEAD_DIM * head
        for j, buffer in enumerate((keys, values)):
            lane = first + (j + 1) * HEAD_DIM
            stale_lane = (j * heads + head) * HEAD_DIM
            buffer[head, :rows] = projected[:, lane : lane + HEAD_DIM]
            buffer[head, rows:filled] = stale_ref[kept, :, stale_lane : stale_lane + HEAD_DIM]
            if filled < span:
                buffer[head, filled:] = jnp.zeros((span - filled, HEAD_DIM), jnp.bfloat16)
        queries = projected[:, first : first + HEAD_DIM]
        scores.append(
            lax.dot_general(queries, keys[head], NT, preferred_element_type=jnp.float32)
        )
    scores = [jnp.where(seen, score * HEAD_DIM ** (-0.5), -jnp.inf) for score in scores]
    tops = [jnp.max(score, axis=-1, keepdims=True) for score in scores]
    weights = [jnp.exp(score - top) for score, top in zip(scores, tops)]
    totals = [jnp.sum(weight, axis=-1, keepdims=True) for weight in weights]
    for head in range(heads):
        probs = (weights[head] / totals[head]).astype(jnp.bfloat16)
        attended[:, head * HEAD_DIM : (head + 1) * HEAD_DIM] = jnp.dot(
            probs, values[head], preferred_element_type=jnp.float32
        ).astype(jnp.bfloat16)


def column_blocks(place, attended, out_ref, block_refs):
    count = len(block_refs)
    columns = out_ref.shape[1] // count
    for k in range(count):
        first = pl.multiple_of((place ^ k) * columns, columns)
        block_refs[k][...] = jnp.dot(
            attended[...], out_ref[:, pl.ds(first, columns)], preferred_element_type=jnp.float32
        ).astype(jnp.bfloat16)


def first_layer_kernel(
    count, order_ref, embed_ref, heads_ref, stale_ref, out_ref, *refs
):
    latent_refs, refs = refs[:count], refs[count:]
    block_refs, (own_ref, latents, attended, keys, values) = refs[:count], refs[count:]
    place = lax.axis_index("seq")
    rows_dev = MICRO * TOK_DEV
    width = embed_ref.shape[0]
    for k in range(count):
        first = pl.multiple_of((place ^ k) * rows_dev, rows_dev)
        latents[pl.ds(first, rows_dev), :width] = (
            latent_refs[k][...].reshape(rows_dev, width).astype(jnp.bfloat16)
        )
    embedded = jnp.dot(latents[:, :width], embed_ref[...], preferred_element_type=jnp.float32)
    embedded = embedded.astype(jnp.bfloat16).astype(jnp.float32)
    square = jnp.mean(embedded * embedded, axis=-1, keepdims=True) + norm_eps
    norm = lax.rsqrt(square)
    size = square * norm
    upper = size.astype(jnp.bfloat16).astype(jnp.float32)
    lane = lax.broadcasted_iota(jnp.int32, (latents.shape[0], width), 1)
    spare = jnp.where(lane < 2, upper, jnp.where(lane == 2, size - upper, 0.0))
    latents[:, width:] = spare.astype(jnp.bfloat16)
    projected = lax.dot_general(
        latents[...], heads_ref[...], NT, preferred_element_type=jnp.float32
    )
    projected = (norm * projected).astype(jnp.bfloat16)
    attend(projected, order_ref, stale_ref, attended, keys, values)
    columns = own_ref.shape[1]
    first = pl.multiple_of(place * columns, columns)
    own_ref[...] = jnp.dot(
        latents[:, :width], embed_ref[:, pl.ds(first, columns)], preferred_element_type=jnp.float32
    ).astype(jnp.bfloat16)
    column_blocks(place, attended, out_ref, block_refs)


def first_layer(patch_order, latents, w_embed, heads, stale, out):
    count = len(latents)
    rows = count * MICRO * TOK_DEV
    lanes, depth = out.shape
    block = jax.ShapeDtypeStruct((rows, depth // count), jnp.bfloat16)
    return pl.pallas_call(
        functools.partial(first_layer_kernel, count),
        in_specs=[whole(pltpu.SMEM)] + [whole()] * (4 + count),
        out_specs=[whole()] * (count + 1),
        out_shape=[block] * (count + 1),
        scratch_shapes=[
            pltpu.VMEM((rows, 2 * w_embed.shape[0]), jnp.bfloat16),
            *attention_scratch(rows, stale.shape[1], lanes),
        ],
        compiler_params=kernel_params(),
    )(patch_order, w_embed, heads, stale, out, *latents)


def turn_kernel(after_ref, qkv_ref, heads_ref, turned_ref, term_ref):
    lanes, depth = qkv_ref.shape
    for i in range(0, lanes, TILE):
        for j in range(0, depth, TILE):
            turned_ref[j : j + TILE, i : i + TILE] = qkv_ref[i : i + TILE, j : j + TILE].T
    count = heads_ref.shape[1] // 2
    for i in range(0, lanes, TILE):
        across = heads_ref[i : i + TILE, :].astype(jnp.float32).T
        term_ref[:, i : i + TILE] = across[count : count + 1] + across[count + 1 : count + 2]


def turned(qkv, heads, after):
    return pl.pallas_call(
        turn_kernel,
        in_specs=[whole(pl.ANY)] + [whole()] * 2,
        out_specs=[whole()] * 2,
        out_shape=[
            pltpu.VMEM(qkv.shape[::-1], qkv.dtype),
            jax.ShapeDtypeStruct((1, qkv.shape[0]), jnp.float32),
        ],
        cost_estimate=pl.CostEstimate(flops=5 * 10**9, bytes_accessed=0, transcendentals=0),
        compiler_params=kernel_params(),
    )(after, qkv, heads)


def block_sum_kernel(rows_ref, own_ref, term_ref, *refs):
    part_refs, block_ref = refs[:-1], refs[-1]
    columns = own_ref.shape[1]
    first = pl.multiple_of(lax.axis_index("seq") * columns, columns)
    mixed = part_refs[0][...].astype(jnp.float32)
    for part_ref in part_refs[1:]:
        mixed = mixed + part_ref[...].astype(jnp.float32)
    gate = rows_ref[2:3, pl.ds(first, columns)]
    block_ref[...] = (own_ref[...].astype(jnp.float32) + gate * mixed).astype(jnp.bfloat16)


def block_sum(mod_rows, own, term, parts):
    return pl.pallas_call(
        block_sum_kernel,
        in_specs=[whole()] * (3 + len(parts)),
        out_specs=whole(),
        out_shape=jax.ShapeDtypeStruct(own.shape, own.dtype),
        compiler_params=kernel_params(),
    )(mod_rows, own, term, *parts)


def scaled_piece(place, k, piece_ref, rows_ref):
    columns = piece_ref.shape[1]
    first = pl.multiple_of((place ^ k) * columns, columns)
    wide = piece_ref[...].astype(jnp.float32)
    scaled = (wide * rows_ref[1:2, pl.ds(first, columns)]).astype(jnp.bfloat16)
    return scaled, jnp.sum(wide * wide, axis=-1, keepdims=True)


def sums_kernel(numbers, rows_ref, turned_ref, *refs):
    count = len(numbers)
    piece_refs, earlier, (sums_ref, squares_ref) = refs[:count], refs[count:-2], refs[-2:]
    place = lax.axis_index("seq")
    columns = piece_refs[0].shape[1]
    squares = earlier[1][...] if earlier else 0.0
    scaled = []
    for k, piece_ref in zip(numbers, piece_refs):
        piece, square = scaled_piece(place, k, piece_ref, rows_ref)
        scaled.append((piece, pl.ds(pl.multiple_of((place ^ k) * columns, columns), columns)))
        squares = squares + square
    squares_ref[...] = squares
    for i in range(0, sums_ref.shape[1], PART):
        lane = slice(i, i + PART)
        total = earlier[0][:, lane] if earlier else 0.0
        for piece, part in scaled:
            total = total + jnp.dot(
                piece, turned_ref[part, lane], preferred_element_type=jnp.float32
            )
        sums_ref[:, lane] = total


def product_sums(numbers, pieces, mod_rows, qkv, earlier):
    rows = pieces[0].shape[0]
    lanes = qkv.shape[1]
    return pl.pallas_call(
        functools.partial(sums_kernel, numbers),
        in_specs=[whole()] * (2 + len(numbers) + len(earlier)),
        out_specs=[whole()] * 2,
        out_shape=[
            jax.ShapeDtypeStruct((rows, lanes), jnp.float32),
            jax.ShapeDtypeStruct((rows, 1), jnp.float32),
        ],
        compiler_params=kernel_params(),
    )(mod_rows, qkv, *pieces, *earlier)


def later_layer_kernel(
    count, last, order_ref, rows_ref, qkv_ref, out_ref, term_ref, stale_ref, sums_ref, squares_ref, *refs
):
    piece_refs, refs = refs[:count], refs[count:]
    block_refs, own_ref, sums, attended, keys, values, partial_out = refs[:count], *refs[count:]
    place = lax.axis_index("seq")
    scaled, squares = scaled_piece(place, count - 1, piece_refs[-1], rows_ref)
    norm = lax.rsqrt((squares_ref[...] + squares) / rows_ref.shape[1] + norm_eps)
    columns = piece_refs[-1].shape[1]
    part = pl.ds(pl.multiple_of((place ^ (count - 1)) * columns, columns), columns)
    for i in range(0, sums.shape[1], PART):
        lane = slice(i, i + PART)
        product = jnp.dot(scaled, qkv_ref[part, lane], preferred_element_type=jnp.float32)
        sums[:, lane] = (norm * (product + sums_ref[:, lane]) + term_ref[:1, lane]).astype(
            jnp.bfloat16
        )
    attend(sums, order_ref, stale_ref, attended, keys, values)
    if not last:
        column_blocks(place, attended, out_ref, block_refs)
        own_ref[...] = piece_refs[0][...]
        return
    partial_out[...] = jnp.dot(
        attended[...], out_ref[...], preferred_element_type=jnp.float32
    ).astype(jnp.bfloat16)
    rows_dev = own_ref.shape[0]
    columns = piece_refs[0].shape[1]
    own_rows = pl.ds(pl.multiple_of(place * rows_dev, rows_dev), rows_dev)
    for k in range(count):
        first = pl.multiple_of((place ^ k) * rows_dev, rows_dev)
        block_refs[k][...] = partial_out[pl.ds(first, rows_dev), :]
        first = pl.multiple_of((place ^ k) * columns, columns)
        own_ref[:, pl.ds(first, columns)] = piece_refs[k][own_rows, :]


def later_layer(last, patch_order, pieces, mod_rows, qkv, out, term, stale, sums, squares):
    count = len(pieces)
    rows, columns = pieces[0].shape
    lanes, depth = out.shape
    shape = (rows // count, depth) if last else (rows, columns)
    block = jax.ShapeDtypeStruct(shape, jnp.bfloat16)
    return pl.pallas_call(
        functools.partial(later_layer_kernel, count, last),
        in_specs=[whole(pltpu.SMEM)] + [whole()] * (7 + count),
        out_specs=[whole()] * (count + 1),
        out_shape=[block] * (count + 1),
        scratch_shapes=[
            pltpu.VMEM(sums.shape, jnp.bfloat16),
            *attention_scratch(rows, stale.shape[1], lanes),
            pltpu.VMEM((rows, depth), jnp.bfloat16),
        ],
        compiler_params=kernel_params(),
    )(patch_order, mod_rows, qkv, out, term, stale, sums, squares, *pieces)


def term_kernel(rows_ref, own_ref, final_ref, *refs):
    part_refs, term_ref = refs[:-1], refs[-1]
    mixed = part_refs[0][...].astype(jnp.float32)
    for part_ref in part_refs[1:]:
        mixed = mixed + part_ref[...].astype(jnp.float32)
    hidden = (own_ref[...].astype(jnp.float32) + rows_ref[2:3] * mixed).astype(jnp.bfloat16)
    predicted = lax.dot_general(
        hidden, final_ref[...], NT, preferred_element_type=jnp.float32
    )
    wide = hidden.astype(jnp.float32)
    norm = lax.rsqrt(jnp.mean(wide * wide, axis=-1, keepdims=True) + norm_eps)
    predicted = norm * predicted
    weight = jnp.where(lax.axis_index("cfg") == 0, 1.0 - guide_scale, guide_scale)
    patches = [predicted[i * TOK_DEV : (i + 1) * TOK_DEV] for i in range(MICRO)]
    term = weight * jnp.concatenate(patches, axis=1)
    term_ref[...] = jnp.broadcast_to(term, term_ref.shape)


def velocity_terms(peers, mod_rows, own, final, parts):
    shape = (peers, TOK_DEV, MICRO * final.shape[0])
    return pl.pallas_call(
        term_kernel,
        in_specs=[whole()] * (3 + len(parts)),
        out_specs=whole(),
        out_shape=jax.ShapeDtypeStruct(shape, jnp.float32),
        compiler_params=kernel_params(),
    )(mod_rows, own, final, *parts)


TAPS = 27
TAP_GROUP = 4
HALF = LAT_W // 2


def window_kernel(sizes, slab_ref, conv_ref, chosen_ref, weights_ref):
    seq_count, slab_most, token_rows = sizes
    place = lax.axis_index("seq")
    rows = seq_count * MICRO * TOK_DEV
    start = 0
    for j in range(seq_count - 1):
        start = start + jnp.where(j < place, slab_ref[j], 0)
    shape = (chosen_ref.shape[0], 2 * rows)
    target = lax.broadcasted_iota(jnp.int32, shape, 0)
    column = lax.broadcasted_iota(jnp.int32, shape, 1)
    across = target % HALF
    down = target // HALF % slab_most
    frame = target // (HALF * slab_most)
    kept = down < slab_ref[place]
    patch_rows = seq_count * TOK_DEV
    for tap in range(TAPS):
        time, row_shift, token_shift = tap // 9, tap // 3 % 3, tap % 3
        source_frame = jnp.maximum(frame + (time - 2), 0)
        row = start + down + (row_shift - 1)
        token = across + (token_shift - 1)
        inside = kept & (row >= 0) & (row < 2 * token_rows) & (token >= 0) & (token < HALF)
        row = jnp.maximum(row, 0)
        index = (source_frame * token_rows + row // 2) * HALF + jnp.maximum(token, 0)
        patch = index // patch_rows
        slot = index % patch_rows
        source = (slot // TOK_DEV * MICRO + patch) * TOK_DEV + slot % TOK_DEV + row % 2 * rows
        chosen_ref[:, tap * 2 * rows : (tap + 1) * 2 * rows] = jnp.where(
            inside & (column == source), 1.0, 0.0
        ).astype(jnp.bfloat16)
    chosen_ref[:, TAPS * 2 * rows :] = jnp.zeros(
        (shape[0], chosen_ref.shape[1] - TAPS * 2 * rows), jnp.bfloat16
    )
    weights_ref[...] = jnp.zeros_like(weights_ref)
    channels = conv_ref.shape[2]
    for tap in range(TAPS):
        for source in range(2):
            for side in range(2):
                shift = 2 * (tap % 3 - 1) + source - side + 1
                if 0 <= shift < 3:
                    first = (tap * 2 + source) * LAT_CH
                    weights_ref[first : first + LAT_CH, side * channels : (side + 1) * channels] = (
                        conv_ref[tap // 3 * 3 + shift]
                    )


def window_parts(seq_count, slab_most, token_rows, slab_rows, w_conv):
    rows = seq_count * MICRO * TOK_DEV
    groups = -(-TAPS // TAP_GROUP)
    return pl.pallas_call(
        functools.partial(window_kernel, (seq_count, slab_most, token_rows)),
        in_specs=[whole(pltpu.SMEM), whole()],
        out_specs=[whole()] * 2,
        out_shape=[
            jax.ShapeDtypeStruct(
                (FRAMES * slab_most * HALF, groups * TAP_GROUP * 2 * rows), jnp.bfloat16
            ),
            jax.ShapeDtypeStruct(
                (groups * TAP_GROUP * 2 * LAT_CH, 2 * w_conv.shape[2]), jnp.bfloat16
            ),
        ],
        compiler_params=kernel_params(),
    )(slab_rows, w_conv)


def decode_kernel(
    segment_count, count, terms_ref, chosen_ref, weights_ref, *refs
):
    latent_refs, refs = refs[:count], refs[count:]
    velocity_ref, decoded_ref, latents, tokens, halves, columns, features = refs
    place = lax.axis_index("seq")
    for k in range(count):
        latents[place ^ k] = latent_refs[k][...]

    def velocity_of(z):
        first = (z * segment_count + segment_count - 1) * 2
        both = terms_ref[first] + terms_ref[first + 1]
        width = both.shape[1] // MICRO
        return [both[:, i * width : (i + 1) * width] for i in range(MICRO)]

    for i, value in enumerate(velocity_of(place)):
        velocity_ref[i] = value
    for z in range(count):
        stepped = [
            latents[z, i] - value / SCHED_STEPS for i, value in enumerate(velocity_of(z))
        ]
        tokens[z * MICRO * TOK_DEV : (z + 1) * MICRO * TOK_DEV] = jnp.concatenate(
            stepped, axis=0
        ).astype(jnp.bfloat16)
    rows, width = tokens.shape
    half = width // 2
    halves[...] = jnp.zeros_like(halves)
    for j in range(TAP_GROUP):
        for side in range(2):
            first = (j * 2 + side) * rows
            halves[first : first + rows, j * half : (j + 1) * half] = tokens[
                :, side * half : (side + 1) * half
            ]
    depth, group_width = halves.shape
    for group in range(chosen_ref.shape[1] // depth):
        columns[:, group * group_width : (group + 1) * group_width] = jnp.dot(
            chosen_ref[:, group * depth : (group + 1) * depth],
            halves[...],
            preferred_element_type=jnp.float32,
        ).astype(jnp.bfloat16)
    result = jnp.dot(columns[...], weights_ref[...], preferred_element_type=jnp.float32)
    channels = features.shape[1]
    for side in range(2):
        features[pl.ds(side, result.shape[0], stride=2), :] = result[
            :, side * channels : (side + 1) * channels
        ]
    decoded_ref[...] = features[...].astype(jnp.bfloat16)


def decoded_slab(segment_count, terms, chosen, weights, latents):
    count = len(latents)
    rows = count * MICRO * TOK_DEV
    width = latents[0].shape[-1]
    targets = chosen.shape[0]
    channels = weights.shape[1] // 2
    return pl.pallas_call(
        functools.partial(decode_kernel, segment_count, count),
        in_specs=[whole()] * (3 + count),
        out_specs=[whole()] * 2,
        out_shape=[
            jax.ShapeDtypeStruct(latents[0].shape, jnp.float32),
            jax.ShapeDtypeStruct((2 * targets, channels), jnp.bfloat16),
        ],
        scratch_shapes=[
            pltpu.VMEM((count,) + latents[0].shape, jnp.float32),
            pltpu.VMEM((rows, width), jnp.bfloat16),
            pltpu.VMEM((TAP_GROUP * 2 * rows, TAP_GROUP * width // 2), jnp.bfloat16),
            pltpu.VMEM((targets, weights.shape[0]), jnp.bfloat16),
            pltpu.VMEM((2 * targets, channels), jnp.float32),
        ],
        compiler_params=kernel_params(),
    )(terms, chosen, weights, *latents)


def shards(
    latent,
    w_embed,
    w_qkv,
    w_out,
    mod_table,
    cond_mod,
    stale_kv,
    w_final,
    w_conv,
    patch_order,
    timestep,
    slab_rows,
):
    seq_count = lax.axis_size("seq")
    segment_count = lax.axis_size("segment")

    def within(k):
        return [(i, i ^ k) for i in range(seq_count)]

    def returned(values):
        far_first = [lax.ppermute(values[k], "seq", within(k)) for k in range(seq_count - 1, 0, -1)]
        return values[:1] + far_first[::-1]

    numbers = tuple(range(seq_count))
    half = (seq_count + 1) // 2
    latents = returned([staged(latent)] * seq_count)
    mod_rows, head_embed, out = prepared(
        timestep,
        jnp.transpose(mod_table, (1, 0, 2)),
        jnp.transpose(cond_mod[0], (1, 0, 2)),
        w_embed,
        w_qkv[0],
        w_out[0],
    )
    stale = stale_kv[0, 0, 0]
    *blocks, own = first_layer(
        patch_order, latents, w_embed, head_embed, stale, out
    )
    qkv, shift_term = turned(w_qkv[0], head_embed, own)
    for step in range(1, segment_count):
        block = block_sum(mod_rows, own, shift_term, returned(blocks))
        pieces = []
        for k in numbers[::-1]:
            pairs = [
                (i * segment_count + j, (i ^ k) * segment_count + (j + 1) % segment_count)
                for i in range(seq_count)
                for j in range(segment_count)
            ]
            pieces.insert(0, lax.ppermute(block, ("seq", "segment"), pairs))
        sums = ()
        for some in (numbers[:half], numbers[half:-1]):
            if some:
                sums = product_sums(
                    some,
                    [pieces[k] for k in some],
                    mod_rows,
                    qkv,
                    sums,
                )
        *blocks, own = later_layer(
            step + 1 == segment_count,
            patch_order,
            pieces,
            mod_rows,
            qkv,
            out,
            shift_term,
            stale,
            *sums,
        )

    blocks, slab_rows, w_conv = lax.optimization_barrier((blocks, slab_rows, w_conv))
    token_rows = MICRO * seq_count * TOK_DEV // (FRAMES * HALF)
    slab_most = 4 * token_rows // seq_count
    chosen, weights = window_parts(seq_count, slab_most, token_rows, slab_rows, w_conv)
    peers = ("seq", "segment", "cfg")
    peer_count = seq_count * segment_count * lax.axis_size("cfg")
    terms = velocity_terms(peer_count, mod_rows, own, w_final.T, returned(blocks))
    terms = lax.all_to_all(terms, peers, split_axis=0, concat_axis=0, tiled=True)
    velocity, decoded = decoded_slab(segment_count, terms, chosen, weights, latents)
    return (velocity, decoded.reshape(1, FRAMES, slab_most, LAT_W, w_conv.shape[2]))


def decoder_input(stepped, w_conv, slab_rows, seq_index, seq_count):
    token_rows = MICRO * seq_count * TOK_DEV // (FRAMES * (LAT_W // 2))
    image_rows = 2 * token_rows
    slab_most = 2 * image_rows // seq_count
    image = stepped.reshape(FRAMES, token_rows, LAT_W // 2, 2, 2, LAT_CH)
    image = (
        jnp.transpose(image, (0, 1, 3, 2, 4, 5))
        .reshape(FRAMES, image_rows, LAT_W, LAT_CH)
    )
    padded = jnp.concatenate([image[:1], image[:1], image], 0)
    padded = jnp.pad(padded, ((0, 0), (1, 1 + slab_most), (1, 1), (0, 0)))
    positions = jnp.arange(seq_count)
    slab_count = jnp.sum(jnp.where(positions == seq_index, slab_rows, 0))
    slab_start = jnp.sum(jnp.where(positions < seq_index, slab_rows, 0))
    window = lax.dynamic_slice_in_dim(padded, slab_start, slab_most + 2, 1)
    pieces = []
    for frame_shift in range(3):
        for row_shift in range(3):
            for col_shift in range(3):
                pieces.append(
                    window[
                        frame_shift : frame_shift + FRAMES,
                        row_shift : row_shift + slab_most,
                        col_shift : col_shift + LAT_W,
                    ]
                )
    columns = jnp.concatenate(pieces, -1).reshape(FRAMES * slab_most * LAT_W, 27 * LAT_CH)
    kernel = w_conv.reshape(27 * LAT_CH, w_conv.shape[2])
    features = jnp.dot(columns, kernel, preferred_element_type=jnp.float32).astype(jnp.bfloat16)
    features = features.reshape(FRAMES, slab_most, LAT_W, w_conv.shape[2])
    row_valid = jnp.arange(slab_most)[None, :, None, None] < slab_count
    decoded = jnp.where(row_valid, features, jnp.zeros_like(features))
    return decoded[None]


def solution(mesh):
    in_specs = (
        P(None, ("groups", "seq"), None),
        P(),
        P("segment", "seq", None),
        P("segment", "seq", None),
        P(),
        P("cfg", ("groups", "segment"), None, None),
        P("segment", "cfg", "seq", None, "groups", None),
        P(),
        P(None, None, ("segment", "cfg")),
        P("groups"),
        P("groups"),
        P("groups"),
    )
    out_specs = (
        P(None, ("groups", "seq"), None),
        P(("groups", "seq"), None, None, None, ("segment", "cfg")),
    )
    whole_groups = 2 <= mesh.shape["seq"] <= 8
    program = shards if whole_groups else cycled_shards
    return jax.shard_map(program, mesh=mesh, in_specs=in_specs, out_specs=out_specs, check_vma=False)
```

```python
import functools

import jax
import jax.numpy as jnp
from jax import lax
from jax.experimental import pallas as pl
from jax.experimental.pallas import tpu as pltpu
from jax.sharding import PartitionSpec as P

HEADS = 24
HEAD_DIM = 128
D = 3072
LAT_CH = 16
SCHED_STEPS = 50
MICRO = 2
TOK_DEV = 8
FRAMES = 4
LAT_W = 8


guide_scale = 5.0
norm_eps = 1e-06


def swapped(value, axis, bit):
    return lax.ppermute(value, axis, [(i, i ^ 1 << bit) for i in range(lax.axis_size(axis))])


def passed_along(value, axis, by):
    size = lax.axis_size(axis)
    pairs = [(i, i + by) for i in range(size) if 0 <= i + by < size]
    return lax.ppermute(value, axis, pairs)


def rms_scaled(values):
    wide = values.astype(jnp.float32)
    return wide * lax.rsqrt(jnp.mean(wide * wide, axis=-1, keepdims=True) + norm_eps)


def cycle_join(piece, seq_index, cycle_bits):
    joined = piece
    for bit_number in range(cycle_bits):
        partner = swapped(joined, "seq", bit_number)
        upper_half = (seq_index // 2**bit_number % 2).astype(jnp.int32)
        part_rows = joined.shape[0]
        combined = jnp.zeros((2 * part_rows,) + joined.shape[1:], joined.dtype)
        combined = lax.dynamic_update_slice_in_dim(combined, joined, upper_half * part_rows, 0)
        joined = lax.dynamic_update_slice_in_dim(combined, partner, (1 - upper_half) * part_rows, 0)
    return joined


def cycled_shards(
    latent,
    w_embed,
    w_qkv,
    w_out,
    mod_table,
    cond_mod,
    stale_kv,
    w_final,
    w_conv,
    patch_order,
    timestep,
    slab_rows,
):
    seq_count = lax.axis_size("seq")
    segment_count = lax.axis_size("segment")
    seq_index = lax.axis_index("seq")
    segment_index = lax.axis_index("segment")
    branch_index = lax.axis_index("cfg")
    group_count = min(seq_count, 8)
    cycle_size = seq_count // group_count
    cycle_bits = cycle_size.bit_length() - 1
    group_heads = HEADS // group_count
    sub_rows = TOK_DEV // cycle_size
    share_rows = seq_count * sub_rows
    kv_lanes = 2 * group_heads * HEAD_DIM
    table_row = lax.dynamic_index_in_dim(mod_table, timestep[0], 0, keepdims=False).astype(
        jnp.float32
    )
    modulation = table_row + cond_mod[0, 0]
    shift_row = modulation[0]
    scale_row = modulation[1]
    gate_row = modulation[2]
    joined_weights = (
        cycle_join(w_qkv[0], seq_index, cycle_bits),
        cycle_join(w_out[0], seq_index, cycle_bits),
    )
    stale_joined = cycle_join(stale_kv[0, 0], seq_index, cycle_bits)
    cache = jnp.transpose(stale_joined, (1, 0, 2, 3)).reshape(
        MICRO, cycle_size * share_rows, kv_lanes
    )
    received = jnp.zeros((TOK_DEV, D), jnp.bfloat16)
    finished = jnp.zeros((MICRO, TOK_DEV, D), jnp.bfloat16)
    slot_ids = jnp.arange(MICRO)
    tick_count = MICRO + segment_count - 1
    for tick_index in range(tick_count):
        qkv_rows, out_rows = joined_weights
        micro_index = tick_index - segment_index
        active = (micro_index >= 0) & (micro_index < MICRO)
        clipped = jnp.clip(micro_index, 0, MICRO - 1)
        patch_id = jnp.sum(jnp.where(slot_ids == clipped, patch_order, 0))
        own_latent = lax.dynamic_index_in_dim(latent, patch_id, 0, keepdims=False).astype(
            jnp.bfloat16
        )
        embedded = jnp.dot(own_latent, w_embed, preferred_element_type=jnp.float32).astype(
            jnp.bfloat16
        )
        layer_input = jnp.where(segment_index == 0, embedded, received)
        normed = (rms_scaled(layer_input) * (1.0 + scale_row) + shift_row).astype(jnp.bfloat16)
        outgoing = jnp.broadcast_to(
            normed.reshape(1, cycle_size, sub_rows, D), (group_count, cycle_size, sub_rows, D)
        )
        shared = lax.all_to_all(
            outgoing.reshape(share_rows, D), "seq", split_axis=0, concat_axis=0, tiled=True
        )
        projected = lax.dot_general(
            shared, qkv_rows, (((1,), (1,)), ((), ())), preferred_element_type=jnp.float32
        )
        projected = projected.astype(jnp.bfloat16).reshape(share_rows, group_heads, 3, HEAD_DIM)
        queries = projected[:, :, 0]
        fresh_local = jnp.transpose(projected[:, :, 1:], (0, 2, 1, 3)).reshape(
            1, share_rows, kv_lanes
        )
        fresh = cycle_join(fresh_local, seq_index, cycle_bits).reshape(
            cycle_size * share_rows, kv_lanes
        )
        previous = lax.dynamic_index_in_dim(cache, patch_id, 0, keepdims=False)
        cache = lax.dynamic_update_index_in_dim(
            cache, jnp.where(active, fresh, previous), patch_id, 0
        )
        keyvals = cache.reshape(MICRO * cycle_size * share_rows, 2, group_heads, HEAD_DIM)
        scores = jnp.einsum(
            "shd,khd->hsk", queries, keyvals[:, 0], preferred_element_type=jnp.float32
        ) * HEAD_DIM ** (-0.5)
        probs = jax.nn.softmax(scores, axis=-1).astype(jnp.bfloat16)
        attended = jnp.einsum(
            "hsk,khd->shd", probs, keyvals[:, 1], preferred_element_type=jnp.float32
        ).astype(jnp.bfloat16)
        partial_out = jnp.dot(
            attended.reshape(share_rows, group_heads * HEAD_DIM),
            out_rows,
            preferred_element_type=jnp.float32,
        )
        returned = lax.all_to_all(
            partial_out.astype(jnp.bfloat16), "seq", split_axis=0, concat_axis=0, tiled=True
        ).astype(partial_out.dtype)
        mixed = jnp.sum(returned.reshape(group_count, cycle_size, sub_rows, D), axis=0).reshape(
            TOK_DEV, D
        )
        layer_output = (layer_input.astype(jnp.float32) + gate_row * mixed).astype(jnp.bfloat16)
        keep_final = active & (segment_index == segment_count - 1)
        earlier = lax.dynamic_index_in_dim(finished, patch_id, 0, keepdims=False)
        finished = lax.dynamic_update_index_in_dim(
            finished, jnp.where(keep_final, layer_output, earlier), patch_id, 0
        )
        if tick_index + 1 < tick_count:
            received = passed_along(layer_output, "segment", 1)
    final_normed = rms_scaled(finished).astype(jnp.bfloat16)
    predicted = jnp.einsum("mtd,dc->mtc", final_normed, w_final, preferred_element_type=jnp.float32)
    is_last = segment_index == segment_count - 1
    branch_weight = jnp.where(branch_index == 0, 1.0 - guide_scale, guide_scale)
    velocity_term = jnp.where(is_last, branch_weight * predicted, 0.0)
    latent_term = jnp.where(is_last & (branch_index == 0), latent, 0.0)
    velocity_own, latent_own = lax.psum((velocity_term, latent_term), ("segment", "cfg"))
    velocity_full, latent_full = (
        lax.all_gather(velocity_own, "seq", axis=1, tiled=True),
        lax.all_gather(latent_own, "seq", axis=1, tiled=True),
    )
    stepped = (latent_full - velocity_full / SCHED_STEPS).astype(jnp.bfloat16)
    decoded = decoder_input(stepped, w_conv, slab_rows, seq_index, seq_count)
    return (velocity_own, decoded)


NT = (((1,), (1,)), ((), ()))
TILE = 256
PART = 768
AHEAD = 4


def kernel_params(mebibytes=8):
    return pltpu.CompilerParams(vmem_limit_bytes=mebibytes * 2**20)


def whole(space=pltpu.VMEM):
    return pl.BlockSpec(memory_space=space)


def in_order(copies, ahead):
    for copy in copies[:ahead]:
        copy.start()

    def landed():
        for i, copy in enumerate(copies):
            copy.wait()
            if i + ahead < len(copies):
                copies[i + ahead].start()
            yield i

    return landed()


def in_hbm(*values):
    return [pltpu.with_memory_space_constraint(value, pltpu.HBM) for value in values]


def stage_kernel(latent_hbm, staged_ref, sem):
    copy = pltpu.make_async_copy(latent_hbm, staged_ref, sem)
    copy.start()
    copy.wait()


def staged(latent):
    return pl.pallas_call(
        stage_kernel,
        in_specs=[whole(pltpu.HBM)],
        out_specs=whole(),
        out_shape=pltpu.VMEM(latent.shape, latent.dtype),
        scratch_shapes=[pltpu.SemaphoreType.DMA],
        cost_estimate=pl.CostEstimate(flops=10**10, bytes_accessed=0, transcendentals=0),
        compiler_params=kernel_params(),
    )(*in_hbm(latent))


def prepare_kernel(
    timestep_ref, table_ref, cond_ref, embed_ref, qkv_ref, out_hbm, rows_ref, heads_ref, out_ref, lhs, sem
):
    out_copy = pltpu.make_async_copy(out_hbm, out_ref, sem)
    out_copy.start()
    steps = table_ref.shape[1]
    chosen = lax.broadcasted_iota(jnp.int32, (16, steps), 1) == timestep_ref[0]
    chosen = jnp.where(chosen, 1.0, 0.0).astype(jnp.bfloat16)
    for j in range(3):
        row = jnp.dot(chosen, table_ref[j], preferred_element_type=jnp.float32)[:1]
        rows_ref[j : j + 1, :] = row + cond_ref[j] + (1.0 if j == 1 else 0.0)
    count = embed_ref.shape[0]
    spare, depth = lhs.shape[0] - count, lhs.shape[1]
    lhs[:count] = (embed_ref[...].astype(jnp.float32) * rows_ref[1:2]).astype(jnp.bfloat16)
    lhs[count:] = jnp.broadcast_to(rows_ref[0:1], (spare, depth)).astype(jnp.bfloat16)
    lane = lax.broadcasted_iota(jnp.int32, (PART, lhs.shape[0]), 1)
    for j in range(0, qkv_ref.shape[0], PART):
        product = lax.dot_general(
            qkv_ref[j : j + PART, :], lhs[...], NT, preferred_element_type=jnp.float32
        )
        upper = product.astype(jnp.bfloat16).astype(jnp.float32)
        value = jnp.where(lane == count + 1, product - upper, upper)
        heads_ref[j : j + PART, :] = jnp.where(lane <= count + 2, value, 0.0).astype(jnp.bfloat16)
    out_copy.wait()


def prepared(timestep, table, cond, w_embed, qkv, out):
    count, depth = w_embed.shape
    lanes = qkv.shape[0]
    return pl.pallas_call(
        prepare_kernel,
        in_specs=[whole(pltpu.SMEM)] + [whole()] * 4 + [whole(pltpu.HBM)],
        out_specs=[whole()] * 3,
        out_shape=[
            jax.ShapeDtypeStruct((3, depth), jnp.float32),
            jax.ShapeDtypeStruct((lanes, 2 * count), jnp.bfloat16),
            pltpu.VMEM(out.shape, out.dtype),
        ],
        scratch_shapes=[
            pltpu.VMEM((2 * count, depth), jnp.bfloat16),
            pltpu.SemaphoreType.DMA,
        ],
        compiler_params=kernel_params(),
    )(timestep, table, cond, w_embed, qkv, *in_hbm(out))


def span_of(rows, patch_rows):
    return -(-(rows + patch_rows) // 128) * 128


def attention_scratch(rows, patch_rows, lanes):
    shape = (lanes // HEAD_DIM, span_of(rows, patch_rows), HEAD_DIM)
    return [pltpu.VMEM((rows, lanes), jnp.bfloat16)] + [pltpu.VMEM(shape, jnp.bfloat16)] * 2


def attend(projected, order_ref, stale_ref, attended, keys, values):
    rows = projected.shape[0]
    patch_rows = stale_ref.shape[1]
    heads, span, _ = keys.shape
    kept = order_ref[1]
    filled = rows + patch_rows

    def micro_of(index):
        return jnp.where(index // TOK_DEV % MICRO == kept, 1, 0)

    query = micro_of(lax.broadcasted_iota(jnp.int32, (rows, span), 0))
    column = lax.broadcasted_iota(jnp.int32, (rows, span), 1)
    fresh_seen = (column < rows) & (query >= micro_of(column))
    stale_seen = (column >= rows) & (column < filled) & (query == 0)
    seen = fresh_seen | stale_seen
    scores = []
    for head in range(heads):
        first = 3 * HEAD_DIM * head
        for j, buffer in enumerate((keys, values)):
            lane = first + (j + 1) * HEAD_DIM
            stale_lane = (j * heads + head) * HEAD_DIM
            buffer[head, :rows] = projected[:, lane : lane + HEAD_DIM]
            buffer[head, rows:filled] = stale_ref[kept, :, stale_lane : stale_lane + HEAD_DIM]
            if filled < span:
                buffer[head, filled:] = jnp.zeros((span - filled, HEAD_DIM), jnp.bfloat16)
        queries = projected[:, first : first + HEAD_DIM]
        scores.append(
            lax.dot_general(queries, keys[head], NT, preferred_element_type=jnp.float32)
        )
    scores = [jnp.where(seen, score * HEAD_DIM ** (-0.5), -jnp.inf) for score in scores]
    tops = [jnp.max(score, axis=-1, keepdims=True) for score in scores]
    weights = [jnp.exp(score - top) for score, top in zip(scores, tops)]
    totals = [jnp.sum(weight, axis=-1, keepdims=True) for weight in weights]
    for head in range(heads):
        probs = (weights[head] / totals[head]).astype(jnp.bfloat16)
        attended[:, head * HEAD_DIM : (head + 1) * HEAD_DIM] = jnp.dot(
            probs, values[head], preferred_element_type=jnp.float32
        ).astype(jnp.bfloat16)


def column_blocks(place, attended, out_ref, block_refs):
    count = len(block_refs)
    columns = out_ref.shape[1] // count
    for k in range(count):
        first = pl.multiple_of((place ^ k) * columns, columns)
        block_refs[k][...] = jnp.dot(
            attended[...], out_ref[:, pl.ds(first, columns)], preferred_element_type=jnp.float32
        ).astype(jnp.bfloat16)


def first_layer_kernel(
    count, order_ref, embed_ref, heads_ref, stale_ref, out_ref, near_ref, *refs
):
    latent_refs, refs = refs[:count], refs[count:]
    block_refs, (own_ref, latents, attended, keys, values) = refs[:count], refs[count:]
    place = lax.axis_index("seq")
    rows_dev = MICRO * TOK_DEV
    width = embed_ref.shape[0]
    for k in range(count):
        first = pl.multiple_of((place ^ k) * rows_dev, rows_dev)
        latents[pl.ds(first, rows_dev), :width] = (
            latent_refs[k][...].reshape(rows_dev, width).astype(jnp.bfloat16)
        )
    embedded = jnp.dot(latents[:, :width], embed_ref[...], preferred_element_type=jnp.float32)
    embedded = embedded.astype(jnp.bfloat16).astype(jnp.float32)
    square = jnp.mean(embedded * embedded, axis=-1, keepdims=True) + norm_eps
    norm = lax.rsqrt(square)
    size = square * norm
    upper = size.astype(jnp.bfloat16).astype(jnp.float32)
    lane = lax.broadcasted_iota(jnp.int32, (latents.shape[0], width), 1)
    spare = jnp.where(lane < 2, upper, jnp.where(lane == 2, size - upper, 0.0))
    latents[:, width:] = spare.astype(jnp.bfloat16)
    projected = lax.dot_general(
        latents[...], heads_ref[...], NT, preferred_element_type=jnp.float32
    )
    projected = (norm * projected).astype(jnp.bfloat16)
    attend(projected, order_ref, stale_ref, attended, keys, values)
    columns = own_ref.shape[1]
    first = pl.multiple_of(place * columns, columns)
    own_ref[...] = jnp.dot(
        latents[:, :width], embed_ref[:, pl.ds(first, columns)], preferred_element_type=jnp.float32
    ).astype(jnp.bfloat16)
    column_blocks(place, attended, out_ref, block_refs)


def first_layer(patch_order, latents, w_embed, heads, stale, out):
    count = len(latents)
    rows = count * MICRO * TOK_DEV
    lanes, depth = out.shape
    block = jax.ShapeDtypeStruct((rows, depth // count), jnp.bfloat16)
    return pl.pallas_call(
        functools.partial(first_layer_kernel, count),
        in_specs=[whole(pltpu.SMEM)] + [whole()] * (5 + count),
        out_specs=[whole()] * (count + 1),
        out_shape=[block] * (count + 1),
        scratch_shapes=[
            pltpu.VMEM((rows, 2 * w_embed.shape[0]), jnp.bfloat16),
            *attention_scratch(rows, stale.shape[1], lanes),
        ],
        compiler_params=kernel_params(),
    )(patch_order, w_embed, heads, stale, out, met(latents[1:2]), *latents)


def turn_kernel(after_ref, qkv_ref, heads_ref, turned_ref, term_ref):
    lanes, depth = qkv_ref.shape
    for i in range(0, lanes, TILE):
        for j in range(0, depth, TILE):
            turned_ref[j : j + TILE, i : i + TILE] = qkv_ref[i : i + TILE, j : j + TILE].T
    count = heads_ref.shape[1] // 2
    for i in range(0, lanes, TILE):
        across = heads_ref[i : i + TILE, :].astype(jnp.float32).T
        term_ref[:, i : i + TILE] = across[count : count + 1] + across[count + 1 : count + 2]


def turned(qkv, heads, after):
    return pl.pallas_call(
        turn_kernel,
        in_specs=[whole(pl.ANY)] + [whole()] * 2,
        out_specs=[whole()] * 2,
        out_shape=[
            pltpu.VMEM(qkv.shape[::-1], qkv.dtype),
            jax.ShapeDtypeStruct((1, qkv.shape[0]), jnp.float32),
        ],
        cost_estimate=pl.CostEstimate(flops=5 * 10**9, bytes_accessed=0, transcendentals=0),
        compiler_params=kernel_params(),
    )(after, qkv, heads)


def meet_kernel(*refs):
    refs[-1][...] = jnp.zeros_like(refs[-1])


def met(values):
    return pl.pallas_call(
        meet_kernel,
        in_specs=[whole(pl.ANY)] * len(values),
        out_specs=whole(),
        out_shape=jax.ShapeDtypeStruct((8, 128), jnp.float32),
        compiler_params=kernel_params(),
    )(*values)


def block_sum_kernel(rows_ref, own_ref, term_ref, *refs):
    part_refs, block_ref = refs[:-1], refs[-1]
    columns = own_ref.shape[1]
    first = pl.multiple_of(lax.axis_index("seq") * columns, columns)
    mixed = part_refs[0][...].astype(jnp.float32)
    for part_ref in part_refs[1:]:
        mixed = mixed + part_ref[...].astype(jnp.float32)
    gate = rows_ref[2:3, pl.ds(first, columns)]
    block_ref[...] = (own_ref[...].astype(jnp.float32) + gate * mixed).astype(jnp.bfloat16)


def block_sum(mod_rows, own, term, parts):
    return pl.pallas_call(
        block_sum_kernel,
        in_specs=[whole()] * (3 + len(parts)),
        out_specs=whole(),
        out_shape=jax.ShapeDtypeStruct(own.shape, own.dtype),
        compiler_params=kernel_params(),
    )(mod_rows, own, term, *parts)


def scaled_piece(place, k, piece_ref, rows_ref):
    columns = piece_ref.shape[1]
    first = pl.multiple_of((place ^ k) * columns, columns)
    wide = piece_ref[...].astype(jnp.float32)
    scaled = (wide * rows_ref[1:2, pl.ds(first, columns)]).astype(jnp.bfloat16)
    return scaled, jnp.sum(wide * wide, axis=-1, keepdims=True)


def sums_kernel(numbers, rows_ref, turned_ref, *refs):
    count = len(numbers)
    piece_refs, earlier, (sums_ref, squares_ref) = refs[:count], refs[count:-2], refs[-2:]
    place = lax.axis_index("seq")
    columns = piece_refs[0].shape[1]
    squares = earlier[1][...] if earlier else 0.0
    scaled = []
    for k, piece_ref in zip(numbers, piece_refs):
        piece, square = scaled_piece(place, k, piece_ref, rows_ref)
        scaled.append((piece, pl.ds(pl.multiple_of((place ^ k) * columns, columns), columns)))
        squares = squares + square
    squares_ref[...] = squares
    for i in range(0, sums_ref.shape[1], PART):
        lane = slice(i, i + PART)
        total = earlier[0][:, lane] if earlier else 0.0
        for piece, part in scaled:
            total = total + jnp.dot(
                piece, turned_ref[part, lane], preferred_element_type=jnp.float32
            )
        sums_ref[:, lane] = total


def product_sums(numbers, pieces, mod_rows, qkv, earlier):
    rows = pieces[0].shape[0]
    lanes = qkv.shape[1]
    return pl.pallas_call(
        functools.partial(sums_kernel, numbers),
        in_specs=[whole()] * (2 + len(numbers) + len(earlier)),
        out_specs=[whole()] * 2,
        out_shape=[
            jax.ShapeDtypeStruct((rows, lanes), jnp.float32),
            jax.ShapeDtypeStruct((rows, 1), jnp.float32),
        ],
        compiler_params=kernel_params(),
    )(mod_rows, qkv, *pieces, *earlier)


def later_layer_kernel(
    count, last, order_ref, rows_ref, qkv_ref, out_ref, term_ref, stale_ref, sums_ref, squares_ref, *refs
):
    piece_refs, refs = refs[:count], refs[count:]
    block_refs, own_ref, sums, attended, keys, values, partial_out = refs[:count], *refs[count:]
    place = lax.axis_index("seq")
    scaled, squares = scaled_piece(place, count - 1, piece_refs[-1], rows_ref)
    norm = lax.rsqrt((squares_ref[...] + squares) / rows_ref.shape[1] + norm_eps)
    columns = piece_refs[-1].shape[1]
    part = pl.ds(pl.multiple_of((place ^ (count - 1)) * columns, columns), columns)
    for i in range(0, sums.shape[1], PART):
        lane = slice(i, i + PART)
        product = jnp.dot(scaled, qkv_ref[part, lane], preferred_element_type=jnp.float32)
        sums[:, lane] = (norm * (product + sums_ref[:, lane]) + term_ref[:1, lane]).astype(
            jnp.bfloat16
        )
    attend(sums, order_ref, stale_ref, attended, keys, values)
    if not last:
        column_blocks(place, attended, out_ref, block_refs)
        own_ref[...] = piece_refs[0][...]
        return
    partial_out[...] = jnp.dot(
        attended[...], out_ref[...], preferred_element_type=jnp.float32
    ).astype(jnp.bfloat16)
    rows_dev = own_ref.shape[0]
    columns = piece_refs[0].shape[1]
    own_rows = pl.ds(pl.multiple_of(place * rows_dev, rows_dev), rows_dev)
    for k in range(count):
        first = pl.multiple_of((place ^ k) * rows_dev, rows_dev)
        block_refs[k][...] = partial_out[pl.ds(first, rows_dev), :]
        first = pl.multiple_of((place ^ k) * columns, columns)
        own_ref[:, pl.ds(first, columns)] = piece_refs[k][own_rows, :]


def later_layer(last, patch_order, pieces, mod_rows, qkv, out, term, stale, sums, squares):
    count = len(pieces)
    rows, columns = pieces[0].shape
    lanes, depth = out.shape
    shape = (rows // count, depth) if last else (rows, columns)
    block = jax.ShapeDtypeStruct(shape, jnp.bfloat16)
    return pl.pallas_call(
        functools.partial(later_layer_kernel, count, last),
        in_specs=[whole(pltpu.SMEM)] + [whole()] * (7 + count),
        out_specs=[whole()] * (count + 1),
        out_shape=[block] * (count + 1),
        scratch_shapes=[
            pltpu.VMEM(sums.shape, jnp.bfloat16),
            *attention_scratch(rows, stale.shape[1], lanes),
            pltpu.VMEM((rows, depth), jnp.bfloat16),
        ],
        compiler_params=kernel_params(),
    )(patch_order, mod_rows, qkv, out, term, stale, sums, squares, *pieces)


def term_kernel(rows_ref, own_ref, final_ref, far_ref, *refs):
    part_refs, term_ref = refs[:-1], refs[-1]
    mixed = part_refs[0][...].astype(jnp.float32)
    for part_ref in part_refs[1:]:
        mixed = mixed + part_ref[...].astype(jnp.float32)
    hidden = (own_ref[...].astype(jnp.float32) + rows_ref[2:3] * mixed).astype(jnp.bfloat16)
    predicted = lax.dot_general(
        hidden, final_ref[...], NT, preferred_element_type=jnp.float32
    )
    wide = hidden.astype(jnp.float32)
    norm = lax.rsqrt(jnp.mean(wide * wide, axis=-1, keepdims=True) + norm_eps)
    predicted = norm * predicted
    weight = jnp.where(lax.axis_index("cfg") == 0, 1.0 - guide_scale, guide_scale)
    patches = [predicted[i * TOK_DEV : (i + 1) * TOK_DEV] for i in range(MICRO)]
    term = weight * jnp.concatenate(patches, axis=1)
    term_ref[...] = jnp.broadcast_to(term, term_ref.shape)


def velocity_terms(peers, mod_rows, own, final, parts):
    shape = (peers, TOK_DEV, MICRO * final.shape[0])
    return pl.pallas_call(
        term_kernel,
        in_specs=[whole()] * (4 + len(parts)),
        out_specs=whole(),
        out_shape=jax.ShapeDtypeStruct(shape, jnp.float32),
        compiler_params=kernel_params(),
    )(mod_rows, own, final, met(parts[2:]), *parts)


TAPS = 27
TAP_GROUP = 4
HALF = LAT_W // 2


def window_kernel(sizes, slab_ref, conv_ref, chosen_ref, weights_ref):
    seq_count, slab_most, token_rows = sizes
    place = lax.axis_index("seq")
    rows = seq_count * MICRO * TOK_DEV
    start = 0
    for j in range(seq_count - 1):
        start = start + jnp.where(j < place, slab_ref[j], 0)
    shape = (chosen_ref.shape[0], 2 * rows)
    target = lax.broadcasted_iota(jnp.int32, shape, 0)
    column = lax.broadcasted_iota(jnp.int32, shape, 1)
    across = target % HALF
    down = target // HALF % slab_most
    frame = target // (HALF * slab_most)
    kept = down < slab_ref[place]
    patch_rows = seq_count * TOK_DEV
    for tap in range(TAPS):
        time, row_shift, token_shift = tap // 9, tap // 3 % 3, tap % 3
        source_frame = jnp.maximum(frame + (time - 2), 0)
        row = start + down + (row_shift - 1)
        token = across + (token_shift - 1)
        inside = kept & (row >= 0) & (row < 2 * token_rows) & (token >= 0) & (token < HALF)
        row = jnp.maximum(row, 0)
        index = (source_frame * token_rows + row // 2) * HALF + jnp.maximum(token, 0)
        patch = index // patch_rows
        slot = index % patch_rows
        source = (slot // TOK_DEV * MICRO + patch) * TOK_DEV + slot % TOK_DEV + row % 2 * rows
        chosen_ref[:, tap * 2 * rows : (tap + 1) * 2 * rows] = jnp.where(
            inside & (column == source), 1.0, 0.0
        ).astype(jnp.bfloat16)
    chosen_ref[:, TAPS * 2 * rows :] = jnp.zeros(
        (shape[0], chosen_ref.shape[1] - TAPS * 2 * rows), jnp.bfloat16
    )
    weights_ref[...] = jnp.zeros_like(weights_ref)
    channels = conv_ref.shape[2]
    for tap in range(TAPS):
        for source in range(2):
            for side in range(2):
                shift = 2 * (tap % 3 - 1) + source - side + 1
                if 0 <= shift < 3:
                    first = (tap * 2 + source) * LAT_CH
                    weights_ref[first : first + LAT_CH, side * channels : (side + 1) * channels] = (
                        conv_ref[tap // 3 * 3 + shift]
                    )


def window_parts(seq_count, slab_most, token_rows, slab_rows, w_conv):
    rows = seq_count * MICRO * TOK_DEV
    groups = -(-TAPS // TAP_GROUP)
    return pl.pallas_call(
        functools.partial(window_kernel, (seq_count, slab_most, token_rows)),
        in_specs=[whole(pltpu.SMEM), whole()],
        out_specs=[whole()] * 2,
        out_shape=[
            jax.ShapeDtypeStruct(
                (FRAMES * slab_most * HALF, groups * TAP_GROUP * 2 * rows), jnp.bfloat16
            ),
            jax.ShapeDtypeStruct(
                (groups * TAP_GROUP * 2 * LAT_CH, 2 * w_conv.shape[2]), jnp.bfloat16
            ),
        ],
        compiler_params=kernel_params(),
    )(slab_rows, w_conv)


def decode_kernel(
    segment_count, count, terms_ref, chosen_ref, weights_ref, *refs
):
    latent_refs, refs = refs[:count], refs[count:]
    velocity_ref, decoded_ref, latents, tokens, halves, columns, features = refs
    place = lax.axis_index("seq")
    for k in range(count):
        latents[place ^ k] = latent_refs[k][...]

    def velocity_of(z):
        first = (z * segment_count + segment_count - 1) * 2
        both = terms_ref[first] + terms_ref[first + 1]
        width = both.shape[1] // MICRO
        return [both[:, i * width : (i + 1) * width] for i in range(MICRO)]

    for i, value in enumerate(velocity_of(place)):
        velocity_ref[i] = value
    for z in range(count):
        stepped = [
            latents[z, i] - value / SCHED_STEPS for i, value in enumerate(velocity_of(z))
        ]
        tokens[z * MICRO * TOK_DEV : (z + 1) * MICRO * TOK_DEV] = jnp.concatenate(
            stepped, axis=0
        ).astype(jnp.bfloat16)
    rows, width = tokens.shape
    half = width // 2
    halves[...] = jnp.zeros_like(halves)
    for j in range(TAP_GROUP):
        for side in range(2):
            first = (j * 2 + side) * rows
            halves[first : first + rows, j * half : (j + 1) * half] = tokens[
                :, side * half : (side + 1) * half
            ]
    depth, group_width = halves.shape
    for group in range(chosen_ref.shape[1] // depth):
        columns[:, group * group_width : (group + 1) * group_width] = jnp.dot(
            chosen_ref[:, group * depth : (group + 1) * depth],
            halves[...],
            preferred_element_type=jnp.float32,
        ).astype(jnp.bfloat16)
    result = jnp.dot(columns[...], weights_ref[...], preferred_element_type=jnp.float32)
    channels = features.shape[1]
    for side in range(2):
        features[pl.ds(side, result.shape[0], stride=2), :] = result[
            :, side * channels : (side + 1) * channels
        ]
    decoded_ref[...] = features[...].astype(jnp.bfloat16)


def decoded_slab(segment_count, terms, chosen, weights, latents):
    count = len(latents)
    rows = count * MICRO * TOK_DEV
    width = latents[0].shape[-1]
    targets = chosen.shape[0]
    channels = weights.shape[1] // 2
    return pl.pallas_call(
        functools.partial(decode_kernel, segment_count, count),
        in_specs=[whole()] * (3 + count),
        out_specs=[whole()] * 2,
        out_shape=[
            jax.ShapeDtypeStruct(latents[0].shape, jnp.float32),
            jax.ShapeDtypeStruct((2 * targets, channels), jnp.bfloat16),
        ],
        scratch_shapes=[
            pltpu.VMEM((count,) + latents[0].shape, jnp.float32),
            pltpu.VMEM((rows, width), jnp.bfloat16),
            pltpu.VMEM((TAP_GROUP * 2 * rows, TAP_GROUP * width // 2), jnp.bfloat16),
            pltpu.VMEM((targets, weights.shape[0]), jnp.bfloat16),
            pltpu.VMEM((2 * targets, channels), jnp.float32),
        ],
        compiler_params=kernel_params(),
    )(terms, chosen, weights, *latents)


def shards(
    latent,
    w_embed,
    w_qkv,
    w_out,
    mod_table,
    cond_mod,
    stale_kv,
    w_final,
    w_conv,
    patch_order,
    timestep,
    slab_rows,
):
    seq_count = lax.axis_size("seq")
    segment_count = lax.axis_size("segment")

    def within(k):
        return [(i, i ^ k) for i in range(seq_count)]

    def returned(values):
        far_first = [lax.ppermute(values[k], "seq", within(k)) for k in range(seq_count - 1, 0, -1)]
        return values[:1] + far_first[::-1]

    numbers = tuple(range(seq_count))
    half = (seq_count + 1) // 2
    latents = returned([staged(latent)] * seq_count)
    mod_rows, head_embed, out = prepared(
        timestep,
        jnp.transpose(mod_table, (1, 0, 2)),
        jnp.transpose(cond_mod[0], (1, 0, 2)),
        w_embed,
        w_qkv[0],
        w_out[0],
    )
    stale = stale_kv[0, 0, 0]
    *blocks, own = first_layer(
        patch_order, latents, w_embed, head_embed, stale, out
    )
    qkv, shift_term = turned(w_qkv[0], head_embed, own)
    for step in range(1, segment_count):
        block = block_sum(mod_rows, own, shift_term, returned(blocks))
        pieces = []
        for k in numbers[::-1]:
            pairs = [
                (i * segment_count + j, (i ^ k) * segment_count + (j + 1) % segment_count)
                for i in range(seq_count)
                for j in range(segment_count)
            ]
            pieces.insert(0, lax.ppermute(block, ("seq", "segment"), pairs))
        sums = ()
        for some in (numbers[:half], numbers[half:-1]):
            if some:
                sums = product_sums(
                    some,
                    [pieces[k] for k in some],
                    mod_rows,
                    qkv,
                    sums,
                )
        *blocks, own = later_layer(
            step + 1 == segment_count,
            patch_order,
            pieces,
            mod_rows,
            qkv,
            out,
            shift_term,
            stale,
            *sums,
        )

    blocks, slab_rows, w_conv = lax.optimization_barrier((blocks, slab_rows, w_conv))
    token_rows = MICRO * seq_count * TOK_DEV // (FRAMES * HALF)
    slab_most = 4 * token_rows // seq_count
    chosen, weights = window_parts(seq_count, slab_most, token_rows, slab_rows, w_conv)
    peers = ("seq", "segment", "cfg")
    peer_count = seq_count * segment_count * lax.axis_size("cfg")
    terms = velocity_terms(peer_count, mod_rows, own, w_final.T, returned(blocks))
    terms = lax.all_to_all(terms, peers, split_axis=0, concat_axis=0, tiled=True)
    velocity, decoded = decoded_slab(segment_count, terms, chosen, weights, latents)
    return (velocity, decoded.reshape(1, FRAMES, slab_most, LAT_W, w_conv.shape[2]))


def decoder_input(stepped, w_conv, slab_rows, seq_index, seq_count):
    token_rows = MICRO * seq_count * TOK_DEV // (FRAMES * (LAT_W // 2))
    image_rows = 2 * token_rows
    slab_most = 2 * image_rows // seq_count
    image = stepped.reshape(FRAMES, token_rows, LAT_W // 2, 2, 2, LAT_CH)
    image = (
        jnp.transpose(image, (0, 1, 3, 2, 4, 5))
        .reshape(FRAMES, image_rows, LAT_W, LAT_CH)
    )
    padded = jnp.concatenate([image[:1], image[:1], image], 0)
    padded = jnp.pad(padded, ((0, 0), (1, 1 + slab_most), (1, 1), (0, 0)))
    positions = jnp.arange(seq_count)
    slab_count = jnp.sum(jnp.where(positions == seq_index, slab_rows, 0))
    slab_start = jnp.sum(jnp.where(positions < seq_index, slab_rows, 0))
    window = lax.dynamic_slice_in_dim(padded, slab_start, slab_most + 2, 1)
    pieces = []
    for frame_shift in range(3):
        for row_shift in range(3):
            for col_shift in range(3):
                pieces.append(
                    window[
                        frame_shift : frame_shift + FRAMES,
                        row_shift : row_shift + slab_most,
                        col_shift : col_shift + LAT_W,
                    ]
                )
    columns = jnp.concatenate(pieces, -1).reshape(FRAMES * slab_most * LAT_W, 27 * LAT_CH)
    kernel = w_conv.reshape(27 * LAT_CH, w_conv.shape[2])
    features = jnp.dot(columns, kernel, preferred_element_type=jnp.float32).astype(jnp.bfloat16)
    features = features.reshape(FRAMES, slab_most, LAT_W, w_conv.shape[2])
    row_valid = jnp.arange(slab_most)[None, :, None, None] < slab_count
    decoded = jnp.where(row_valid, features, jnp.zeros_like(features))
    return decoded[None]


def solution(mesh):
    in_specs = (
        P(None, ("groups", "seq"), None),
        P(),
        P("segment", "seq", None),
        P("segment", "seq", None),
        P(),
        P("cfg", ("groups", "segment"), None, None),
        P("segment", "cfg", "seq", None, "groups", None),
        P(),
        P(None, None, ("segment", "cfg")),
        P("groups"),
        P("groups"),
        P("groups"),
    )
    out_specs = (
        P(None, ("groups", "seq"), None),
        P(("groups", "seq"), None, None, None, ("segment", "cfg")),
    )
    whole_groups = 2 <= mesh.shape["seq"] <= 8
    program = shards if whole_groups else cycled_shards
    return jax.shard_map(program, mesh=mesh, in_specs=in_specs, out_specs=out_specs, check_vma=False)
```

```python
import functools

import jax
import jax.numpy as jnp
from jax import lax
from jax.experimental import pallas as pl
from jax.experimental.pallas import tpu as pltpu
from jax.sharding import PartitionSpec as P

HEADS = 24
HEAD_DIM = 128
D = 3072
LAT_CH = 16
SCHED_STEPS = 50
MICRO = 2
TOK_DEV = 8
FRAMES = 4
LAT_W = 8


guide_scale = 5.0
norm_eps = 1e-06


def swapped(value, axis, bit):
    return lax.ppermute(value, axis, [(i, i ^ 1 << bit) for i in range(lax.axis_size(axis))])


def passed_along(value, axis, by):
    size = lax.axis_size(axis)
    pairs = [(i, i + by) for i in range(size) if 0 <= i + by < size]
    return lax.ppermute(value, axis, pairs)


def rms_scaled(values):
    wide = values.astype(jnp.float32)
    return wide * lax.rsqrt(jnp.mean(wide * wide, axis=-1, keepdims=True) + norm_eps)


def cycle_join(piece, seq_index, cycle_bits):
    joined = piece
    for bit_number in range(cycle_bits):
        partner = swapped(joined, "seq", bit_number)
        upper_half = (seq_index // 2**bit_number % 2).astype(jnp.int32)
        part_rows = joined.shape[0]
        combined = jnp.zeros((2 * part_rows,) + joined.shape[1:], joined.dtype)
        combined = lax.dynamic_update_slice_in_dim(combined, joined, upper_half * part_rows, 0)
        joined = lax.dynamic_update_slice_in_dim(combined, partner, (1 - upper_half) * part_rows, 0)
    return joined


def cycled_shards(
    latent,
    w_embed,
    w_qkv,
    w_out,
    mod_table,
    cond_mod,
    stale_kv,
    w_final,
    w_conv,
    patch_order,
    timestep,
    slab_rows,
):
    seq_count = lax.axis_size("seq")
    segment_count = lax.axis_size("segment")
    seq_index = lax.axis_index("seq")
    segment_index = lax.axis_index("segment")
    branch_index = lax.axis_index("cfg")
    group_count = min(seq_count, 8)
    cycle_size = seq_count // group_count
    cycle_bits = cycle_size.bit_length() - 1
    group_heads = HEADS // group_count
    sub_rows = TOK_DEV // cycle_size
    share_rows = seq_count * sub_rows
    kv_lanes = 2 * group_heads * HEAD_DIM
    table_row = lax.dynamic_index_in_dim(mod_table, timestep[0], 0, keepdims=False).astype(
        jnp.float32
    )
    modulation = table_row + cond_mod[0, 0]
    shift_row = modulation[0]
    scale_row = modulation[1]
    gate_row = modulation[2]
    joined_weights = (
        cycle_join(w_qkv[0], seq_index, cycle_bits),
        cycle_join(w_out[0], seq_index, cycle_bits),
    )
    stale_joined = cycle_join(stale_kv[0, 0], seq_index, cycle_bits)
    cache = jnp.transpose(stale_joined, (1, 0, 2, 3)).reshape(
        MICRO, cycle_size * share_rows, kv_lanes
    )
    received = jnp.zeros((TOK_DEV, D), jnp.bfloat16)
    finished = jnp.zeros((MICRO, TOK_DEV, D), jnp.bfloat16)
    slot_ids = jnp.arange(MICRO)
    tick_count = MICRO + segment_count - 1
    for tick_index in range(tick_count):
        qkv_rows, out_rows = joined_weights
        micro_index = tick_index - segment_index
        active = (micro_index >= 0) & (micro_index < MICRO)
        clipped = jnp.clip(micro_index, 0, MICRO - 1)
        patch_id = jnp.sum(jnp.where(slot_ids == clipped, patch_order, 0))
        own_latent = lax.dynamic_index_in_dim(latent, patch_id, 0, keepdims=False).astype(
            jnp.bfloat16
        )
        embedded = jnp.dot(own_latent, w_embed, preferred_element_type=jnp.float32).astype(
            jnp.bfloat16
        )
        layer_input = jnp.where(segment_index == 0, embedded, received)
        normed = (rms_scaled(layer_input) * (1.0 + scale_row) + shift_row).astype(jnp.bfloat16)
        outgoing = jnp.broadcast_to(
            normed.reshape(1, cycle_size, sub_rows, D), (group_count, cycle_size, sub_rows, D)
        )
        shared = lax.all_to_all(
            outgoing.reshape(share_rows, D), "seq", split_axis=0, concat_axis=0, tiled=True
        )
        projected = lax.dot_general(
            shared, qkv_rows, (((1,), (1,)), ((), ())), preferred_element_type=jnp.float32
        )
        projected = projected.astype(jnp.bfloat16).reshape(share_rows, group_heads, 3, HEAD_DIM)
        queries = projected[:, :, 0]
        fresh_local = jnp.transpose(projected[:, :, 1:], (0, 2, 1, 3)).reshape(
            1, share_rows, kv_lanes
        )
        fresh = cycle_join(fresh_local, seq_index, cycle_bits).reshape(
            cycle_size * share_rows, kv_lanes
        )
        previous = lax.dynamic_index_in_dim(cache, patch_id, 0, keepdims=False)
        cache = lax.dynamic_update_index_in_dim(
            cache, jnp.where(active, fresh, previous), patch_id, 0
        )
        keyvals = cache.reshape(MICRO * cycle_size * share_rows, 2, group_heads, HEAD_DIM)
        scores = jnp.einsum(
            "shd,khd->hsk", queries, keyvals[:, 0], preferred_element_type=jnp.float32
        ) * HEAD_DIM ** (-0.5)
        probs = jax.nn.softmax(scores, axis=-1).astype(jnp.bfloat16)
        attended = jnp.einsum(
            "hsk,khd->shd", probs, keyvals[:, 1], preferred_element_type=jnp.float32
        ).astype(jnp.bfloat16)
        partial_out = jnp.dot(
            attended.reshape(share_rows, group_heads * HEAD_DIM),
            out_rows,
            preferred_element_type=jnp.float32,
        )
        returned = lax.all_to_all(
            partial_out.astype(jnp.bfloat16), "seq", split_axis=0, concat_axis=0, tiled=True
        ).astype(partial_out.dtype)
        mixed = jnp.sum(returned.reshape(group_count, cycle_size, sub_rows, D), axis=0).reshape(
            TOK_DEV, D
        )
        layer_output = (layer_input.astype(jnp.float32) + gate_row * mixed).astype(jnp.bfloat16)
        keep_final = active & (segment_index == segment_count - 1)
        earlier = lax.dynamic_index_in_dim(finished, patch_id, 0, keepdims=False)
        finished = lax.dynamic_update_index_in_dim(
            finished, jnp.where(keep_final, layer_output, earlier), patch_id, 0
        )
        if tick_index + 1 < tick_count:
            received = passed_along(layer_output, "segment", 1)
    final_normed = rms_scaled(finished).astype(jnp.bfloat16)
    predicted = jnp.einsum("mtd,dc->mtc", final_normed, w_final, preferred_element_type=jnp.float32)
    is_last = segment_index == segment_count - 1
    branch_weight = jnp.where(branch_index == 0, 1.0 - guide_scale, guide_scale)
    velocity_term = jnp.where(is_last, branch_weight * predicted, 0.0)
    latent_term = jnp.where(is_last & (branch_index == 0), latent, 0.0)
    velocity_own, latent_own = lax.psum((velocity_term, latent_term), ("segment", "cfg"))
    velocity_full, latent_full = (
        lax.all_gather(velocity_own, "seq", axis=1, tiled=True),
        lax.all_gather(latent_own, "seq", axis=1, tiled=True),
    )
    stepped = (latent_full - velocity_full / SCHED_STEPS).astype(jnp.bfloat16)
    decoded = decoder_input(stepped, w_conv, slab_rows, seq_index, seq_count)
    return (velocity_own, decoded)


NT = (((1,), (1,)), ((), ()))
TILE = 256
PART = 768
AHEAD = 4


def kernel_params(mebibytes=8):
    return pltpu.CompilerParams(vmem_limit_bytes=mebibytes * 2**20)


def whole(space=pltpu.VMEM):
    return pl.BlockSpec(memory_space=space)


def in_order(copies, ahead):
    for copy in copies[:ahead]:
        copy.start()

    def landed():
        for i, copy in enumerate(copies):
            copy.wait()
            if i + ahead < len(copies):
                copies[i + ahead].start()
            yield i

    return landed()


def in_hbm(*values):
    return [pltpu.with_memory_space_constraint(value, pltpu.HBM) for value in values]


def stage_kernel(latent_hbm, staged_ref, sem):
    copy = pltpu.make_async_copy(latent_hbm, staged_ref, sem)
    copy.start()
    copy.wait()


def staged(latent):
    return pl.pallas_call(
        stage_kernel,
        in_specs=[whole(pltpu.HBM)],
        out_specs=whole(),
        out_shape=pltpu.VMEM(latent.shape, latent.dtype),
        scratch_shapes=[pltpu.SemaphoreType.DMA],
        cost_estimate=pl.CostEstimate(flops=10**10, bytes_accessed=0, transcendentals=0),
        compiler_params=kernel_params(),
    )(*in_hbm(latent))


def prepare_kernel(
    timestep_ref, table_ref, cond_ref, embed_ref, qkv_ref, out_hbm, rows_ref, heads_ref, out_ref, lhs, sem
):
    out_copy = pltpu.make_async_copy(out_hbm, out_ref, sem)
    out_copy.start()
    steps = table_ref.shape[1]
    chosen = lax.broadcasted_iota(jnp.int32, (16, steps), 1) == timestep_ref[0]
    chosen = jnp.where(chosen, 1.0, 0.0).astype(jnp.bfloat16)
    for j in range(3):
        row = jnp.dot(chosen, table_ref[j], preferred_element_type=jnp.float32)[:1]
        rows_ref[j : j + 1, :] = row + cond_ref[j] + (1.0 if j == 1 else 0.0)
    count = embed_ref.shape[0]
    spare, depth = lhs.shape[0] - count, lhs.shape[1]
    lhs[:count] = (embed_ref[...].astype(jnp.float32) * rows_ref[1:2]).astype(jnp.bfloat16)
    lhs[count:] = jnp.broadcast_to(rows_ref[0:1], (spare, depth)).astype(jnp.bfloat16)
    lane = lax.broadcasted_iota(jnp.int32, (PART, lhs.shape[0]), 1)
    for j in range(0, qkv_ref.shape[0], PART):
        product = lax.dot_general(
            qkv_ref[j : j + PART, :], lhs[...], NT, preferred_element_type=jnp.float32
        )
        upper = product.astype(jnp.bfloat16).astype(jnp.float32)
        value = jnp.where(lane == count + 1, product - upper, upper)
        heads_ref[j : j + PART, :] = jnp.where(lane <= count + 2, value, 0.0).astype(jnp.bfloat16)
    out_copy.wait()


def prepared(timestep, table, cond, w_embed, qkv, out):
    count, depth = w_embed.shape
    lanes = qkv.shape[0]
    return pl.pallas_call(
        prepare_kernel,
        in_specs=[whole(pltpu.SMEM)] + [whole()] * 4 + [whole(pltpu.HBM)],
        out_specs=[whole()] * 3,
        out_shape=[
            jax.ShapeDtypeStruct((3, depth), jnp.float32),
            jax.ShapeDtypeStruct((lanes, 2 * count), jnp.bfloat16),
            pltpu.VMEM(out.shape, out.dtype),
        ],
        scratch_shapes=[
            pltpu.VMEM((2 * count, depth), jnp.bfloat16),
            pltpu.SemaphoreType.DMA,
        ],
        compiler_params=kernel_params(),
    )(timestep, table, cond, w_embed, qkv, *in_hbm(out))


def span_of(rows, patch_rows):
    return -(-(rows + patch_rows) // 128) * 128


def attention_scratch(rows, patch_rows, lanes):
    shape = (lanes // HEAD_DIM, span_of(rows, patch_rows), HEAD_DIM)
    return [pltpu.VMEM((rows, lanes), jnp.bfloat16)] + [pltpu.VMEM(shape, jnp.bfloat16)] * 2


def attend(projected, order_ref, stale_ref, attended, keys, values):
    rows = projected.shape[0]
    patch_rows = stale_ref.shape[1]
    heads, span, _ = keys.shape
    kept = order_ref[1]
    filled = rows + patch_rows

    def micro_of(index):
        return jnp.where(index // TOK_DEV % MICRO == kept, 1, 0)

    query = micro_of(lax.broadcasted_iota(jnp.int32, (rows, span), 0))
    column = lax.broadcasted_iota(jnp.int32, (rows, span), 1)
    fresh_seen = (column < rows) & (query >= micro_of(column))
    stale_seen = (column >= rows) & (column < filled) & (query == 0)
    seen = fresh_seen | stale_seen
    scores = []
    for head in range(heads):
        first = 3 * HEAD_DIM * head
        for j, buffer in enumerate((keys, values)):
            lane = first + (j + 1) * HEAD_DIM
            stale_lane = (j * heads + head) * HEAD_DIM
            buffer[head, :rows] = projected[:, lane : lane + HEAD_DIM]
            buffer[head, rows:filled] = stale_ref[kept, :, stale_lane : stale_lane + HEAD_DIM]
            if filled < span:
                buffer[head, filled:] = jnp.zeros((span - filled, HEAD_DIM), jnp.bfloat16)
        queries = projected[:, first : first + HEAD_DIM]
        scores.append(
            lax.dot_general(queries, keys[head], NT, preferred_element_type=jnp.float32)
        )
    scores = [jnp.where(seen, score * HEAD_DIM ** (-0.5), -jnp.inf) for score in scores]
    tops = [jnp.max(score, axis=-1, keepdims=True) for score in scores]
    weights = [jnp.exp(score - top) for score, top in zip(scores, tops)]
    totals = [jnp.sum(weight, axis=-1, keepdims=True) for weight in weights]
    for head in range(heads):
        probs = (weights[head] / totals[head]).astype(jnp.bfloat16)
        attended[:, head * HEAD_DIM : (head + 1) * HEAD_DIM] = jnp.dot(
            probs, values[head], preferred_element_type=jnp.float32
        ).astype(jnp.bfloat16)


def column_blocks(place, attended, out_ref, block_refs):
    count = len(block_refs)
    columns = out_ref.shape[1] // count
    for k in range(count):
        first = pl.multiple_of((place ^ k) * columns, columns)
        block_refs[k][...] = jnp.dot(
            attended[...], out_ref[:, pl.ds(first, columns)], preferred_element_type=jnp.float32
        ).astype(jnp.bfloat16)


def first_layer_kernel(
    count, order_ref, embed_ref, heads_ref, stale_ref, out_ref, near_ref, *refs
):
    latent_refs, refs = refs[:count], refs[count:]
    block_refs, (own_ref, latents, attended, keys, values) = refs[:count], refs[count:]
    place = lax.axis_index("seq")
    rows_dev = MICRO * TOK_DEV
    width = embed_ref.shape[0]
    for k in range(count):
        first = pl.multiple_of((place ^ k) * rows_dev, rows_dev)
        latents[pl.ds(first, rows_dev), :width] = (
            latent_refs[k][...].reshape(rows_dev, width).astype(jnp.bfloat16)
        )
    embedded = jnp.dot(latents[:, :width], embed_ref[...], preferred_element_type=jnp.float32)
    embedded = embedded.astype(jnp.bfloat16).astype(jnp.float32)
    square = jnp.mean(embedded * embedded, axis=-1, keepdims=True) + norm_eps
    norm = lax.rsqrt(square)
    size = square * norm
    upper = size.astype(jnp.bfloat16).astype(jnp.float32)
    lane = lax.broadcasted_iota(jnp.int32, (latents.shape[0], width), 1)
    spare = jnp.where(lane < 2, upper, jnp.where(lane == 2, size - upper, 0.0))
    latents[:, width:] = spare.astype(jnp.bfloat16)
    projected = lax.dot_general(
        latents[...], heads_ref[...], NT, preferred_element_type=jnp.float32
    )
    projected = (norm * projected).astype(jnp.bfloat16)
    attend(projected, order_ref, stale_ref, attended, keys, values)
    columns = own_ref.shape[1]
    first = pl.multiple_of(place * columns, columns)
    own_ref[...] = jnp.dot(
        latents[:, :width], embed_ref[:, pl.ds(first, columns)], preferred_element_type=jnp.float32
    ).astype(jnp.bfloat16)
    column_blocks(place, attended, out_ref, block_refs)


def first_layer(patch_order, latents, w_embed, heads, stale, out):
    count = len(latents)
    rows = count * MICRO * TOK_DEV
    lanes, depth = out.shape
    block = jax.ShapeDtypeStruct((rows, depth // count), jnp.bfloat16)
    return pl.pallas_call(
        functools.partial(first_layer_kernel, count),
        in_specs=[whole(pltpu.SMEM)] + [whole()] * (5 + count),
        out_specs=[whole()] * (count + 1),
        out_shape=[block] * (count + 1),
        scratch_shapes=[
            pltpu.VMEM((rows, 2 * w_embed.shape[0]), jnp.bfloat16),
            *attention_scratch(rows, stale.shape[1], lanes),
        ],
        compiler_params=kernel_params(),
    )(patch_order, w_embed, heads, stale, out, met(latents[1:2]), *latents)


def turn_kernel(after_ref, qkv_ref, heads_ref, turned_ref, term_ref):
    lanes, depth = qkv_ref.shape
    for i in range(0, lanes, TILE):
        for j in range(0, depth, TILE):
            turned_ref[j : j + TILE, i : i + TILE] = qkv_ref[i : i + TILE, j : j + TILE].T
    count = heads_ref.shape[1] // 2
    for i in range(0, lanes, TILE):
        across = heads_ref[i : i + TILE, :].astype(jnp.float32).T
        term_ref[:, i : i + TILE] = across[count : count + 1] + across[count + 1 : count + 2]


def turned(qkv, heads, after):
    return pl.pallas_call(
        turn_kernel,
        in_specs=[whole(pl.ANY)] + [whole()] * 2,
        out_specs=[whole()] * 2,
        out_shape=[
            pltpu.VMEM(qkv.shape[::-1], qkv.dtype),
            jax.ShapeDtypeStruct((1, qkv.shape[0]), jnp.float32),
        ],
        cost_estimate=pl.CostEstimate(flops=5 * 10**9, bytes_accessed=0, transcendentals=0),
        compiler_params=kernel_params(),
    )(after, qkv, heads)


def meet_kernel(*refs):
    refs[-1][...] = jnp.zeros_like(refs[-1])


def met(values):
    return pl.pallas_call(
        meet_kernel,
        in_specs=[whole(pl.ANY)] * len(values),
        out_specs=whole(),
        out_shape=jax.ShapeDtypeStruct((8, 128), jnp.float32),
        compiler_params=kernel_params(),
    )(*values)


def block_sum_kernel(rows_ref, own_ref, term_ref, *refs):
    part_refs, block_ref = refs[:-1], refs[-1]
    columns = own_ref.shape[1]
    first = pl.multiple_of(lax.axis_index("seq") * columns, columns)
    mixed = part_refs[0][...].astype(jnp.float32)
    for part_ref in part_refs[1:]:
        mixed = mixed + part_ref[...].astype(jnp.float32)
    gate = rows_ref[2:3, pl.ds(first, columns)]
    block_ref[...] = (own_ref[...].astype(jnp.float32) + gate * mixed).astype(jnp.bfloat16)


def block_sum(mod_rows, own, term, parts):
    return pl.pallas_call(
        block_sum_kernel,
        in_specs=[whole()] * (3 + len(parts)),
        out_specs=whole(),
        out_shape=jax.ShapeDtypeStruct(own.shape, own.dtype),
        compiler_params=kernel_params(),
    )(mod_rows, own, term, *parts)


def scaled_piece(place, k, piece_ref, rows_ref):
    columns = piece_ref.shape[1]
    first = pl.multiple_of((place ^ k) * columns, columns)
    wide = piece_ref[...].astype(jnp.float32)
    scaled = (wide * rows_ref[1:2, pl.ds(first, columns)]).astype(jnp.bfloat16)
    return scaled, jnp.sum(wide * wide, axis=-1, keepdims=True)


def sums_kernel(numbers, rows_ref, turned_ref, *refs):
    count = len(numbers)
    piece_refs, earlier, (sums_ref, squares_ref) = refs[:count], refs[count:-2], refs[-2:]
    place = lax.axis_index("seq")
    columns = piece_refs[0].shape[1]
    squares = earlier[1][...] if earlier else 0.0
    scaled = []
    for k, piece_ref in zip(numbers, piece_refs):
        piece, square = scaled_piece(place, k, piece_ref, rows_ref)
        scaled.append((piece, pl.ds(pl.multiple_of((place ^ k) * columns, columns), columns)))
        squares = squares + square
    squares_ref[...] = squares
    for i in range(0, sums_ref.shape[1], PART):
        lane = slice(i, i + PART)
        total = earlier[0][:, lane] if earlier else 0.0
        for piece, part in scaled:
            total = total + jnp.dot(
                piece, turned_ref[part, lane], preferred_element_type=jnp.float32
            )
        sums_ref[:, lane] = total


def product_sums(numbers, pieces, mod_rows, qkv, earlier):
    rows = pieces[0].shape[0]
    lanes = qkv.shape[1]
    return pl.pallas_call(
        functools.partial(sums_kernel, numbers),
        in_specs=[whole()] * (2 + len(numbers) + len(earlier)),
        out_specs=[whole()] * 2,
        out_shape=[
            jax.ShapeDtypeStruct((rows, lanes), jnp.float32),
            jax.ShapeDtypeStruct((rows, 1), jnp.float32),
        ],
        compiler_params=kernel_params(),
    )(mod_rows, qkv, *pieces, *earlier)


def later_layer_kernel(
    count, last, order_ref, rows_ref, qkv_ref, out_ref, term_ref, stale_ref, sums_ref, squares_ref, *refs
):
    piece_refs, refs = refs[:count], refs[count:]
    block_refs, own_ref, sums, attended, keys, values, partial_out = refs[:count], *refs[count:]
    place = lax.axis_index("seq")
    scaled, squares = scaled_piece(place, count - 1, piece_refs[-1], rows_ref)
    norm = lax.rsqrt((squares_ref[...] + squares) / rows_ref.shape[1] + norm_eps)
    columns = piece_refs[-1].shape[1]
    part = pl.ds(pl.multiple_of((place ^ (count - 1)) * columns, columns), columns)
    for i in range(0, sums.shape[1], PART):
        lane = slice(i, i + PART)
        product = jnp.dot(scaled, qkv_ref[part, lane], preferred_element_type=jnp.float32)
        sums[:, lane] = (norm * (product + sums_ref[:, lane]) + term_ref[:1, lane]).astype(
            jnp.bfloat16
        )
    attend(sums, order_ref, stale_ref, attended, keys, values)
    if not last:
        column_blocks(place, attended, out_ref, block_refs)
        own_ref[...] = piece_refs[0][...]
        return
    partial_out[...] = jnp.dot(
        attended[...], out_ref[...], preferred_element_type=jnp.float32
    ).astype(jnp.bfloat16)
    rows_dev = own_ref.shape[0]
    columns = piece_refs[0].shape[1]
    own_rows = pl.ds(pl.multiple_of(place * rows_dev, rows_dev), rows_dev)
    for k in range(count):
        first = pl.multiple_of((place ^ k) * rows_dev, rows_dev)
        block_refs[k][...] = partial_out[pl.ds(first, rows_dev), :]
        first = pl.multiple_of((place ^ k) * columns, columns)
        own_ref[:, pl.ds(first, columns)] = piece_refs[k][own_rows, :]


def later_layer(last, patch_order, pieces, mod_rows, qkv, out, term, stale, sums, squares):
    count = len(pieces)
    rows, columns = pieces[0].shape
    lanes, depth = out.shape
    shape = (rows // count, depth) if last else (rows, columns)
    block = jax.ShapeDtypeStruct(shape, jnp.bfloat16)
    return pl.pallas_call(
        functools.partial(later_layer_kernel, count, last),
        in_specs=[whole(pltpu.SMEM)] + [whole()] * (7 + count),
        out_specs=[whole()] * (count + 1),
        out_shape=[block] * (count + 1),
        scratch_shapes=[
            pltpu.VMEM(sums.shape, jnp.bfloat16),
            *attention_scratch(rows, stale.shape[1], lanes),
            pltpu.VMEM((rows, depth), jnp.bfloat16),
        ],
        compiler_params=kernel_params(),
    )(patch_order, mod_rows, qkv, out, term, stale, sums, squares, *pieces)


def term_kernel(rows_ref, own_ref, final_ref, far_ref, *refs):
    part_refs, term_ref = refs[:-1], refs[-1]
    mixed = part_refs[0][...].astype(jnp.float32)
    for part_ref in part_refs[1:]:
        mixed = mixed + part_ref[...].astype(jnp.float32)
    hidden = (own_ref[...].astype(jnp.float32) + rows_ref[2:3] * mixed).astype(jnp.bfloat16)
    predicted = lax.dot_general(
        hidden, final_ref[...], NT, preferred_element_type=jnp.float32
    )
    wide = hidden.astype(jnp.float32)
    norm = lax.rsqrt(jnp.mean(wide * wide, axis=-1, keepdims=True) + norm_eps)
    predicted = norm * predicted
    weight = jnp.where(lax.axis_index("cfg") == 0, 1.0 - guide_scale, guide_scale)
    patches = [predicted[i * TOK_DEV : (i + 1) * TOK_DEV] for i in range(MICRO)]
    term = weight * jnp.concatenate(patches, axis=1)
    term_ref[...] = jnp.broadcast_to(term, term_ref.shape)


def velocity_terms(peers, mod_rows, own, final, parts):
    shape = (peers, TOK_DEV, MICRO * final.shape[0])
    return pl.pallas_call(
        term_kernel,
        in_specs=[whole()] * (4 + len(parts)),
        out_specs=whole(),
        out_shape=jax.ShapeDtypeStruct(shape, jnp.float32),
        compiler_params=kernel_params(),
    )(mod_rows, own, final, met(parts[3:]), *parts)


TAPS = 27
TAP_GROUP = 4
HALF = LAT_W // 2


def window_kernel(sizes, slab_ref, conv_ref, chosen_ref, weights_ref):
    seq_count, slab_most, token_rows = sizes
    place = lax.axis_index("seq")
    rows = seq_count * MICRO * TOK_DEV
    start = 0
    for j in range(seq_count - 1):
        start = start + jnp.where(j < place, slab_ref[j], 0)
    shape = (chosen_ref.shape[0], 2 * rows)
    target = lax.broadcasted_iota(jnp.int32, shape, 0)
    column = lax.broadcasted_iota(jnp.int32, shape, 1)
    across = target % HALF
    down = target // HALF % slab_most
    frame = target // (HALF * slab_most)
    kept = down < slab_ref[place]
    patch_rows = seq_count * TOK_DEV
    for tap in range(TAPS):
        time, row_shift, token_shift = tap // 9, tap // 3 % 3, tap % 3
        source_frame = jnp.maximum(frame + (time - 2), 0)
        row = start + down + (row_shift - 1)
        token = across + (token_shift - 1)
        inside = kept & (row >= 0) & (row < 2 * token_rows) & (token >= 0) & (token < HALF)
        row = jnp.maximum(row, 0)
        index = (source_frame * token_rows + row // 2) * HALF + jnp.maximum(token, 0)
        patch = index // patch_rows
        slot = index % patch_rows
        source = (slot // TOK_DEV * MICRO + patch) * TOK_DEV + slot % TOK_DEV + row % 2 * rows
        chosen_ref[:, tap * 2 * rows : (tap + 1) * 2 * rows] = jnp.where(
            inside & (column == source), 1.0, 0.0
        ).astype(jnp.bfloat16)
    chosen_ref[:, TAPS * 2 * rows :] = jnp.zeros(
        (shape[0], chosen_ref.shape[1] - TAPS * 2 * rows), jnp.bfloat16
    )
    weights_ref[...] = jnp.zeros_like(weights_ref)
    channels = conv_ref.shape[2]
    for tap in range(TAPS):
        for source in range(2):
            for side in range(2):
                shift = 2 * (tap % 3 - 1) + source - side + 1
                if 0 <= shift < 3:
                    first = (tap * 2 + source) * LAT_CH
                    weights_ref[first : first + LAT_CH, side * channels : (side + 1) * channels] = (
                        conv_ref[tap // 3 * 3 + shift]
                    )


def window_parts(seq_count, slab_most, token_rows, slab_rows, w_conv):
    rows = seq_count * MICRO * TOK_DEV
    groups = -(-TAPS // TAP_GROUP)
    return pl.pallas_call(
        functools.partial(window_kernel, (seq_count, slab_most, token_rows)),
        in_specs=[whole(pltpu.SMEM), whole()],
        out_specs=[whole()] * 2,
        out_shape=[
            jax.ShapeDtypeStruct(
                (FRAMES * slab_most * HALF, groups * TAP_GROUP * 2 * rows), jnp.bfloat16
            ),
            jax.ShapeDtypeStruct(
                (groups * TAP_GROUP * 2 * LAT_CH, 2 * w_conv.shape[2]), jnp.bfloat16
            ),
        ],
        compiler_params=kernel_params(),
    )(slab_rows, w_conv)


def decode_kernel(
    segment_count, count, terms_ref, chosen_ref, weights_ref, *refs
):
    latent_refs, refs = refs[:count], refs[count:]
    velocity_ref, decoded_ref, latents, tokens, halves, columns, features = refs
    place = lax.axis_index("seq")
    for k in range(count):
        latents[place ^ k] = latent_refs[k][...]

    def velocity_of(z):
        first = (z * segment_count + segment_count - 1) * 2
        both = terms_ref[first] + terms_ref[first + 1]
        width = both.shape[1] // MICRO
        return [both[:, i * width : (i + 1) * width] for i in range(MICRO)]

    for i, value in enumerate(velocity_of(place)):
        velocity_ref[i] = value
    for z in range(count):
        stepped = [
            latents[z, i] - value / SCHED_STEPS for i, value in enumerate(velocity_of(z))
        ]
        tokens[z * MICRO * TOK_DEV : (z + 1) * MICRO * TOK_DEV] = jnp.concatenate(
            stepped, axis=0
        ).astype(jnp.bfloat16)
    rows, width = tokens.shape
    half = width // 2
    halves[...] = jnp.zeros_like(halves)
    for j in range(TAP_GROUP):
        for side in range(2):
            first = (j * 2 + side) * rows
            halves[first : first + rows, j * half : (j + 1) * half] = tokens[
                :, side * half : (side + 1) * half
            ]
    depth, group_width = halves.shape
    for group in range(chosen_ref.shape[1] // depth):
        columns[:, group * group_width : (group + 1) * group_width] = jnp.dot(
            chosen_ref[:, group * depth : (group + 1) * depth],
            halves[...],
            preferred_element_type=jnp.float32,
        ).astype(jnp.bfloat16)
    result = jnp.dot(columns[...], weights_ref[...], preferred_element_type=jnp.float32)
    channels = features.shape[1]
    for side in range(2):
        features[pl.ds(side, result.shape[0], stride=2), :] = result[
            :, side * channels : (side + 1) * channels
        ]
    decoded_ref[...] = features[...].astype(jnp.bfloat16)


def decoded_slab(segment_count, terms, chosen, weights, latents):
    count = len(latents)
    rows = count * MICRO * TOK_DEV
    width = latents[0].shape[-1]
    targets = chosen.shape[0]
    channels = weights.shape[1] // 2
    return pl.pallas_call(
        functools.partial(decode_kernel, segment_count, count),
        in_specs=[whole()] * (3 + count),
        out_specs=[whole()] * 2,
        out_shape=[
            jax.ShapeDtypeStruct(latents[0].shape, jnp.float32),
            jax.ShapeDtypeStruct((2 * targets, channels), jnp.bfloat16),
        ],
        scratch_shapes=[
            pltpu.VMEM((count,) + latents[0].shape, jnp.float32),
            pltpu.VMEM((rows, width), jnp.bfloat16),
            pltpu.VMEM((TAP_GROUP * 2 * rows, TAP_GROUP * width // 2), jnp.bfloat16),
            pltpu.VMEM((targets, weights.shape[0]), jnp.bfloat16),
            pltpu.VMEM((2 * targets, channels), jnp.float32),
        ],
        compiler_params=kernel_params(),
    )(terms, chosen, weights, *latents)


def shards(
    latent,
    w_embed,
    w_qkv,
    w_out,
    mod_table,
    cond_mod,
    stale_kv,
    w_final,
    w_conv,
    patch_order,
    timestep,
    slab_rows,
):
    seq_count = lax.axis_size("seq")
    segment_count = lax.axis_size("segment")

    def within(k):
        return [(i, i ^ k) for i in range(seq_count)]

    def returned(values):
        far_first = [lax.ppermute(values[k], "seq", within(k)) for k in range(seq_count - 1, 0, -1)]
        return values[:1] + far_first[::-1]

    numbers = tuple(range(seq_count))
    half = (seq_count + 1) // 2
    latents = returned([staged(latent)] * seq_count)
    mod_rows, head_embed, out = prepared(
        timestep,
        jnp.transpose(mod_table, (1, 0, 2)),
        jnp.transpose(cond_mod[0], (1, 0, 2)),
        w_embed,
        w_qkv[0],
        w_out[0],
    )
    stale = stale_kv[0, 0, 0]
    *blocks, own = first_layer(
        patch_order, latents, w_embed, head_embed, stale, out
    )
    qkv, shift_term = turned(w_qkv[0], head_embed, own)
    for step in range(1, segment_count):
        block = block_sum(mod_rows, own, shift_term, returned(blocks))
        pieces = []
        for k in numbers[::-1]:
            pairs = [
                (i * segment_count + j, (i ^ k) * segment_count + (j + 1) % segment_count)
                for i in range(seq_count)
                for j in range(segment_count)
            ]
            pieces.insert(0, lax.ppermute(block, ("seq", "segment"), pairs))
        sums = ()
        for some in (numbers[:1], numbers[1:-1]):
            if some:
                sums = product_sums(
                    some,
                    [pieces[k] for k in some],
                    mod_rows,
                    qkv,
                    sums,
                )
        *blocks, own = later_layer(
            step + 1 == segment_count,
            patch_order,
            pieces,
            mod_rows,
            qkv,
            out,
            shift_term,
            stale,
            *sums,
        )

    blocks, slab_rows, w_conv = lax.optimization_barrier((blocks, slab_rows, w_conv))
    token_rows = MICRO * seq_count * TOK_DEV // (FRAMES * HALF)
    slab_most = 4 * token_rows // seq_count
    chosen, weights = window_parts(seq_count, slab_most, token_rows, slab_rows, w_conv)
    peers = ("seq", "segment", "cfg")
    peer_count = seq_count * segment_count * lax.axis_size("cfg")
    terms = velocity_terms(peer_count, mod_rows, own, w_final.T, returned(blocks))
    terms = lax.all_to_all(terms, peers, split_axis=0, concat_axis=0, tiled=True)
    velocity, decoded = decoded_slab(segment_count, terms, chosen, weights, latents)
    return (velocity, decoded.reshape(1, FRAMES, slab_most, LAT_W, w_conv.shape[2]))


def decoder_input(stepped, w_conv, slab_rows, seq_index, seq_count):
    token_rows = MICRO * seq_count * TOK_DEV // (FRAMES * (LAT_W // 2))
    image_rows = 2 * token_rows
    slab_most = 2 * image_rows // seq_count
    image = stepped.reshape(FRAMES, token_rows, LAT_W // 2, 2, 2, LAT_CH)
    image = (
        jnp.transpose(image, (0, 1, 3, 2, 4, 5))
        .reshape(FRAMES, image_rows, LAT_W, LAT_CH)
    )
    padded = jnp.concatenate([image[:1], image[:1], image], 0)
    padded = jnp.pad(padded, ((0, 0), (1, 1 + slab_most), (1, 1), (0, 0)))
    positions = jnp.arange(seq_count)
    slab_count = jnp.sum(jnp.where(positions == seq_index, slab_rows, 0))
    slab_start = jnp.sum(jnp.where(positions < seq_index, slab_rows, 0))
    window = lax.dynamic_slice_in_dim(padded, slab_start, slab_most + 2, 1)
    pieces = []
    for frame_shift in range(3):
        for row_shift in range(3):
            for col_shift in range(3):
                pieces.append(
                    window[
                        frame_shift : frame_shift + FRAMES,
                        row_shift : row_shift + slab_most,
                        col_shift : col_shift + LAT_W,
                    ]
                )
    columns = jnp.concatenate(pieces, -1).reshape(FRAMES * slab_most * LAT_W, 27 * LAT_CH)
    kernel = w_conv.reshape(27 * LAT_CH, w_conv.shape[2])
    features = jnp.dot(columns, kernel, preferred_element_type=jnp.float32).astype(jnp.bfloat16)
    features = features.reshape(FRAMES, slab_most, LAT_W, w_conv.shape[2])
    row_valid = jnp.arange(slab_most)[None, :, None, None] < slab_count
    decoded = jnp.where(row_valid, features, jnp.zeros_like(features))
    return decoded[None]


def solution(mesh):
    in_specs = (
        P(None, ("groups", "seq"), None),
        P(),
        P("segment", "seq", None),
        P("segment", "seq", None),
        P(),
        P("cfg", ("groups", "segment"), None, None),
        P("segment", "cfg", "seq", None, "groups", None),
        P(),
        P(None, None, ("segment", "cfg")),
        P("groups"),
        P("groups"),
        P("groups"),
    )
    out_specs = (
        P(None, ("groups", "seq"), None),
        P(("groups", "seq"), None, None, None, ("segment", "cfg")),
    )
    whole_groups = 2 <= mesh.shape["seq"] <= 8
    program = shards if whole_groups else cycled_shards
    return jax.shard_map(program, mesh=mesh, in_specs=in_specs, out_specs=out_specs, check_vma=False)
```

```python
import functools

import jax
import jax.numpy as jnp
from jax import lax
from jax.experimental import pallas as pl
from jax.experimental.pallas import tpu as pltpu
from jax.sharding import PartitionSpec as P

HEADS = 24
HEAD_DIM = 128
D = 3072
LAT_CH = 16
SCHED_STEPS = 50
MICRO = 2
TOK_DEV = 8
FRAMES = 4
LAT_W = 8


guide_scale = 5.0
norm_eps = 1e-06


def swapped(value, axis, bit):
    return lax.ppermute(value, axis, [(i, i ^ 1 << bit) for i in range(lax.axis_size(axis))])


def passed_along(value, axis, by):
    size = lax.axis_size(axis)
    pairs = [(i, i + by) for i in range(size) if 0 <= i + by < size]
    return lax.ppermute(value, axis, pairs)


def rms_scaled(values):
    wide = values.astype(jnp.float32)
    return wide * lax.rsqrt(jnp.mean(wide * wide, axis=-1, keepdims=True) + norm_eps)


def cycle_join(piece, seq_index, cycle_bits):
    joined = piece
    for bit_number in range(cycle_bits):
        partner = swapped(joined, "seq", bit_number)
        upper_half = (seq_index // 2**bit_number % 2).astype(jnp.int32)
        part_rows = joined.shape[0]
        combined = jnp.zeros((2 * part_rows,) + joined.shape[1:], joined.dtype)
        combined = lax.dynamic_update_slice_in_dim(combined, joined, upper_half * part_rows, 0)
        joined = lax.dynamic_update_slice_in_dim(combined, partner, (1 - upper_half) * part_rows, 0)
    return joined


def cycled_shards(
    latent,
    w_embed,
    w_qkv,
    w_out,
    mod_table,
    cond_mod,
    stale_kv,
    w_final,
    w_conv,
    patch_order,
    timestep,
    slab_rows,
):
    seq_count = lax.axis_size("seq")
    segment_count = lax.axis_size("segment")
    seq_index = lax.axis_index("seq")
    segment_index = lax.axis_index("segment")
    branch_index = lax.axis_index("cfg")
    group_count = min(seq_count, 8)
    cycle_size = seq_count // group_count
    cycle_bits = cycle_size.bit_length() - 1
    group_heads = HEADS // group_count
    sub_rows = TOK_DEV // cycle_size
    share_rows = seq_count * sub_rows
    kv_lanes = 2 * group_heads * HEAD_DIM
    table_row = lax.dynamic_index_in_dim(mod_table, timestep[0], 0, keepdims=False).astype(
        jnp.float32
    )
    modulation = table_row + cond_mod[0, 0]
    shift_row = modulation[0]
    scale_row = modulation[1]
    gate_row = modulation[2]
    joined_weights = (
        cycle_join(w_qkv[0], seq_index, cycle_bits),
        cycle_join(w_out[0], seq_index, cycle_bits),
    )
    stale_joined = cycle_join(stale_kv[0, 0], seq_index, cycle_bits)
    cache = jnp.transpose(stale_joined, (1, 0, 2, 3)).reshape(
        MICRO, cycle_size * share_rows, kv_lanes
    )
    received = jnp.zeros((TOK_DEV, D), jnp.bfloat16)
    finished = jnp.zeros((MICRO, TOK_DEV, D), jnp.bfloat16)
    slot_ids = jnp.arange(MICRO)
    tick_count = MICRO + segment_count - 1
    for tick_index in range(tick_count):
        qkv_rows, out_rows = joined_weights
        micro_index = tick_index - segment_index
        active = (micro_index >= 0) & (micro_index < MICRO)
        clipped = jnp.clip(micro_index, 0, MICRO - 1)
        patch_id = jnp.sum(jnp.where(slot_ids == clipped, patch_order, 0))
        own_latent = lax.dynamic_index_in_dim(latent, patch_id, 0, keepdims=False).astype(
            jnp.bfloat16
        )
        embedded = jnp.dot(own_latent, w_embed, preferred_element_type=jnp.float32).astype(
            jnp.bfloat16
        )
        layer_input = jnp.where(segment_index == 0, embedded, received)
        normed = (rms_scaled(layer_input) * (1.0 + scale_row) + shift_row).astype(jnp.bfloat16)
        outgoing = jnp.broadcast_to(
            normed.reshape(1, cycle_size, sub_rows, D), (group_count, cycle_size, sub_rows, D)
        )
        shared = lax.all_to_all(
            outgoing.reshape(share_rows, D), "seq", split_axis=0, concat_axis=0, tiled=True
        )
        projected = lax.dot_general(
            shared, qkv_rows, (((1,), (1,)), ((), ())), preferred_element_type=jnp.float32
        )
        projected = projected.astype(jnp.bfloat16).reshape(share_rows, group_heads, 3, HEAD_DIM)
        queries = projected[:, :, 0]
        fresh_local = jnp.transpose(projected[:, :, 1:], (0, 2, 1, 3)).reshape(
            1, share_rows, kv_lanes
        )
        fresh = cycle_join(fresh_local, seq_index, cycle_bits).reshape(
            cycle_size * share_rows, kv_lanes
        )
        previous = lax.dynamic_index_in_dim(cache, patch_id, 0, keepdims=False)
        cache = lax.dynamic_update_index_in_dim(
            cache, jnp.where(active, fresh, previous), patch_id, 0
        )
        keyvals = cache.reshape(MICRO * cycle_size * share_rows, 2, group_heads, HEAD_DIM)
        scores = jnp.einsum(
            "shd,khd->hsk", queries, keyvals[:, 0], preferred_element_type=jnp.float32
        ) * HEAD_DIM ** (-0.5)
        probs = jax.nn.softmax(scores, axis=-1).astype(jnp.bfloat16)
        attended = jnp.einsum(
            "hsk,khd->shd", probs, keyvals[:, 1], preferred_element_type=jnp.float32
        ).astype(jnp.bfloat16)
        partial_out = jnp.dot(
            attended.reshape(share_rows, group_heads * HEAD_DIM),
            out_rows,
            preferred_element_type=jnp.float32,
        )
        returned = lax.all_to_all(
            partial_out.astype(jnp.bfloat16), "seq", split_axis=0, concat_axis=0, tiled=True
        ).astype(partial_out.dtype)
        mixed = jnp.sum(returned.reshape(group_count, cycle_size, sub_rows, D), axis=0).reshape(
            TOK_DEV, D
        )
        layer_output = (layer_input.astype(jnp.float32) + gate_row * mixed).astype(jnp.bfloat16)
        keep_final = active & (segment_index == segment_count - 1)
        earlier = lax.dynamic_index_in_dim(finished, patch_id, 0, keepdims=False)
        finished = lax.dynamic_update_index_in_dim(
            finished, jnp.where(keep_final, layer_output, earlier), patch_id, 0
        )
        if tick_index + 1 < tick_count:
            received = passed_along(layer_output, "segment", 1)
    final_normed = rms_scaled(finished).astype(jnp.bfloat16)
    predicted = jnp.einsum("mtd,dc->mtc", final_normed, w_final, preferred_element_type=jnp.float32)
    is_last = segment_index == segment_count - 1
    branch_weight = jnp.where(branch_index == 0, 1.0 - guide_scale, guide_scale)
    velocity_term = jnp.where(is_last, branch_weight * predicted, 0.0)
    latent_term = jnp.where(is_last & (branch_index == 0), latent, 0.0)
    velocity_own, latent_own = lax.psum((velocity_term, latent_term), ("segment", "cfg"))
    velocity_full, latent_full = (
        lax.all_gather(velocity_own, "seq", axis=1, tiled=True),
        lax.all_gather(latent_own, "seq", axis=1, tiled=True),
    )
    stepped = (latent_full - velocity_full / SCHED_STEPS).astype(jnp.bfloat16)
    decoded = decoder_input(stepped, w_conv, slab_rows, seq_index, seq_count)
    return (velocity_own, decoded)


NT = (((1,), (1,)), ((), ()))
TILE = 256
PART = 768
AHEAD = 4


def kernel_params(mebibytes=8):
    return pltpu.CompilerParams(vmem_limit_bytes=mebibytes * 2**20)


def whole(space=pltpu.VMEM):
    return pl.BlockSpec(memory_space=space)


def in_order(copies, ahead):
    for copy in copies[:ahead]:
        copy.start()

    def landed():
        for i, copy in enumerate(copies):
            copy.wait()
            if i + ahead < len(copies):
                copies[i + ahead].start()
            yield i

    return landed()


def in_hbm(*values):
    return [pltpu.with_memory_space_constraint(value, pltpu.HBM) for value in values]


def stage_kernel(latent_hbm, staged_ref, sem):
    copy = pltpu.make_async_copy(latent_hbm, staged_ref, sem)
    copy.start()
    copy.wait()


def staged(latent):
    return pl.pallas_call(
        stage_kernel,
        in_specs=[whole(pltpu.HBM)],
        out_specs=whole(),
        out_shape=pltpu.VMEM(latent.shape, latent.dtype),
        scratch_shapes=[pltpu.SemaphoreType.DMA],
        cost_estimate=pl.CostEstimate(flops=10**10, bytes_accessed=0, transcendentals=0),
        compiler_params=kernel_params(),
    )(*in_hbm(latent))


def prepare_kernel(
    timestep_ref, table_ref, cond_ref, embed_ref, qkv_ref, out_hbm, rows_ref, heads_ref, out_ref, lhs, sem
):
    out_copy = pltpu.make_async_copy(out_hbm, out_ref, sem)
    out_copy.start()
    steps = table_ref.shape[1]
    chosen = lax.broadcasted_iota(jnp.int32, (16, steps), 1) == timestep_ref[0]
    chosen = jnp.where(chosen, 1.0, 0.0).astype(jnp.bfloat16)
    for j in range(3):
        row = jnp.dot(chosen, table_ref[j], preferred_element_type=jnp.float32)[:1]
        rows_ref[j : j + 1, :] = row + cond_ref[j] + (1.0 if j == 1 else 0.0)
    count = embed_ref.shape[0]
    spare, depth = lhs.shape[0] - count, lhs.shape[1]
    lhs[:count] = (embed_ref[...].astype(jnp.float32) * rows_ref[1:2]).astype(jnp.bfloat16)
    lhs[count:] = jnp.broadcast_to(rows_ref[0:1], (spare, depth)).astype(jnp.bfloat16)
    lane = lax.broadcasted_iota(jnp.int32, (PART, lhs.shape[0]), 1)
    for j in range(0, qkv_ref.shape[0], PART):
        product = lax.dot_general(
            qkv_ref[j : j + PART, :], lhs[...], NT, preferred_element_type=jnp.float32
        )
        upper = product.astype(jnp.bfloat16).astype(jnp.float32)
        value = jnp.where(lane == count + 1, product - upper, upper)
        heads_ref[j : j + PART, :] = jnp.where(lane <= count + 2, value, 0.0).astype(jnp.bfloat16)
    out_copy.wait()


def prepared(timestep, table, cond, w_embed, qkv, out):
    count, depth = w_embed.shape
    lanes = qkv.shape[0]
    return pl.pallas_call(
        prepare_kernel,
        in_specs=[whole(pltpu.SMEM)] + [whole()] * 4 + [whole(pltpu.HBM)],
        out_specs=[whole()] * 3,
        out_shape=[
            jax.ShapeDtypeStruct((3, depth), jnp.float32),
            jax.ShapeDtypeStruct((lanes, 2 * count), jnp.bfloat16),
            pltpu.VMEM(out.shape, out.dtype),
        ],
        scratch_shapes=[
            pltpu.VMEM((2 * count, depth), jnp.bfloat16),
            pltpu.SemaphoreType.DMA,
        ],
        compiler_params=kernel_params(),
    )(timestep, table, cond, w_embed, qkv, *in_hbm(out))


def span_of(rows, patch_rows):
    return -(-(rows + patch_rows) // 128) * 128


def attention_scratch(rows, patch_rows, lanes):
    shape = (lanes // HEAD_DIM, span_of(rows, patch_rows), HEAD_DIM)
    return [pltpu.VMEM((rows, lanes), jnp.bfloat16)] + [pltpu.VMEM(shape, jnp.bfloat16)] * 2


def attend(projected, order_ref, stale_ref, attended, keys, values):
    rows = projected.shape[0]
    patch_rows = stale_ref.shape[1]
    heads, span, _ = keys.shape
    kept = order_ref[1]
    filled = rows + patch_rows

    def micro_of(index):
        return jnp.where(index // TOK_DEV % MICRO == kept, 1, 0)

    query = micro_of(lax.broadcasted_iota(jnp.int32, (rows, span), 0))
    column = lax.broadcasted_iota(jnp.int32, (rows, span), 1)
    fresh_seen = (column < rows) & (query >= micro_of(column))
    stale_seen = (column >= rows) & (column < filled) & (query == 0)
    seen = fresh_seen | stale_seen
    scores = []
    for head in range(heads):
        first = 3 * HEAD_DIM * head
        for j, buffer in enumerate((keys, values)):
            lane = first + (j + 1) * HEAD_DIM
            stale_lane = (j * heads + head) * HEAD_DIM
            buffer[head, :rows] = projected[:, lane : lane + HEAD_DIM]
            buffer[head, rows:filled] = stale_ref[kept, :, stale_lane : stale_lane + HEAD_DIM]
            if filled < span:
                buffer[head, filled:] = jnp.zeros((span - filled, HEAD_DIM), jnp.bfloat16)
        queries = projected[:, first : first + HEAD_DIM]
        scores.append(
            lax.dot_general(queries, keys[head], NT, preferred_element_type=jnp.float32)
        )
    scores = [jnp.where(seen, score * HEAD_DIM ** (-0.5), -jnp.inf) for score in scores]
    tops = [jnp.max(score, axis=-1, keepdims=True) for score in scores]
    weights = [jnp.exp(score - top) for score, top in zip(scores, tops)]
    totals = [jnp.sum(weight, axis=-1, keepdims=True) for weight in weights]
    for head in range(heads):
        probs = (weights[head] * (1.0 / totals[head])).astype(jnp.bfloat16)
        attended[:, head * HEAD_DIM : (head + 1) * HEAD_DIM] = jnp.dot(
            probs, values[head], preferred_element_type=jnp.float32
        ).astype(jnp.bfloat16)


def column_blocks(place, attended, out_ref, block_refs):
    count = len(block_refs)
    columns = out_ref.shape[1] // count
    for k in range(count):
        first = pl.multiple_of((place ^ k) * columns, columns)
        block_refs[k][...] = jnp.dot(
            attended[...], out_ref[:, pl.ds(first, columns)], preferred_element_type=jnp.float32
        ).astype(jnp.bfloat16)


def first_layer_kernel(
    count, order_ref, embed_ref, heads_ref, stale_ref, out_ref, near_ref, *refs
):
    latent_refs, refs = refs[:count], refs[count:]
    block_refs, (own_ref, latents, attended, keys, values) = refs[:count], refs[count:]
    place = lax.axis_index("seq")
    rows_dev = MICRO * TOK_DEV
    width = embed_ref.shape[0]
    for k in range(count):
        first = pl.multiple_of((place ^ k) * rows_dev, rows_dev)
        latents[pl.ds(first, rows_dev), :width] = (
            latent_refs[k][...].reshape(rows_dev, width).astype(jnp.bfloat16)
        )
    embedded = jnp.dot(latents[:, :width], embed_ref[...], preferred_element_type=jnp.float32)
    embedded = embedded.astype(jnp.bfloat16).astype(jnp.float32)
    square = jnp.mean(embedded * embedded, axis=-1, keepdims=True) + norm_eps
    norm = lax.rsqrt(square)
    size = square * norm
    upper = size.astype(jnp.bfloat16).astype(jnp.float32)
    lane = lax.broadcasted_iota(jnp.int32, (latents.shape[0], width), 1)
    spare = jnp.where(lane < 2, upper, jnp.where(lane == 2, size - upper, 0.0))
    latents[:, width:] = spare.astype(jnp.bfloat16)
    projected = lax.dot_general(
        latents[...], heads_ref[...], NT, preferred_element_type=jnp.float32
    )
    projected = (norm * projected).astype(jnp.bfloat16)
    attend(projected, order_ref, stale_ref, attended, keys, values)
    columns = own_ref.shape[1]
    first = pl.multiple_of(place * columns, columns)
    own_ref[...] = jnp.dot(
        latents[:, :width], embed_ref[:, pl.ds(first, columns)], preferred_element_type=jnp.float32
    ).astype(jnp.bfloat16)
    column_blocks(place, attended, out_ref, block_refs)


def first_layer(patch_order, latents, w_embed, heads, stale, out):
    count = len(latents)
    rows = count * MICRO * TOK_DEV
    lanes, depth = out.shape
    block = jax.ShapeDtypeStruct((rows, depth // count), jnp.bfloat16)
    return pl.pallas_call(
        functools.partial(first_layer_kernel, count),
        in_specs=[whole(pltpu.SMEM)] + [whole()] * (5 + count),
        out_specs=[whole()] * (count + 1),
        out_shape=[block] * (count + 1),
        scratch_shapes=[
            pltpu.VMEM((rows, 2 * w_embed.shape[0]), jnp.bfloat16),
            *attention_scratch(rows, stale.shape[1], lanes),
        ],
        compiler_params=kernel_params(),
    )(patch_order, w_embed, heads, stale, out, met(latents[1:2]), *latents)


def turn_kernel(after_ref, qkv_ref, heads_ref, turned_ref, term_ref):
    lanes, depth = qkv_ref.shape
    for i in range(0, lanes, TILE):
        for j in range(0, depth, TILE):
            turned_ref[j : j + TILE, i : i + TILE] = qkv_ref[i : i + TILE, j : j + TILE].T
    count = heads_ref.shape[1] // 2
    for i in range(0, lanes, TILE):
        across = heads_ref[i : i + TILE, :].astype(jnp.float32).T
        term_ref[:, i : i + TILE] = across[count : count + 1] + across[count + 1 : count + 2]


def turned(qkv, heads, after):
    return pl.pallas_call(
        turn_kernel,
        in_specs=[whole(pl.ANY)] + [whole()] * 2,
        out_specs=[whole()] * 2,
        out_shape=[
            pltpu.VMEM(qkv.shape[::-1], qkv.dtype),
            jax.ShapeDtypeStruct((1, qkv.shape[0]), jnp.float32),
        ],
        cost_estimate=pl.CostEstimate(flops=5 * 10**9, bytes_accessed=0, transcendentals=0),
        compiler_params=kernel_params(),
    )(after, qkv, heads)


def meet_kernel(*refs):
    refs[-1][...] = jnp.zeros_like(refs[-1])


def met(values):
    return pl.pallas_call(
        meet_kernel,
        in_specs=[whole(pl.ANY)] * len(values),
        out_specs=whole(),
        out_shape=jax.ShapeDtypeStruct((8, 128), jnp.float32),
        compiler_params=kernel_params(),
    )(*values)


def block_sum_kernel(rows_ref, own_ref, term_ref, mark_ref, *refs):
    part_refs, block_ref = refs[:-1], refs[-1]
    columns = own_ref.shape[1]
    first = pl.multiple_of(lax.axis_index("seq") * columns, columns)
    mixed = part_refs[0][...].astype(jnp.float32)
    for part_ref in part_refs[1:]:
        mixed = mixed + part_ref[...].astype(jnp.float32)
    gate = rows_ref[2:3, pl.ds(first, columns)]
    block_ref[...] = (own_ref[...].astype(jnp.float32) + gate * mixed).astype(jnp.bfloat16)


def block_sum(mod_rows, own, term, parts):
    return pl.pallas_call(
        block_sum_kernel,
        in_specs=[whole()] * (4 + len(parts)),
        out_specs=whole(),
        out_shape=jax.ShapeDtypeStruct(own.shape, own.dtype),
        compiler_params=kernel_params(),
    )(mod_rows, own, term, met(parts[1:2]), *parts)


def scaled_piece(place, k, piece_ref, rows_ref):
    columns = piece_ref.shape[1]
    first = pl.multiple_of((place ^ k) * columns, columns)
    wide = piece_ref[...].astype(jnp.float32)
    scaled = (wide * rows_ref[1:2, pl.ds(first, columns)]).astype(jnp.bfloat16)
    return scaled, jnp.sum(wide * wide, axis=-1, keepdims=True)


def sums_kernel(numbers, rows_ref, turned_ref, *refs):
    count = len(numbers)
    piece_refs, earlier, (sums_ref, squares_ref) = refs[:count], refs[count:-2], refs[-2:]
    place = lax.axis_index("seq")
    columns = piece_refs[0].shape[1]
    squares = earlier[1][...] if earlier else 0.0
    scaled = []
    for k, piece_ref in zip(numbers, piece_refs):
        piece, square = scaled_piece(place, k, piece_ref, rows_ref)
        scaled.append((piece, pl.ds(pl.multiple_of((place ^ k) * columns, columns), columns)))
        squares = squares + square
    squares_ref[...] = squares
    for i in range(0, sums_ref.shape[1], PART):
        lane = slice(i, i + PART)
        total = earlier[0][:, lane] if earlier else 0.0
        for piece, part in scaled:
            total = total + jnp.dot(
                piece, turned_ref[part, lane], preferred_element_type=jnp.float32
            )
        sums_ref[:, lane] = total


def product_sums(numbers, pieces, mod_rows, qkv, earlier):
    rows = pieces[0].shape[0]
    lanes = qkv.shape[1]
    return pl.pallas_call(
        functools.partial(sums_kernel, numbers),
        in_specs=[whole()] * (2 + len(numbers) + len(earlier)),
        out_specs=[whole()] * 2,
        out_shape=[
            jax.ShapeDtypeStruct((rows, lanes), jnp.float32),
            jax.ShapeDtypeStruct((rows, 1), jnp.float32),
        ],
        compiler_params=kernel_params(),
    )(mod_rows, qkv, *pieces, *earlier)


def later_layer_kernel(
    count, last, order_ref, rows_ref, qkv_ref, out_ref, term_ref, stale_ref, sums_ref, squares_ref, *refs
):
    piece_refs, refs = refs[:count], refs[count:]
    block_refs, own_ref, sums, attended, keys, values, partial_out = refs[:count], *refs[count:]
    place = lax.axis_index("seq")
    scaled, squares = scaled_piece(place, count - 1, piece_refs[-1], rows_ref)
    norm = lax.rsqrt((squares_ref[...] + squares) / rows_ref.shape[1] + norm_eps)
    columns = piece_refs[-1].shape[1]
    part = pl.ds(pl.multiple_of((place ^ (count - 1)) * columns, columns), columns)
    for i in range(0, sums.shape[1], PART):
        lane = slice(i, i + PART)
        product = jnp.dot(scaled, qkv_ref[part, lane], preferred_element_type=jnp.float32)
        sums[:, lane] = (norm * (product + sums_ref[:, lane]) + term_ref[:1, lane]).astype(
            jnp.bfloat16
        )
    attend(sums, order_ref, stale_ref, attended, keys, values)
    if not last:
        column_blocks(place, attended, out_ref, block_refs)
        own_ref[...] = piece_refs[0][...]
        return
    partial_out[...] = jnp.dot(
        attended[...], out_ref[...], preferred_element_type=jnp.float32
    ).astype(jnp.bfloat16)
    rows_dev = own_ref.shape[0]
    columns = piece_refs[0].shape[1]
    own_rows = pl.ds(pl.multiple_of(place * rows_dev, rows_dev), rows_dev)
    for k in range(count):
        first = pl.multiple_of((place ^ k) * rows_dev, rows_dev)
        block_refs[k][...] = partial_out[pl.ds(first, rows_dev), :]
        first = pl.multiple_of((place ^ k) * columns, columns)
        own_ref[:, pl.ds(first, columns)] = piece_refs[k][own_rows, :]


def later_layer(last, patch_order, pieces, mod_rows, qkv, out, term, stale, sums, squares):
    count = len(pieces)
    rows, columns = pieces[0].shape
    lanes, depth = out.shape
    shape = (rows // count, depth) if last else (rows, columns)
    block = jax.ShapeDtypeStruct(shape, jnp.bfloat16)
    return pl.pallas_call(
        functools.partial(later_layer_kernel, count, last),
        in_specs=[whole(pltpu.SMEM)] + [whole()] * (7 + count),
        out_specs=[whole()] * (count + 1),
        out_shape=[block] * (count + 1),
        scratch_shapes=[
            pltpu.VMEM(sums.shape, jnp.bfloat16),
            *attention_scratch(rows, stale.shape[1], lanes),
            pltpu.VMEM((rows, depth), jnp.bfloat16),
        ],
        compiler_params=kernel_params(),
    )(patch_order, mod_rows, qkv, out, term, stale, sums, squares, *pieces)


def term_kernel(rows_ref, own_ref, final_ref, far_ref, *refs):
    part_refs, term_ref = refs[:-1], refs[-1]
    mixed = part_refs[0][...].astype(jnp.float32)
    for part_ref in part_refs[1:]:
        mixed = mixed + part_ref[...].astype(jnp.float32)
    hidden = (own_ref[...].astype(jnp.float32) + rows_ref[2:3] * mixed).astype(jnp.bfloat16)
    predicted = lax.dot_general(
        hidden, final_ref[...], NT, preferred_element_type=jnp.float32
    )
    wide = hidden.astype(jnp.float32)
    norm = lax.rsqrt(jnp.mean(wide * wide, axis=-1, keepdims=True) + norm_eps)
    predicted = norm * predicted
    weight = jnp.where(lax.axis_index("cfg") == 0, 1.0 - guide_scale, guide_scale)
    patches = [predicted[i * TOK_DEV : (i + 1) * TOK_DEV] for i in range(MICRO)]
    term = weight * jnp.concatenate(patches, axis=1)
    term_ref[...] = jnp.broadcast_to(term, term_ref.shape)


def velocity_terms(peers, mod_rows, own, final, parts):
    shape = (peers, TOK_DEV, MICRO * final.shape[0])
    return pl.pallas_call(
        term_kernel,
        in_specs=[whole()] * (4 + len(parts)),
        out_specs=whole(),
        out_shape=jax.ShapeDtypeStruct(shape, jnp.float32),
        compiler_params=kernel_params(),
    )(mod_rows, own, final, met(parts[3:]), *parts)


TAPS = 27
TAP_GROUP = 4
HALF = LAT_W // 2


def window_kernel(sizes, slab_ref, conv_ref, chosen_ref, weights_ref):
    seq_count, slab_most, token_rows = sizes
    place = lax.axis_index("seq")
    rows = seq_count * MICRO * TOK_DEV
    start = 0
    for j in range(seq_count - 1):
        start = start + jnp.where(j < place, slab_ref[j], 0)
    shape = (chosen_ref.shape[0], 2 * rows)
    target = lax.broadcasted_iota(jnp.int32, shape, 0)
    column = lax.broadcasted_iota(jnp.int32, shape, 1)
    across = target % HALF
    down = target // HALF % slab_most
    frame = target // (HALF * slab_most)
    kept = down < slab_ref[place]
    patch_rows = seq_count * TOK_DEV
    for tap in range(TAPS):
        time, row_shift, token_shift = tap // 9, tap // 3 % 3, tap % 3
        source_frame = jnp.maximum(frame + (time - 2), 0)
        row = start + down + (row_shift - 1)
        token = across + (token_shift - 1)
        inside = kept & (row >= 0) & (row < 2 * token_rows) & (token >= 0) & (token < HALF)
        row = jnp.maximum(row, 0)
        index = (source_frame * token_rows + row // 2) * HALF + jnp.maximum(token, 0)
        patch = index // patch_rows
        slot = index % patch_rows
        source = (slot // TOK_DEV * MICRO + patch) * TOK_DEV + slot % TOK_DEV + row % 2 * rows
        chosen_ref[:, tap * 2 * rows : (tap + 1) * 2 * rows] = jnp.where(
            inside & (column == source), 1.0, 0.0
        ).astype(jnp.bfloat16)
    chosen_ref[:, TAPS * 2 * rows :] = jnp.zeros(
        (shape[0], chosen_ref.shape[1] - TAPS * 2 * rows), jnp.bfloat16
    )
    weights_ref[...] = jnp.zeros_like(weights_ref)
    channels = conv_ref.shape[2]
    for tap in range(TAPS):
        for source in range(2):
            for side in range(2):
                shift = 2 * (tap % 3 - 1) + source - side + 1
                if 0 <= shift < 3:
                    first = (tap * 2 + source) * LAT_CH
                    weights_ref[first : first + LAT_CH, side * channels : (side + 1) * channels] = (
                        conv_ref[tap // 3 * 3 + shift]
                    )


def window_parts(seq_count, slab_most, token_rows, slab_rows, w_conv):
    rows = seq_count * MICRO * TOK_DEV
    groups = -(-TAPS // TAP_GROUP)
    return pl.pallas_call(
        functools.partial(window_kernel, (seq_count, slab_most, token_rows)),
        in_specs=[whole(pltpu.SMEM), whole()],
        out_specs=[whole()] * 2,
        out_shape=[
            jax.ShapeDtypeStruct(
                (FRAMES * slab_most * HALF, groups * TAP_GROUP * 2 * rows), jnp.bfloat16
            ),
            jax.ShapeDtypeStruct(
                (groups * TAP_GROUP * 2 * LAT_CH, 2 * w_conv.shape[2]), jnp.bfloat16
            ),
        ],
        compiler_params=kernel_params(),
    )(slab_rows, w_conv)


def decode_kernel(
    segment_count, count, terms_ref, chosen_ref, weights_ref, *refs
):
    latent_refs, refs = refs[:count], refs[count:]
    velocity_ref, decoded_ref, latents, tokens, halves, columns, features = refs
    place = lax.axis_index("seq")
    for k in range(count):
        latents[place ^ k] = latent_refs[k][...]

    def velocity_of(z):
        first = (z * segment_count + segment_count - 1) * 2
        both = terms_ref[first] + terms_ref[first + 1]
        width = both.shape[1] // MICRO
        return [both[:, i * width : (i + 1) * width] for i in range(MICRO)]

    for i, value in enumerate(velocity_of(place)):
        velocity_ref[i] = value
    for z in range(count):
        stepped = [
            latents[z, i] - value / SCHED_STEPS for i, value in enumerate(velocity_of(z))
        ]
        tokens[z * MICRO * TOK_DEV : (z + 1) * MICRO * TOK_DEV] = jnp.concatenate(
            stepped, axis=0
        ).astype(jnp.bfloat16)
    rows, width = tokens.shape
    half = width // 2
    halves[...] = jnp.zeros_like(halves)
    for j in range(TAP_GROUP):
        for side in range(2):
            first = (j * 2 + side) * rows
            halves[first : first + rows, j * half : (j + 1) * half] = tokens[
                :, side * half : (side + 1) * half
            ]
    depth, group_width = halves.shape
    for group in range(chosen_ref.shape[1] // depth):
        columns[:, group * group_width : (group + 1) * group_width] = jnp.dot(
            chosen_ref[:, group * depth : (group + 1) * depth],
            halves[...],
            preferred_element_type=jnp.float32,
        ).astype(jnp.bfloat16)
    result = jnp.dot(columns[...], weights_ref[...], preferred_element_type=jnp.float32)
    channels = features.shape[1]
    for side in range(2):
        features[pl.ds(side, result.shape[0], stride=2), :] = result[
            :, side * channels : (side + 1) * channels
        ]
    decoded_ref[...] = features[...].astype(jnp.bfloat16)


def decoded_slab(segment_count, terms, chosen, weights, latents):
    count = len(latents)
    rows = count * MICRO * TOK_DEV
    width = latents[0].shape[-1]
    targets = chosen.shape[0]
    channels = weights.shape[1] // 2
    return pl.pallas_call(
        functools.partial(decode_kernel, segment_count, count),
        in_specs=[whole()] * (3 + count),
        out_specs=[whole()] * 2,
        out_shape=[
            jax.ShapeDtypeStruct(latents[0].shape, jnp.float32),
            jax.ShapeDtypeStruct((2 * targets, channels), jnp.bfloat16),
        ],
        scratch_shapes=[
            pltpu.VMEM((count,) + latents[0].shape, jnp.float32),
            pltpu.VMEM((rows, width), jnp.bfloat16),
            pltpu.VMEM((TAP_GROUP * 2 * rows, TAP_GROUP * width // 2), jnp.bfloat16),
            pltpu.VMEM((targets, weights.shape[0]), jnp.bfloat16),
            pltpu.VMEM((2 * targets, channels), jnp.float32),
        ],
        compiler_params=kernel_params(),
    )(terms, chosen, weights, *latents)


def shards(
    latent,
    w_embed,
    w_qkv,
    w_out,
    mod_table,
    cond_mod,
    stale_kv,
    w_final,
    w_conv,
    patch_order,
    timestep,
    slab_rows,
):
    seq_count = lax.axis_size("seq")
    segment_count = lax.axis_size("segment")

    def within(k):
        return [(i, i ^ k) for i in range(seq_count)]

    def returned(values):
        far_first = [lax.ppermute(values[k], "seq", within(k)) for k in range(seq_count - 1, 0, -1)]
        return values[:1] + far_first[::-1]

    numbers = tuple(range(seq_count))
    half = (seq_count + 1) // 2
    latents = returned([staged(latent)] * seq_count)
    mod_rows, head_embed, out = prepared(
        timestep,
        jnp.transpose(mod_table, (1, 0, 2)),
        jnp.transpose(cond_mod[0], (1, 0, 2)),
        w_embed,
        w_qkv[0],
        w_out[0],
    )
    stale = stale_kv[0, 0, 0]
    *blocks, own = first_layer(
        patch_order, latents, w_embed, head_embed, stale, out
    )
    qkv, shift_term = turned(w_qkv[0], head_embed, own)
    for step in range(1, segment_count):
        block = block_sum(mod_rows, own, shift_term, returned(blocks))
        pieces = []
        for k in numbers[::-1]:
            pairs = [
                (i * segment_count + j, (i ^ k) * segment_count + (j + 1) % segment_count)
                for i in range(seq_count)
                for j in range(segment_count)
            ]
            pieces.insert(0, lax.ppermute(block, ("seq", "segment"), pairs))
        sums = ()
        for some in (numbers[:1], numbers[1:-1]):
            if some:
                sums = product_sums(
                    some,
                    [pieces[k] for k in some],
                    mod_rows,
                    qkv,
                    sums,
                )
        *blocks, own = later_layer(
            step + 1 == segment_count,
            patch_order,
            pieces,
            mod_rows,
            qkv,
            out,
            shift_term,
            stale,
            *sums,
        )

    blocks, slab_rows, w_conv = lax.optimization_barrier((blocks, slab_rows, w_conv))
    token_rows = MICRO * seq_count * TOK_DEV // (FRAMES * HALF)
    slab_most = 4 * token_rows // seq_count
    chosen, weights = window_parts(seq_count, slab_most, token_rows, slab_rows, w_conv)
    peers = ("seq", "segment", "cfg")
    peer_count = seq_count * segment_count * lax.axis_size("cfg")
    terms = velocity_terms(peer_count, mod_rows, own, w_final.T, returned(blocks))
    terms = lax.all_to_all(terms, peers, split_axis=0, concat_axis=0, tiled=True)
    velocity, decoded = decoded_slab(segment_count, terms, chosen, weights, latents)
    return (velocity, decoded.reshape(1, FRAMES, slab_most, LAT_W, w_conv.shape[2]))


def decoder_input(stepped, w_conv, slab_rows, seq_index, seq_count):
    token_rows = MICRO * seq_count * TOK_DEV // (FRAMES * (LAT_W // 2))
    image_rows = 2 * token_rows
    slab_most = 2 * image_rows // seq_count
    image = stepped.reshape(FRAMES, token_rows, LAT_W // 2, 2, 2, LAT_CH)
    image = (
        jnp.transpose(image, (0, 1, 3, 2, 4, 5))
        .reshape(FRAMES, image_rows, LAT_W, LAT_CH)
    )
    padded = jnp.concatenate([image[:1], image[:1], image], 0)
    padded = jnp.pad(padded, ((0, 0), (1, 1 + slab_most), (1, 1), (0, 0)))
    positions = jnp.arange(seq_count)
    slab_count = jnp.sum(jnp.where(positions == seq_index, slab_rows, 0))
    slab_start = jnp.sum(jnp.where(positions < seq_index, slab_rows, 0))
    window = lax.dynamic_slice_in_dim(padded, slab_start, slab_most + 2, 1)
    pieces = []
    for frame_shift in range(3):
        for row_shift in range(3):
            for col_shift in range(3):
                pieces.append(
                    window[
                        frame_shift : frame_shift + FRAMES,
                        row_shift : row_shift + slab_most,
                        col_shift : col_shift + LAT_W,
                    ]
                )
    columns = jnp.concatenate(pieces, -1).reshape(FRAMES * slab_most * LAT_W, 27 * LAT_CH)
    kernel = w_conv.reshape(27 * LAT_CH, w_conv.shape[2])
    features = jnp.dot(columns, kernel, preferred_element_type=jnp.float32).astype(jnp.bfloat16)
    features = features.reshape(FRAMES, slab_most, LAT_W, w_conv.shape[2])
    row_valid = jnp.arange(slab_most)[None, :, None, None] < slab_count
    decoded = jnp.where(row_valid, features, jnp.zeros_like(features))
    return decoded[None]


def solution(mesh):
    in_specs = (
        P(None, ("groups", "seq"), None),
        P(),
        P("segment", "seq", None),
        P("segment", "seq", None),
        P(),
        P("cfg", ("groups", "segment"), None, None),
        P("segment", "cfg", "seq", None, "groups", None),
        P(),
        P(None, None, ("segment", "cfg")),
        P("groups"),
        P("groups"),
        P("groups"),
    )
    out_specs = (
        P(None, ("groups", "seq"), None),
        P(("groups", "seq"), None, None, None, ("segment", "cfg")),
    )
    whole_groups = 2 <= mesh.shape["seq"] <= 8
    program = shards if whole_groups else cycled_shards
    return jax.shard_map(program, mesh=mesh, in_specs=in_specs, out_specs=out_specs, check_vma=False)
```

```python
import functools

import jax
import jax.numpy as jnp
from jax import lax
from jax.experimental import pallas as pl
from jax.experimental.pallas import tpu as pltpu
from jax.sharding import PartitionSpec as P

HEADS = 24
HEAD_DIM = 128
D = 3072
LAT_CH = 16
SCHED_STEPS = 50
MICRO = 2
TOK_DEV = 8
FRAMES = 4
LAT_W = 8


guide_scale = 5.0
norm_eps = 1e-06


def swapped(value, axis, bit):
    return lax.ppermute(value, axis, [(i, i ^ 1 << bit) for i in range(lax.axis_size(axis))])


def passed_along(value, axis, by):
    size = lax.axis_size(axis)
    pairs = [(i, i + by) for i in range(size) if 0 <= i + by < size]
    return lax.ppermute(value, axis, pairs)


def rms_scaled(values):
    wide = values.astype(jnp.float32)
    return wide * lax.rsqrt(jnp.mean(wide * wide, axis=-1, keepdims=True) + norm_eps)


def cycle_join(piece, seq_index, cycle_bits):
    joined = piece
    for bit_number in range(cycle_bits):
        partner = swapped(joined, "seq", bit_number)
        upper_half = (seq_index // 2**bit_number % 2).astype(jnp.int32)
        part_rows = joined.shape[0]
        combined = jnp.zeros((2 * part_rows,) + joined.shape[1:], joined.dtype)
        combined = lax.dynamic_update_slice_in_dim(combined, joined, upper_half * part_rows, 0)
        joined = lax.dynamic_update_slice_in_dim(combined, partner, (1 - upper_half) * part_rows, 0)
    return joined


def cycled_shards(
    latent,
    w_embed,
    w_qkv,
    w_out,
    mod_table,
    cond_mod,
    stale_kv,
    w_final,
    w_conv,
    patch_order,
    timestep,
    slab_rows,
):
    seq_count = lax.axis_size("seq")
    segment_count = lax.axis_size("segment")
    seq_index = lax.axis_index("seq")
    segment_index = lax.axis_index("segment")
    branch_index = lax.axis_index("cfg")
    group_count = min(seq_count, 8)
    cycle_size = seq_count // group_count
    cycle_bits = cycle_size.bit_length() - 1
    group_heads = HEADS // group_count
    sub_rows = TOK_DEV // cycle_size
    share_rows = seq_count * sub_rows
    kv_lanes = 2 * group_heads * HEAD_DIM
    table_row = lax.dynamic_index_in_dim(mod_table, timestep[0], 0, keepdims=False).astype(
        jnp.float32
    )
    modulation = table_row + cond_mod[0, 0]
    shift_row = modulation[0]
    scale_row = modulation[1]
    gate_row = modulation[2]
    joined_weights = (
        cycle_join(w_qkv[0], seq_index, cycle_bits),
        cycle_join(w_out[0], seq_index, cycle_bits),
    )
    stale_joined = cycle_join(stale_kv[0, 0], seq_index, cycle_bits)
    cache = jnp.transpose(stale_joined, (1, 0, 2, 3)).reshape(
        MICRO, cycle_size * share_rows, kv_lanes
    )
    received = jnp.zeros((TOK_DEV, D), jnp.bfloat16)
    finished = jnp.zeros((MICRO, TOK_DEV, D), jnp.bfloat16)
    slot_ids = jnp.arange(MICRO)
    tick_count = MICRO + segment_count - 1
    for tick_index in range(tick_count):
        qkv_rows, out_rows = joined_weights
        micro_index = tick_index - segment_index
        active = (micro_index >= 0) & (micro_index < MICRO)
        clipped = jnp.clip(micro_index, 0, MICRO - 1)
        patch_id = jnp.sum(jnp.where(slot_ids == clipped, patch_order, 0))
        own_latent = lax.dynamic_index_in_dim(latent, patch_id, 0, keepdims=False).astype(
            jnp.bfloat16
        )
        embedded = jnp.dot(own_latent, w_embed, preferred_element_type=jnp.float32).astype(
            jnp.bfloat16
        )
        layer_input = jnp.where(segment_index == 0, embedded, received)
        normed = (rms_scaled(layer_input) * (1.0 + scale_row) + shift_row).astype(jnp.bfloat16)
        outgoing = jnp.broadcast_to(
            normed.reshape(1, cycle_size, sub_rows, D), (group_count, cycle_size, sub_rows, D)
        )
        shared = lax.all_to_all(
            outgoing.reshape(share_rows, D), "seq", split_axis=0, concat_axis=0, tiled=True
        )
        projected = lax.dot_general(
            shared, qkv_rows, (((1,), (1,)), ((), ())), preferred_element_type=jnp.float32
        )
        projected = projected.astype(jnp.bfloat16).reshape(share_rows, group_heads, 3, HEAD_DIM)
        queries = projected[:, :, 0]
        fresh_local = jnp.transpose(projected[:, :, 1:], (0, 2, 1, 3)).reshape(
            1, share_rows, kv_lanes
        )
        fresh = cycle_join(fresh_local, seq_index, cycle_bits).reshape(
            cycle_size * share_rows, kv_lanes
        )
        previous = lax.dynamic_index_in_dim(cache, patch_id, 0, keepdims=False)
        cache = lax.dynamic_update_index_in_dim(
            cache, jnp.where(active, fresh, previous), patch_id, 0
        )
        keyvals = cache.reshape(MICRO * cycle_size * share_rows, 2, group_heads, HEAD_DIM)
        scores = jnp.einsum(
            "shd,khd->hsk", queries, keyvals[:, 0], preferred_element_type=jnp.float32
        ) * HEAD_DIM ** (-0.5)
        probs = jax.nn.softmax(scores, axis=-1).astype(jnp.bfloat16)
        attended = jnp.einsum(
            "hsk,khd->shd", probs, keyvals[:, 1], preferred_element_type=jnp.float32
        ).astype(jnp.bfloat16)
        partial_out = jnp.dot(
            attended.reshape(share_rows, group_heads * HEAD_DIM),
            out_rows,
            preferred_element_type=jnp.float32,
        )
        returned = lax.all_to_all(
            partial_out.astype(jnp.bfloat16), "seq", split_axis=0, concat_axis=0, tiled=True
        ).astype(partial_out.dtype)
        mixed = jnp.sum(returned.reshape(group_count, cycle_size, sub_rows, D), axis=0).reshape(
            TOK_DEV, D
        )
        layer_output = (layer_input.astype(jnp.float32) + gate_row * mixed).astype(jnp.bfloat16)
        keep_final = active & (segment_index == segment_count - 1)
        earlier = lax.dynamic_index_in_dim(finished, patch_id, 0, keepdims=False)
        finished = lax.dynamic_update_index_in_dim(
            finished, jnp.where(keep_final, layer_output, earlier), patch_id, 0
        )
        if tick_index + 1 < tick_count:
            received = passed_along(layer_output, "segment", 1)
    final_normed = rms_scaled(finished).astype(jnp.bfloat16)
    predicted = jnp.einsum("mtd,dc->mtc", final_normed, w_final, preferred_element_type=jnp.float32)
    is_last = segment_index == segment_count - 1
    branch_weight = jnp.where(branch_index == 0, 1.0 - guide_scale, guide_scale)
    velocity_term = jnp.where(is_last, branch_weight * predicted, 0.0)
    latent_term = jnp.where(is_last & (branch_index == 0), latent, 0.0)
    velocity_own, latent_own = lax.psum((velocity_term, latent_term), ("segment", "cfg"))
    velocity_full, latent_full = (
        lax.all_gather(velocity_own, "seq", axis=1, tiled=True),
        lax.all_gather(latent_own, "seq", axis=1, tiled=True),
    )
    stepped = (latent_full - velocity_full / SCHED_STEPS).astype(jnp.bfloat16)
    decoded = decoder_input(stepped, w_conv, slab_rows, seq_index, seq_count)
    return (velocity_own, decoded)


NT = (((1,), (1,)), ((), ()))
TILE = 256
PART = 768
AHEAD = 4


def kernel_params(mebibytes=8):
    return pltpu.CompilerParams(vmem_limit_bytes=mebibytes * 2**20)


def whole(space=pltpu.VMEM):
    return pl.BlockSpec(memory_space=space)


def in_order(copies, ahead):
    for copy in copies[:ahead]:
        copy.start()

    def landed():
        for i, copy in enumerate(copies):
            copy.wait()
            if i + ahead < len(copies):
                copies[i + ahead].start()
            yield i

    return landed()


def in_hbm(*values):
    return [pltpu.with_memory_space_constraint(value, pltpu.HBM) for value in values]


def stage_kernel(latent_hbm, staged_ref, sem):
    copy = pltpu.make_async_copy(latent_hbm, staged_ref, sem)
    copy.start()
    copy.wait()


def staged(latent):
    return pl.pallas_call(
        stage_kernel,
        in_specs=[whole(pltpu.HBM)],
        out_specs=whole(),
        out_shape=pltpu.VMEM(latent.shape, latent.dtype),
        scratch_shapes=[pltpu.SemaphoreType.DMA],
        cost_estimate=pl.CostEstimate(flops=10**10, bytes_accessed=0, transcendentals=0),
        compiler_params=kernel_params(),
    )(*in_hbm(latent))


def prepare_kernel(
    timestep_ref, table_ref, cond_ref, embed_ref, qkv_ref, out_hbm, rows_ref, heads_ref, out_ref, lhs, sem
):
    out_copy = pltpu.make_async_copy(out_hbm, out_ref, sem)
    out_copy.start()
    steps = table_ref.shape[1]
    chosen = lax.broadcasted_iota(jnp.int32, (16, steps), 1) == timestep_ref[0]
    chosen = jnp.where(chosen, 1.0, 0.0).astype(jnp.bfloat16)
    for j in range(3):
        row = jnp.dot(chosen, table_ref[j], preferred_element_type=jnp.float32)[:1]
        rows_ref[j : j + 1, :] = row + cond_ref[j] + (1.0 if j == 1 else 0.0)
    count = embed_ref.shape[0]
    spare, depth = lhs.shape[0] - count, lhs.shape[1]
    lhs[:count] = (embed_ref[...].astype(jnp.float32) * rows_ref[1:2]).astype(jnp.bfloat16)
    lhs[count:] = jnp.broadcast_to(rows_ref[0:1], (spare, depth)).astype(jnp.bfloat16)
    lane = lax.broadcasted_iota(jnp.int32, (PART, lhs.shape[0]), 1)
    for j in range(0, qkv_ref.shape[0], PART):
        product = lax.dot_general(
            qkv_ref[j : j + PART, :], lhs[...], NT, preferred_element_type=jnp.float32
        )
        upper = product.astype(jnp.bfloat16).astype(jnp.float32)
        value = jnp.where(lane == count + 1, product - upper, upper)
        heads_ref[j : j + PART, :] = jnp.where(lane <= count + 2, value, 0.0).astype(jnp.bfloat16)
    out_copy.wait()


def prepared(timestep, table, cond, w_embed, qkv, out):
    count, depth = w_embed.shape
    lanes = qkv.shape[0]
    return pl.pallas_call(
        prepare_kernel,
        in_specs=[whole(pltpu.SMEM)] + [whole()] * 4 + [whole(pltpu.HBM)],
        out_specs=[whole()] * 3,
        out_shape=[
            jax.ShapeDtypeStruct((3, depth), jnp.float32),
            jax.ShapeDtypeStruct((lanes, 2 * count), jnp.bfloat16),
            pltpu.VMEM(out.shape, out.dtype),
        ],
        scratch_shapes=[
            pltpu.VMEM((2 * count, depth), jnp.bfloat16),
            pltpu.SemaphoreType.DMA,
        ],
        compiler_params=kernel_params(),
    )(timestep, table, cond, w_embed, qkv, *in_hbm(out))


def span_of(rows, patch_rows):
    return -(-(rows + patch_rows) // 128) * 128


def attention_scratch(rows, patch_rows, lanes):
    shape = (lanes // HEAD_DIM, span_of(rows, patch_rows), HEAD_DIM)
    return [pltpu.VMEM((rows, lanes), jnp.bfloat16)] + [pltpu.VMEM(shape, jnp.bfloat16)] * 2


def attend(projected, order_ref, stale_ref, attended, keys, values):
    rows = projected.shape[0]
    patch_rows = stale_ref.shape[1]
    heads, span, _ = keys.shape
    kept = order_ref[1]
    filled = rows + patch_rows

    def micro_of(index):
        return jnp.where(index // TOK_DEV % MICRO == kept, 1, 0)

    query = micro_of(lax.broadcasted_iota(jnp.int32, (rows, span), 0))
    column = lax.broadcasted_iota(jnp.int32, (rows, span), 1)
    fresh_seen = (column < rows) & (query >= micro_of(column))
    stale_seen = (column >= rows) & (column < filled) & (query == 0)
    seen = fresh_seen | stale_seen
    scores = []
    for head in range(heads):
        first = 3 * HEAD_DIM * head
        for j, buffer in enumerate((keys, values)):
            lane = first + (j + 1) * HEAD_DIM
            stale_lane = (j * heads + head) * HEAD_DIM
            buffer[head, :rows] = projected[:, lane : lane + HEAD_DIM]
            buffer[head, rows:filled] = stale_ref[kept, :, stale_lane : stale_lane + HEAD_DIM]
            if filled < span:
                buffer[head, filled:] = jnp.zeros((span - filled, HEAD_DIM), jnp.bfloat16)
        queries = projected[:, first : first + HEAD_DIM]
        scores.append(
            lax.dot_general(queries, keys[head], NT, preferred_element_type=jnp.float32)
        )
    scores = [jnp.where(seen, score * HEAD_DIM ** (-0.5), -jnp.inf) for score in scores]
    tops = [jnp.max(score, axis=-1, keepdims=True) for score in scores]
    weights = [jnp.exp(score - top) for score, top in zip(scores, tops)]
    totals = [jnp.sum(weight, axis=-1, keepdims=True) for weight in weights]
    for head in range(heads):
        probs = (weights[head] * (1.0 / totals[head])).astype(jnp.bfloat16)
        attended[:, head * HEAD_DIM : (head + 1) * HEAD_DIM] = jnp.dot(
            probs, values[head], preferred_element_type=jnp.float32
        ).astype(jnp.bfloat16)


def column_blocks(place, attended, out_ref, block_refs):
    count = len(block_refs)
    columns = out_ref.shape[1] // count
    for k in range(count):
        first = pl.multiple_of((place ^ k) * columns, columns)
        block_refs[k][...] = jnp.dot(
            attended[...], out_ref[:, pl.ds(first, columns)], preferred_element_type=jnp.float32
        ).astype(jnp.bfloat16)


def first_layer_kernel(
    count, order_ref, embed_ref, heads_ref, stale_ref, out_ref, near_ref, *refs
):
    latent_refs, refs = refs[:count], refs[count:]
    block_refs, (own_ref, latents, attended, keys, values) = refs[:count], refs[count:]
    place = lax.axis_index("seq")
    rows_dev = MICRO * TOK_DEV
    width = embed_ref.shape[0]
    for k in range(count):
        first = pl.multiple_of((place ^ k) * rows_dev, rows_dev)
        latents[pl.ds(first, rows_dev), :width] = (
            latent_refs[k][...].reshape(rows_dev, width).astype(jnp.bfloat16)
        )
    embedded = jnp.dot(latents[:, :width], embed_ref[...], preferred_element_type=jnp.float32)
    embedded = embedded.astype(jnp.bfloat16).astype(jnp.float32)
    square = jnp.mean(embedded * embedded, axis=-1, keepdims=True) + norm_eps
    norm = lax.rsqrt(square)
    size = square * norm
    upper = size.astype(jnp.bfloat16).astype(jnp.float32)
    lane = lax.broadcasted_iota(jnp.int32, (latents.shape[0], width), 1)
    spare = jnp.where(lane < 2, upper, jnp.where(lane == 2, size - upper, 0.0))
    latents[:, width:] = spare.astype(jnp.bfloat16)
    projected = lax.dot_general(
        latents[...], heads_ref[...], NT, preferred_element_type=jnp.float32
    )
    projected = (norm * projected).astype(jnp.bfloat16)
    attend(projected, order_ref, stale_ref, attended, keys, values)
    columns = own_ref.shape[1]
    first = pl.multiple_of(place * columns, columns)
    own_ref[...] = jnp.dot(
        latents[:, :width], embed_ref[:, pl.ds(first, columns)], preferred_element_type=jnp.float32
    ).astype(jnp.bfloat16)
    column_blocks(place, attended, out_ref, block_refs)


def first_layer(patch_order, latents, w_embed, heads, stale, out):
    count = len(latents)
    rows = count * MICRO * TOK_DEV
    lanes, depth = out.shape
    block = jax.ShapeDtypeStruct((rows, depth // count), jnp.bfloat16)
    return pl.pallas_call(
        functools.partial(first_layer_kernel, count),
        in_specs=[whole(pltpu.SMEM)] + [whole()] * (5 + count),
        out_specs=[whole()] * (count + 1),
        out_shape=[block] * (count + 1),
        scratch_shapes=[
            pltpu.VMEM((rows, 2 * w_embed.shape[0]), jnp.bfloat16),
            *attention_scratch(rows, stale.shape[1], lanes),
        ],
        compiler_params=kernel_params(),
    )(patch_order, w_embed, heads, stale, out, met(latents[1:2]), *latents)


def turn_kernel(after_ref, qkv_ref, heads_ref, turned_ref, term_ref):
    lanes, depth = qkv_ref.shape
    for i in range(0, lanes, TILE):
        for j in range(0, depth, TILE):
            turned_ref[j : j + TILE, i : i + TILE] = qkv_ref[i : i + TILE, j : j + TILE].T
    count = heads_ref.shape[1] // 2
    for i in range(0, lanes, TILE):
        across = heads_ref[i : i + TILE, :].astype(jnp.float32).T
        term_ref[:, i : i + TILE] = across[count : count + 1] + across[count + 1 : count + 2]


def turned(qkv, heads, after):
    return pl.pallas_call(
        turn_kernel,
        in_specs=[whole(pl.ANY)] + [whole()] * 2,
        out_specs=[whole()] * 2,
        out_shape=[
            pltpu.VMEM(qkv.shape[::-1], qkv.dtype),
            jax.ShapeDtypeStruct((1, qkv.shape[0]), jnp.float32),
        ],
        cost_estimate=pl.CostEstimate(flops=5 * 10**9, bytes_accessed=0, transcendentals=0),
        compiler_params=kernel_params(),
    )(after, qkv, heads)


def meet_kernel(*refs):
    refs[-1][...] = jnp.zeros_like(refs[-1])


def met(values):
    return pl.pallas_call(
        meet_kernel,
        in_specs=[whole(pl.ANY)] * len(values),
        out_specs=whole(),
        out_shape=jax.ShapeDtypeStruct((8, 128), jnp.float32),
        compiler_params=kernel_params(),
    )(*values)


def block_sum_kernel(rows_ref, own_ref, term_ref, *refs):
    part_refs, block_ref = refs[:-1], refs[-1]
    columns = own_ref.shape[1]
    first = pl.multiple_of(lax.axis_index("seq") * columns, columns)
    mixed = part_refs[0][...].astype(jnp.float32)
    for part_ref in part_refs[1:]:
        mixed = mixed + part_ref[...].astype(jnp.float32)
    gate = rows_ref[2:3, pl.ds(first, columns)]
    block_ref[...] = (own_ref[...].astype(jnp.float32) + gate * mixed).astype(jnp.bfloat16)


def block_sum(mod_rows, own, term, parts):
    return pl.pallas_call(
        block_sum_kernel,
        in_specs=[whole()] * (3 + len(parts)),
        out_specs=whole(),
        out_shape=jax.ShapeDtypeStruct(own.shape, own.dtype),
        compiler_params=kernel_params(),
    )(mod_rows, own, term, *parts)


def scaled_piece(place, k, piece_ref, rows_ref):
    columns = piece_ref.shape[1]
    first = pl.multiple_of((place ^ k) * columns, columns)
    wide = piece_ref[...].astype(jnp.float32)
    scaled = (wide * rows_ref[1:2, pl.ds(first, columns)]).astype(jnp.bfloat16)
    return scaled, jnp.sum(wide * wide, axis=-1, keepdims=True)


def sums_kernel(numbers, rows_ref, turned_ref, *refs):
    count = len(numbers)
    piece_refs, earlier, (sums_ref, squares_ref) = refs[:count], refs[count:-2], refs[-2:]
    place = lax.axis_index("seq")
    columns = piece_refs[0].shape[1]
    squares = earlier[1][...] if earlier else 0.0
    scaled = []
    for k, piece_ref in zip(numbers, piece_refs):
        piece, square = scaled_piece(place, k, piece_ref, rows_ref)
        scaled.append((piece, pl.ds(pl.multiple_of((place ^ k) * columns, columns), columns)))
        squares = squares + square
    squares_ref[...] = squares
    for i in range(0, sums_ref.shape[1], PART):
        lane = slice(i, i + PART)
        total = earlier[0][:, lane] if earlier else 0.0
        for piece, part in scaled:
            total = total + jnp.dot(
                piece, turned_ref[part, lane], preferred_element_type=jnp.float32
            )
        sums_ref[:, lane] = total


def product_sums(numbers, pieces, mod_rows, qkv, earlier):
    rows = pieces[0].shape[0]
    lanes = qkv.shape[1]
    return pl.pallas_call(
        functools.partial(sums_kernel, numbers),
        in_specs=[whole()] * (2 + len(numbers) + len(earlier)),
        out_specs=[whole()] * 2,
        out_shape=[
            jax.ShapeDtypeStruct((rows, lanes), jnp.float32),
            jax.ShapeDtypeStruct((rows, 1), jnp.float32),
        ],
        compiler_params=kernel_params(),
    )(mod_rows, qkv, *pieces, *earlier)


def later_layer_kernel(
    count, last, order_ref, rows_ref, qkv_ref, out_ref, term_ref, stale_ref, sums_ref, squares_ref, *refs
):
    piece_refs, refs = refs[:count], refs[count:]
    block_refs, own_ref, sums, attended, keys, values, partial_out = refs[:count], *refs[count:]
    place = lax.axis_index("seq")
    scaled, squares = scaled_piece(place, count - 1, piece_refs[-1], rows_ref)
    norm = lax.rsqrt((squares_ref[...] + squares) / rows_ref.shape[1] + norm_eps)
    columns = piece_refs[-1].shape[1]
    part = pl.ds(pl.multiple_of((place ^ (count - 1)) * columns, columns), columns)
    for i in range(0, sums.shape[1], PART):
        lane = slice(i, i + PART)
        product = jnp.dot(scaled, qkv_ref[part, lane], preferred_element_type=jnp.float32)
        sums[:, lane] = (norm * (product + sums_ref[:, lane]) + term_ref[:1, lane]).astype(
            jnp.bfloat16
        )
    attend(sums, order_ref, stale_ref, attended, keys, values)
    if not last:
        column_blocks(place, attended, out_ref, block_refs)
        own_ref[...] = piece_refs[0][...]
        return
    partial_out[...] = jnp.dot(
        attended[...], out_ref[...], preferred_element_type=jnp.float32
    ).astype(jnp.bfloat16)
    rows_dev = own_ref.shape[0]
    columns = piece_refs[0].shape[1]
    own_rows = pl.ds(pl.multiple_of(place * rows_dev, rows_dev), rows_dev)
    for k in range(count):
        first = pl.multiple_of((place ^ k) * rows_dev, rows_dev)
        block_refs[k][...] = partial_out[pl.ds(first, rows_dev), :]
        first = pl.multiple_of((place ^ k) * columns, columns)
        own_ref[:, pl.ds(first, columns)] = piece_refs[k][own_rows, :]


def later_layer(last, patch_order, pieces, mod_rows, qkv, out, term, stale, sums, squares):
    count = len(pieces)
    rows, columns = pieces[0].shape
    lanes, depth = out.shape
    shape = (rows // count, depth) if last else (rows, columns)
    block = jax.ShapeDtypeStruct(shape, jnp.bfloat16)
    return pl.pallas_call(
        functools.partial(later_layer_kernel, count, last),
        in_specs=[whole(pltpu.SMEM)] + [whole()] * (7 + count),
        out_specs=[whole()] * (count + 1),
        out_shape=[block] * (count + 1),
        scratch_shapes=[
            pltpu.VMEM(sums.shape, jnp.bfloat16),
            *attention_scratch(rows, stale.shape[1], lanes),
            pltpu.VMEM((rows, depth), jnp.bfloat16),
        ],
        compiler_params=kernel_params(),
    )(patch_order, mod_rows, qkv, out, term, stale, sums, squares, *pieces)


def term_kernel(rows_ref, own_ref, final_ref, far_ref, *refs):
    part_refs, term_ref = refs[:-1], refs[-1]
    mixed = part_refs[0][...].astype(jnp.float32)
    for part_ref in part_refs[1:]:
        mixed = mixed + part_ref[...].astype(jnp.float32)
    hidden = (own_ref[...].astype(jnp.float32) + rows_ref[2:3] * mixed).astype(jnp.bfloat16)
    predicted = lax.dot_general(
        hidden, final_ref[...], NT, preferred_element_type=jnp.float32
    )
    wide = hidden.astype(jnp.float32)
    norm = lax.rsqrt(jnp.mean(wide * wide, axis=-1, keepdims=True) + norm_eps)
    predicted = norm * predicted
    weight = jnp.where(lax.axis_index("cfg") == 0, 1.0 - guide_scale, guide_scale)
    patches = [predicted[i * TOK_DEV : (i + 1) * TOK_DEV] for i in range(MICRO)]
    term = weight * jnp.concatenate(patches, axis=1)
    term_ref[...] = jnp.broadcast_to(term, term_ref.shape)


def velocity_terms(peers, mod_rows, own, final, parts):
    shape = (peers, TOK_DEV, MICRO * final.shape[0])
    return pl.pallas_call(
        term_kernel,
        in_specs=[whole()] * (4 + len(parts)),
        out_specs=whole(),
        out_shape=jax.ShapeDtypeStruct(shape, jnp.float32),
        compiler_params=kernel_params(),
    )(mod_rows, own, final, met(parts[3:]), *parts)


TAPS = 27
TAP_GROUP = 4
HALF = LAT_W // 2


def window_kernel(sizes, slab_ref, conv_ref, chosen_ref, weights_ref):
    seq_count, slab_most, token_rows = sizes
    place = lax.axis_index("seq")
    rows = seq_count * MICRO * TOK_DEV
    start = 0
    for j in range(seq_count - 1):
        start = start + jnp.where(j < place, slab_ref[j], 0)
    shape = (chosen_ref.shape[0], 2 * rows)
    target = lax.broadcasted_iota(jnp.int32, shape, 0)
    column = lax.broadcasted_iota(jnp.int32, shape, 1)
    across = target % HALF
    down = target // HALF % slab_most
    frame = target // (HALF * slab_most)
    kept = down < slab_ref[place]
    patch_rows = seq_count * TOK_DEV
    for tap in range(TAPS):
        time, row_shift, token_shift = tap // 9, tap // 3 % 3, tap % 3
        source_frame = jnp.maximum(frame + (time - 2), 0)
        row = start + down + (row_shift - 1)
        token = across + (token_shift - 1)
        inside = kept & (row >= 0) & (row < 2 * token_rows) & (token >= 0) & (token < HALF)
        row = jnp.maximum(row, 0)
        index = (source_frame * token_rows + row // 2) * HALF + jnp.maximum(token, 0)
        patch = index // patch_rows
        slot = index % patch_rows
        source = (slot // TOK_DEV * MICRO + patch) * TOK_DEV + slot % TOK_DEV + row % 2 * rows
        chosen_ref[:, tap * 2 * rows : (tap + 1) * 2 * rows] = jnp.where(
            inside & (column == source), 1.0, 0.0
        ).astype(jnp.bfloat16)
    chosen_ref[:, TAPS * 2 * rows :] = jnp.zeros(
        (shape[0], chosen_ref.shape[1] - TAPS * 2 * rows), jnp.bfloat16
    )
    weights_ref[...] = jnp.zeros_like(weights_ref)
    channels = conv_ref.shape[2]
    for tap in range(TAPS):
        for source in range(2):
            for side in range(2):
                shift = 2 * (tap % 3 - 1) + source - side + 1
                if 0 <= shift < 3:
                    first = (tap * 2 + source) * LAT_CH
                    weights_ref[first : first + LAT_CH, side * channels : (side + 1) * channels] = (
                        conv_ref[tap // 3 * 3 + shift]
                    )


def window_parts(seq_count, slab_most, token_rows, slab_rows, w_conv):
    rows = seq_count * MICRO * TOK_DEV
    groups = -(-TAPS // TAP_GROUP)
    return pl.pallas_call(
        functools.partial(window_kernel, (seq_count, slab_most, token_rows)),
        in_specs=[whole(pltpu.SMEM), whole()],
        out_specs=[whole()] * 2,
        out_shape=[
            jax.ShapeDtypeStruct(
                (FRAMES * slab_most * HALF, groups * TAP_GROUP * 2 * rows), jnp.bfloat16
            ),
            jax.ShapeDtypeStruct(
                (groups * TAP_GROUP * 2 * LAT_CH, 2 * w_conv.shape[2]), jnp.bfloat16
            ),
        ],
        compiler_params=kernel_params(),
    )(slab_rows, w_conv)


def decode_kernel(
    segment_count, count, terms_ref, chosen_ref, weights_ref, *refs
):
    latent_refs, refs = refs[:count], refs[count:]
    velocity_ref, decoded_ref, latents, tokens, halves, columns, features = refs
    place = lax.axis_index("seq")
    for k in range(count):
        latents[place ^ k] = latent_refs[k][...]

    def velocity_of(z):
        first = (z * segment_count + segment_count - 1) * 2
        both = terms_ref[first] + terms_ref[first + 1]
        width = both.shape[1] // MICRO
        return [both[:, i * width : (i + 1) * width] for i in range(MICRO)]

    for i, value in enumerate(velocity_of(place)):
        velocity_ref[i] = value
    for z in range(count):
        stepped = [
            latents[z, i] - value / SCHED_STEPS for i, value in enumerate(velocity_of(z))
        ]
        tokens[z * MICRO * TOK_DEV : (z + 1) * MICRO * TOK_DEV] = jnp.concatenate(
            stepped, axis=0
        ).astype(jnp.bfloat16)
    rows, width = tokens.shape
    half = width // 2
    halves[...] = jnp.zeros_like(halves)
    for j in range(TAP_GROUP):
        for side in range(2):
            first = (j * 2 + side) * rows
            halves[first : first + rows, j * half : (j + 1) * half] = tokens[
                :, side * half : (side + 1) * half
            ]
    depth, group_width = halves.shape
    for group in range(chosen_ref.shape[1] // depth):
        columns[:, group * group_width : (group + 1) * group_width] = jnp.dot(
            chosen_ref[:, group * depth : (group + 1) * depth],
            halves[...],
            preferred_element_type=jnp.float32,
        ).astype(jnp.bfloat16)
    result = jnp.dot(columns[...], weights_ref[...], preferred_element_type=jnp.float32)
    channels = features.shape[1]
    for side in range(2):
        features[pl.ds(side, result.shape[0], stride=2), :] = result[
            :, side * channels : (side + 1) * channels
        ]
    decoded_ref[...] = features[...].astype(jnp.bfloat16)


def decoded_slab(segment_count, terms, chosen, weights, latents):
    count = len(latents)
    rows = count * MICRO * TOK_DEV
    width = latents[0].shape[-1]
    targets = chosen.shape[0]
    channels = weights.shape[1] // 2
    return pl.pallas_call(
        functools.partial(decode_kernel, segment_count, count),
        in_specs=[whole()] * (3 + count),
        out_specs=[whole()] * 2,
        out_shape=[
            jax.ShapeDtypeStruct(latents[0].shape, jnp.float32),
            jax.ShapeDtypeStruct((2 * targets, channels), jnp.bfloat16),
        ],
        scratch_shapes=[
            pltpu.VMEM((count,) + latents[0].shape, jnp.float32),
            pltpu.VMEM((rows, width), jnp.bfloat16),
            pltpu.VMEM((TAP_GROUP * 2 * rows, TAP_GROUP * width // 2), jnp.bfloat16),
            pltpu.VMEM((targets, weights.shape[0]), jnp.bfloat16),
            pltpu.VMEM((2 * targets, channels), jnp.float32),
        ],
        compiler_params=kernel_params(),
    )(terms, chosen, weights, *latents)


def shards(
    latent,
    w_embed,
    w_qkv,
    w_out,
    mod_table,
    cond_mod,
    stale_kv,
    w_final,
    w_conv,
    patch_order,
    timestep,
    slab_rows,
):
    seq_count = lax.axis_size("seq")
    segment_count = lax.axis_size("segment")

    def within(k):
        return [(i, i ^ k) for i in range(seq_count)]

    def returned(values):
        far_first = [lax.ppermute(values[k], "seq", within(k)) for k in range(seq_count - 1, 0, -1)]
        return values[:1] + far_first[::-1]

    numbers = tuple(range(seq_count))
    half = (seq_count + 1) // 2
    latents = returned([staged(latent)] * seq_count)
    mod_rows, head_embed, out = prepared(
        timestep,
        jnp.transpose(mod_table, (1, 0, 2)),
        jnp.transpose(cond_mod[0], (1, 0, 2)),
        w_embed,
        w_qkv[0],
        w_out[0],
    )
    stale = stale_kv[0, 0, 0]
    *blocks, own = first_layer(
        patch_order, latents, w_embed, head_embed, stale, out
    )
    qkv, shift_term = turned(w_qkv[0], head_embed, own)
    for step in range(1, segment_count):
        block = block_sum(mod_rows, own, shift_term, returned(blocks))
        pieces = []
        for k in numbers[::-1]:
            pairs = [
                (i * segment_count + j, (i ^ k) * segment_count + (j + 1) % segment_count)
                for i in range(seq_count)
                for j in range(segment_count)
            ]
            pieces.insert(0, lax.ppermute(block, ("seq", "segment"), pairs))
        sums = ()
        for some in (numbers[:1], numbers[1:-1]):
            if some:
                sums = product_sums(
                    some,
                    [pieces[k] for k in some],
                    mod_rows,
                    qkv,
                    sums,
                )
        *blocks, own = later_layer(
            step + 1 == segment_count,
            patch_order,
            pieces,
            mod_rows,
            qkv,
            out,
            shift_term,
            stale,
            *sums,
        )

    blocks, slab_rows, w_conv = lax.optimization_barrier((blocks, slab_rows, w_conv))
    token_rows = MICRO * seq_count * TOK_DEV // (FRAMES * HALF)
    slab_most = 4 * token_rows // seq_count
    chosen, weights = window_parts(seq_count, slab_most, token_rows, slab_rows, w_conv)
    peers = ("seq", "segment", "cfg")
    peer_count = seq_count * segment_count * lax.axis_size("cfg")
    terms = velocity_terms(peer_count, mod_rows, own, w_final.T, returned(blocks))
    terms = lax.all_to_all(terms, peers, split_axis=0, concat_axis=0, tiled=True)
    velocity, decoded = decoded_slab(segment_count, terms, chosen, weights, latents)
    return (velocity, decoded.reshape(1, FRAMES, slab_most, LAT_W, w_conv.shape[2]))


def decoder_input(stepped, w_conv, slab_rows, seq_index, seq_count):
    token_rows = MICRO * seq_count * TOK_DEV // (FRAMES * (LAT_W // 2))
    image_rows = 2 * token_rows
    slab_most = 2 * image_rows // seq_count
    image = stepped.reshape(FRAMES, token_rows, LAT_W // 2, 2, 2, LAT_CH)
    image = (
        jnp.transpose(image, (0, 1, 3, 2, 4, 5))
        .reshape(FRAMES, image_rows, LAT_W, LAT_CH)
    )
    padded = jnp.concatenate([image[:1], image[:1], image], 0)
    padded = jnp.pad(padded, ((0, 0), (1, 1 + slab_most), (1, 1), (0, 0)))
    positions = jnp.arange(seq_count)
    slab_count = jnp.sum(jnp.where(positions == seq_index, slab_rows, 0))
    slab_start = jnp.sum(jnp.where(positions < seq_index, slab_rows, 0))
    window = lax.dynamic_slice_in_dim(padded, slab_start, slab_most + 2, 1)
    pieces = []
    for frame_shift in range(3):
        for row_shift in range(3):
            for col_shift in range(3):
                pieces.append(
                    window[
                        frame_shift : frame_shift + FRAMES,
                        row_shift : row_shift + slab_most,
                        col_shift : col_shift + LAT_W,
                    ]
                )
    columns = jnp.concatenate(pieces, -1).reshape(FRAMES * slab_most * LAT_W, 27 * LAT_CH)
    kernel = w_conv.reshape(27 * LAT_CH, w_conv.shape[2])
    features = jnp.dot(columns, kernel, preferred_element_type=jnp.float32).astype(jnp.bfloat16)
    features = features.reshape(FRAMES, slab_most, LAT_W, w_conv.shape[2])
    row_valid = jnp.arange(slab_most)[None, :, None, None] < slab_count
    decoded = jnp.where(row_valid, features, jnp.zeros_like(features))
    return decoded[None]


def solution(mesh):
    in_specs = (
        P(None, ("groups", "seq"), None),
        P(),
        P("segment", "seq", None),
        P("segment", "seq", None),
        P(),
        P("cfg", ("groups", "segment"), None, None),
        P("segment", "cfg", "seq", None, "groups", None),
        P(),
        P(None, None, ("segment", "cfg")),
        P("groups"),
        P("groups"),
        P("groups"),
    )
    out_specs = (
        P(None, ("groups", "seq"), None),
        P(("groups", "seq"), None, None, None, ("segment", "cfg")),
    )
    whole_groups = 2 <= mesh.shape["seq"] <= 8
    program = shards if whole_groups else cycled_shards
    return jax.shard_map(program, mesh=mesh, in_specs=in_specs, out_specs=out_specs, check_vma=False)
```
